32 devices in a mesh: parts: 2 (over y), chan: 4 (over z), lad: 2 (over x), sub: 2 (over core).
Axes of the slice: x: 2, y: 2, z: 4, core: 2. Of those that a mesh axis runs over, the one named last changes fastest.
Arguments:
- amplitudes: bfloat16 [8, 3072, 512], P(('parts', 'chan'), ('lad', 'sub')), parts along dimension 0, may hold values from -6 to 6
- driving: bfloat16 [8, 3072, 512], P(('parts', 'chan'), ('lad', 'sub')), parts along dimension 0, may hold values from -6 to 6
- route: int32 [4, 3072, 1], P('chan', ('lad', 'sub')), may hold values from 0 to 3; in each aligned block of 768 rows (0 to 767, 768 to 1535, ..., all dimensions but the last counted through in order) at most 384 rows name the same one
- ladder_weight: bfloat16 [4, 3072, 3072], P('chan', None, ('lad', 'sub')), may hold values from -0.15625 to 0.15625
- ph_weight: bfloat16 [4, 4, 1536, 1536], P('chan', ('lad', 'sub')), may hold values from -0.15625 to 0.15625
- recouple: bfloat16 [4, 4, 12, 128, 128], P('chan', ('lad', 'sub')), may hold values from -1 to 2, as said below
- gap_part: float32 [8, 3072], P(('parts', 'chan'), ('lad', 'sub')), parts along dimension 0, may hold values from 1 to 4
- gap_hole: float32 [1024], P('parts'), parts along dimension 0, may hold values from 1 to 4
Outputs:
- updated: bfloat16 [8, 3072, 512], P(('parts', 'chan'), ('lad', 'sub')), parts along dimension 0
The draws below stay inside these ranges and needn't reach their ends.
There are 2 independent parts, one for each index of `parts`. The reference program is written for one: setup_inputs(seed, part) draws one part's arguments, and reference() takes and returns one part's arrays. A program takes and returns all parts, laid end to end along the dimension named above; an argument that names none is the same for every part. Nothing has to cross between parts.
Inputs may be any that keep to these rules, and one draw needn't show every extreme that they name: `route`: in each aligned block of 768 rows (the rows of one device), at most 384 rows name one cycle block, and some cycle block is named by exactly 384 rows in some blocks. `recouple`: each mixing matrix is the identity plus independent coefficients.
All inputs are finite; a program needn't handle non-finite values.
Results may differ from the reference program's by a relative error of at most 0.007.
Values may be sent and summed in bfloat16 or wider, within the bound.
No kernel may reach another device: no remote copies, remote signals or barrier semaphores. Data moves between devices by JAX's collectives and lax.ppermute only.
A program may use at most 64 MiB of HBM per device.

```python
import math
import jax
import jax.numpy as jnp
import numpy as np
from jax import lax

PP = 3072
HH = 512
GRP = 128
NG = 4
ROWS = 768
CAP = 1536
SEND = 384
GROUPS = 12
N_CHAN = 4


def draw_recouple(key, part):
    key = jax.random.fold_in(key, 7)
    block_shape = (N_CHAN, NG, GROUPS, GRP, GRP)
    spread = 0.5 / math.sqrt(GRP)
    offdiag = spread * jax.random.normal(key, block_shape, jnp.float32)
    identity = jnp.eye(GRP, dtype=jnp.float32)
    return (identity + offdiag).astype(jnp.bfloat16)


def spiked(drawn, own_key, source, target, parts, factor):
    def block_of(axis_at):
        return (jnp.arange(drawn.shape[axis_at]) // (drawn.shape[axis_at] // parts)).reshape((-1,) + (1,) * (drawn.ndim - 1 - axis_at))

    first = jax.random.permutation(own_key, parts)[block_of(target)]
    other_side = (block_of(target) + parts // 2) % parts
    return jnp.where((block_of(source) == first) | (block_of(source) == other_side), factor * drawn, drawn)


def levels(stream_key, shape, cuts, low, high):
    level = 1.0
    for dim, shards_of in cuts:
        steps = jax.random.uniform(jax.random.fold_in(jax.random.fold_in(stream_key, 6), dim), (shards_of,), jnp.float32, low / len(cuts), high / len(cuts))
        level = level * jnp.repeat(jnp.exp(steps), shape[dim] // shards_of).reshape((-1,) + (1,) * (len(shape) - 1 - dim))
    return level


def shared_out(stream_key, own, number, rows, number_of, top, reach, lean):
    sequence = jax.random.permutation(stream_key, number_of)
    heavy_load, usual = portions_of(number_of, rows * top, reach, lean, True), portions_of(number_of, rows * top, reach, lean, False)
    places = jnp.arange(number_of)

    def named(tallies, rotation):
        used = int((tallies > 0).sum())
        fixed = max(1, used // 4)
        passed = fixed + (places - fixed + rotation * (used - fixed)) % max(1, number_of - fixed)
        return jnp.zeros((number_of,), jnp.int32).at[sequence[jnp.where(places < fixed, places, passed)]].set(jnp.asarray(tallies, jnp.int32))

    tallies = jnp.where(number % 4 == 0, named(heavy_load, number // 4), named(usual, number - number // 4 - 1))
    mixed = jax.random.permutation(jax.random.fold_in(own, 3), number_of)
    giver, receiver = mixed[0:number_of // 2 * 2:2], mixed[1:number_of // 2 * 2:2]
    slack = jnp.minimum(tallies[giver] - 1, reach - tallies[receiver]) // 2
    slack = jnp.where((giver == sequence[0]) | (receiver == sequence[0]) | (tallies[receiver] == 0), 0, jnp.maximum(slack, 0))
    passed = jax.random.randint(jax.random.fold_in(own, 4), (number_of // 2,), 0, 1 << 20) % (slack + 1)
    tallies = tallies.at[giver].add(-passed).at[receiver].add(passed)
    items = jnp.searchsorted(jnp.cumsum(tallies), jnp.arange(rows * top), side="right").astype(jnp.int32)
    table = items.reshape(top, rows).T
    table = table[jax.random.permutation(jax.random.fold_in(own, 1), rows)]
    rotation = jax.random.randint(jax.random.fold_in(own, 2), (rows, 1), 0, top)
    return jnp.take_along_axis(table, (jnp.arange(top)[None, :] + rotation) % top, axis=1)


def portions_of(count, total, bound, lean, full):
    weights = [(1 << 20) // math.isqrt(rank ** lean) + 1 for rank in range(1, count + 1)]
    largest = bound if full else min(bound, max(-(-total // count), total * weights[0] // sum(weights)))
    least = 1 if total - largest >= count - 1 else 0
    holding, rest = [largest] + [least] * (count - 1), total - largest - least * (count - 1)
    while rest > 0:
        free = [i for i in range(1, count) if holding[i] < largest] or [i for i in range(1, count) if holding[i] < bound]
        pool, budget = sum([weights[i] for i in free]), rest
        for i in free:
            addition = min(bound - holding[i], max(1, budget * weights[i] // pool), rest)
            holding[i] = holding[i] + addition
            rest = rest - addition
    return np.array(holding)


def noise(own_key, extent, scale, most, cuts=(), held_as=jnp.bfloat16):
    array = scale * jax.random.normal(own_key, extent, jnp.float32)
    if cuts:
        array = array * levels(own_key, extent, cuts, -0.22, 0.18)
    return jnp.clip(array, -most, most).astype(held_as)


def noise_with(own_key, extent, deviation, most, cuts, heavy, kind=jnp.bfloat16):
    entries = deviation * jax.random.normal(own_key, extent, jnp.float32)
    if cuts:
        entries = entries * levels(own_key, extent, cuts, -0.22, 0.18)
    return jnp.clip(spiked(entries, jax.random.fold_in(own_key, 3), *heavy), -most, most).astype(kind)


def setup_inputs(seed: int = 0, part: int = 0) -> dict:
    splits = jax.random.split(jax.random.key(seed), 9)
    part_splits = jax.random.split(jax.random.fold_in(splits[8], part), 9)
    amplitudes = noise(part_splits[0], (N_CHAN, PP, HH), 1.0, 6.0, ((0, 4), (1, 4)))
    driving = noise(part_splits[1], (N_CHAN, PP, HH), 1.0, 6.0, ((0, 4), (1, 4)))
    route_keys = jax.random.split(jax.random.fold_in(splits[2], 1), N_CHAN * PP // ROWS)
    route_turns = jax.random.permutation(jax.random.fold_in(splits[2], 3), N_CHAN * PP // ROWS)
    route = jax.vmap(lambda own, number: shared_out(jax.random.fold_in(splits[2], 2), own, number, ROWS, N_CHAN, 1, SEND, 2))(route_keys, route_turns).reshape((N_CHAN, PP, 1))
    ladder_weight = noise_with(splits[3], (N_CHAN, PP, PP), PP ** -0.5, 0.15625, ((0, 4), (2, 4)), (2, 1, 4, 2.0))
    ph_weight = noise(splits[4], (N_CHAN, NG, CAP, CAP), CAP ** -0.5, 0.15625, ((0, 4), (1, 4)))
    recouple = draw_recouple(jax.random.fold_in(splits[8], 71), part)
    gap_part = jnp.clip(jnp.exp(math.log(4.0) - 1.3862944 * jax.random.uniform(part_splits[6], (N_CHAN, PP), jnp.float32) ** levels(part_splits[6], (N_CHAN, PP), ((0, 4), (1, 4)), -0.2, 0.2)), 1.0, 4.0)
    gap_hole = jnp.clip(jnp.exp(jax.random.uniform(part_splits[7], (HH,), jnp.float32, math.log(1.0), math.log(4.0))), 1.0, 4.0)
    return dict(amplitudes=amplitudes, driving=driving, route=route, ladder_weight=ladder_weight, ph_weight=ph_weight, recouple=recouple, gap_part=gap_part, gap_hole=gap_hole)


def cycle_block(operands):
    block, mixing, cycle_weight = operands
    grouped = block.reshape(GROUPS, GRP, HH).astype(jnp.float32)
    recoupled = jnp.einsum('gab,gbk->gak', mixing.astype(jnp.float32), grouped).astype(jnp.bfloat16)
    cycle_part = jnp.dot(cycle_weight, recoupled.reshape(CAP, HH), preferred_element_type=jnp.float32).astype(jnp.bfloat16)
    cycle_back = jnp.einsum('gba,gbk->gak', mixing.astype(jnp.float32), cycle_part.reshape(GROUPS, GRP, HH).astype(jnp.float32))
    return cycle_back.astype(jnp.bfloat16).reshape(CAP, HH)


def ladder_block(operands):
    weight, block_amps = operands
    columns = weight.reshape(PP, NG, ROWS).astype(jnp.float32)
    pieces = block_amps.reshape(NG, ROWS, HH).astype(jnp.float32)
    terms = jnp.einsum('ogr,grh->goh', columns, pieces).astype(jnp.bfloat16)
    terms = lax.optimization_barrier(terms)
    return jnp.sum(terms.astype(jnp.float32), axis=0)


def reference(amplitudes, driving, route, ladder_weight, ph_weight, recouple, gap_part, gap_hole):
    owners = route[:, :, 0].reshape(N_CHAN, NG, ROWS).astype(jnp.int32)
    one_hot = (owners[..., None] == jnp.arange(N_CHAN, dtype=jnp.int32)).astype(jnp.int32)
    earlier = (jnp.cumsum(one_hot, axis=2) - one_hot).astype(jnp.int32)
    slot_index = jnp.sum(earlier * one_hot, axis=3).astype(jnp.int32)
    source = jnp.arange(N_CHAN, dtype=jnp.int32)[:, None, None]
    group = jnp.arange(NG, dtype=jnp.int32)[None, :, None]
    target = (((owners * NG + group) * N_CHAN + source) * SEND + slot_index).reshape(-1).astype(jnp.int32)
    flat_amps = amplitudes.reshape(N_CHAN * PP, HH)
    gathered = jnp.zeros((N_CHAN * NG * CAP, HH), jnp.bfloat16).at[target].set(flat_amps)
    backs = lax.map(cycle_block, (gathered.reshape(N_CHAN * NG, CAP, HH),
                                 recouple.reshape(N_CHAN * NG, GROUPS, GRP, GRP),
                                 ph_weight.reshape(N_CHAN * NG, CAP, CAP)))
    returned = backs.reshape(N_CHAN * NG * CAP, HH)[target].reshape(N_CHAN, PP, HH)
    ladder = lax.map(ladder_block, (ladder_weight, amplitudes))
    gap_sum = gap_part[:, :, None] + gap_hole[None, None, :]
    total = driving.astype(jnp.float32) + ladder + returned.astype(jnp.float32)
    return (total / gap_sum).astype(jnp.bfloat16)
```

```python
import functools

import jax
import jax.numpy as jnp
from jax import lax
from jax.experimental import pallas as pl
from jax.experimental.pallas import tpu as pltpu
from jax.sharding import PartitionSpec as P

VMEM_LIMIT = 48 * 1024 * 1024
F32 = jnp.float32
BF16 = jnp.bfloat16


def params():
    return pltpu.CompilerParams(vmem_limit_bytes=VMEM_LIMIT)


def whole(memory=pltpu.VMEM):
    return pl.BlockSpec(memory_space=memory)


def selection(match):
    return jnp.where(match, 1.0, 0.0).astype(BF16)


def pack_kernel(chan_count, send, off_ref, route_ref, amps_ref, *out_refs):
    target_ref, block_refs = out_refs[0], out_refs[1:]
    owners = route_ref[...]
    rows = owners.shape[1]
    lanes = max(16, chan_count)
    hot = lax.broadcasted_iota(jnp.int32, (lanes, rows), 0) == owners
    before = selection(
        lax.broadcasted_iota(jnp.int32, (rows, rows), 0)
        < lax.broadcasted_iota(jnp.int32, (rows, rows), 1)
    )
    earlier = jnp.dot(selection(hot), before, preferred_element_type=F32)
    slot = jnp.sum(jnp.where(hot, earlier, 0.0), axis=0, keepdims=True)
    target = owners * send + slot.astype(jnp.int32)
    target_ref[...] = target
    place_rows(off_ref, target, amps_ref, block_refs)


def place_rows(off_ref, target, amps_ref, block_refs):
    for k, block_ref in enumerate(block_refs):
        slots = lax.broadcasted_iota(jnp.int32, (block_ref.shape[0], target.shape[1]), 0)
        pick = selection(slots == target - off_ref[k])
        block_ref[...] = jnp.dot(pick, amps_ref[...], preferred_element_type=F32).astype(BF16)


def more_kernel(off_ref, target_ref, amps_ref, *block_refs):
    place_rows(off_ref, target_ref[...], amps_ref, block_refs)


def pack(offsets, route_row, amps, chan_count, send, block_rows):
    rows, holes = amps.shape
    block = jax.ShapeDtypeStruct((block_rows, holes), BF16)
    count = offsets.shape[0]
    first = (count + 1) // 2
    outs = pl.pallas_call(
        functools.partial(pack_kernel, chan_count, send),
        out_shape=[jax.ShapeDtypeStruct((1, rows), jnp.int32)] + [block] * first,
        in_specs=[whole(pltpu.SMEM), whole(), whole()],
        out_specs=[whole()] * (1 + first),
        compiler_params=params(),
        name="pack_far",
    )(offsets[count - first :], route_row, amps)
    target, far = outs[0], list(outs[1:])
    near = []
    if count > first:
        near = pl.pallas_call(
            more_kernel,
            out_shape=[block] * (count - first),
            in_specs=[whole(pltpu.SMEM), whole(), whole()],
            out_specs=[whole()] * (count - first),
            compiler_params=params(),
            name="pack_near",
        )(offsets[: count - first], target, amps)
    return target, list(near) + far


def ladder_kernel(share_ref, weight_ref, amps_ref, out_ref):
    out_ref[...] = jnp.dot(weight_ref[...], amps_ref[...], preferred_element_type=F32).astype(BF16)[None]


def ladder_share(share, weight, amps, lad_count, sub_count):
    rows, holes = amps.shape
    return pl.pallas_call(
        ladder_kernel,
        out_shape=jax.ShapeDtypeStruct((lad_count, rows, holes), BF16),
        grid_spec=pltpu.PrefetchScalarGridSpec(
            num_scalar_prefetch=1,
            grid=(lad_count,),
            in_specs=[
                pl.BlockSpec((rows, rows), lambda i, share: (i * sub_count + share[0], 0)),
                pl.BlockSpec((rows, holes), lambda i, share: (0, 0)),
            ],
            out_specs=pl.BlockSpec((1, rows, holes), lambda i, share: (i, 0, 0)),
        ),
        compiler_params=params(),
        cost_estimate=pl.CostEstimate(
            flops=2 * lad_count * rows * rows * holes,
            bytes_accessed=2 * lad_count * rows * (rows + holes),
            transcendentals=0,
        ),
        name="ladder_share",
    )(share, weight, amps)


def operator_kernel(group, block_index, weight_ref, mixing_ref, out_ref, half_ref):
    k = pl.program_id(0)
    block_rows, capacity = weight_ref.shape
    per_block = block_rows // group
    for a in range(per_block):
        mix = mixing_ref[block_index[k] * per_block + a]
        half_ref[pl.ds(a * group, group), :] = lax.dot_general(
            mix,
            weight_ref[pl.ds(a * group, group), :],
            (((0,), (0,)), ((), ())),
            preferred_element_type=F32,
        ).astype(BF16)
    for j in range(capacity // block_rows):
        for b in range(per_block):
            at = block_index[j] * per_block + b
            columns = pl.ds(pl.multiple_of(at * group, group), group)
            out_ref[:, pl.ds(j * block_rows + b * group, group)] = jnp.dot(
                half_ref[:, columns], mixing_ref[at], preferred_element_type=F32
            ).astype(BF16)


def cycle_operator(block_index, weight, mixing, block_rows):
    capacity = weight.shape[0]
    group = mixing.shape[1]
    return pl.pallas_call(
        functools.partial(operator_kernel, group),
        out_shape=jax.ShapeDtypeStruct((capacity, capacity), BF16),
        grid_spec=pltpu.PrefetchScalarGridSpec(
            num_scalar_prefetch=1,
            grid=(capacity // block_rows,),
            in_specs=[
                pl.BlockSpec((block_rows, capacity), lambda k, index: (index[k], 0)),
                pl.BlockSpec(mixing.shape, lambda k, index: (0, 0, 0)),
            ],
            out_specs=pl.BlockSpec((block_rows, capacity), lambda k, index: (k, 0)),
            scratch_shapes=[pltpu.VMEM((block_rows, capacity), BF16)],
        ),
        compiler_params=params(),
        cost_estimate=pl.CostEstimate(
            flops=4 * capacity * capacity * group, bytes_accessed=4 * capacity * capacity, transcendentals=0
        ),
        name="cycle_operator",
    )(block_index, weight, mixing)


def cycle_kernel(operator_ref, *refs):
    count = len(refs) // 2
    in_refs, out_refs = refs[:count], refs[count:]
    block_rows = in_refs[0].shape[0]
    for k in reversed(range(count)):
        total = None
        for j in range(count):
            part = jnp.dot(
                operator_ref[pl.ds(k * block_rows, block_rows), pl.ds(j * block_rows, block_rows)],
                in_refs[j][...],
                preferred_element_type=F32,
            )
            total = part if total is None else total + part
        out_refs[k][...] = total.astype(BF16)


def apply_cycle(operator, blocks):
    return pl.pallas_call(
        cycle_kernel,
        out_shape=[jax.ShapeDtypeStruct(b.shape, BF16) for b in blocks],
        in_specs=[whole()] * (1 + len(blocks)),
        out_specs=[whole()] * len(blocks),
        compiler_params=params(),
        name="apply_cycle",
    )(operator, *blocks)


def finish_kernel(off_ref, target_ref, base_ref, part_ref, hole_ref, *refs):
    block_refs, out_ref = refs[:-1], refs[-1]
    total = base_ref[...]
    target = target_ref[...]
    for k, block_ref in enumerate(block_refs):
        slots = lax.broadcasted_iota(jnp.int32, (target.shape[0], block_ref.shape[0]), 1)
        pick = selection(slots == target - off_ref[k])
        total = total + jnp.dot(pick, block_ref[...], preferred_element_type=F32)
    out_ref[...] = (total / (part_ref[...] + hole_ref[...])).astype(BF16)


def finish(offsets, target_column, base, part_column, hole_row, blocks):
    rows, holes = base.shape
    tile = 128 if rows % 128 == 0 else rows
    row_spec = lambda width: pl.BlockSpec((tile, width), lambda i: (i, 0))
    return pl.pallas_call(
        finish_kernel,
        out_shape=jax.ShapeDtypeStruct((rows, holes), BF16),
        grid=(rows // tile,),
        in_specs=[whole(pltpu.SMEM), row_spec(1), row_spec(holes), row_spec(1), pl.BlockSpec((1, holes), lambda i: (0, 0))]
        + [pl.BlockSpec(b.shape, lambda i: (0, 0)) for b in blocks],
        out_specs=row_spec(holes),
        compiler_params=params(),
        name="finish",
    )(offsets, target_column, base, part_column, hole_row, *blocks)


def body(amplitudes, driving, route, ladder_weight, ph_weight, recouple, gap_part, gap_hole):
    amps = amplitudes[0]
    rows, holes = amps.shape
    chan_count = lax.axis_size("chan")
    lad_count = lax.axis_size("lad")
    sub_count = lax.axis_size("sub")
    chan, lad, sub = lax.axis_index("chan"), lax.axis_index("lad"), lax.axis_index("sub")
    weight, mixing = ph_weight[0, 0], recouple[0, 0]
    capacity = weight.shape[0]
    send = capacity // chan_count
    paired = send % mixing.shape[1] == 0 and chan_count & (chan_count - 1) == 0
    if paired:
        block_rows = send
        block_index = jnp.stack([chan ^ k for k in range(chan_count)]).astype(jnp.int32)
    else:
        block_rows = capacity
        block_index = jnp.zeros((1,), jnp.int32)
    offsets = block_index * block_rows

    def exchange(blocks):
        if not paired:
            whole_block = blocks[0].reshape(chan_count, send, holes)
            whole_block = lax.all_to_all(whole_block, "chan", split_axis=0, concat_axis=0, tiled=True)
            return [whole_block.reshape(capacity, holes)]
        arrived = [blocks[0]]
        for k in range(1, chan_count):
            pairs = [(i, i ^ k) for i in range(chan_count)]
            arrived.append(lax.ppermute(blocks[k], "chan", pairs))
        return arrived

    target, outgoing = pack(offsets, route[0].reshape(1, rows), amps, chan_count, send, block_rows)
    blocks = exchange(outgoing)

    kept = None
    for step in reversed(range(sub_count)):
        share = lax.rem(sub + step, sub_count).astype(jnp.int32).reshape(1)
        part = ladder_share(share, ladder_weight[0], amps, lad_count, sub_count)
        if step:
            pairs = [(i, (i + step) % sub_count) for i in range(sub_count)]
            part = lax.ppermute(part, "sub", pairs)
        kept = [part] if kept is None else kept + [part]

    def chip_sum(position):
        picked = [lax.dynamic_index_in_dim(p, position, 0, keepdims=False) for p in kept]
        return sum(p.astype(F32) for p in picked)

    base = driving[0].astype(F32) + chip_sum(lad)
    for step in range(1, lad_count):
        pairs = [(i, (i + step) % lad_count) for i in range(lad_count)]
        term = chip_sum(lax.rem(lad + step, lad_count)).astype(BF16)
        base = base + lax.ppermute(term, "lad", pairs).astype(F32)

    operator = cycle_operator(block_index, weight, mixing, block_rows)
    returned = exchange(apply_cycle(operator, blocks))
    updated = finish(
        offsets,
        target.reshape(rows, 1),
        base,
        gap_part[0].reshape(rows, 1),
        gap_hole.reshape(1, holes),
        returned,
    )
    return updated[None]


def solution(mesh):
    placed = (
        P(("parts", "chan"), ("lad", "sub"), None),
        P(("parts", "chan"), ("lad", "sub"), None),
        P("chan", ("lad", "sub"), None),
        P("chan", None, ("lad", "sub")),
        P("chan", ("lad", "sub"), None, None),
        P("chan", ("lad", "sub"), None, None, None),
        P(("parts", "chan"), ("lad", "sub")),
        P("parts"),
    )
    return jax.shard_map(
        body,
        mesh=mesh,
        in_specs=placed,
        out_specs=P(("parts", "chan"), ("lad", "sub"), None),
        check_vma=False,
    )
```

```python
import functools

import jax
import jax.numpy as jnp
from jax import lax
from jax.experimental import pallas as pl
from jax.experimental.pallas import tpu as pltpu
from jax.sharding import PartitionSpec as P

VMEM_LIMIT = 20 * 1024 * 1024
HALVES = 2
F32 = jnp.float32
BF16 = jnp.bfloat16
CHEAP = pl.CostEstimate(flops=0, bytes_accessed=0, transcendentals=0)
DEAR = pl.CostEstimate(flops=3 * 10**10, bytes_accessed=10**6, transcendentals=0)


def params():
    return pltpu.CompilerParams(vmem_limit_bytes=VMEM_LIMIT)


def whole(memory=pltpu.VMEM):
    return pl.BlockSpec(memory_space=memory)


def selection(match):
    return jnp.where(match, 1.0, 0.0).astype(BF16)


def place_rows(offset, target, amps, block_refs):
    slots = lax.broadcasted_iota(jnp.int32, (block_refs[0].shape[0], target.shape[1]), 0)
    pick = selection(slots == target - offset)
    for block_ref, columns in zip(block_refs, amps):
        block_ref[...] = jnp.dot(pick, columns, preferred_element_type=F32).astype(BF16)


def first_kernel(chan_count, send, off_ref, route_ref, amps_ref, target_ref, *block_refs):
    owners = route_ref[...]
    rows = owners.shape[1]
    lanes = max(16, chan_count)
    hot = lax.broadcasted_iota(jnp.int32, (lanes, rows), 0) == owners
    before = selection(
        lax.broadcasted_iota(jnp.int32, (rows, rows), 0)
        < lax.broadcasted_iota(jnp.int32, (rows, rows), 1)
    )
    earlier = jnp.dot(selection(hot), before, preferred_element_type=F32)
    slot = jnp.sum(jnp.where(hot, earlier, 0.0), axis=0, keepdims=True)
    target = owners * send + slot.astype(jnp.int32)
    target_ref[...] = target
    first = off_ref.shape[0] - len(block_refs)
    for i, block_ref in enumerate(block_refs):
        place_rows(off_ref[first + i], target, [amps_ref[:, : block_ref.shape[1]]], [block_ref])


def rest_kernel(parts, skipped, off_ref, target_ref, amps_ref, *block_refs):
    target = target_ref[...]
    width = amps_ref.shape[1] // parts
    columns = [amps_ref[:, pl.ds(h * width, width)] for h in range(parts)]
    left = list(block_refs)
    for k in range(off_ref.shape[0]):
        wanted = columns if k < skipped else columns[1:]
        refs, left = left[: len(wanted)], left[len(wanted) :]
        place_rows(off_ref[k], target, wanted, refs)


def pack(offsets, route_row, amps, chan_count, send, block_rows):
    rows, holes = amps.shape
    count = offsets.shape[0]
    far = count // 2 if count > 1 else 1
    near = count - far
    block = jax.ShapeDtypeStruct((block_rows, holes // HALVES), BF16)
    outs = pl.pallas_call(
        functools.partial(first_kernel, chan_count, send),
        out_shape=[jax.ShapeDtypeStruct((1, rows), jnp.int32)] + [block] * far,
        in_specs=[whole(pltpu.SMEM), whole(), whole()],
        out_specs=[whole()] * (1 + far),
        compiler_params=params(),
        cost_estimate=CHEAP,
        name="pack_first",
    )(offsets, route_row, amps)
    target, early = outs[0], list(outs[1:])
    number = near * HALVES + far * (HALVES - 1)
    late = list(
        pl.pallas_call(
            functools.partial(rest_kernel, HALVES, near),
            out_shape=[block] * number,
            in_specs=[whole(pltpu.SMEM), whole(), whole()],
            out_specs=[whole()] * number,
            compiler_params=params(),
            name="pack_rest",
        )(offsets, target, amps)
    )
    blocks = [[None] * count for _ in range(HALVES)]
    for k in range(count):
        if k >= near:
            blocks[0][k] = early[k - near]
        for h in range(0 if k < near else 1, HALVES):
            blocks[h][k] = late.pop(0)
    return target, blocks


def unpack_kernel(off_ref, target_ref, out_ref):
    count = off_ref.shape[0]
    rows, capacity = out_ref.shape
    block_rows = capacity // count
    target = target_ref[...]
    slots = lax.broadcasted_iota(jnp.int32, (rows, block_rows), 1)
    for k in range(count):
        out_ref[:, pl.ds(k * block_rows, block_rows)] = selection(slots == target - off_ref[k])


def unpack_matrix(offsets, target_column, capacity):
    return pl.pallas_call(
        unpack_kernel,
        out_shape=jax.ShapeDtypeStruct((target_column.shape[0], capacity), BF16),
        in_specs=[whole(pltpu.SMEM), whole()],
        out_specs=whole(),
        compiler_params=params(),
        cost_estimate=CHEAP,
        name="unpack_matrix",
    )(offsets, target_column)


def ladder_kernel(share_ref, weight_ref, amps_ref, out_ref):
    out_ref[...] = jnp.dot(weight_ref[...], amps_ref[...], preferred_element_type=F32).astype(BF16)[None]


def ladder_share(share, weight, amps, lad_count, sub_count):
    rows, holes = amps.shape
    return pl.pallas_call(
        ladder_kernel,
        out_shape=jax.ShapeDtypeStruct((lad_count, rows, holes), BF16),
        grid_spec=pltpu.PrefetchScalarGridSpec(
            num_scalar_prefetch=1,
            grid=(lad_count,),
            in_specs=[
                pl.BlockSpec((rows, rows), lambda i, share: (i * sub_count + share[0], 0)),
                pl.BlockSpec((rows, holes), lambda i, share: (0, 0)),
            ],
            out_specs=pl.BlockSpec((1, rows, holes), lambda i, share: (i, 0, 0)),
        ),
        compiler_params=params(),
        cost_estimate=CHEAP,
        name="ladder_share",
    )(share, weight, amps)


def operator_kernel(group, block_index, weight_ref, mixing_ref, out_ref, half_ref):
    k = pl.program_id(0)
    block_rows, capacity = weight_ref.shape
    per_block = block_rows // group
    for a in range(per_block):
        mix = mixing_ref[block_index[k] * per_block + a]
        half_ref[pl.ds(a * group, group), :] = lax.dot_general(
            mix,
            weight_ref[pl.ds(a * group, group), :],
            (((0,), (0,)), ((), ())),
            preferred_element_type=F32,
        ).astype(BF16)
    for j in range(capacity // block_rows):
        for b in range(per_block):
            at = block_index[j] * per_block + b
            columns = pl.ds(pl.multiple_of(at * group, group), group)
            out_ref[:, pl.ds(j * block_rows + b * group, group)] = jnp.dot(
                half_ref[:, columns], mixing_ref[at], preferred_element_type=F32
            ).astype(BF16)


def cycle_operator(block_index, weight, mixing, block_rows):
    capacity = weight.shape[0]
    group = mixing.shape[1]
    return pl.pallas_call(
        functools.partial(operator_kernel, group),
        out_shape=jax.ShapeDtypeStruct((capacity, capacity), BF16),
        grid_spec=pltpu.PrefetchScalarGridSpec(
            num_scalar_prefetch=1,
            grid=(capacity // block_rows,),
            in_specs=[
                pl.BlockSpec((block_rows, capacity), lambda k, index: (index[k], 0)),
                pl.BlockSpec(mixing.shape, lambda k, index: (0, 0, 0)),
            ],
            out_specs=pl.BlockSpec((block_rows, capacity), lambda k, index: (k, 0)),
            scratch_shapes=[pltpu.VMEM((block_rows, capacity), BF16)],
        ),
        compiler_params=params(),
        cost_estimate=CHEAP,
        name="cycle_operator",
    )(block_index, weight, mixing)


def cycle_kernel(operator_ref, *refs):
    count = len(refs) // 2
    in_refs, out_refs, block_ref = refs[:count], refs[count : 2 * count], refs[2 * count]
    block_rows = in_refs[0].shape[0]
    for j in range(count):
        block_ref[pl.ds(j * block_rows, block_rows), :] = in_refs[j][...]
    for k in reversed(range(count)):
        out_refs[k][...] = jnp.dot(
            operator_ref[pl.ds(k * block_rows, block_rows), :], block_ref[...], preferred_element_type=F32
        ).astype(BF16)


def apply_cycle(operator, blocks):
    return pl.pallas_call(
        cycle_kernel,
        out_shape=[jax.ShapeDtypeStruct(b.shape, BF16) for b in blocks],
        in_specs=[whole()] * (1 + len(blocks)),
        out_specs=[whole()] * len(blocks),
        scratch_shapes=[pltpu.VMEM((operator.shape[0], blocks[0].shape[1]), BF16)],
        compiler_params=params(),
        cost_estimate=DEAR,
        name="apply_cycle",
    )(operator, *blocks)


def finish_kernel(pick_ref, base_ref, part_ref, hole_ref, *refs):
    out_ref = refs[-1]
    count = (pick_ref.shape[1]) // refs[0].shape[0]
    block_rows = refs[0].shape[0]
    total = base_ref[...]
    for k in range(count):
        total = total + jnp.dot(
            pick_ref[:, pl.ds(k * block_rows, block_rows)], refs[k][...], preferred_element_type=F32
        )
    out_ref[...] = (total / (part_ref[...] + hole_ref[...])).astype(BF16)


def finish(half, pick, base, part_column, hole_row, blocks, earlier):
    rows, holes = base.shape
    tile = rows // 2
    width = holes // HALVES
    in_specs = [
        pl.BlockSpec((tile, pick.shape[1]), lambda i: (i, 0)),
        pl.BlockSpec((tile, width), lambda i: (i, half)),
        pl.BlockSpec((tile, 1), lambda i: (i, 0)),
        pl.BlockSpec((1, width), lambda i: (0, half)),
    ] + [pl.BlockSpec(b.shape, lambda i: (0, 0)) for b in blocks]
    operands = [pick, base, part_column, hole_row, *blocks]
    aliases = {}
    if earlier is not None:
        aliases = {len(operands): 0}
        operands.append(earlier)
        in_specs.append(pl.BlockSpec(memory_space=pl.ANY))
    return pl.pallas_call(
        finish_kernel,
        out_shape=jax.ShapeDtypeStruct((rows, holes), BF16),
        grid=(rows // tile,),
        in_specs=in_specs,
        out_specs=pl.BlockSpec((tile, width), lambda i: (i, half)),
        input_output_aliases=aliases,
        compiler_params=params(),
        cost_estimate=CHEAP,
        name="finish",
    )(*operands)


def body(amplitudes, driving, route, ladder_weight, ph_weight, recouple, gap_part, gap_hole):
    amps = amplitudes[0]
    rows, holes = amps.shape
    chan_count = lax.axis_size("chan")
    lad_count = lax.axis_size("lad")
    sub_count = lax.axis_size("sub")
    chan, lad, sub = lax.axis_index("chan"), lax.axis_index("lad"), lax.axis_index("sub")
    weight, mixing = ph_weight[0, 0], recouple[0, 0]
    capacity = weight.shape[0]
    send = capacity // chan_count
    paired = send % mixing.shape[1] == 0 and chan_count & (chan_count - 1) == 0
    if paired:
        block_rows = send
        block_index = jnp.stack([chan ^ k for k in range(chan_count)]).astype(jnp.int32)
    else:
        block_rows = capacity
        block_index = jnp.zeros((1,), jnp.int32)
    offsets = block_index * block_rows

    def exchange(blocks):
        if not paired:
            split = blocks[0].reshape(chan_count, send, -1)
            split = lax.all_to_all(split, "chan", split_axis=0, concat_axis=0, tiled=True)
            return [split.reshape(capacity, -1)]
        arrived = [blocks[0]] + [None] * (chan_count - 1)
        for k in reversed(range(1, chan_count)):
            pairs = [(i, i ^ k) for i in range(chan_count)]
            arrived[k] = lax.ppermute(blocks[k], "chan", pairs)
        return arrived

    target, outgoing = pack(offsets, route[0].reshape(1, rows), amps, chan_count, send, block_rows)
    blocks = [exchange(part) for part in outgoing]
    amps, outgoing = lax.optimization_barrier((amps, outgoing))
    pick = unpack_matrix(offsets, target.reshape(rows, 1), capacity)

    kept = None
    for step in reversed(range(sub_count)):
        share = lax.rem(sub + step, sub_count).astype(jnp.int32).reshape(1)
        part = ladder_share(share, ladder_weight[0], amps, lad_count, sub_count)
        if step:
            pairs = [(i, (i + step) % sub_count) for i in range(sub_count)]
            part = lax.ppermute(part, "sub", pairs)
        kept = [part] if kept is None else kept + [part]

    def chip_sum(position):
        picked = [lax.dynamic_index_in_dim(p, position, 0, keepdims=False) for p in kept]
        return sum(p.astype(F32) for p in picked)

    base = driving[0].astype(F32) + chip_sum(lad)
    for step in range(1, lad_count):
        pairs = [(i, (i + step) % lad_count) for i in range(lad_count)]
        term = chip_sum(lax.rem(lad + step, lad_count)).astype(BF16)
        base = base + lax.ppermute(term, "lad", pairs).astype(F32)

    operator = cycle_operator(block_index, weight, mixing, block_rows)
    part_column, hole_row = gap_part[0].reshape(rows, 1), gap_hole.reshape(1, holes)
    returned = [exchange(apply_cycle(operator, part)) for part in blocks]
    updated = None
    for half in range(HALVES):
        updated = finish(half, pick, base, part_column, hole_row, returned[half], updated)
    return updated[None]


def solution(mesh):
    placed = (
        P(("parts", "chan"), ("lad", "sub"), None),
        P(("parts", "chan"), ("lad", "sub"), None),
        P("chan", ("lad", "sub"), None),
        P("chan", None, ("lad", "sub")),
        P("chan", ("lad", "sub"), None, None),
        P("chan", ("lad", "sub"), None, None, None),
        P(("parts", "chan"), ("lad", "sub")),
        P("parts"),
    )
    return jax.shard_map(
        body,
        mesh=mesh,
        in_specs=placed,
        out_specs=P(("parts", "chan"), ("lad", "sub"), None),
        check_vma=False,
    )
```

```python
import functools

import jax
import jax.numpy as jnp
from jax import lax
from jax.experimental import pallas as pl
from jax.experimental.pallas import tpu as pltpu
from jax.sharding import PartitionSpec as P

VMEM_LIMIT = 20 * 1024 * 1024
HALVES = 2
F32 = jnp.float32
BF16 = jnp.bfloat16
CHEAP = pl.CostEstimate(flops=0, bytes_accessed=0, transcendentals=0)
DEAR = pl.CostEstimate(flops=3 * 10**10, bytes_accessed=10**6, transcendentals=0)


def params():
    return pltpu.CompilerParams(vmem_limit_bytes=VMEM_LIMIT)


def whole(memory=pltpu.VMEM):
    return pl.BlockSpec(memory_space=memory)


def selection(match):
    return jnp.where(match, 1.0, 0.0).astype(BF16)


def pack_kernel(chan_count, send, off_ref, route_hbm, amps_hbm, target_ref, *refs):
    block_refs, (route_ref, amps_ref, sems) = refs[:-3], refs[-3:]
    rows, width = amps_ref.shape[0], amps_ref.shape[1] // HALVES
    parts = [pl.ds(h * width, width) for h in range(HALVES)]
    copies = [pltpu.make_async_copy(route_hbm, route_ref, sems.at[0])] + [
        pltpu.make_async_copy(amps_hbm.at[:, part], amps_ref.at[:, part], sems.at[1 + h])
        for h, part in enumerate(parts)
    ]
    for copy in copies:
        copy.start()
    lane = 128
    pieces = rows // lane
    before = selection(
        lax.broadcasted_iota(jnp.int32, (lane, 2 * lane), 0)
        < lax.broadcasted_iota(jnp.int32, (lane, 2 * lane), 1)
    )
    names = max(16, chan_count)
    copies[0].wait()
    owners = route_ref[...]
    hot = [
        lax.broadcasted_iota(jnp.int32, (names, lane), 0) == owners[:, i * lane : (i + 1) * lane]
        for i in range(pieces)
    ]
    counts = jnp.dot(
        jnp.concatenate([selection(h) for h in hot], axis=0), before, preferred_element_type=F32
    )
    passed = jnp.zeros((names, lane), F32)
    slots = []
    for i in range(pieces):
        within = counts[i * names : (i + 1) * names]
        slots.append(jnp.sum(jnp.where(hot[i], within[:, :lane] + passed, 0.0), axis=0, keepdims=True))
        passed = passed + within[:, lane:]
    target = owners * send + jnp.concatenate(slots, axis=1).astype(jnp.int32)
    target_ref[...] = target
    count = off_ref.shape[0]
    slot = lax.broadcasted_iota(jnp.int32, (block_refs[0].shape[0], rows), 0)
    for k in reversed(range(count)):
        pick = selection(slot == target - off_ref[k])
        for h in range(HALVES):
            if k == count - 1:
                copies[1 + h].wait()
            block_refs[k * HALVES + h][...] = jnp.dot(
                pick, amps_ref[:, parts[h]], preferred_element_type=F32
            ).astype(BF16)


def pack(offsets, route_row, amps, chan_count, send, block_rows):
    rows, holes = amps.shape
    count = offsets.shape[0]
    block = jax.ShapeDtypeStruct((block_rows, holes // HALVES), BF16)
    outs = pl.pallas_call(
        functools.partial(pack_kernel, chan_count, send),
        out_shape=[jax.ShapeDtypeStruct((1, rows), jnp.int32)] + [block] * (count * HALVES),
        in_specs=[whole(pltpu.SMEM), whole(pltpu.HBM), whole(pltpu.HBM)],
        out_specs=[whole()] * (1 + count * HALVES),
        scratch_shapes=[
            pltpu.VMEM((1, rows), jnp.int32),
            pltpu.VMEM((rows, holes), BF16),
            pltpu.SemaphoreType.DMA((1 + HALVES,)),
        ],
        compiler_params=params(),
        name="pack",
    )(offsets, route_row, amps)
    return outs[0], [[outs[1 + k * HALVES + h] for k in range(count)] for h in range(HALVES)]


def unpack_kernel(off_ref, target_ref, out_ref):
    count = off_ref.shape[0]
    rows, capacity = out_ref.shape
    block_rows = capacity // count
    target = target_ref[...]
    slots = lax.broadcasted_iota(jnp.int32, (rows, block_rows), 1)
    for k in range(count):
        out_ref[:, pl.ds(k * block_rows, block_rows)] = selection(slots == target - off_ref[k])


def unpack_matrix(offsets, target_column, capacity):
    return pl.pallas_call(
        unpack_kernel,
        out_shape=jax.ShapeDtypeStruct((target_column.shape[0], capacity), BF16),
        in_specs=[whole(pltpu.SMEM), whole()],
        out_specs=whole(),
        compiler_params=params(),
        cost_estimate=CHEAP,
        name="unpack_matrix",
    )(offsets, target_column)


def ladder_kernel(share_ref, weight_ref, amps_ref, out_ref):
    out_ref[...] = jnp.dot(weight_ref[...], amps_ref[...], preferred_element_type=F32).astype(BF16)[None]


def ladder_share(share, weight, amps, lad_count, sub_count):
    rows, holes = amps.shape
    return pl.pallas_call(
        ladder_kernel,
        out_shape=jax.ShapeDtypeStruct((lad_count, rows, holes), BF16),
        grid_spec=pltpu.PrefetchScalarGridSpec(
            num_scalar_prefetch=1,
            grid=(lad_count,),
            in_specs=[
                pl.BlockSpec((rows, rows), lambda i, share: (i * sub_count + share[0], 0)),
                pl.BlockSpec((rows, holes), lambda i, share: (0, 0)),
            ],
            out_specs=pl.BlockSpec((1, rows, holes), lambda i, share: (i, 0, 0)),
        ),
        compiler_params=params(),
        cost_estimate=CHEAP,
        name="ladder_share",
    )(share, weight, amps)


def operator_kernel(group, block_index, weight_ref, mixing_ref, out_ref, half_ref):
    k = pl.program_id(0)
    block_rows, capacity = weight_ref.shape
    per_block = block_rows // group
    for a in range(per_block):
        mix = mixing_ref[block_index[k] * per_block + a]
        half_ref[pl.ds(a * group, group), :] = lax.dot_general(
            mix,
            weight_ref[pl.ds(a * group, group), :],
            (((0,), (0,)), ((), ())),
            preferred_element_type=F32,
        ).astype(BF16)
    for j in range(capacity // block_rows):
        for b in range(per_block):
            at = block_index[j] * per_block + b
            columns = pl.ds(pl.multiple_of(at * group, group), group)
            out_ref[:, pl.ds(j * block_rows + b * group, group)] = jnp.dot(
                half_ref[:, columns], mixing_ref[at], preferred_element_type=F32
            ).astype(BF16)


def cycle_operator(block_index, weight, mixing, block_rows):
    capacity = weight.shape[0]
    group = mixing.shape[1]
    return pl.pallas_call(
        functools.partial(operator_kernel, group),
        out_shape=jax.ShapeDtypeStruct((capacity, capacity), BF16),
        grid_spec=pltpu.PrefetchScalarGridSpec(
            num_scalar_prefetch=1,
            grid=(capacity // block_rows,),
            in_specs=[
                pl.BlockSpec((block_rows, capacity), lambda k, index: (index[k], 0)),
                pl.BlockSpec(mixing.shape, lambda k, index: (0, 0, 0)),
            ],
            out_specs=pl.BlockSpec((block_rows, capacity), lambda k, index: (k, 0)),
            scratch_shapes=[pltpu.VMEM((block_rows, capacity), BF16)],
        ),
        compiler_params=params(),
        cost_estimate=CHEAP,
        name="cycle_operator",
    )(block_index, weight, mixing)


def cycle_kernel(operator_ref, *refs):
    count = len(refs) // 2
    in_refs, out_refs, block_ref = refs[:count], refs[count : 2 * count], refs[2 * count]
    block_rows = in_refs[0].shape[0]
    for j in range(count):
        block_ref[pl.ds(j * block_rows, block_rows), :] = in_refs[count - 1 - j][...]
    for k in reversed(range(count)):
        out_refs[count - 1 - k][...] = jnp.dot(
            operator_ref[pl.ds(k * block_rows, block_rows), :], block_ref[...], preferred_element_type=F32
        ).astype(BF16)


def apply_cycle(operator, blocks):
    outs = pl.pallas_call(
        cycle_kernel,
        out_shape=[jax.ShapeDtypeStruct(b.shape, BF16) for b in blocks],
        in_specs=[whole()] * (1 + len(blocks)),
        out_specs=[whole()] * len(blocks),
        scratch_shapes=[pltpu.VMEM((operator.shape[0], blocks[0].shape[1]), BF16)],
        compiler_params=params(),
        cost_estimate=DEAR,
        name="apply_cycle",
    )(operator, *reversed(blocks))
    return list(reversed(outs))


def finish_kernel(half, count, tiles, pick_ref, base_ref, part_ref, hole_ref, *refs):
    in_refs, (out_hbm, block_ref, out_ref, sems) = refs[:count], refs[-4:]
    block_rows, width = in_refs[0].shape
    tile = out_ref.shape[0] // tiles
    columns = pl.ds(half * width, width)
    for k in range(count):
        block_ref[pl.ds(k * block_rows, block_rows), :] = in_refs[count - 1 - k][...]
    copies = []
    for t in range(tiles):
        at = pl.ds(t * tile, tile)
        back = jnp.dot(pick_ref[at, :], block_ref[...], preferred_element_type=F32)
        total = base_ref[at, columns] + back
        out_ref[at, :] = (total / (part_ref[at, :] + hole_ref[:, columns])).astype(BF16)
        copies.append(pltpu.make_async_copy(out_ref.at[at, :], out_hbm.at[at, columns], sems.at[t]))
        copies[-1].start()
    for copy in copies:
        copy.wait()


def finish(half, pick, base, part_column, hole_row, blocks, earlier):
    rows, holes = base.shape
    tiles = 3
    count, width = len(blocks), blocks[0].shape[1]
    operands = [pick, base, part_column, hole_row, *reversed(blocks)]
    in_specs = [whole()] * len(operands)
    aliases = {}
    if earlier is not None:
        aliases = {len(operands): 0}
        operands.append(earlier)
        in_specs.append(whole(pltpu.HBM))
    return pl.pallas_call(
        functools.partial(finish_kernel, half, count, tiles),
        out_shape=jax.ShapeDtypeStruct((rows, holes), BF16),
        in_specs=in_specs,
        out_specs=whole(pltpu.HBM),
        scratch_shapes=[
            pltpu.VMEM((pick.shape[1], width), BF16),
            pltpu.VMEM((rows, width), BF16),
            pltpu.SemaphoreType.DMA((tiles,)),
        ],
        input_output_aliases=aliases,
        compiler_params=params(),
        cost_estimate=CHEAP,
        name="finish",
    )(*operands)


def body(amplitudes, driving, route, ladder_weight, ph_weight, recouple, gap_part, gap_hole):
    amps = amplitudes[0]
    rows, holes = amps.shape
    chan_count = lax.axis_size("chan")
    lad_count = lax.axis_size("lad")
    sub_count = lax.axis_size("sub")
    chan, lad, sub = lax.axis_index("chan"), lax.axis_index("lad"), lax.axis_index("sub")
    weight, mixing = ph_weight[0, 0], recouple[0, 0]
    capacity = weight.shape[0]
    send = capacity // chan_count
    paired = send % mixing.shape[1] == 0 and chan_count & (chan_count - 1) == 0
    if paired:
        block_rows = send
        block_index = jnp.stack([chan ^ k for k in range(chan_count)]).astype(jnp.int32)
    else:
        block_rows = capacity
        block_index = jnp.zeros((1,), jnp.int32)
    offsets = block_index * block_rows

    def exchange(blocks):
        if not paired:
            split = blocks[0].reshape(chan_count, send, -1)
            split = lax.all_to_all(split, "chan", split_axis=0, concat_axis=0, tiled=True)
            return [split.reshape(capacity, -1)]
        arrived = [blocks[0]] + [None] * (chan_count - 1)
        for k in reversed(range(1, chan_count)):
            pairs = [(i, i ^ k) for i in range(chan_count)]
            arrived[k] = lax.ppermute(blocks[k], "chan", pairs)
        return arrived

    target, outgoing = pack(offsets, route[0].reshape(1, rows), amps, chan_count, send, block_rows)
    blocks = [exchange(part) for part in outgoing]
    amps, outgoing = lax.optimization_barrier((amps, outgoing))
    pick = unpack_matrix(offsets, target.reshape(rows, 1), capacity)

    kept = None
    for step in reversed(range(sub_count)):
        share = lax.rem(sub + step, sub_count).astype(jnp.int32).reshape(1)
        part = ladder_share(share, ladder_weight[0], amps, lad_count, sub_count)
        if step:
            pairs = [(i, (i + step) % sub_count) for i in range(sub_count)]
            part = lax.ppermute(part, "sub", pairs)
        kept = [part] if kept is None else kept + [part]

    def chip_sum(position):
        picked = [lax.dynamic_index_in_dim(p, position, 0, keepdims=False) for p in kept]
        return sum(p.astype(F32) for p in picked)

    base = driving[0].astype(F32) + chip_sum(lad)
    for step in range(1, lad_count):
        pairs = [(i, (i + step) % lad_count) for i in range(lad_count)]
        term = chip_sum(lax.rem(lad + step, lad_count)).astype(BF16)
        base = base + lax.ppermute(term, "lad", pairs).astype(F32)

    operator = cycle_operator(block_index, weight, mixing, block_rows)
    part_column, hole_row = gap_part[0].reshape(rows, 1), gap_hole.reshape(1, holes)
    returned = [exchange(apply_cycle(operator, part)) for part in blocks]
    updated = None
    for half in range(HALVES):
        updated = finish(half, pick, base, part_column, hole_row, returned[half], updated)
    return updated[None]


def solution(mesh):
    placed = (
        P(("parts", "chan"), ("lad", "sub"), None),
        P(("parts", "chan"), ("lad", "sub"), None),
        P("chan", ("lad", "sub"), None),
        P("chan", None, ("lad", "sub")),
        P("chan", ("lad", "sub"), None, None),
        P("chan", ("lad", "sub"), None, None, None),
        P(("parts", "chan"), ("lad", "sub")),
        P("parts"),
    )
    return jax.shard_map(
        body,
        mesh=mesh,
        in_specs=placed,
        out_specs=P(("parts", "chan"), ("lad", "sub"), None),
        check_vma=False,
    )
```

```python
import functools

import jax
import jax.numpy as jnp
from jax import lax
from jax.experimental import pallas as pl
from jax.experimental.pallas import tpu as pltpu
from jax.sharding import PartitionSpec as P

VMEM_LIMIT = 24 * 1024 * 1024
VMEM_MOST = 60 * 1024 * 1024
HALVES = 2
F32 = jnp.float32
BF16 = jnp.bfloat16
CHEAP = pl.CostEstimate(flops=0, bytes_accessed=0, transcendentals=0)
DEAR = pl.CostEstimate(flops=3 * 10**10, bytes_accessed=10**6, transcendentals=0)


def params(limit=VMEM_LIMIT):
    return pltpu.CompilerParams(vmem_limit_bytes=limit)


def whole(memory=pltpu.VMEM):
    return pl.BlockSpec(memory_space=memory)


def selection(match):
    return jnp.where(match, 1.0, 0.0).astype(BF16)


def parted(k, count):
    return count > 2 and k >= 2


def layout(count):
    far = [(k, h) for h in range(HALVES) for k in reversed(range(count)) if parted(k, count)]
    return far + [(k, None) for k in reversed(range(count)) if not parted(k, count)]


def pack_kernel(chan_count, send, off_ref, route_hbm, amps_hbm, *refs):
    items = layout(off_ref.shape[0])
    outs, (target_ref, route_ref, amps_ref, *kept) = refs[: len(items) + 1], refs[len(items) + 1 :]
    target_hbm, block_hbm = outs[0], outs[1:]
    block_refs, (in_sems, out_sems) = kept[: len(items)], kept[len(items) :]
    rows, holes = amps_ref.shape
    width = holes // HALVES
    parts = [pl.ds(h * width, width) for h in range(HALVES)]
    copies = [pltpu.make_async_copy(route_hbm, route_ref, in_sems.at[0])] + [
        pltpu.make_async_copy(amps_hbm.at[:, part], amps_ref.at[:, part], in_sems.at[1 + h])
        for h, part in enumerate(parts)
    ]
    for copy in copies:
        copy.start()
    lane = 128
    pieces = rows // lane
    before = selection(
        lax.broadcasted_iota(jnp.int32, (lane, 2 * lane), 0)
        < lax.broadcasted_iota(jnp.int32, (lane, 2 * lane), 1)
    )
    names = max(16, chan_count)
    copies[0].wait()
    owners = route_ref[...]
    hot = [
        lax.broadcasted_iota(jnp.int32, (names, lane), 0) == owners[:, i * lane : (i + 1) * lane]
        for i in range(pieces)
    ]
    counts = jnp.dot(
        jnp.concatenate([selection(h) for h in hot], axis=0), before, preferred_element_type=F32
    )
    passed = jnp.zeros((names, lane), F32)
    slots = []
    for i in range(pieces):
        within = counts[i * names : (i + 1) * names]
        slots.append(jnp.sum(jnp.where(hot[i], within[:, :lane] + passed, 0.0), axis=0, keepdims=True))
        passed = passed + within[:, lane:]
    target = owners * send + jnp.concatenate(slots, axis=1).astype(jnp.int32)
    target_ref[...] = target
    out_copies = [pltpu.make_async_copy(target_ref, target_hbm, out_sems.at[len(items)])]
    out_copies[0].start()
    for copy in copies[1:]:
        copy.wait()
    slot = lax.broadcasted_iota(jnp.int32, (block_refs[0].shape[0], rows), 0)
    picks = {}
    for i, (k, half) in enumerate(items):
        if k not in picks:
            picks[k] = selection(slot == target - off_ref[k])
        rows_in = amps_ref[...] if half is None else amps_ref[:, parts[half]]
        block_refs[i][...] = jnp.dot(picks[k], rows_in, preferred_element_type=F32).astype(BF16)
        out_copies.append(pltpu.make_async_copy(block_refs[i], block_hbm[i], out_sems.at[i]))
        out_copies[-1].start()
    for copy in out_copies:
        copy.wait()


def pack(offsets, route_row, amps, chan_count, send, block_rows):
    rows, holes = amps.shape
    items = layout(offsets.shape[0])
    shapes = [(block_rows, holes if half is None else holes // HALVES) for _, half in items]
    outs = pl.pallas_call(
        functools.partial(pack_kernel, chan_count, send),
        out_shape=[jax.ShapeDtypeStruct((1, rows), jnp.int32)]
        + [jax.ShapeDtypeStruct(shape, BF16) for shape in shapes],
        in_specs=[whole(pltpu.SMEM), whole(pl.ANY), whole(pl.ANY)],
        out_specs=[whole(pl.ANY)] * (1 + len(items)),
        scratch_shapes=[
            pltpu.VMEM((1, rows), jnp.int32),
            pltpu.VMEM((1, rows), jnp.int32),
            pltpu.VMEM((rows, holes), BF16),
        ]
        + [pltpu.VMEM(shape, BF16) for shape in shapes]
        + [pltpu.SemaphoreType.DMA((1 + HALVES,)), pltpu.SemaphoreType.DMA((1 + len(items),))],
        compiler_params=params(VMEM_MOST),
        name="pack",
    )(offsets, route_row, amps)
    return outs[0], dict(zip(items, outs[1:]))


def unpack_kernel(off_ref, target_ref, out_ref):
    count = off_ref.shape[0]
    rows, capacity = out_ref.shape
    block_rows = capacity // count
    target = target_ref[...]
    slots = lax.broadcasted_iota(jnp.int32, (rows, block_rows), 1)
    for k in range(count):
        out_ref[:, pl.ds(k * block_rows, block_rows)] = selection(slots == target - off_ref[k])


def unpack_matrix(offsets, target_column, capacity):
    return pl.pallas_call(
        unpack_kernel,
        out_shape=jax.ShapeDtypeStruct((target_column.shape[0], capacity), BF16),
        in_specs=[whole(pltpu.SMEM), whole()],
        out_specs=whole(),
        compiler_params=params(),
        cost_estimate=CHEAP,
        name="unpack_matrix",
    )(offsets, target_column)


def ladder_kernel(share_ref, weight_ref, amps_ref, out_ref):
    out_ref[...] = jnp.dot(weight_ref[...], amps_ref[...], preferred_element_type=F32).astype(BF16)[None]


def ladder_share(share, weight, amps, lad_count, sub_count):
    rows, holes = amps.shape
    return pl.pallas_call(
        ladder_kernel,
        out_shape=jax.ShapeDtypeStruct((lad_count, rows, holes), BF16),
        grid_spec=pltpu.PrefetchScalarGridSpec(
            num_scalar_prefetch=1,
            grid=(lad_count,),
            in_specs=[
                pl.BlockSpec((rows, rows), lambda i, share: (i * sub_count + share[0], 0)),
                pl.BlockSpec((rows, holes), lambda i, share: (0, 0)),
            ],
            out_specs=pl.BlockSpec((1, rows, holes), lambda i, share: (i, 0, 0)),
        ),
        compiler_params=params(VMEM_MOST),
        cost_estimate=CHEAP,
        name="ladder_share",
    )(share, weight, amps)


def operator_kernel(group, block_index, weight_ref, mixing_ref, out_ref, half_ref):
    k = pl.program_id(0)
    block_rows, capacity = weight_ref.shape
    per_block = block_rows // group
    for a in range(per_block):
        mix = mixing_ref[block_index[k] * per_block + a]
        half_ref[pl.ds(a * group, group), :] = lax.dot_general(
            mix,
            weight_ref[pl.ds(a * group, group), :],
            (((0,), (0,)), ((), ())),
            preferred_element_type=F32,
        ).astype(BF16)
    for j in range(capacity // block_rows):
        for b in range(per_block):
            at = block_index[j] * per_block + b
            columns = pl.ds(pl.multiple_of(at * group, group), group)
            out_ref[:, pl.ds(j * block_rows + b * group, group)] = jnp.dot(
                half_ref[:, columns], mixing_ref[at], preferred_element_type=F32
            ).astype(BF16)


def cycle_operator(block_index, weight, mixing, block_rows):
    capacity = weight.shape[0]
    group = mixing.shape[1]
    return pl.pallas_call(
        functools.partial(operator_kernel, group),
        out_shape=jax.ShapeDtypeStruct((capacity, capacity), BF16),
        grid_spec=pltpu.PrefetchScalarGridSpec(
            num_scalar_prefetch=1,
            grid=(capacity // block_rows,),
            in_specs=[
                pl.BlockSpec((block_rows, capacity), lambda k, index: (index[k], 0)),
                pl.BlockSpec(mixing.shape, lambda k, index: (0, 0, 0)),
            ],
            out_specs=pl.BlockSpec((block_rows, capacity), lambda k, index: (k, 0)),
            scratch_shapes=[pltpu.VMEM((block_rows, capacity), BF16)],
        ),
        compiler_params=params(),
        cost_estimate=CHEAP,
        name="cycle_operator",
    )(block_index, weight, mixing)


def cycle_kernel(half, operator_ref, *refs):
    count = len(refs) // 2
    in_refs, out_refs, block_ref = refs[:count], refs[count : 2 * count], refs[2 * count]
    block_rows, width = out_refs[0].shape
    for i, in_ref in enumerate(in_refs):
        at = pl.ds((count - 1 - i) * block_rows, block_rows)
        block_ref[at, :] = in_ref[...] if in_ref.shape[1] == width else in_ref[:, pl.ds(half * width, width)]
    for i, out_ref in enumerate(out_refs):
        at = pl.ds((count - 1 - i) * block_rows, block_rows)
        out_ref[...] = jnp.dot(operator_ref[at, :], block_ref[...], preferred_element_type=F32).astype(BF16)


def apply_cycle(half, operator, arrays, width):
    return pl.pallas_call(
        functools.partial(cycle_kernel, half),
        out_shape=[jax.ShapeDtypeStruct((a.shape[0], width), BF16) for a in arrays],
        in_specs=[whole()] * (1 + len(arrays)),
        out_specs=[whole()] * len(arrays),
        scratch_shapes=[pltpu.VMEM((operator.shape[0], width), BF16)],
        compiler_params=params(),
        cost_estimate=DEAR,
        name="apply_cycle",
    )(operator, *arrays)


def finish_kernel(half, count, tiles, pick_ref, base_ref, part_ref, hole_ref, *refs):
    in_refs, (out_hbm, block_ref, out_ref, sems) = refs[:count], refs[-4:]
    block_rows, width = in_refs[0].shape
    tile = out_ref.shape[0] // tiles
    columns = pl.ds(half * width, width)
    for i, in_ref in enumerate(in_refs):
        block_ref[pl.ds((count - 1 - i) * block_rows, block_rows), :] = in_ref[...]
    copies = []
    for t in range(tiles):
        at = pl.ds(t * tile, tile)
        back = jnp.dot(pick_ref[at, :], block_ref[...], preferred_element_type=F32)
        total = base_ref[at, columns] + back
        out_ref[at, :] = (total / (part_ref[at, :] + hole_ref[:, columns])).astype(BF16)
        copies.append(pltpu.make_async_copy(out_ref.at[at, :], out_hbm.at[at, columns], sems.at[t]))
        copies[-1].start()
    for copy in copies:
        copy.wait()


def finish(half, pick, base, part_column, hole_row, arrays, earlier):
    rows, holes = base.shape
    tiles, width = 3, holes // HALVES
    operands = [pick, base, part_column, hole_row, *arrays]
    in_specs = [whole()] * len(operands)
    aliases = {}
    if earlier is not None:
        aliases = {len(operands): 0}
        operands.append(earlier)
        in_specs.append(whole(pl.ANY))
    return pl.pallas_call(
        functools.partial(finish_kernel, half, len(arrays), tiles),
        out_shape=jax.ShapeDtypeStruct((rows, holes), BF16),
        in_specs=in_specs,
        out_specs=whole(pl.ANY),
        scratch_shapes=[
            pltpu.VMEM((pick.shape[1], width), BF16),
            pltpu.VMEM((rows, width), BF16),
            pltpu.SemaphoreType.DMA((tiles,)),
        ],
        input_output_aliases=aliases,
        compiler_params=params(),
        cost_estimate=CHEAP,
        name="finish",
    )(*operands)


def body(amplitudes, driving, route, ladder_weight, ph_weight, recouple, gap_part, gap_hole):
    amps = amplitudes[0]
    rows, holes = amps.shape
    chan_count = lax.axis_size("chan")
    lad_count = lax.axis_size("lad")
    sub_count = lax.axis_size("sub")
    chan, lad, sub = lax.axis_index("chan"), lax.axis_index("lad"), lax.axis_index("sub")
    weight, mixing = ph_weight[0, 0], recouple[0, 0]
    capacity = weight.shape[0]
    send = capacity // chan_count
    paired = send % mixing.shape[1] == 0 and chan_count & (chan_count - 1) == 0
    if paired:
        block_rows = send
        block_index = jnp.stack([chan ^ k for k in range(chan_count)]).astype(jnp.int32)
    else:
        block_rows = capacity
        block_index = jnp.zeros((1,), jnp.int32)
    offsets = block_index * block_rows

    def exchange(block, k):
        if not paired:
            split = block.reshape(chan_count, send, -1)
            split = lax.all_to_all(split, "chan", split_axis=0, concat_axis=0, tiled=True)
            return split.reshape(capacity, -1)
        return lax.ppermute(block, "chan", [(i, i ^ k) for i in range(chan_count)]) if k else block

    far_first = list(reversed(range(block_index.shape[0])))
    target, outgoing = pack(offsets, route[0].reshape(1, rows), amps, chan_count, send, block_rows)
    arrived = {item: exchange(block, item[0]) for item, block in outgoing.items()}
    amps, outgoing = lax.optimization_barrier((amps, outgoing))
    pick = unpack_matrix(offsets, target.reshape(rows, 1), capacity)

    kept = None
    for step in reversed(range(sub_count)):
        share = lax.rem(sub + step, sub_count).astype(jnp.int32).reshape(1)
        part = ladder_share(share, ladder_weight[0], amps, lad_count, sub_count)
        if step:
            pairs = [(i, (i + step) % sub_count) for i in range(sub_count)]
            part = lax.ppermute(part, "sub", pairs)
        kept = [part] if kept is None else kept + [part]

    def chip_sum(position):
        picked = [lax.dynamic_index_in_dim(p, position, 0, keepdims=False) for p in kept]
        return sum(p.astype(F32) for p in picked)

    base = driving[0].astype(F32) + chip_sum(lad)
    for step in range(1, lad_count):
        pairs = [(i, (i + step) % lad_count) for i in range(lad_count)]
        term = chip_sum(lax.rem(lad + step, lad_count)).astype(BF16)
        base = base + lax.ppermute(term, "lad", pairs).astype(F32)

    operator = cycle_operator(block_index, weight, mixing, block_rows)
    part_column, hole_row = gap_part[0].reshape(rows, 1), gap_hole.reshape(1, holes)
    returned = []
    for half in range(HALVES):
        blocks = [arrived[(k, half if parted(k, len(far_first)) else None)] for k in far_first]
        if returned:
            blocks, made = lax.optimization_barrier((blocks, made))
        made = apply_cycle(half, operator, blocks, holes // HALVES)
        returned.append([exchange(block, k) for k, block in zip(far_first, made)])
    updated = None
    for half in range(HALVES):
        updated = finish(half, pick, base, part_column, hole_row, returned[half], updated)
    return updated[None]


def solution(mesh):
    placed = (
        P(("parts", "chan"), ("lad", "sub"), None),
        P(("parts", "chan"), ("lad", "sub"), None),
        P("chan", ("lad", "sub"), None),
        P("chan", None, ("lad", "sub")),
        P("chan", ("lad", "sub"), None, None),
        P("chan", ("lad", "sub"), None, None, None),
        P(("parts", "chan"), ("lad", "sub")),
        P("parts"),
    )
    return jax.shard_map(
        body,
        mesh=mesh,
        in_specs=placed,
        out_specs=P(("parts", "chan"), ("lad", "sub"), None),
        check_vma=False,
    )
```

```python
import functools

import jax
import jax.numpy as jnp
from jax import lax
from jax.experimental import pallas as pl
from jax.experimental.pallas import tpu as pltpu
from jax.sharding import PartitionSpec as P

VMEM_LIMIT = 24 * 1024 * 1024
VMEM_MOST = 60 * 1024 * 1024
HALVES = 2
F32 = jnp.float32
BF16 = jnp.bfloat16
CHEAP = pl.CostEstimate(flops=0, bytes_accessed=0, transcendentals=0)
DEAR = pl.CostEstimate(flops=3 * 10**10, bytes_accessed=10**6, transcendentals=0)


def params(limit=VMEM_LIMIT):
    return pltpu.CompilerParams(vmem_limit_bytes=limit)


def whole(memory=pltpu.VMEM):
    return pl.BlockSpec(memory_space=memory)


def selection(match):
    return jnp.where(match, 1.0, 0.0).astype(BF16)


def block_offsets(paired, chan_count, block_rows):
    chan = lax.axis_index("chan")
    return [(chan ^ k) * block_rows for k in range(chan_count)] if paired else [0]


def slots_of(owners, send, names):
    lane = 128
    pieces = owners.shape[1] // lane
    before = selection(
        lax.broadcasted_iota(jnp.int32, (lane, 2 * lane), 0)
        < lax.broadcasted_iota(jnp.int32, (lane, 2 * lane), 1)
    )
    hot = [
        lax.broadcasted_iota(jnp.int32, (names, lane), 0) == owners[:, i * lane : (i + 1) * lane]
        for i in range(pieces)
    ]
    counts = jnp.dot(
        jnp.concatenate([selection(h) for h in hot], axis=0), before, preferred_element_type=F32
    )
    passed = jnp.zeros((names, lane), F32)
    slots = []
    for i in range(pieces):
        within = counts[i * names : (i + 1) * names]
        slots.append(jnp.sum(jnp.where(hot[i], within[:, :lane] + passed, 0.0), axis=0, keepdims=True))
        passed = passed + within[:, lane:]
    return owners * send + jnp.concatenate(slots, axis=1).astype(jnp.int32)


def pack_kernel(plan, given, route_hbm, amps_hbm, *refs):
    paired, chan_count, send, block_rows, items = plan
    extra = 0 if given else 1
    outs, (route_ref, amps_ref, *kept) = refs[: len(items) + extra], refs[len(items) + extra :]
    block_hbm, block_refs, (in_sems, out_sems) = outs[extra:], kept[: len(items)], kept[len(items) :]
    copies = [
        pltpu.make_async_copy(route_hbm, route_ref, in_sems.at[0]),
        pltpu.make_async_copy(amps_hbm.at[:, pl.ds(0, amps_ref.shape[1])], amps_ref, in_sems.at[1]),
    ]
    for copy in copies:
        copy.start()
    copies[0].wait()
    target = route_ref[...]
    out_copies = []
    if not given:
        target = slots_of(target, send, max(16, chan_count))
        route_ref[...] = target
        out_copies.append(pltpu.make_async_copy(route_ref, outs[0], out_sems.at[len(items)]))
        out_copies[0].start()
    offsets = block_offsets(paired, chan_count, block_rows)
    slot = lax.broadcasted_iota(jnp.int32, (block_rows, target.shape[1]), 0)
    for i, (k, first, width) in enumerate(items):
        pick = selection(slot == target - offsets[k])
        if i == 0:
            copies[1].wait()
        block_refs[i][...] = jnp.dot(
            pick, amps_ref[:, pl.ds(first, width)], preferred_element_type=F32
        ).astype(BF16)
        out_copies.append(pltpu.make_async_copy(block_refs[i], block_hbm[i], out_sems.at[i]))
        out_copies[-1].start()
    for copy in out_copies:
        copy.wait()


def pack(plan, given, route_row, amps, name):
    rows = amps.shape[0]
    block_rows, items = plan[3], plan[4]
    columns = max(first + width for _, first, width in items)
    shapes = [(block_rows, width) for _, _, width in items]
    extra = [] if given else [jax.ShapeDtypeStruct((1, rows), jnp.int32)]
    return pl.pallas_call(
        functools.partial(pack_kernel, plan, given),
        out_shape=extra + [jax.ShapeDtypeStruct(shape, BF16) for shape in shapes],
        in_specs=[whole(pl.ANY), whole(pl.ANY)],
        out_specs=[whole(pl.ANY)] * (len(extra) + len(items)),
        scratch_shapes=[pltpu.VMEM((1, rows), jnp.int32), pltpu.VMEM((rows, columns), BF16)]
        + [pltpu.VMEM(shape, BF16) for shape in shapes]
        + [pltpu.SemaphoreType.DMA((2,)), pltpu.SemaphoreType.DMA((1 + len(items),))],
        compiler_params=params(VMEM_LIMIT if given else VMEM_MOST),
        name=name,
    )(route_row, amps)


def unpack_kernel(off_ref, target_ref, out_ref):
    count = off_ref.shape[0]
    rows, capacity = out_ref.shape
    block_rows = capacity // count
    target = target_ref[...]
    slots = lax.broadcasted_iota(jnp.int32, (rows, block_rows), 1)
    for k in range(count):
        out_ref[:, pl.ds(k * block_rows, block_rows)] = selection(slots == target - off_ref[k])


def unpack_matrix(offsets, target_column, capacity):
    return pl.pallas_call(
        unpack_kernel,
        out_shape=jax.ShapeDtypeStruct((target_column.shape[0], capacity), BF16),
        in_specs=[whole(pltpu.SMEM), whole()],
        out_specs=whole(),
        compiler_params=params(),
        cost_estimate=CHEAP,
        name="unpack_matrix",
    )(offsets, target_column)


def ladder_kernel(share_ref, weight_ref, amps_ref, out_ref):
    out_ref[...] = jnp.dot(weight_ref[...], amps_ref[...], preferred_element_type=F32).astype(BF16)[None]


def ladder_share(share, weight, amps, lad_count, sub_count):
    rows, holes = amps.shape
    return pl.pallas_call(
        ladder_kernel,
        out_shape=jax.ShapeDtypeStruct((lad_count, rows, holes), BF16),
        grid_spec=pltpu.PrefetchScalarGridSpec(
            num_scalar_prefetch=1,
            grid=(lad_count,),
            in_specs=[
                pl.BlockSpec((rows, rows), lambda i, share: (i * sub_count + share[0], 0)),
                pl.BlockSpec((rows, holes), lambda i, share: (0, 0)),
            ],
            out_specs=pl.BlockSpec((1, rows, holes), lambda i, share: (i, 0, 0)),
        ),
        compiler_params=params(VMEM_MOST),
        cost_estimate=DEAR,
        name="ladder_share",
    )(share, weight, amps)


def operator_kernel(group, block_index, weight_ref, mixing_ref, out_ref, half_ref):
    k = pl.program_id(0)
    block_rows, capacity = weight_ref.shape
    per_block = block_rows // group
    for a in range(per_block):
        mix = mixing_ref[block_index[k] * per_block + a]
        half_ref[pl.ds(a * group, group), :] = lax.dot_general(
            mix,
            weight_ref[pl.ds(a * group, group), :],
            (((0,), (0,)), ((), ())),
            preferred_element_type=F32,
        ).astype(BF16)
    for j in range(capacity // block_rows):
        for b in range(per_block):
            at = block_index[j] * per_block + b
            columns = pl.ds(pl.multiple_of(at * group, group), group)
            out_ref[:, pl.ds(j * block_rows + b * group, group)] = jnp.dot(
                half_ref[:, columns], mixing_ref[at], preferred_element_type=F32
            ).astype(BF16)


def cycle_operator(block_index, weight, mixing, block_rows):
    capacity = weight.shape[0]
    group = mixing.shape[1]
    return pl.pallas_call(
        functools.partial(operator_kernel, group),
        out_shape=jax.ShapeDtypeStruct((capacity, capacity), BF16),
        grid_spec=pltpu.PrefetchScalarGridSpec(
            num_scalar_prefetch=1,
            grid=(capacity // block_rows,),
            in_specs=[
                pl.BlockSpec((block_rows, capacity), lambda k, index: (index[k], 0)),
                pl.BlockSpec(mixing.shape, lambda k, index: (0, 0, 0)),
            ],
            out_specs=pl.BlockSpec((block_rows, capacity), lambda k, index: (k, 0)),
            scratch_shapes=[pltpu.VMEM((block_rows, capacity), BF16)],
        ),
        compiler_params=params(),
        cost_estimate=CHEAP,
        name="cycle_operator",
    )(block_index, weight, mixing)


def cycle_kernel(half, operator_ref, *refs):
    count = len(refs) // 2
    in_refs, out_refs, block_ref = refs[:count], refs[count : 2 * count], refs[2 * count]
    block_rows, width = out_refs[0].shape
    for i, in_ref in enumerate(in_refs):
        at = pl.ds((count - 1 - i) * block_rows, block_rows)
        block_ref[at, :] = in_ref[...] if in_ref.shape[1] == width else in_ref[:, pl.ds(half * width, width)]
    for i, out_ref in enumerate(out_refs):
        at = pl.ds((count - 1 - i) * block_rows, block_rows)
        out_ref[...] = jnp.dot(operator_ref[at, :], block_ref[...], preferred_element_type=F32).astype(BF16)


def apply_cycle(half, operator, arrays, width):
    return pl.pallas_call(
        functools.partial(cycle_kernel, half),
        out_shape=[jax.ShapeDtypeStruct((a.shape[0], width), BF16) for a in arrays],
        in_specs=[whole()] * (1 + len(arrays)),
        out_specs=[whole()] * len(arrays),
        scratch_shapes=[pltpu.VMEM((operator.shape[0], width), BF16)],
        compiler_params=params(),
        cost_estimate=DEAR,
        name="apply_cycle",
    )(operator, *arrays)


def finish_kernel(half, count, tiles, pick_ref, base_ref, part_ref, hole_ref, *refs):
    in_refs, (out_hbm, block_ref, out_ref, sems) = refs[:count], refs[-4:]
    block_rows, width = in_refs[0].shape
    tile = out_ref.shape[0] // tiles
    columns = pl.ds(half * width, width)
    for i, in_ref in enumerate(in_refs):
        block_ref[pl.ds((count - 1 - i) * block_rows, block_rows), :] = in_ref[...]
    copies = []
    for t in range(tiles):
        at = pl.ds(t * tile, tile)
        back = jnp.dot(pick_ref[at, :], block_ref[...], preferred_element_type=F32)
        total = base_ref[at, columns] + back
        out_ref[at, :] = (total / (part_ref[at, :] + hole_ref[:, columns])).astype(BF16)
        copies.append(pltpu.make_async_copy(out_ref.at[at, :], out_hbm.at[at, columns], sems.at[t]))
        copies[-1].start()
    for copy in copies:
        copy.wait()


def finish(half, pick, base, part_column, hole_row, arrays, earlier):
    rows, holes = base.shape
    tiles, width = 3, holes // HALVES
    operands = [pick, base, part_column, hole_row, *arrays]
    in_specs = [whole()] * len(operands)
    aliases = {}
    if earlier is not None:
        aliases = {len(operands): 0}
        operands.append(earlier)
        in_specs.append(whole(pl.ANY))
    return pl.pallas_call(
        functools.partial(finish_kernel, half, len(arrays), tiles),
        out_shape=jax.ShapeDtypeStruct((rows, holes), BF16),
        in_specs=in_specs,
        out_specs=whole(pl.ANY),
        scratch_shapes=[
            pltpu.VMEM((pick.shape[1], width), BF16),
            pltpu.VMEM((rows, width), BF16),
            pltpu.SemaphoreType.DMA((tiles,)),
        ],
        input_output_aliases=aliases,
        compiler_params=params(),
        cost_estimate=CHEAP,
        name="finish",
    )(*operands)


def body(amplitudes, driving, route, ladder_weight, ph_weight, recouple, gap_part, gap_hole):
    amps = amplitudes[0]
    rows, holes = amps.shape
    chan_count = lax.axis_size("chan")
    lad_count = lax.axis_size("lad")
    sub_count = lax.axis_size("sub")
    chan, lad, sub = lax.axis_index("chan"), lax.axis_index("lad"), lax.axis_index("sub")
    weight, mixing = ph_weight[0, 0], recouple[0, 0]
    capacity = weight.shape[0]
    send = capacity // chan_count
    paired = send % mixing.shape[1] == 0 and chan_count & (chan_count - 1) == 0
    if paired:
        block_rows = send
        block_index = jnp.stack([chan ^ k for k in range(chan_count)]).astype(jnp.int32)
    else:
        block_rows = capacity
        block_index = jnp.zeros((1,), jnp.int32)
    offsets = block_index * block_rows

    def exchange(block, k):
        if not paired:
            split = block.reshape(chan_count, send, -1)
            split = lax.all_to_all(split, "chan", split_axis=0, concat_axis=0, tiled=True)
            return split.reshape(capacity, -1)
        return lax.ppermute(block, "chan", [(i, i ^ k) for i in range(chan_count)]) if k else block

    far_first = list(reversed(range(block_index.shape[0])))
    count = len(far_first)
    width = holes // HALVES
    route_row = route[0].reshape(1, rows)
    plan = (paired, chan_count, send, block_rows)
    early = [(k, 0, width) for k in far_first if k or not paired]
    late = [(k, h * width, width) for h in range(1, HALVES) for k in far_first if k or not paired]
    late += [(0, 0, holes)] if paired else []
    target, *blocks = pack(plan + (early,), False, route_row, amps, "pack_first")
    arrived = {(k, 0): exchange(block, k) for (k, _, _), block in zip(early, blocks)}
    amps, target = lax.optimization_barrier((amps, target))

    kept = None
    for step in reversed(range(sub_count)):
        share = lax.rem(sub + step, sub_count).astype(jnp.int32).reshape(1)
        part = ladder_share(share, ladder_weight[0], amps, lad_count, sub_count)
        if step:
            pairs = [(i, (i + step) % sub_count) for i in range(sub_count)]
            part = lax.ppermute(part, "sub", pairs)
        kept = [part] if kept is None else kept + [part]

    def chip_sum(position):
        picked = [lax.dynamic_index_in_dim(p, position, 0, keepdims=False) for p in kept]
        return sum(p.astype(F32) for p in picked)

    base = driving[0].astype(F32) + chip_sum(lad)
    terms = [chip_sum(lax.rem(lad + step, lad_count)).astype(BF16) for step in range(1, lad_count)]
    target, terms, weight = lax.optimization_barrier((target, terms, weight))
    for step, term in enumerate(terms, 1):
        pairs = [(i, (i + step) % lad_count) for i in range(lad_count)]
        base = base + lax.ppermute(term, "lad", pairs).astype(F32)

    blocks = pack(plan + (late,), True, target, amps, "pack_rest")
    for (k, first, _), block in zip(late, blocks):
        arrived[(k, first // width)] = exchange(block, k)

    pick = unpack_matrix(offsets, target.reshape(rows, 1), capacity)
    operator = cycle_operator(block_index, weight, mixing, block_rows)
    part_column, hole_row = gap_part[0].reshape(rows, 1), gap_hole.reshape(1, holes)
    returned = []
    for half in range(HALVES):
        blocks = [arrived[(k, half if k or not paired else 0)] for k in far_first]
        if returned:
            blocks, made = lax.optimization_barrier((blocks, made))
        made = apply_cycle(half, operator, blocks, holes // HALVES)
        returned.append([exchange(block, k) for k, block in zip(far_first, made)])
    updated = None
    for half in range(HALVES):
        updated = finish(half, pick, base, part_column, hole_row, returned[half], updated)
    return updated[None]


def solution(mesh):
    placed = (
        P(("parts", "chan"), ("lad", "sub"), None),
        P(("parts", "chan"), ("lad", "sub"), None),
        P("chan", ("lad", "sub"), None),
        P("chan", None, ("lad", "sub")),
        P("chan", ("lad", "sub"), None, None),
        P("chan", ("lad", "sub"), None, None, None),
        P(("parts", "chan"), ("lad", "sub")),
        P("parts"),
    )
    return jax.shard_map(
        body,
        mesh=mesh,
        in_specs=placed,
        out_specs=P(("parts", "chan"), ("lad", "sub"), None),
        check_vma=False,
    )
```

```python
import functools

import jax
import jax.numpy as jnp
from jax import lax
from jax.experimental import pallas as pl
from jax.experimental.pallas import tpu as pltpu
from jax.sharding import PartitionSpec as P

VMEM_LIMIT = 24 * 1024 * 1024
VMEM_MOST = 60 * 1024 * 1024
VMEM_LADDER = 49 * 1024 * 1024
VMEM_OPERATOR = 44 * 1024 * 1024
HALVES = 2
F32 = jnp.float32
BF16 = jnp.bfloat16
CHEAP = pl.CostEstimate(flops=0, bytes_accessed=0, transcendentals=0)
DEAR = pl.CostEstimate(flops=3 * 10**10, bytes_accessed=10**6, transcendentals=0)


def params(limit=VMEM_LIMIT):
    return pltpu.CompilerParams(vmem_limit_bytes=limit)


def whole(memory=pltpu.VMEM):
    return pl.BlockSpec(memory_space=memory)


def selection(match):
    return jnp.where(match, 1.0, 0.0).astype(BF16)


def block_offsets(paired, chan_count, block_rows):
    chan = lax.axis_index("chan")
    return [(chan ^ k) * block_rows for k in range(chan_count)] if paired else [0]


def slots_of(owners, send, names):
    lane = 128
    pieces = owners.shape[1] // lane
    before = selection(
        lax.broadcasted_iota(jnp.int32, (lane, 2 * lane), 0)
        < lax.broadcasted_iota(jnp.int32, (lane, 2 * lane), 1)
    )
    hot = [
        lax.broadcasted_iota(jnp.int32, (names, lane), 0) == owners[:, i * lane : (i + 1) * lane]
        for i in range(pieces)
    ]
    counts = jnp.dot(
        jnp.concatenate([selection(h) for h in hot], axis=0), before, preferred_element_type=F32
    )
    passed = jnp.zeros((names, lane), F32)
    slots = []
    for i in range(pieces):
        within = counts[i * names : (i + 1) * names]
        slots.append(jnp.sum(jnp.where(hot[i], within[:, :lane] + passed, 0.0), axis=0, keepdims=True))
        passed = passed + within[:, lane:]
    return owners * send + jnp.concatenate(slots, axis=1).astype(jnp.int32)


def pack_kernel(plan, given, route_hbm, amps_hbm, *refs):
    paired, chan_count, send, block_rows, items = plan
    extra = 0 if given else 1
    outs, (route_ref, amps_ref, *kept) = refs[: len(items) + extra], refs[len(items) + extra :]
    block_hbm, block_refs, (in_sems, out_sems) = outs[extra:], kept[: len(items)], kept[len(items) :]
    copies = [
        pltpu.make_async_copy(route_hbm, route_ref, in_sems.at[0]),
        pltpu.make_async_copy(amps_hbm.at[:, pl.ds(0, amps_ref.shape[1])], amps_ref, in_sems.at[1]),
    ]
    for copy in copies:
        copy.start()
    copies[0].wait()
    target = route_ref[...]
    out_copies = []
    if not given:
        target = slots_of(target, send, max(16, chan_count))
        route_ref[...] = target
        out_copies.append(pltpu.make_async_copy(route_ref, outs[0], out_sems.at[len(items)]))
        out_copies[0].start()
    offsets = block_offsets(paired, chan_count, block_rows)
    slot = lax.broadcasted_iota(jnp.int32, (block_rows, target.shape[1]), 0)
    for i, (k, first, width) in enumerate(items):
        pick = selection(slot == target - offsets[k])
        if i == 0:
            copies[1].wait()
        block_refs[i][...] = jnp.dot(
            pick, amps_ref[:, pl.ds(first, width)], preferred_element_type=F32
        ).astype(BF16)
        out_copies.append(pltpu.make_async_copy(block_refs[i], block_hbm[i], out_sems.at[i]))
        out_copies[-1].start()
    for copy in out_copies:
        copy.wait()


def pack(plan, given, route_row, amps, name):
    rows = amps.shape[0]
    block_rows, items = plan[3], plan[4]
    columns = max(first + width for _, first, width in items)
    shapes = [(block_rows, width) for _, _, width in items]
    extra = [] if given else [jax.ShapeDtypeStruct((1, rows), jnp.int32)]
    return pl.pallas_call(
        functools.partial(pack_kernel, plan, given),
        out_shape=extra + [jax.ShapeDtypeStruct(shape, BF16) for shape in shapes],
        in_specs=[whole(pl.ANY), whole(pl.ANY)],
        out_specs=[whole(pl.ANY)] * (len(extra) + len(items)),
        scratch_shapes=[pltpu.VMEM((1, rows), jnp.int32), pltpu.VMEM((rows, columns), BF16)]
        + [pltpu.VMEM(shape, BF16) for shape in shapes]
        + [pltpu.SemaphoreType.DMA((2,)), pltpu.SemaphoreType.DMA((1 + len(items),))],
        compiler_params=params(VMEM_LIMIT if given else VMEM_MOST),
        name=name,
    )(route_row, amps)


def unpack_kernel(off_ref, target_ref, out_ref):
    count = off_ref.shape[0]
    rows, capacity = out_ref.shape
    block_rows = capacity // count
    target = target_ref[...]
    slots = lax.broadcasted_iota(jnp.int32, (rows, block_rows), 1)
    for k in range(count):
        out_ref[:, pl.ds(k * block_rows, block_rows)] = selection(slots == target - off_ref[k])


def unpack_matrix(offsets, target_column, capacity):
    return pl.pallas_call(
        unpack_kernel,
        out_shape=jax.ShapeDtypeStruct((target_column.shape[0], capacity), BF16),
        in_specs=[whole(pltpu.SMEM), whole()],
        out_specs=whole(),
        compiler_params=params(),
        cost_estimate=CHEAP,
        name="unpack_matrix",
    )(offsets, target_column)


def ladder_kernel(share_ref, weight_ref, amps_ref, out_ref):
    out_ref[...] = jnp.dot(weight_ref[...], amps_ref[...], preferred_element_type=F32).astype(BF16)[None]


def ladder_share(share, weight, amps, lad_count, sub_count):
    rows, holes = amps.shape
    tile = 256 if rows % 256 == 0 else 128
    steps = rows // tile
    return pl.pallas_call(
        ladder_kernel,
        out_shape=jax.ShapeDtypeStruct((lad_count, rows, holes), BF16),
        grid_spec=pltpu.PrefetchScalarGridSpec(
            num_scalar_prefetch=1,
            grid=(lad_count, steps),
            in_specs=[
                pl.BlockSpec((tile, rows), lambda i, t, share: ((i * sub_count + share[0]) * steps + t, 0)),
                pl.BlockSpec((rows, holes), lambda i, t, share: (0, 0)),
            ],
            out_specs=pl.BlockSpec((1, tile, holes), lambda i, t, share: (i, t, 0)),
        ),
        compiler_params=params(VMEM_LADDER),
        cost_estimate=DEAR,
        name="ladder_share",
    )(share, weight, amps)


def operator_kernel(group, block_index, weight_ref, mixing_ref, out_ref, half_ref):
    k = pl.program_id(0)
    block_rows, capacity = weight_ref.shape
    per_block = block_rows // group
    for a in range(per_block):
        mix = mixing_ref[block_index[k] * per_block + a]
        half_ref[pl.ds(a * group, group), :] = lax.dot_general(
            mix,
            weight_ref[pl.ds(a * group, group), :],
            (((0,), (0,)), ((), ())),
            preferred_element_type=F32,
        ).astype(BF16)
    for j in range(capacity // block_rows):
        for b in range(per_block):
            at = block_index[j] * per_block + b
            columns = pl.ds(pl.multiple_of(at * group, group), group)
            out_ref[:, pl.ds(j * block_rows + b * group, group)] = jnp.dot(
                half_ref[:, columns], mixing_ref[at], preferred_element_type=F32
            ).astype(BF16)


def cycle_operator(block_index, weight, mixing, block_rows):
    capacity = weight.shape[0]
    group = mixing.shape[1]
    return pl.pallas_call(
        functools.partial(operator_kernel, group),
        out_shape=jax.ShapeDtypeStruct((capacity, capacity), BF16),
        grid_spec=pltpu.PrefetchScalarGridSpec(
            num_scalar_prefetch=1,
            grid=(capacity // block_rows,),
            in_specs=[
                pl.BlockSpec((block_rows, capacity), lambda k, index: (index[k], 0)),
                pl.BlockSpec(mixing.shape, lambda k, index: (0, 0, 0)),
            ],
            out_specs=pl.BlockSpec((block_rows, capacity), lambda k, index: (k, 0)),
            scratch_shapes=[pltpu.VMEM((block_rows, capacity), BF16)],
        ),
        compiler_params=params(VMEM_OPERATOR),
        cost_estimate=CHEAP,
        name="cycle_operator",
    )(block_index, weight, mixing)


def cycle_kernel(half, operator_ref, *refs):
    count = len(refs) // 2
    in_refs, out_refs, block_ref = refs[:count], refs[count : 2 * count], refs[2 * count]
    block_rows, width = out_refs[0].shape
    for i, in_ref in enumerate(in_refs):
        at = pl.ds((count - 1 - i) * block_rows, block_rows)
        block_ref[at, :] = in_ref[...] if in_ref.shape[1] == width else in_ref[:, pl.ds(half * width, width)]
    for i, out_ref in enumerate(out_refs):
        at = pl.ds((count - 1 - i) * block_rows, block_rows)
        out_ref[...] = jnp.dot(operator_ref[at, :], block_ref[...], preferred_element_type=F32).astype(BF16)


def apply_cycle(half, operator, arrays, width):
    return pl.pallas_call(
        functools.partial(cycle_kernel, half),
        out_shape=[jax.ShapeDtypeStruct((a.shape[0], width), BF16) for a in arrays],
        in_specs=[whole()] * (1 + len(arrays)),
        out_specs=[whole()] * len(arrays),
        scratch_shapes=[pltpu.VMEM((operator.shape[0], width), BF16)],
        compiler_params=params(),
        cost_estimate=DEAR,
        name="apply_cycle",
    )(operator, *arrays)


def finish_kernel(half, count, tiles, pick_ref, base_ref, part_ref, hole_ref, *refs):
    in_refs, (out_hbm, block_ref, out_ref, sems) = refs[:count], refs[-4:]
    block_rows, width = in_refs[0].shape
    tile = out_ref.shape[0] // tiles
    columns = pl.ds(half * width, width)
    for i, in_ref in enumerate(in_refs):
        block_ref[pl.ds((count - 1 - i) * block_rows, block_rows), :] = in_ref[...]
    copies = []
    for t in range(tiles):
        at = pl.ds(t * tile, tile)
        back = jnp.dot(pick_ref[at, :], block_ref[...], preferred_element_type=F32)
        total = base_ref[at, columns] + back
        out_ref[at, :] = (total / (part_ref[at, :] + hole_ref[:, columns])).astype(BF16)
        copies.append(pltpu.make_async_copy(out_ref.at[at, :], out_hbm.at[at, columns], sems.at[t]))
        copies[-1].start()
    for copy in copies:
        copy.wait()


def finish(half, pick, base, part_column, hole_row, arrays, earlier):
    rows, holes = base.shape
    tiles, width = 3, holes // HALVES
    operands = [pick, base, part_column, hole_row, *arrays]
    in_specs = [whole()] * len(operands)
    aliases = {}
    if earlier is not None:
        aliases = {len(operands): 0}
        operands.append(earlier)
        in_specs.append(whole(pl.ANY))
    return pl.pallas_call(
        functools.partial(finish_kernel, half, len(arrays), tiles),
        out_shape=jax.ShapeDtypeStruct((rows, holes), BF16),
        in_specs=in_specs,
        out_specs=whole(pl.ANY),
        scratch_shapes=[
            pltpu.VMEM((pick.shape[1], width), BF16),
            pltpu.VMEM((rows, width), BF16),
            pltpu.SemaphoreType.DMA((tiles,)),
        ],
        input_output_aliases=aliases,
        compiler_params=params(),
        cost_estimate=CHEAP,
        name="finish",
    )(*operands)


def body(amplitudes, driving, route, ladder_weight, ph_weight, recouple, gap_part, gap_hole):
    amps = amplitudes[0]
    rows, holes = amps.shape
    chan_count = lax.axis_size("chan")
    lad_count = lax.axis_size("lad")
    sub_count = lax.axis_size("sub")
    chan, lad, sub = lax.axis_index("chan"), lax.axis_index("lad"), lax.axis_index("sub")
    weight, mixing = ph_weight[0, 0], recouple[0, 0]
    capacity = weight.shape[0]
    send = capacity // chan_count
    paired = send % mixing.shape[1] == 0 and chan_count & (chan_count - 1) == 0
    if paired:
        block_rows = send
        block_index = jnp.stack([chan ^ k for k in range(chan_count)]).astype(jnp.int32)
    else:
        block_rows = capacity
        block_index = jnp.zeros((1,), jnp.int32)
    offsets = block_index * block_rows

    def exchange(block, k):
        if not paired:
            split = block.reshape(chan_count, send, -1)
            split = lax.all_to_all(split, "chan", split_axis=0, concat_axis=0, tiled=True)
            return split.reshape(capacity, -1)
        return lax.ppermute(block, "chan", [(i, i ^ k) for i in range(chan_count)]) if k else block

    far_first = list(reversed(range(block_index.shape[0])))
    count = len(far_first)
    width = holes // HALVES
    route_row = route[0].reshape(1, rows)
    plan = (paired, chan_count, send, block_rows)
    early = [(k, 0, width) for k in far_first if k or not paired]
    late = [(k, h * width, width) for h in range(1, HALVES) for k in far_first if k or not paired]
    late += [(0, 0, holes)] if paired else []
    target, *blocks = pack(plan + (early,), False, route_row, amps, "pack_first")
    arrived = {(k, 0): exchange(block, k) for (k, _, _), block in zip(early, blocks)}
    amps, target = lax.optimization_barrier((amps, target))

    kept = None
    for step in reversed(range(sub_count)):
        share = lax.rem(sub + step, sub_count).astype(jnp.int32).reshape(1)
        part = ladder_share(share, ladder_weight[0], amps, lad_count, sub_count)
        if step:
            pairs = [(i, (i + step) % sub_count) for i in range(sub_count)]
            part = lax.ppermute(part, "sub", pairs)
        kept = [part] if kept is None else kept + [part]

    def chip_sum(position):
        picked = [lax.dynamic_index_in_dim(p, position, 0, keepdims=False) for p in kept]
        return sum(p.astype(F32) for p in picked)

    base = driving[0].astype(F32) + chip_sum(lad)
    terms = [chip_sum(lax.rem(lad + step, lad_count)).astype(BF16) for step in range(1, lad_count)]
    target, terms, weight = lax.optimization_barrier((target, terms, weight))
    for step, term in enumerate(terms, 1):
        pairs = [(i, (i + step) % lad_count) for i in range(lad_count)]
        base = base + lax.ppermute(term, "lad", pairs).astype(F32)

    blocks = pack(plan + (late,), True, target, amps, "pack_rest")
    for (k, first, _), block in zip(late, blocks):
        arrived[(k, first // width)] = exchange(block, k)

    pick = unpack_matrix(offsets, target.reshape(rows, 1), capacity)
    if paired:
        near = (1, 0)
        weight, arrived[near] = lax.optimization_barrier((weight, arrived[near]))
    operator = cycle_operator(block_index, weight, mixing, block_rows)
    part_column, hole_row = gap_part[0].reshape(rows, 1), gap_hole.reshape(1, holes)
    returned = []
    for half in range(HALVES):
        blocks = [arrived[(k, half if k or not paired else 0)] for k in far_first]
        if returned:
            blocks, made = lax.optimization_barrier((blocks, made))
        made = apply_cycle(half, operator, blocks, holes // HALVES)
        returned.append([exchange(block, k) for k, block in zip(far_first, made)])
    updated = None
    for half in range(HALVES):
        updated = finish(half, pick, base, part_column, hole_row, returned[half], updated)
    return updated[None]


def solution(mesh):
    placed = (
        P(("parts", "chan"), ("lad", "sub"), None),
        P(("parts", "chan"), ("lad", "sub"), None),
        P("chan", ("lad", "sub"), None),
        P("chan", None, ("lad", "sub")),
        P("chan", ("lad", "sub"), None, None),
        P("chan", ("lad", "sub"), None, None, None),
        P(("parts", "chan"), ("lad", "sub")),
        P("parts"),
    )
    return jax.shard_map(
        body,
        mesh=mesh,
        in_specs=placed,
        out_specs=P(("parts", "chan"), ("lad", "sub"), None),
        check_vma=False,
    )
```

```python
import functools

import jax
import jax.numpy as jnp
from jax import lax
from jax.experimental import pallas as pl
from jax.experimental.pallas import tpu as pltpu
from jax.sharding import PartitionSpec as P

VMEM_LIMIT = 32 * 1024 * 1024
HALVES = 2
F32 = jnp.float32
BF16 = jnp.bfloat16
CHEAP = pl.CostEstimate(flops=0, bytes_accessed=0, transcendentals=0)
DEAR = pl.CostEstimate(flops=3 * 10**10, bytes_accessed=10**6, transcendentals=0)


def params():
    return pltpu.CompilerParams(vmem_limit_bytes=VMEM_LIMIT)


def in_hbm(*arrays):
    return [pltpu.with_memory_space_constraint(a, pltpu.HBM) for a in arrays]


def whole(memory=pltpu.VMEM):
    return pl.BlockSpec(memory_space=memory)


def selection(match):
    return jnp.where(match, 1.0, 0.0).astype(BF16)


def block_offsets(paired, chan_count, block_rows):
    chan = lax.axis_index("chan")
    return [(chan ^ k) * block_rows for k in range(chan_count)] if paired else [0]


def slots_of(owners, send, names):
    lane = 128
    pieces = owners.shape[1] // lane
    before = selection(
        lax.broadcasted_iota(jnp.int32, (lane, 2 * lane), 0)
        < lax.broadcasted_iota(jnp.int32, (lane, 2 * lane), 1)
    )
    hot = [
        lax.broadcasted_iota(jnp.int32, (names, lane), 0) == owners[:, i * lane : (i + 1) * lane]
        for i in range(pieces)
    ]
    counts = jnp.dot(
        jnp.concatenate([selection(h) for h in hot], axis=0), before, preferred_element_type=F32
    )
    passed = jnp.zeros((names, lane), F32)
    slots = []
    for i in range(pieces):
        within = counts[i * names : (i + 1) * names]
        slots.append(jnp.sum(jnp.where(hot[i], within[:, :lane] + passed, 0.0), axis=0, keepdims=True))
        passed = passed + within[:, lane:]
    return owners * send + jnp.concatenate(slots, axis=1).astype(jnp.int32)


def pack_kernel(plan, given, route_hbm, amps_hbm, *refs):
    paired, chan_count, send, block_rows, items = plan
    outs, (route_ref, amps_ref, sems) = refs[:-3], refs[-3:]
    block_refs = outs if given else outs[1:]
    copies = [
        pltpu.make_async_copy(route_hbm, route_ref, sems.at[0]),
        pltpu.make_async_copy(amps_hbm.at[:, pl.ds(0, amps_ref.shape[1])], amps_ref, sems.at[1]),
    ]
    for copy in copies:
        copy.start()
    copies[0].wait()
    target = route_ref[...]
    if not given:
        target = slots_of(target, send, max(16, chan_count))
        outs[0][...] = target
    offsets = block_offsets(paired, chan_count, block_rows)
    slot = lax.broadcasted_iota(jnp.int32, (block_rows, target.shape[1]), 0)
    for i, (k, first, width) in enumerate(items):
        pick = selection(slot == target - offsets[k])
        if i == 0:
            copies[1].wait()
        block_refs[i][...] = jnp.dot(
            pick, amps_ref[:, pl.ds(first, width)], preferred_element_type=F32
        ).astype(BF16)


def pack(plan, given, route_row, amps, name):
    rows = amps.shape[0]
    block_rows, items = plan[3], plan[4]
    columns = max(first + width for _, first, width in items)
    extra = [] if given else [pltpu.VMEM((1, rows), jnp.int32)]
    return pl.pallas_call(
        functools.partial(pack_kernel, plan, given),
        out_shape=extra + [pltpu.VMEM((block_rows, width), BF16) for _, _, width in items],
        in_specs=[whole(pl.ANY), whole(pl.ANY)],
        out_specs=[whole()] * (len(extra) + len(items)),
        scratch_shapes=[
            pltpu.VMEM((1, rows), jnp.int32),
            pltpu.VMEM((rows, columns), BF16),
            pltpu.SemaphoreType.DMA((2,)),
        ],
        compiler_params=params(),
        name=name,
    )(*in_hbm(route_row, amps))


def unpack_kernel(off_ref, target_ref, out_ref):
    count = off_ref.shape[0]
    rows, capacity = out_ref.shape
    block_rows = capacity // count
    target = target_ref[...]
    slots = lax.broadcasted_iota(jnp.int32, (rows, block_rows), 1)
    for k in range(count):
        out_ref[:, pl.ds(k * block_rows, block_rows)] = selection(slots == target - off_ref[k])


def unpack_matrix(offsets, target_column, capacity):
    return pl.pallas_call(
        unpack_kernel,
        out_shape=jax.ShapeDtypeStruct((target_column.shape[0], capacity), BF16),
        in_specs=[whole(pltpu.SMEM), whole()],
        out_specs=whole(),
        compiler_params=params(),
        cost_estimate=CHEAP,
        name="unpack_matrix",
    )(offsets, target_column)


def ladder_kernel(step, sub_count, weight_hbm, amps_hbm, *refs):
    moved = (len(refs) - 4) // 2
    source_refs, part_ref, held_refs = refs[:moved], refs[moved], refs[moved + 1 : 2 * moved + 1]
    weight_ref, amps_ref, sems = refs[2 * moved + 1 :]
    rows, lad_count = amps_ref.shape[0], part_ref.shape[0]
    share = lax.rem(lax.axis_index("sub") + step, sub_count)
    copies = [pltpu.make_async_copy(amps_hbm, amps_ref, sems.at[0])]
    for i in range(lad_count):
        start = pl.multiple_of((i * sub_count + share) * rows, rows)
        copies.append(pltpu.make_async_copy(weight_hbm.at[pl.ds(start, rows), :], weight_ref.at[i], sems.at[1 + i]))
    for n, (source, held) in enumerate(zip(source_refs, held_refs)):
        copies.append(pltpu.make_async_copy(source, held, sems.at[1 + lad_count + n]))
    for copy in copies:
        copy.start()
    copies[0].wait()
    for i in range(lad_count):
        copies[1 + i].wait()
        part_ref[i] = jnp.dot(weight_ref[i], amps_ref[...], preferred_element_type=F32).astype(BF16)
    for copy in copies[1 + lad_count :]:
        copy.wait()


def ladder_part(step, weight, amps, lad_count, sub_count, moved):
    rows, holes = amps.shape
    return pl.pallas_call(
        functools.partial(ladder_kernel, step, sub_count),
        out_shape=[pltpu.VMEM((lad_count, rows, holes), BF16)] + [pltpu.VMEM(m.shape, BF16) for m in moved],
        in_specs=[whole(pl.ANY)] * (2 + len(moved)),
        out_specs=[whole()] * (1 + len(moved)),
        scratch_shapes=[
            pltpu.VMEM((lad_count, rows, rows), BF16),
            pltpu.VMEM((rows, holes), BF16),
            pltpu.SemaphoreType.DMA((1 + lad_count + len(moved),)),
        ],
        compiler_params=params(),
        cost_estimate=DEAR,
        name="ladder_part",
    )(*in_hbm(weight, amps, *moved))


def cycle_kernel(half, plan, weight_ref, mixing_ref, *refs):
    paired, chan_count, _, _ = plan
    count = len(refs) // 2 - 1
    in_refs, out_refs, (mixed_ref, back_ref) = refs[:count], refs[count : 2 * count], refs[2 * count :]
    block_rows, width = out_refs[0].shape
    group = mixing_ref.shape[1]
    offsets = block_offsets(paired, chan_count, block_rows)
    for i, in_ref in enumerate(in_refs):
        start = pl.multiple_of(offsets[count - 1 - i], block_rows)
        for a in range(block_rows // group):
            at = pl.ds(a * group, group)
            part = in_ref[at, :] if in_ref.shape[1] == width else in_ref[at, pl.ds(half * width, width)]
            mix = mixing_ref[lax.div(start, group) + a]
            mixed_ref[pl.ds(pl.multiple_of(start + a * group, group), group), :] = jnp.dot(
                mix, part, preferred_element_type=F32
            ).astype(BF16)
    for i, out_ref in enumerate(out_refs):
        start = pl.multiple_of(offsets[count - 1 - i], block_rows)
        back_ref[...] = jnp.dot(
            weight_ref[pl.ds(start, block_rows), :], mixed_ref[...], preferred_element_type=F32
        ).astype(BF16)
        for a in range(block_rows // group):
            at = pl.ds(a * group, group)
            mix = mixing_ref[lax.div(start, group) + a]
            out_ref[at, :] = lax.dot_general(
                mix, back_ref[at, :], (((0,), (0,)), ((), ())), preferred_element_type=F32
            ).astype(BF16)


def apply_cycle(half, plan, weight, mixing, arrays, width):
    return pl.pallas_call(
        functools.partial(cycle_kernel, half, plan),
        out_shape=[jax.ShapeDtypeStruct((a.shape[0], width), BF16) for a in arrays],
        in_specs=[whole()] * (2 + len(arrays)),
        out_specs=[whole()] * len(arrays),
        scratch_shapes=[pltpu.VMEM((weight.shape[0], width), BF16), pltpu.VMEM((arrays[0].shape[0], width), BF16)],
        compiler_params=params(),
        cost_estimate=DEAR,
        name="apply_cycle",
    )(weight, mixing, *arrays)


def finish_kernel(half, count, tiles, pick_ref, base_ref, part_ref, hole_ref, *refs):
    in_refs, (out_hbm, block_ref, out_ref, sems) = refs[:count], refs[-4:]
    block_rows, width = in_refs[0].shape
    tile = out_ref.shape[0] // tiles
    columns = pl.ds(half * width, width)
    for i, in_ref in enumerate(in_refs):
        block_ref[pl.ds((count - 1 - i) * block_rows, block_rows), :] = in_ref[...]
    copies = []
    for t in range(tiles):
        at = pl.ds(t * tile, tile)
        back = jnp.dot(pick_ref[at, :], block_ref[...], preferred_element_type=F32)
        total = base_ref[at, columns] + back
        out_ref[at, :] = (total / (part_ref[at, :] + hole_ref[:, columns])).astype(BF16)
        copies.append(pltpu.make_async_copy(out_ref.at[at, :], out_hbm.at[at, columns], sems.at[t]))
        copies[-1].start()
    for copy in copies:
        copy.wait()


def finish(half, pick, base, part_column, hole_row, arrays, earlier):
    rows, holes = base.shape
    tiles, width = 3, holes // HALVES
    operands = [pick, base, part_column, hole_row, *arrays]
    in_specs = [whole()] * len(operands)
    aliases = {}
    if earlier is not None:
        aliases = {len(operands): 0}
        operands.append(earlier)
        in_specs.append(whole(pl.ANY))
    return pl.pallas_call(
        functools.partial(finish_kernel, half, len(arrays), tiles),
        out_shape=jax.ShapeDtypeStruct((rows, holes), BF16),
        in_specs=in_specs,
        out_specs=whole(pl.ANY),
        scratch_shapes=[
            pltpu.VMEM((pick.shape[1], width), BF16),
            pltpu.VMEM((rows, width), BF16),
            pltpu.SemaphoreType.DMA((tiles,)),
        ],
        input_output_aliases=aliases,
        compiler_params=params(),
        cost_estimate=CHEAP,
        name="finish",
    )(*operands)


def body(amplitudes, driving, route, ladder_weight, ph_weight, recouple, gap_part, gap_hole):
    amps = amplitudes[0]
    rows, holes = amps.shape
    chan_count = lax.axis_size("chan")
    lad_count = lax.axis_size("lad")
    sub_count = lax.axis_size("sub")
    chan, lad, sub = lax.axis_index("chan"), lax.axis_index("lad"), lax.axis_index("sub")
    weight, mixing = ph_weight[0, 0], recouple[0, 0]
    capacity = weight.shape[0]
    send = capacity // chan_count
    paired = send % mixing.shape[1] == 0 and chan_count & (chan_count - 1) == 0
    if paired:
        block_rows = send
        block_index = jnp.stack([chan ^ k for k in range(chan_count)]).astype(jnp.int32)
    else:
        block_rows = capacity
        block_index = jnp.zeros((1,), jnp.int32)
    offsets = block_index * block_rows

    def exchange(block, k):
        if not paired:
            split = block.reshape(chan_count, send, -1)
            split = lax.all_to_all(split, "chan", split_axis=0, concat_axis=0, tiled=True)
            return split.reshape(capacity, -1)
        return lax.ppermute(block, "chan", [(i, i ^ k) for i in range(chan_count)]) if k else block

    far_first = list(reversed(range(block_index.shape[0])))
    count = len(far_first)
    width = holes // HALVES
    route_row = route[0].reshape(1, rows)
    plan = (paired, chan_count, send, block_rows)
    early = [(k, 0, width) for k in far_first if k or not paired]
    late = [(k, h * width, width) for h in range(1, HALVES) for k in far_first if k or not paired]
    late += [(0, 0, holes)] if paired else []
    target, *blocks = pack(plan + (early,), False, route_row, amps, "pack_first")
    arrived = {(k, 0): exchange(block, k) for (k, _, _), block in zip(early, blocks)}
    if paired:
        near = (1, 0)
        target, arrived[near] = lax.optimization_barrier((target, arrived[near]))
    blocks = pack(plan + (late,), True, target, amps, "pack_rest")
    for (k, first, _), block in zip(late, blocks):
        arrived[(k, first // width)] = exchange(block, k)

    part_column, hole_row = gap_part[0].reshape(rows, 1), gap_hole.reshape(1, holes)
    amps, blocks = lax.optimization_barrier((amps, blocks))
    pick = unpack_matrix(offsets, target.reshape(rows, 1), capacity)

    kept = []
    for step in reversed(range(sub_count)):
        moved = [] if step else [mixing, weight]
        part, *moved = ladder_part(step, ladder_weight[0], amps, lad_count, sub_count, moved)
        if step:
            part = lax.ppermute(part, "sub", [(i, (i + step) % sub_count) for i in range(sub_count)])
        else:
            mixing, weight = moved
        kept.append(part)

    def chip_sum(position):
        picked = [lax.dynamic_index_in_dim(p, position, 0, keepdims=False) for p in kept]
        return sum(p.astype(F32) for p in picked)

    base = driving[0].astype(F32) + chip_sum(lad)
    terms = [chip_sum(lax.rem(lad + step, lad_count)).astype(BF16) for step in range(1, lad_count)]
    returned = []
    for half in range(HALVES):
        blocks = [arrived[(k, half if k or not paired else 0)] for k in far_first]
        if returned:
            blocks, made = lax.optimization_barrier((blocks, made))
        made = apply_cycle(half, plan, weight, mixing, blocks, width)
        if not half:
            behind, terms = lax.optimization_barrier((made[1:], terms))
            made = [made[0], *behind]
        returned.append([exchange(block, k) for k, block in zip(far_first, made)])
    for step, term in enumerate(terms, 1):
        pairs = [(i, (i + step) % lad_count) for i in range(lad_count)]
        base = base + lax.ppermute(term, "lad", pairs).astype(F32)
    updated = None
    for half in range(HALVES):
        updated = finish(half, pick, base, part_column, hole_row, returned[half], updated)
    return updated[None]


def solution(mesh):
    placed = (
        P(("parts", "chan"), ("lad", "sub"), None),
        P(("parts", "chan"), ("lad", "sub"), None),
        P("chan", ("lad", "sub"), None),
        P("chan", None, ("lad", "sub")),
        P("chan", ("lad", "sub"), None, None),
        P("chan", ("lad", "sub"), None, None, None),
        P(("parts", "chan"), ("lad", "sub")),
        P("parts"),
    )
    return jax.shard_map(
        body,
        mesh=mesh,
        in_specs=placed,
        out_specs=P(("parts", "chan"), ("lad", "sub"), None),
        check_vma=False,
    )
```

```python
import functools

import jax
import jax.numpy as jnp
from jax import lax
from jax.experimental import pallas as pl
from jax.experimental.pallas import tpu as pltpu
from jax.sharding import PartitionSpec as P

VMEM_LIMIT = 16 * 1024 * 1024
HALVES = 2
F32 = jnp.float32
BF16 = jnp.bfloat16
CHEAP = pl.CostEstimate(flops=0, bytes_accessed=0, transcendentals=0)
DEAR = pl.CostEstimate(flops=3 * 10**10, bytes_accessed=10**6, transcendentals=0)


def params():
    return pltpu.CompilerParams(vmem_limit_bytes=VMEM_LIMIT)


def in_hbm(*arrays):
    return [pltpu.with_memory_space_constraint(a, pltpu.HBM) for a in arrays]


def whole(memory=pltpu.VMEM):
    return pl.BlockSpec(memory_space=memory)


def selection(match):
    return jnp.where(match, 1.0, 0.0).astype(BF16)


def block_offsets(paired, chan_count, block_rows):
    chan = lax.axis_index("chan")
    return [(chan ^ k) * block_rows for k in range(chan_count)] if paired else [0]


def slots_of(owners, send, names):
    lane = 128
    pieces = owners.shape[1] // lane
    before = selection(
        lax.broadcasted_iota(jnp.int32, (lane, 2 * lane), 0)
        < lax.broadcasted_iota(jnp.int32, (lane, 2 * lane), 1)
    )
    hot = [
        lax.broadcasted_iota(jnp.int32, (names, lane), 0) == owners[:, i * lane : (i + 1) * lane]
        for i in range(pieces)
    ]
    counts = jnp.dot(
        jnp.concatenate([selection(h) for h in hot], axis=0), before, preferred_element_type=F32
    )
    passed = jnp.zeros((names, lane), F32)
    slots = []
    for i in range(pieces):
        within = counts[i * names : (i + 1) * names]
        slots.append(jnp.sum(jnp.where(hot[i], within[:, :lane] + passed, 0.0), axis=0, keepdims=True))
        passed = passed + within[:, lane:]
    return owners * send + jnp.concatenate(slots, axis=1).astype(jnp.int32)


def pack_kernel(plan, given, route_in, amps_hbm, *refs):
    paired, chan_count, send, block_rows, items = plan
    outs, (route_ref, amps_ref, sems) = refs[:-3], refs[-3:]
    block_refs = outs if given else outs[1:]
    amps_copy = pltpu.make_async_copy(amps_hbm.at[:, pl.ds(0, amps_ref.shape[1])], amps_ref, sems.at[1])
    if given:
        amps_copy.start()
        target = route_in[...]
    else:
        route_copy = pltpu.make_async_copy(route_in, route_ref, sems.at[0])
        route_copy.start()
        amps_copy.start()
        route_copy.wait()
        target = slots_of(route_ref[...], send, max(16, chan_count))
        outs[0][...] = target
    offsets = block_offsets(paired, chan_count, block_rows)
    slot = lax.broadcasted_iota(jnp.int32, (block_rows, target.shape[1]), 0)
    for i, (k, first, width) in enumerate(items):
        pick = selection(slot == target - offsets[k])
        if i == 0:
            amps_copy.wait()
        block_refs[i][...] = jnp.dot(
            pick, amps_ref[:, pl.ds(first, width)], preferred_element_type=F32
        ).astype(BF16)


def pack(plan, given, route_row, amps, name):
    rows = amps.shape[0]
    block_rows, items = plan[3], plan[4]
    columns = max(first + width for _, first, width in items)
    extra = [] if given else [pltpu.VMEM((1, rows), jnp.int32)]
    return pl.pallas_call(
        functools.partial(pack_kernel, plan, given),
        out_shape=extra + [pltpu.VMEM((block_rows, width), BF16) for _, _, width in items],
        in_specs=[whole() if given else whole(pl.ANY), whole(pl.ANY)],
        out_specs=[whole()] * (len(extra) + len(items)),
        scratch_shapes=[
            pltpu.VMEM((1, rows), jnp.int32),
            pltpu.VMEM((rows, columns), BF16),
            pltpu.SemaphoreType.DMA((2,)),
        ],
        compiler_params=params(),
        name=name,
    )(*([route_row] if given else in_hbm(route_row)), *in_hbm(amps))


def unpack_kernel(off_ref, target_ref, out_ref):
    count = off_ref.shape[0]
    rows, capacity = out_ref.shape
    block_rows = capacity // count
    target = target_ref[...]
    slots = lax.broadcasted_iota(jnp.int32, (rows, block_rows), 1)
    for k in range(count):
        out_ref[:, pl.ds(k * block_rows, block_rows)] = selection(slots == target - off_ref[k])


def unpack_matrix(offsets, target_column, capacity):
    return pl.pallas_call(
        unpack_kernel,
        out_shape=jax.ShapeDtypeStruct((target_column.shape[0], capacity), BF16),
        in_specs=[whole(pltpu.SMEM), whole()],
        out_specs=whole(),
        compiler_params=params(),
        cost_estimate=CHEAP,
        name="unpack_matrix",
    )(offsets, target_column)


def ladder_kernel(step, sub_count, weight_hbm, amps_hbm, part_ref, weight_ref, amps_ref, sems):
    rows, lad_count = amps_ref.shape[0], part_ref.shape[0]
    share = lax.rem(lax.axis_index("sub") + step, sub_count)
    copies = [pltpu.make_async_copy(amps_hbm, amps_ref, sems.at[0])]
    for i in range(lad_count):
        start = pl.multiple_of((i * sub_count + share) * rows, rows)
        copies.append(pltpu.make_async_copy(weight_hbm.at[pl.ds(start, rows), :], weight_ref.at[i], sems.at[1 + i]))
    for copy in copies:
        copy.start()
    copies[0].wait()
    for i in range(lad_count):
        copies[1 + i].wait()
        part_ref[i] = jnp.dot(weight_ref[i], amps_ref[...], preferred_element_type=F32).astype(BF16)


def ladder_part(step, weight, amps, lad_count, sub_count):
    rows, holes = amps.shape
    return pl.pallas_call(
        functools.partial(ladder_kernel, step, sub_count),
        out_shape=pltpu.VMEM((lad_count, rows, holes), BF16),
        in_specs=[whole(pl.ANY)] * 2,
        out_specs=whole(),
        scratch_shapes=[
            pltpu.VMEM((lad_count, rows, rows), BF16),
            pltpu.VMEM((rows, holes), BF16),
            pltpu.SemaphoreType.DMA((1 + lad_count,)),
        ],
        compiler_params=params(),
        cost_estimate=DEAR,
        name="ladder_part",
    )(*in_hbm(weight, amps))


def cycle_kernel(half, plan, weight_hbm, mixing_hbm, *refs):
    paired, chan_count, _, _ = plan
    count = (len(refs) - 5) // 2
    in_refs, out_refs = refs[:count], refs[count : 2 * count]
    weight_ref, mixing_ref, mixed_ref, back_ref, sems = refs[2 * count :]
    block_rows, width = out_refs[0].shape
    group = mixing_ref.shape[1]
    offsets = block_offsets(paired, chan_count, block_rows)
    starts = [pl.multiple_of(offsets[count - 1 - i], block_rows) for i in range(count)]
    mixing_copy = pltpu.make_async_copy(mixing_hbm, mixing_ref, sems.at[0])
    copies = [
        pltpu.make_async_copy(weight_hbm.at[pl.ds(start, block_rows), :], weight_ref.at[i], sems.at[1 + i])
        for i, start in enumerate(starts)
    ]
    for copy in [mixing_copy] + copies:
        copy.start()
    mixing_copy.wait()
    for in_ref, start in zip(in_refs, starts):
        for a in range(block_rows // group):
            at = pl.ds(a * group, group)
            part = in_ref[at, :] if in_ref.shape[1] == width else in_ref[at, pl.ds(half * width, width)]
            mix = mixing_ref[lax.div(start, group) + a]
            mixed_ref[pl.ds(pl.multiple_of(start + a * group, group), group), :] = jnp.dot(
                mix, part, preferred_element_type=F32
            ).astype(BF16)
    for i, (out_ref, start) in enumerate(zip(out_refs, starts)):
        copies[i].wait()
        back_ref[...] = jnp.dot(weight_ref[i], mixed_ref[...], preferred_element_type=F32).astype(BF16)
        for a in range(block_rows // group):
            at = pl.ds(a * group, group)
            mix = mixing_ref[lax.div(start, group) + a]
            out_ref[at, :] = lax.dot_general(
                mix, back_ref[at, :], (((0,), (0,)), ((), ())), preferred_element_type=F32
            ).astype(BF16)


def apply_cycle(half, plan, weight, mixing, arrays, width):
    count, block_rows = len(arrays), arrays[0].shape[0]
    capacity = weight.shape[0]
    return pl.pallas_call(
        functools.partial(cycle_kernel, half, plan),
        out_shape=[pltpu.VMEM((block_rows, width), BF16)] * count,
        in_specs=[whole(pl.ANY)] * 2 + [whole()] * count,
        out_specs=[whole()] * count,
        scratch_shapes=[
            pltpu.VMEM((count, block_rows, capacity), BF16),
            pltpu.VMEM(mixing.shape, BF16),
            pltpu.VMEM((capacity, width), BF16),
            pltpu.VMEM((block_rows, width), BF16),
            pltpu.SemaphoreType.DMA((1 + count,)),
        ],
        compiler_params=params(),
        cost_estimate=DEAR,
        name="apply_cycle",
    )(*in_hbm(weight, mixing), *arrays)


def finish_kernel(half, count, tiles, pick_ref, base_ref, part_ref, hole_ref, *refs):
    in_refs, (out_hbm, block_ref, out_ref, sems) = refs[:count], refs[-4:]
    block_rows, width = in_refs[0].shape
    tile = out_ref.shape[0] // tiles
    columns = pl.ds(half * width, width)
    for i, in_ref in enumerate(in_refs):
        block_ref[pl.ds((count - 1 - i) * block_rows, block_rows), :] = in_ref[...]
    copies = []
    for t in range(tiles):
        at = pl.ds(t * tile, tile)
        back = jnp.dot(pick_ref[at, :], block_ref[...], preferred_element_type=F32)
        total = base_ref[at, columns] + back
        out_ref[at, :] = (total / (part_ref[at, :] + hole_ref[:, columns])).astype(BF16)
        copies.append(pltpu.make_async_copy(out_ref.at[at, :], out_hbm.at[at, columns], sems.at[t]))
        copies[-1].start()
    for copy in copies:
        copy.wait()


def finish(half, pick, base, part_column, hole_row, arrays, earlier):
    rows, holes = base.shape
    tiles, width = 3, holes // HALVES
    operands = [pick, base, part_column, hole_row, *arrays]
    in_specs = [whole()] * len(operands)
    aliases = {}
    if earlier is not None:
        aliases = {len(operands): 0}
        operands.append(earlier)
        in_specs.append(whole(pl.ANY))
    return pl.pallas_call(
        functools.partial(finish_kernel, half, len(arrays), tiles),
        out_shape=jax.ShapeDtypeStruct((rows, holes), BF16),
        in_specs=in_specs,
        out_specs=whole(pl.ANY),
        scratch_shapes=[
            pltpu.VMEM((pick.shape[1], width), BF16),
            pltpu.VMEM((rows, width), BF16),
            pltpu.SemaphoreType.DMA((tiles,)),
        ],
        input_output_aliases=aliases,
        compiler_params=params(),
        cost_estimate=CHEAP,
        name="finish",
    )(*operands)


def body(amplitudes, driving, route, ladder_weight, ph_weight, recouple, gap_part, gap_hole):
    amps = amplitudes[0]
    rows, holes = amps.shape
    chan_count = lax.axis_size("chan")
    lad_count = lax.axis_size("lad")
    sub_count = lax.axis_size("sub")
    chan, lad, sub = lax.axis_index("chan"), lax.axis_index("lad"), lax.axis_index("sub")
    weight, mixing = ph_weight[0, 0], recouple[0, 0]
    capacity = weight.shape[0]
    send = capacity // chan_count
    paired = send % mixing.shape[1] == 0 and chan_count & (chan_count - 1) == 0
    if paired:
        block_rows = send
        block_index = jnp.stack([chan ^ k for k in range(chan_count)]).astype(jnp.int32)
    else:
        block_rows = capacity
        block_index = jnp.zeros((1,), jnp.int32)
    offsets = block_index * block_rows

    def exchange(block, k):
        if not paired:
            split = block.reshape(chan_count, send, -1)
            split = lax.all_to_all(split, "chan", split_axis=0, concat_axis=0, tiled=True)
            return split.reshape(capacity, -1)
        return lax.ppermute(block, "chan", [(i, i ^ k) for i in range(chan_count)]) if k else block

    far_first = list(reversed(range(block_index.shape[0])))
    count = len(far_first)
    width = holes // HALVES
    route_row = route[0].reshape(1, rows)
    plan = (paired, chan_count, send, block_rows)
    early = [(k, 0, width) for k in far_first if k or not paired]
    late = [(k, h * width, width) for h in range(1, HALVES) for k in far_first if k or not paired]
    late += [(0, 0, holes)] if paired else []
    target, *blocks = pack(plan + (early,), False, route_row, amps, "pack_first")
    arrived = {(k, 0): exchange(block, k) for (k, _, _), block in zip(early, blocks)}
    if paired:
        near = (1, 0)
        target, arrived[near] = lax.optimization_barrier((target, arrived[near]))
    blocks = pack(plan + (late,), True, target, amps, "pack_rest")
    for (k, first, _), block in zip(late, blocks):
        arrived[(k, first // width)] = exchange(block, k)

    part_column, hole_row = gap_part[0].reshape(rows, 1), gap_hole.reshape(1, holes)
    amps, blocks = lax.optimization_barrier((amps, blocks))
    pick = unpack_matrix(offsets, target.reshape(rows, 1), capacity)

    kept = []
    for step in reversed(range(sub_count)):
        part = ladder_part(step, ladder_weight[0], amps, lad_count, sub_count)
        if step:
            part = lax.ppermute(part, "sub", [(i, (i + step) % sub_count) for i in range(sub_count)])
        kept.append(part)

    def chip_sum(position):
        picked = [lax.dynamic_index_in_dim(p, position, 0, keepdims=False) for p in kept]
        return sum(p.astype(F32) for p in picked)

    base = driving[0].astype(F32) + chip_sum(lad)
    terms = [chip_sum(lax.rem(lad + step, lad_count)).astype(BF16) for step in range(1, lad_count)]
    returned = []
    for half in range(HALVES):
        blocks = [arrived[(k, half if k or not paired else 0)] for k in far_first]
        if returned:
            blocks, made = lax.optimization_barrier((blocks, made))
        made = apply_cycle(half, plan, weight, mixing, blocks, width)
        if not half:
            behind, terms = lax.optimization_barrier((made[1:], terms))
            made = [made[0], *behind]
        returned.append([exchange(block, k) for k, block in zip(far_first, made)])
    for step, term in enumerate(terms, 1):
        pairs = [(i, (i + step) % lad_count) for i in range(lad_count)]
        base = base + lax.ppermute(term, "lad", pairs).astype(F32)
    updated = None
    for half in range(HALVES):
        updated = finish(half, pick, base, part_column, hole_row, returned[half], updated)
    return updated[None]


def solution(mesh):
    placed = (
        P(("parts", "chan"), ("lad", "sub"), None),
        P(("parts", "chan"), ("lad", "sub"), None),
        P("chan", ("lad", "sub"), None),
        P("chan", None, ("lad", "sub")),
        P("chan", ("lad", "sub"), None, None),
        P("chan", ("lad", "sub"), None, None, None),
        P(("parts", "chan"), ("lad", "sub")),
        P("parts"),
    )
    return jax.shard_map(
        body,
        mesh=mesh,
        in_specs=placed,
        out_specs=P(("parts", "chan"), ("lad", "sub"), None),
        check_vma=False,
    )
```

```python
import functools

import jax
import jax.numpy as jnp
from jax import lax
from jax.experimental import pallas as pl
from jax.experimental.pallas import tpu as pltpu
from jax.sharding import PartitionSpec as P

VMEM_LIMIT = 28 * 1024 * 1024
HALVES = 2
F32 = jnp.float32
BF16 = jnp.bfloat16
CHEAP = pl.CostEstimate(flops=0, bytes_accessed=0, transcendentals=0)
DEAR = pl.CostEstimate(flops=3 * 10**10, bytes_accessed=10**6, transcendentals=0)


def params():
    return pltpu.CompilerParams(vmem_limit_bytes=VMEM_LIMIT)


def in_hbm(*arrays):
    return [pltpu.with_memory_space_constraint(a, pltpu.HBM) for a in arrays]


def whole(memory=pltpu.VMEM):
    return pl.BlockSpec(memory_space=memory)


def selection(match):
    return jnp.where(match, 1.0, 0.0).astype(BF16)


def block_offsets(paired, chan_count, block_rows):
    chan = lax.axis_index("chan")
    return [(chan ^ k) * block_rows for k in range(chan_count)] if paired else [0]


def slots_of(owners, send, names):
    lane = 128
    pieces = owners.shape[1] // lane
    before = selection(
        lax.broadcasted_iota(jnp.int32, (lane, 2 * lane), 0)
        < lax.broadcasted_iota(jnp.int32, (lane, 2 * lane), 1)
    )
    hot = [
        lax.broadcasted_iota(jnp.int32, (names, lane), 0) == owners[:, i * lane : (i + 1) * lane]
        for i in range(pieces)
    ]
    counts = jnp.dot(
        jnp.concatenate([selection(h) for h in hot], axis=0), before, preferred_element_type=F32
    )
    passed = jnp.zeros((names, lane), F32)
    slots = []
    for i in range(pieces):
        within = counts[i * names : (i + 1) * names]
        slots.append(jnp.sum(jnp.where(hot[i], within[:, :lane] + passed, 0.0), axis=0, keepdims=True))
        passed = passed + within[:, lane:]
    return owners * send + jnp.concatenate(slots, axis=1).astype(jnp.int32)


def pack_kernel(plan, given, route_in, amps_hbm, *refs):
    paired, chan_count, send, block_rows, items = plan
    outs, (route_ref, amps_ref, sems) = refs[:-3], refs[-3:]
    block_refs = outs if given else outs[1:]
    amps_copy = pltpu.make_async_copy(amps_hbm.at[:, pl.ds(0, amps_ref.shape[1])], amps_ref, sems.at[1])
    if given:
        amps_copy.start()
        target = route_in[...]
    else:
        route_copy = pltpu.make_async_copy(route_in, route_ref, sems.at[0])
        route_copy.start()
        amps_copy.start()
        route_copy.wait()
        target = slots_of(route_ref[...], send, max(16, chan_count))
        outs[0][...] = target
    offsets = block_offsets(paired, chan_count, block_rows)
    slot = lax.broadcasted_iota(jnp.int32, (block_rows, target.shape[1]), 0)
    for i, (k, first, width) in enumerate(items):
        pick = selection(slot == target - offsets[k])
        if i == 0:
            amps_copy.wait()
        block_refs[i][...] = jnp.dot(
            pick, amps_ref[:, pl.ds(first, width)], preferred_element_type=F32
        ).astype(BF16)


def pack(plan, given, route_row, amps, name):
    rows = amps.shape[0]
    block_rows, items = plan[3], plan[4]
    columns = max(first + width for _, first, width in items)
    extra = [] if given else [pltpu.VMEM((1, rows), jnp.int32)]
    return pl.pallas_call(
        functools.partial(pack_kernel, plan, given),
        out_shape=extra + [pltpu.VMEM((block_rows, width), BF16) for _, _, width in items],
        in_specs=[whole() if given else whole(pl.ANY), whole(pl.ANY)],
        out_specs=[whole()] * (len(extra) + len(items)),
        scratch_shapes=[
            pltpu.VMEM((1, rows), jnp.int32),
            pltpu.VMEM((rows, columns), BF16),
            pltpu.SemaphoreType.DMA((2,)),
        ],
        compiler_params=params(),
        name=name,
    )(*([route_row] if given else in_hbm(route_row)), *in_hbm(amps))


def unpack_kernel(off_ref, target_ref, out_ref):
    count = off_ref.shape[0]
    rows, capacity = out_ref.shape
    block_rows = capacity // count
    target = target_ref[...]
    slots = lax.broadcasted_iota(jnp.int32, (rows, block_rows), 1)
    for k in range(count):
        out_ref[:, pl.ds(k * block_rows, block_rows)] = selection(slots == target - off_ref[k])


def unpack_matrix(offsets, target_column, capacity):
    return pl.pallas_call(
        unpack_kernel,
        out_shape=jax.ShapeDtypeStruct((target_column.shape[0], capacity), BF16),
        in_specs=[whole(pltpu.SMEM), whole()],
        out_specs=whole(),
        compiler_params=params(),
        cost_estimate=CHEAP,
        name="unpack_matrix",
    )(offsets, target_column)


def prepare_kernel(sub_count, weight_hbm, amps_hbm, cycle_hbm, mixing_hbm, *refs):
    part_refs, out_ref = refs[:sub_count], refs[sub_count]
    weight_ref, amps_ref, cycle_ref, half_ref, mixing_ref, pair_ref, sems = refs[sub_count + 1 :]
    rows, lad_count = amps_ref.shape[0], part_refs[0].shape[0]
    chunks, chunk, capacity = cycle_ref.shape
    group = mixing_ref.shape[1]
    pairs, wide = pair_ref.shape[0], pair_ref.shape[1]
    sub = lax.axis_index("sub")
    moves, ladder = [(amps_hbm, amps_ref)], []
    for n in range(sub_count):
        share = lax.rem(sub + sub_count - 1 - n, sub_count)
        for i in range(lad_count):
            start = pl.multiple_of((i * sub_count + share) * rows, rows)
            moves.append((weight_hbm.at[pl.ds(start, rows), :], weight_ref.at[len(ladder)]))
            ladder.append((n, i))
    moves.append((mixing_hbm, mixing_ref))
    moves += [(cycle_hbm.at[pl.ds(i * chunk, chunk), :], cycle_ref.at[i]) for i in range(chunks)]
    copies = [pltpu.make_async_copy(source, held, sems.at[n]) for n, (source, held) in enumerate(moves)]
    for copy in copies:
        copy.start()
    pair_ref[...] = jnp.zeros(pair_ref.shape, BF16)
    copies[0].wait()
    for m, (n, i) in enumerate(ladder):
        copies[1 + m].wait()
        part_refs[n][i] = jnp.dot(weight_ref[m], amps_ref[...], preferred_element_type=F32).astype(BF16)
    copies[1 + len(ladder)].wait()
    for q in range(capacity // group):
        at = pl.ds(q * group % wide, group)
        pair_ref[q * group // wide, at, at] = mixing_ref[q]
    for i in range(chunks):
        copies[2 + len(ladder) + i].wait()
        for a in range(chunk // group):
            at = pl.ds(a * group, group)
            half_ref[pl.ds(i * chunk + a * group, group), :] = lax.dot_general(
                mixing_ref[i * chunk // group + a],
                cycle_ref[i, at, :],
                (((0,), (0,)), ((), ())),
                preferred_element_type=F32,
            ).astype(BF16)
    for j in range(pairs):
        at = pl.ds(j * wide, wide)
        out_ref[:, at] = jnp.dot(half_ref[:, at], pair_ref[j], preferred_element_type=F32).astype(BF16)


def prepare(weight, amps, cycle_weight, mixing, lad_count, sub_count):
    rows, holes = amps.shape
    capacity = cycle_weight.shape[0]
    groups, group = mixing.shape[0], mixing.shape[1]
    wide = group * (2 if groups % 2 == 0 else 1)
    chunks = groups // 3 if groups % 3 == 0 else 1
    outs = pl.pallas_call(
        functools.partial(prepare_kernel, sub_count),
        out_shape=[jax.ShapeDtypeStruct((lad_count, rows, holes), BF16)] * sub_count
        + [jax.ShapeDtypeStruct((capacity, capacity), BF16)],
        in_specs=[whole(pl.ANY)] * 4,
        out_specs=[whole()] * (sub_count + 1),
        scratch_shapes=[
            pltpu.VMEM((lad_count * sub_count, rows, rows), BF16),
            pltpu.VMEM((rows, holes), BF16),
            pltpu.VMEM((chunks, capacity // chunks, capacity), BF16),
            pltpu.VMEM((capacity, capacity), BF16),
            pltpu.VMEM(mixing.shape, BF16),
            pltpu.VMEM((capacity // wide, wide, wide), BF16),
            pltpu.SemaphoreType.DMA((2 + lad_count * sub_count + chunks,)),
        ],
        compiler_params=params(),
        cost_estimate=DEAR,
        name="prepare",
    )(*in_hbm(weight, amps, cycle_weight, mixing))
    return outs[:sub_count], outs[sub_count]


def cycle_kernel(half, plan, operator_ref, *refs):
    paired, chan_count, _, _ = plan
    count = len(refs) // 2
    in_refs, out_refs, block_ref = refs[:count], refs[count : 2 * count], refs[2 * count]
    block_rows, width = out_refs[0].shape
    offsets = block_offsets(paired, chan_count, block_rows)
    starts = [pl.multiple_of(offsets[count - 1 - i], block_rows) for i in range(count)]
    for in_ref, start in zip(in_refs, starts):
        part = in_ref[...] if in_ref.shape[1] == width else in_ref[:, pl.ds(half * width, width)]
        block_ref[pl.ds(start, block_rows), :] = part
    for out_ref, start in zip(out_refs, starts):
        out_ref[...] = jnp.dot(
            operator_ref[pl.ds(start, block_rows), :], block_ref[...], preferred_element_type=F32
        ).astype(BF16)


def apply_cycle(half, plan, operator, arrays, width):
    block_rows = arrays[0].shape[0]
    return pl.pallas_call(
        functools.partial(cycle_kernel, half, plan),
        out_shape=[jax.ShapeDtypeStruct((block_rows, width), BF16)] * len(arrays),
        in_specs=[whole()] * (1 + len(arrays)),
        out_specs=[whole()] * len(arrays),
        scratch_shapes=[pltpu.VMEM((operator.shape[0], width), BF16)],
        compiler_params=params(),
        cost_estimate=DEAR,
        name="apply_cycle",
    )(operator, *arrays)


def finish_kernel(half, count, tiles, pick_ref, base_ref, part_ref, hole_ref, *refs):
    in_refs, (out_hbm, block_ref, out_ref, sems) = refs[:count], refs[-4:]
    block_rows, width = in_refs[0].shape
    tile = out_ref.shape[0] // tiles
    columns = pl.ds(half * width, width)
    for i, in_ref in enumerate(in_refs):
        block_ref[pl.ds((count - 1 - i) * block_rows, block_rows), :] = in_ref[...]
    copies = []
    for t in range(tiles):
        at = pl.ds(t * tile, tile)
        back = jnp.dot(pick_ref[at, :], block_ref[...], preferred_element_type=F32)
        total = base_ref[at, columns] + back
        out_ref[at, :] = (total / (part_ref[at, :] + hole_ref[:, columns])).astype(BF16)
        copies.append(pltpu.make_async_copy(out_ref.at[at, :], out_hbm.at[at, columns], sems.at[t]))
        copies[-1].start()
    for copy in copies:
        copy.wait()


def finish(half, pick, base, part_column, hole_row, arrays, earlier):
    rows, holes = base.shape
    tiles, width = 3, holes // HALVES
    operands = [pick, base, part_column, hole_row, *arrays]
    in_specs = [whole()] * len(operands)
    aliases = {}
    if earlier is not None:
        aliases = {len(operands): 0}
        operands.append(earlier)
        in_specs.append(whole(pl.ANY))
    return pl.pallas_call(
        functools.partial(finish_kernel, half, len(arrays), tiles),
        out_shape=jax.ShapeDtypeStruct((rows, holes), BF16),
        in_specs=in_specs,
        out_specs=whole(pl.ANY),
        scratch_shapes=[
            pltpu.VMEM((pick.shape[1], width), BF16),
            pltpu.VMEM((rows, width), BF16),
            pltpu.SemaphoreType.DMA((tiles,)),
        ],
        input_output_aliases=aliases,
        compiler_params=params(),
        cost_estimate=CHEAP,
        name="finish",
    )(*operands)


def body(amplitudes, driving, route, ladder_weight, ph_weight, recouple, gap_part, gap_hole):
    amps = amplitudes[0]
    rows, holes = amps.shape
    chan_count = lax.axis_size("chan")
    lad_count = lax.axis_size("lad")
    sub_count = lax.axis_size("sub")
    chan, lad, sub = lax.axis_index("chan"), lax.axis_index("lad"), lax.axis_index("sub")
    weight, mixing = ph_weight[0, 0], recouple[0, 0]
    capacity = weight.shape[0]
    send = capacity // chan_count
    paired = send % mixing.shape[1] == 0 and chan_count & (chan_count - 1) == 0
    if paired:
        block_rows = send
        block_index = jnp.stack([chan ^ k for k in range(chan_count)]).astype(jnp.int32)
    else:
        block_rows = capacity
        block_index = jnp.zeros((1,), jnp.int32)
    offsets = block_index * block_rows

    def exchange(block, k):
        if not paired:
            split = block.reshape(chan_count, send, -1)
            split = lax.all_to_all(split, "chan", split_axis=0, concat_axis=0, tiled=True)
            return split.reshape(capacity, -1)
        return lax.ppermute(block, "chan", [(i, i ^ k) for i in range(chan_count)]) if k else block

    far_first = list(reversed(range(block_index.shape[0])))
    count = len(far_first)
    width = holes // HALVES
    route_row = route[0].reshape(1, rows)
    plan = (paired, chan_count, send, block_rows)
    early = [(k, 0, width) for k in far_first if k or not paired]
    late = [(k, h * width, width) for h in range(1, HALVES) for k in far_first if k or not paired]
    late += [(0, 0, holes)] if paired else []
    target, *blocks = pack(plan + (early,), False, route_row, amps, "pack_first")
    arrived = {(k, 0): exchange(block, k) for (k, _, _), block in zip(early, blocks)}
    if paired:
        near = (1, 0)
        target, arrived[near] = lax.optimization_barrier((target, arrived[near]))
    blocks = pack(plan + (late,), True, target, amps, "pack_rest")
    for (k, first, _), block in zip(late, blocks):
        arrived[(k, first // width)] = exchange(block, k)

    part_column, hole_row = gap_part[0].reshape(rows, 1), gap_hole.reshape(1, holes)
    amps, blocks = lax.optimization_barrier((amps, blocks))
    pick = unpack_matrix(offsets, target.reshape(rows, 1), capacity)

    parts, operator = prepare(ladder_weight[0], amps, weight, mixing, lad_count, sub_count)
    kept = [parts[-1]]
    for step in range(1, sub_count):
        pairs = [(i, (i + step) % sub_count) for i in range(sub_count)]
        kept.append(lax.ppermute(parts[sub_count - 1 - step], "sub", pairs))

    def chip_sum(position):
        picked = [lax.dynamic_index_in_dim(p, position, 0, keepdims=False) for p in kept]
        return sum(p.astype(F32) for p in picked)

    base = driving[0].astype(F32) + chip_sum(lad)
    terms = [chip_sum(lax.rem(lad + step, lad_count)).astype(BF16) for step in range(1, lad_count)]
    returned = []
    for half in range(HALVES):
        blocks = [arrived[(k, half if k or not paired else 0)] for k in far_first]
        if returned:
            blocks, made = lax.optimization_barrier((blocks, made))
        made = apply_cycle(half, plan, operator, blocks, width)
        if not half:
            behind, terms = lax.optimization_barrier((made[1:], terms))
            made = [made[0], *behind]
        returned.append([exchange(block, k) for k, block in zip(far_first, made)])
    for step, term in enumerate(terms, 1):
        pairs = [(i, (i + step) % lad_count) for i in range(lad_count)]
        base = base + lax.ppermute(term, "lad", pairs).astype(F32)
    updated = None
    for half in range(HALVES):
        updated = finish(half, pick, base, part_column, hole_row, returned[half], updated)
    return updated[None]


def solution(mesh):
    placed = (
        P(("parts", "chan"), ("lad", "sub"), None),
        P(("parts", "chan"), ("lad", "sub"), None),
        P("chan", ("lad", "sub"), None),
        P("chan", None, ("lad", "sub")),
        P("chan", ("lad", "sub"), None, None),
        P("chan", ("lad", "sub"), None, None, None),
        P(("parts", "chan"), ("lad", "sub")),
        P("parts"),
    )
    return jax.shard_map(
        body,
        mesh=mesh,
        in_specs=placed,
        out_specs=P(("parts", "chan"), ("lad", "sub"), None),
        check_vma=False,
    )
```

```python
import functools

import jax
import jax.numpy as jnp
from jax import lax
from jax.experimental import pallas as pl
from jax.experimental.pallas import tpu as pltpu
from jax.sharding import PartitionSpec as P

VMEM_LIMIT = 28 * 1024 * 1024
F32 = jnp.float32
BF16 = jnp.bfloat16
CHEAP = pl.CostEstimate(flops=0, bytes_accessed=0, transcendentals=0)
DEAR = pl.CostEstimate(flops=3 * 10**10, bytes_accessed=10**6, transcendentals=0)


def params():
    return pltpu.CompilerParams(vmem_limit_bytes=VMEM_LIMIT)


def in_hbm(*arrays):
    return [pltpu.with_memory_space_constraint(a, pltpu.HBM) for a in arrays]


def whole(memory=pltpu.VMEM):
    return pl.BlockSpec(memory_space=memory)


def selection(match):
    return jnp.where(match, 1.0, 0.0).astype(BF16)


def block_offsets(paired, chan_count, send):
    chan = lax.axis_index("chan")
    return [(chan ^ k) * send for k in range(chan_count)] if paired else [0]


def slots_of(owners, send, names):
    lane = 128
    pieces = owners.shape[1] // lane
    before = selection(
        lax.broadcasted_iota(jnp.int32, (lane, 2 * lane), 0)
        < lax.broadcasted_iota(jnp.int32, (lane, 2 * lane), 1)
    )
    hot = [
        lax.broadcasted_iota(jnp.int32, (names, lane), 0) == owners[:, i * lane : (i + 1) * lane]
        for i in range(pieces)
    ]
    counts = jnp.dot(
        jnp.concatenate([selection(h) for h in hot], axis=0), before, preferred_element_type=F32
    )
    passed = jnp.zeros((names, lane), F32)
    slots = []
    for i in range(pieces):
        within = counts[i * names : (i + 1) * names]
        slots.append(jnp.sum(jnp.where(hot[i], within[:, :lane] + passed, 0.0), axis=0, keepdims=True))
        passed = passed + within[:, lane:]
    return owners * send + jnp.concatenate(slots, axis=1).astype(jnp.int32), passed


def pack_kernel(plan, given, route_in, amps_hbm, *refs):
    paired, chan_count, send, items = plan
    outs, (route_ref, amps_ref, sems) = refs[:-3], refs[-3:]
    block_refs = outs if given else outs[2:]
    amps_copy = pltpu.make_async_copy(amps_hbm, amps_ref, sems.at[1])
    if given:
        amps_copy.start()
        target = route_in[...]
    else:
        route_copy = pltpu.make_async_copy(route_in, route_ref, sems.at[0])
        route_copy.start()
        amps_copy.start()
        route_copy.wait()
        target, counts = slots_of(route_ref[...], send, outs[1].shape[0])
        outs[0][...] = target
        outs[1][...] = counts
    offsets = block_offsets(paired, chan_count, send)
    for i, (k, first, size) in enumerate(items):
        slot = lax.broadcasted_iota(jnp.int32, (size, target.shape[1]), 0)
        pick = selection(slot == target - (offsets[k] + first))
        if i == 0:
            amps_copy.wait()
        block_refs[i][...] = jnp.dot(pick, amps_ref[...], preferred_element_type=F32).astype(BF16)


def pack(plan, given, route_row, amps, name):
    rows, holes = amps.shape
    items = plan[3]
    extra = [] if given else [pltpu.VMEM((1, rows), jnp.int32), pltpu.VMEM((max(16, plan[1]), 128), F32)]
    return pl.pallas_call(
        functools.partial(pack_kernel, plan, given),
        out_shape=extra + [pltpu.VMEM((size, holes), BF16) for _, _, size in items],
        in_specs=[whole() if given else whole(pl.ANY), whole(pl.ANY)],
        out_specs=[whole()] * (len(extra) + len(items)),
        scratch_shapes=[
            pltpu.VMEM((1, rows), jnp.int32),
            pltpu.VMEM((rows, holes), BF16),
            pltpu.SemaphoreType.DMA((2,)),
        ],
        compiler_params=params(),
        name=name,
    )(*([route_row] if given else in_hbm(route_row)), *in_hbm(amps))


def unpack_kernel(off_ref, target_ref, out_ref):
    count = off_ref.shape[0]
    rows, capacity = out_ref.shape
    block_rows = capacity // count
    target = target_ref[...]
    slots = lax.broadcasted_iota(jnp.int32, (rows, block_rows), 1)
    for k in range(count):
        out_ref[:, pl.ds(k * block_rows, block_rows)] = selection(slots == target - off_ref[k])


def unpack_matrix(offsets, target_column, capacity):
    return pl.pallas_call(
        unpack_kernel,
        out_shape=jax.ShapeDtypeStruct((target_column.shape[0], capacity), BF16),
        in_specs=[whole(pltpu.SMEM), whole()],
        out_specs=whole(),
        compiler_params=params(),
        cost_estimate=CHEAP,
        name="unpack_matrix",
    )(offsets, target_column)


def prepare_kernel(sub_count, weight_hbm, amps_hbm, cycle_hbm, mixing_hbm, *refs):
    part_refs, out_ref = refs[:sub_count], refs[sub_count]
    weight_ref, amps_ref, cycle_ref, half_ref, mixing_ref, pair_ref, sems = refs[sub_count + 1 :]
    rows, lad_count = amps_ref.shape[0], part_refs[0].shape[0]
    chunks, chunk, capacity = cycle_ref.shape
    group = mixing_ref.shape[1]
    pairs, wide = pair_ref.shape[0], pair_ref.shape[1]
    sub = lax.axis_index("sub")
    moves, ladder = [(amps_hbm, amps_ref)], []
    for n in range(sub_count):
        share = lax.rem(sub + sub_count - 1 - n, sub_count)
        for i in range(lad_count):
            start = pl.multiple_of((i * sub_count + share) * rows, rows)
            moves.append((weight_hbm.at[pl.ds(start, rows), :], weight_ref.at[len(ladder)]))
            ladder.append((n, i))
    moves.append((mixing_hbm, mixing_ref))
    moves += [(cycle_hbm.at[pl.ds(i * chunk, chunk), :], cycle_ref.at[i]) for i in range(chunks)]
    copies = [pltpu.make_async_copy(source, held, sems.at[n]) for n, (source, held) in enumerate(moves)]
    for copy in copies:
        copy.start()
    pair_ref[...] = jnp.zeros(pair_ref.shape, BF16)
    copies[0].wait()
    for m, (n, i) in enumerate(ladder):
        copies[1 + m].wait()
        part_refs[n][i] = jnp.dot(weight_ref[m], amps_ref[...], preferred_element_type=F32).astype(BF16)
    copies[1 + len(ladder)].wait()
    for q in range(capacity // group):
        at = pl.ds(q * group % wide, group)
        pair_ref[q * group // wide, at, at] = mixing_ref[q]
    for i in range(chunks):
        copies[2 + len(ladder) + i].wait()
        for a in range(chunk // group):
            at = pl.ds(a * group, group)
            half_ref[pl.ds(i * chunk + a * group, group), :] = lax.dot_general(
                mixing_ref[i * chunk // group + a],
                cycle_ref[i, at, :],
                (((0,), (0,)), ((), ())),
                preferred_element_type=F32,
            ).astype(BF16)
    for j in range(pairs):
        at = pl.ds(j * wide, wide)
        out_ref[:, at] = jnp.dot(half_ref[:, at], pair_ref[j], preferred_element_type=F32).astype(BF16)


def prepare(weight, amps, cycle_weight, mixing, lad_count, sub_count):
    rows, holes = amps.shape
    capacity = cycle_weight.shape[0]
    groups, group = mixing.shape[0], mixing.shape[1]
    wide = group * (2 if groups % 2 == 0 else 1)
    chunks = groups // 3 if groups % 3 == 0 else 1
    outs = pl.pallas_call(
        functools.partial(prepare_kernel, sub_count),
        out_shape=[jax.ShapeDtypeStruct((lad_count, rows, holes), BF16)] * sub_count
        + [jax.ShapeDtypeStruct((capacity, capacity), BF16)],
        in_specs=[whole(pl.ANY)] * 4,
        out_specs=[whole()] * (sub_count + 1),
        scratch_shapes=[
            pltpu.VMEM((lad_count * sub_count, rows, rows), BF16),
            pltpu.VMEM((rows, holes), BF16),
            pltpu.VMEM((chunks, capacity // chunks, capacity), BF16),
            pltpu.VMEM((capacity, capacity), BF16),
            pltpu.VMEM(mixing.shape, BF16),
            pltpu.VMEM((capacity // wide, wide, wide), BF16),
            pltpu.SemaphoreType.DMA((2 + lad_count * sub_count + chunks,)),
        ],
        compiler_params=params(),
        cost_estimate=DEAR,
        name="prepare",
    )(*in_hbm(weight, amps, cycle_weight, mixing))
    return outs[:sub_count], outs[sub_count]


def cycle_kernel(plan, operator_ref, *refs):
    paired, chan_count, send, items = plan
    in_refs, out_refs, block_ref = refs[: len(items)], refs[len(items) : -1], refs[-1]
    offsets = block_offsets(paired, chan_count, send)
    align = 128 if paired else block_ref.shape[0]
    places = [pl.ds(pl.multiple_of(offsets[k] + first, align), size) for k, first, size in items]
    for in_ref, at in zip(in_refs, places):
        block_ref[at, :] = in_ref[...]
    for out_ref, at in zip(out_refs, places):
        out_ref[...] = jnp.dot(operator_ref[at, :], block_ref[...], preferred_element_type=F32).astype(BF16)


def apply_cycle(plan, operator, arrays):
    return pl.pallas_call(
        functools.partial(cycle_kernel, plan),
        out_shape=[jax.ShapeDtypeStruct(a.shape, BF16) for a in arrays],
        in_specs=[whole()] * (1 + len(arrays)),
        out_specs=[whole()] * len(arrays),
        scratch_shapes=[pltpu.VMEM((operator.shape[0], arrays[0].shape[1]), BF16)],
        compiler_params=params(),
        cost_estimate=DEAR,
        name="apply_cycle",
    )(operator, *arrays)


def finish_kernel(plan, tiles, pick_ref, base_ref, part_ref, hole_ref, *refs):
    _, _, send, items = plan
    in_refs, (out_hbm, block_ref, out_ref, sems) = refs[: len(items)], refs[len(items) :]
    tile = out_ref.shape[0] // tiles
    for (k, first, size), in_ref in zip(items, in_refs):
        block_ref[pl.ds(k * send + first, size), :] = in_ref[...]
    copies = []
    for t in range(tiles):
        at = pl.ds(t * tile, tile)
        back = jnp.dot(pick_ref[at, :], block_ref[...], preferred_element_type=F32)
        total = base_ref[at, :] + back
        out_ref[at, :] = (total / (part_ref[at, :] + hole_ref[...])).astype(BF16)
        copies.append(pltpu.make_async_copy(out_ref.at[at, :], out_hbm.at[at, :], sems.at[t]))
        copies[-1].start()
    for copy in copies:
        copy.wait()


def finish(plan, pick, base, part_column, hole_row, arrays):
    rows, holes = base.shape
    tiles = 3
    operands = [pick, base, part_column, hole_row, *arrays]
    return pl.pallas_call(
        functools.partial(finish_kernel, plan, tiles),
        out_shape=jax.ShapeDtypeStruct((rows, holes), BF16),
        in_specs=[whole()] * len(operands),
        out_specs=whole(pl.ANY),
        scratch_shapes=[
            pltpu.VMEM((pick.shape[1], holes), BF16),
            pltpu.VMEM((rows, holes), BF16),
            pltpu.SemaphoreType.DMA((tiles,)),
        ],
        compiler_params=params(),
        cost_estimate=CHEAP,
        name="finish",
    )(*operands)


def body(amplitudes, driving, route, ladder_weight, ph_weight, recouple, gap_part, gap_hole):
    amps = amplitudes[0]
    rows, holes = amps.shape
    chan_count = lax.axis_size("chan")
    lad_count = lax.axis_size("lad")
    sub_count = lax.axis_size("sub")
    chan, lad, sub = lax.axis_index("chan"), lax.axis_index("lad"), lax.axis_index("sub")
    weight, mixing = ph_weight[0, 0], recouple[0, 0]
    capacity = weight.shape[0]
    send = capacity // chan_count
    paired = send % mixing.shape[1] == 0 and chan_count & (chan_count - 1) == 0
    if paired:
        offsets = jnp.stack([(chan ^ k) * send for k in range(chan_count)]).astype(jnp.int32)
        first = send - mixing.shape[1] if send > mixing.shape[1] else send
        early = [(k, 0, first) for k in reversed(range(1, chan_count))]
        late = [(k, first, send - first) for k in reversed(range(1, chan_count)) if send > first]
        own = [(0, 0, send)]
    else:
        offsets = jnp.zeros((1,), jnp.int32)
        early, late, own = [(0, 0, capacity)], [], []
    items = early + late + own
    plan = (paired, chan_count, send)

    def exchange(arrays):
        if not paired:
            split = arrays[0].reshape(chan_count, send, holes)
            split = lax.all_to_all(split, "chan", split_axis=0, concat_axis=0, tiled=True)
            return [split.reshape(capacity, holes)]
        return [
            lax.ppermute(a, "chan", [(i, i ^ k) for i in range(chan_count)]) for (k, _, _), a in zip(early, arrays)
        ]

    def crowded(counts):
        others = chan_count * lad_count * sub_count
        lines = -(-chan_count // 8) * 8
        sent = jnp.broadcast_to(counts[:lines][None], (others, lines, 128))
        every = lax.all_to_all(sent, ("chan", "lad", "sub"), split_axis=0, concat_axis=0, tiled=True)
        over = (jnp.max(every, axis=(0, 2))[:chan_count] > first).astype(jnp.int32)
        which = jnp.sum(over * (1 + jnp.arange(chan_count, dtype=jnp.int32)))
        return jnp.where(jnp.sum(over) > 1, chan_count + 1, which)

    def along(axis, arrays):
        size = lax.axis_size(axis)
        return [
            lax.ppermute(a, axis, [(i, (i + step) % size) for i in range(size)]) for step, a in enumerate(arrays, 1)
        ]

    def exchange_late(index, before, axis, terms, arrays, back):
        def case(pairs_of, before, terms, arrays):
            sent = exchange(before) if before else []
            moved = [
                lax.ppermute(a, "chan", pairs_of(k)) if pairs_of else jnp.zeros_like(a)
                for (k, _, _), a in zip(late, arrays)
            ]
            return sent, along(axis, terms), moved

        def single(d, k):
            return [(d, d ^ k) if back else (d ^ k, d)]

        def several(k):
            return [(i, i ^ k) for i in range(chan_count)]

        if not late:
            return case(None, before, terms, arrays)
        kinds = [None] + [functools.partial(single, d) for d in range(chan_count)] + [several]
        return lax.switch(index, [functools.partial(case, kind) for kind in kinds], before, terms, arrays)

    route_row = route[0].reshape(1, rows)
    target, counts, *blocks = pack(plan + (early,), False, route_row, amps, "pack_first")
    arrived = exchange(blocks)
    amps, target, counts = lax.optimization_barrier((amps, target, counts))
    if paired:
        amps, target, arrived[-1] = lax.optimization_barrier((amps, target, arrived[-1]))
    index = crowded(counts) if late else None
    packed = []
    if late or own:
        packed = pack(plan + (late + own,), True, target, amps, "pack_rest")
        amps, packed = lax.optimization_barrier((amps, packed))
    extra, mine = packed[: len(late)], packed[len(late) :]
    pick = unpack_matrix(offsets, target.reshape(rows, 1), capacity)
    amps, pick = lax.optimization_barrier((amps, pick))
    parts, operator = prepare(ladder_weight[0], amps, weight, mixing, lad_count, sub_count)
    _, _, extra = exchange_late(index, [], "sub", [], extra, False)
    extra, parts = lax.optimization_barrier((extra, parts))
    kept = [parts[-1], *along("sub", list(reversed(parts[:-1])))]

    def chip_sum(position):
        picked = [lax.dynamic_index_in_dim(p, position, 0, keepdims=False) for p in kept]
        return sum(p.astype(F32) for p in picked)

    part_column, hole_row = gap_part[0].reshape(rows, 1), gap_hole.reshape(1, holes)
    base = driving[0].astype(F32) + chip_sum(lad)
    terms = [chip_sum(lax.rem(lad + step, lad_count)).astype(BF16) for step in range(1, lad_count)]
    made = apply_cycle(plan + (items,), operator, [*arrived, *extra, *mine])
    made_early, made_late, made_own = made[: len(early)], made[len(early) : len(early + late)], made[len(early + late) :]
    returned, arrived_terms, returned_late = exchange_late(index, made_early, "lad", terms, made_late, True)
    for term in arrived_terms:
        base = base + term.astype(F32)
    updated = finish(plan + (items,), pick, base, part_column, hole_row, [*returned, *returned_late, *made_own])
    return updated[None]


def solution(mesh):
    placed = (
        P(("parts", "chan"), ("lad", "sub"), None),
        P(("parts", "chan"), ("lad", "sub"), None),
        P("chan", ("lad", "sub"), None),
        P("chan", None, ("lad", "sub")),
        P("chan", ("lad", "sub"), None, None),
        P("chan", ("lad", "sub"), None, None, None),
        P(("parts", "chan"), ("lad", "sub")),
        P("parts"),
    )
    return jax.shard_map(
        body,
        mesh=mesh,
        in_specs=placed,
        out_specs=P(("parts", "chan"), ("lad", "sub"), None),
        check_vma=False,
    )
```

```python
import functools

import jax
import jax.numpy as jnp
from jax import lax
from jax.experimental import pallas as pl
from jax.experimental.pallas import tpu as pltpu
from jax.sharding import PartitionSpec as P

VMEM_LIMIT = 28 * 1024 * 1024
HALVES = 2
F32 = jnp.float32
BF16 = jnp.bfloat16
CHEAP = pl.CostEstimate(flops=0, bytes_accessed=0, transcendentals=0)
DEAR = pl.CostEstimate(flops=3 * 10**10, bytes_accessed=10**6, transcendentals=0)


def params():
    return pltpu.CompilerParams(vmem_limit_bytes=VMEM_LIMIT)


def in_hbm(*arrays):
    return [pltpu.with_memory_space_constraint(a, pltpu.HBM) for a in arrays]


def whole(memory=pltpu.VMEM):
    return pl.BlockSpec(memory_space=memory)


def selection(match):
    return jnp.where(match, 1.0, 0.0).astype(BF16)


def block_offsets(paired, chan_count, block_rows):
    chan = lax.axis_index("chan")
    return [(chan ^ k) * block_rows for k in range(chan_count)] if paired else [0]


def slots_of(owners, send, names):
    lane = 128
    pieces = owners.shape[1] // lane
    before = selection(
        lax.broadcasted_iota(jnp.int32, (lane, 2 * lane), 0)
        < lax.broadcasted_iota(jnp.int32, (lane, 2 * lane), 1)
    )
    hot = [
        lax.broadcasted_iota(jnp.int32, (names, lane), 0) == owners[:, i * lane : (i + 1) * lane]
        for i in range(pieces)
    ]
    counts = jnp.dot(
        jnp.concatenate([selection(h) for h in hot], axis=0), before, preferred_element_type=F32
    )
    passed = jnp.zeros((names, lane), F32)
    slots = []
    for i in range(pieces):
        within = counts[i * names : (i + 1) * names]
        slots.append(jnp.sum(jnp.where(hot[i], within[:, :lane] + passed, 0.0), axis=0, keepdims=True))
        passed = passed + within[:, lane:]
    return owners * send + jnp.concatenate(slots, axis=1).astype(jnp.int32)


def pack_kernel(plan, given, route_in, amps_hbm, *refs):
    paired, chan_count, send, block_rows, items = plan
    outs, (route_ref, amps_ref, sems) = refs[:-3], refs[-3:]
    block_refs = outs if given else outs[1:]
    amps_copy = pltpu.make_async_copy(amps_hbm.at[:, pl.ds(0, amps_ref.shape[1])], amps_ref, sems.at[1])
    if given:
        amps_copy.start()
        target = route_in[...]
    else:
        route_copy = pltpu.make_async_copy(route_in, route_ref, sems.at[0])
        route_copy.start()
        amps_copy.start()
        route_copy.wait()
        target = slots_of(route_ref[...], send, max(16, chan_count))
        outs[0][...] = target
    offsets = block_offsets(paired, chan_count, block_rows)
    slot = lax.broadcasted_iota(jnp.int32, (block_rows, target.shape[1]), 0)
    for i, (k, first, width) in enumerate(items):
        pick = selection(slot == target - offsets[k])
        if i == 0:
            amps_copy.wait()
        block_refs[i][...] = jnp.dot(
            pick, amps_ref[:, pl.ds(first, width)], preferred_element_type=F32
        ).astype(BF16)


def pack(plan, given, route_row, amps, name):
    rows = amps.shape[0]
    block_rows, items = plan[3], plan[4]
    columns = max(first + width for _, first, width in items)
    extra = [] if given else [pltpu.VMEM((1, rows), jnp.int32)]
    return pl.pallas_call(
        functools.partial(pack_kernel, plan, given),
        out_shape=extra + [pltpu.VMEM((block_rows, width), BF16) for _, _, width in items],
        in_specs=[whole() if given else whole(pl.ANY), whole(pl.ANY)],
        out_specs=[whole()] * (len(extra) + len(items)),
        scratch_shapes=[
            pltpu.VMEM((1, rows), jnp.int32),
            pltpu.VMEM((rows, columns), BF16),
            pltpu.SemaphoreType.DMA((2,)),
        ],
        compiler_params=params(),
        name=name,
    )(*([route_row] if given else in_hbm(route_row)), *in_hbm(amps))


def unpack_kernel(off_ref, target_ref, out_ref):
    count = off_ref.shape[0]
    rows, capacity = out_ref.shape
    block_rows = capacity // count
    target = target_ref[...]
    slots = lax.broadcasted_iota(jnp.int32, (rows, block_rows), 1)
    for k in range(count):
        out_ref[:, pl.ds(k * block_rows, block_rows)] = selection(slots == target - off_ref[k])


def unpack_matrix(offsets, target_column, capacity):
    return pl.pallas_call(
        unpack_kernel,
        out_shape=jax.ShapeDtypeStruct((target_column.shape[0], capacity), BF16),
        in_specs=[whole(pltpu.SMEM), whole()],
        out_specs=whole(),
        compiler_params=params(),
        cost_estimate=CHEAP,
        name="unpack_matrix",
    )(offsets, target_column)


def prepare_kernel(sub_count, weight_hbm, amps_hbm, cycle_hbm, mixing_hbm, *refs):
    part_refs, out_ref = refs[:sub_count], refs[sub_count]
    weight_ref, amps_ref, cycle_ref, half_ref, mixing_ref, pair_ref, sems = refs[sub_count + 1 :]
    rows, lad_count = amps_ref.shape[0], part_refs[0].shape[0]
    chunks, chunk, capacity = cycle_ref.shape
    group = mixing_ref.shape[1]
    pairs, wide = pair_ref.shape[0], pair_ref.shape[1]
    sub = lax.axis_index("sub")
    moves, ladder = [(amps_hbm, amps_ref)], []
    for n in range(sub_count):
        share = lax.rem(sub + sub_count - 1 - n, sub_count)
        for i in range(lad_count):
            start = pl.multiple_of((i * sub_count + share) * rows, rows)
            moves.append((weight_hbm.at[pl.ds(start, rows), :], weight_ref.at[len(ladder)]))
            ladder.append((n, i))
    moves.append((mixing_hbm, mixing_ref))
    moves += [(cycle_hbm.at[pl.ds(i * chunk, chunk), :], cycle_ref.at[i]) for i in range(chunks)]
    copies = [pltpu.make_async_copy(source, held, sems.at[n]) for n, (source, held) in enumerate(moves)]
    for copy in copies:
        copy.start()
    pair_ref[...] = jnp.zeros(pair_ref.shape, BF16)
    copies[0].wait()
    for m, (n, i) in enumerate(ladder):
        copies[1 + m].wait()
        part_refs[n][i] = jnp.dot(weight_ref[m], amps_ref[...], preferred_element_type=F32).astype(BF16)
    copies[1 + len(ladder)].wait()
    for q in range(capacity // group):
        at = pl.ds(q * group % wide, group)
        pair_ref[q * group // wide, at, at] = mixing_ref[q]
    for i in range(chunks):
        copies[2 + len(ladder) + i].wait()
        for a in range(chunk // group):
            at = pl.ds(a * group, group)
            half_ref[pl.ds(i * chunk + a * group, group), :] = lax.dot_general(
                mixing_ref[i * chunk // group + a],
                cycle_ref[i, at, :],
                (((0,), (0,)), ((), ())),
                preferred_element_type=F32,
            ).astype(BF16)
    for j in range(pairs):
        at = pl.ds(j * wide, wide)
        out_ref[:, at] = jnp.dot(half_ref[:, at], pair_ref[j], preferred_element_type=F32).astype(BF16)


def prepare(weight, amps, cycle_weight, mixing, lad_count, sub_count):
    rows, holes = amps.shape
    capacity = cycle_weight.shape[0]
    groups, group = mixing.shape[0], mixing.shape[1]
    wide = group * (2 if groups % 2 == 0 else 1)
    chunks = groups // 3 if groups % 3 == 0 else 1
    outs = pl.pallas_call(
        functools.partial(prepare_kernel, sub_count),
        out_shape=[jax.ShapeDtypeStruct((lad_count, rows, holes), BF16)] * sub_count
        + [jax.ShapeDtypeStruct((capacity, capacity), BF16)],
        in_specs=[whole(pl.ANY)] * 4,
        out_specs=[whole()] * (sub_count + 1),
        scratch_shapes=[
            pltpu.VMEM((lad_count * sub_count, rows, rows), BF16),
            pltpu.VMEM((rows, holes), BF16),
            pltpu.VMEM((chunks, capacity // chunks, capacity), BF16),
            pltpu.VMEM((capacity, capacity), BF16),
            pltpu.VMEM(mixing.shape, BF16),
            pltpu.VMEM((capacity // wide, wide, wide), BF16),
            pltpu.SemaphoreType.DMA((2 + lad_count * sub_count + chunks,)),
        ],
        compiler_params=params(),
        cost_estimate=DEAR,
        name="prepare",
    )(*in_hbm(weight, amps, cycle_weight, mixing))
    return outs[:sub_count], outs[sub_count]


def cycle_kernel(half, plan, operator_ref, *refs):
    paired, chan_count, _, _ = plan
    count = len(refs) // 2
    in_refs, out_refs, block_ref = refs[:count], refs[count : 2 * count], refs[2 * count]
    block_rows, width = out_refs[0].shape
    offsets = block_offsets(paired, chan_count, block_rows)
    starts = [pl.multiple_of(offsets[count - 1 - i], block_rows) for i in range(count)]
    for in_ref, start in zip(in_refs, starts):
        part = in_ref[...] if in_ref.shape[1] == width else in_ref[:, pl.ds(half * width, width)]
        block_ref[pl.ds(start, block_rows), :] = part
    for out_ref, start in zip(out_refs, starts):
        out_ref[...] = jnp.dot(
            operator_ref[pl.ds(start, block_rows), :], block_ref[...], preferred_element_type=F32
        ).astype(BF16)


def apply_cycle(half, plan, operator, arrays, width):
    block_rows = arrays[0].shape[0]
    return pl.pallas_call(
        functools.partial(cycle_kernel, half, plan),
        out_shape=[jax.ShapeDtypeStruct((block_rows, width), BF16)] * len(arrays),
        in_specs=[whole()] * (1 + len(arrays)),
        out_specs=[whole()] * len(arrays),
        scratch_shapes=[pltpu.VMEM((operator.shape[0], width), BF16)],
        compiler_params=params(),
        cost_estimate=DEAR,
        name="apply_cycle",
    )(operator, *arrays)


def finish_kernel(half, count, tiles, pick_ref, base_ref, part_ref, hole_ref, *refs):
    in_refs, (out_hbm, block_ref, out_ref, sems) = refs[:count], refs[-4:]
    block_rows, width = in_refs[0].shape
    tile = out_ref.shape[0] // tiles
    columns = pl.ds(half * width, width)
    for i, in_ref in enumerate(in_refs):
        block_ref[pl.ds((count - 1 - i) * block_rows, block_rows), :] = in_ref[...]
    copies = []
    for t in range(tiles):
        at = pl.ds(t * tile, tile)
        back = jnp.dot(pick_ref[at, :], block_ref[...], preferred_element_type=F32)
        total = base_ref[at, columns] + back
        out_ref[at, :] = (total / (part_ref[at, :] + hole_ref[:, columns])).astype(BF16)
        copies.append(pltpu.make_async_copy(out_ref.at[at, :], out_hbm.at[at, columns], sems.at[t]))
        copies[-1].start()
    for copy in copies:
        copy.wait()


def finish(half, pick, base, part_column, hole_row, arrays, earlier):
    rows, holes = base.shape
    tiles, width = 3, holes // HALVES
    operands = [pick, base, part_column, hole_row, *arrays]
    in_specs = [whole()] * len(operands)
    aliases = {}
    if earlier is not None:
        aliases = {len(operands): 0}
        operands.append(earlier)
        in_specs.append(whole(pl.ANY))
    return pl.pallas_call(
        functools.partial(finish_kernel, half, len(arrays), tiles),
        out_shape=jax.ShapeDtypeStruct((rows, holes), BF16),
        in_specs=in_specs,
        out_specs=whole(pl.ANY),
        scratch_shapes=[
            pltpu.VMEM((pick.shape[1], width), BF16),
            pltpu.VMEM((rows, width), BF16),
            pltpu.SemaphoreType.DMA((tiles,)),
        ],
        input_output_aliases=aliases,
        compiler_params=params(),
        cost_estimate=CHEAP,
        name="finish",
    )(*operands)


def body(amplitudes, driving, route, ladder_weight, ph_weight, recouple, gap_part, gap_hole):
    amps = amplitudes[0]
    rows, holes = amps.shape
    chan_count = lax.axis_size("chan")
    lad_count = lax.axis_size("lad")
    sub_count = lax.axis_size("sub")
    chan, lad, sub = lax.axis_index("chan"), lax.axis_index("lad"), lax.axis_index("sub")
    weight, mixing = ph_weight[0, 0], recouple[0, 0]
    capacity = weight.shape[0]
    send = capacity // chan_count
    paired = send % mixing.shape[1] == 0 and chan_count & (chan_count - 1) == 0
    if paired:
        block_rows = send
        block_index = jnp.stack([chan ^ k for k in range(chan_count)]).astype(jnp.int32)
    else:
        block_rows = capacity
        block_index = jnp.zeros((1,), jnp.int32)
    offsets = block_index * block_rows

    def exchange(block, k):
        if not paired:
            split = block.reshape(chan_count, send, -1)
            split = lax.all_to_all(split, "chan", split_axis=0, concat_axis=0, tiled=True)
            return split.reshape(capacity, -1)
        return lax.ppermute(block, "chan", [(i, i ^ k) for i in range(chan_count)]) if k else block

    far_first = list(reversed(range(block_index.shape[0])))
    count = len(far_first)
    width = holes // HALVES
    route_row = route[0].reshape(1, rows)
    plan = (paired, chan_count, send, block_rows)
    early = [(k, 0, holes if k == 1 else width) for k in far_first if k or not paired]
    late = [(k, h * width, width) for h in range(1, HALVES) for k in far_first if k > 1 or not paired]
    late += [(0, 0, holes)] if paired else []
    target, *blocks = pack(plan + (early,), False, route_row, amps, "pack_first")
    arrived = {(k, 0): exchange(block, k) for (k, _, _), block in zip(early, blocks)}
    if paired:
        near = (1, 0)
        target, arrived[near] = lax.optimization_barrier((target, arrived[near]))
    blocks = pack(plan + (late,), True, target, amps, "pack_rest")
    for (k, first, _), block in zip(late, blocks):
        arrived[(k, first // width)] = exchange(block, k)

    part_column, hole_row = gap_part[0].reshape(rows, 1), gap_hole.reshape(1, holes)
    amps, blocks = lax.optimization_barrier((amps, blocks))
    pick = unpack_matrix(offsets, target.reshape(rows, 1), capacity)

    parts, operator = prepare(ladder_weight[0], amps, weight, mixing, lad_count, sub_count)
    kept = [parts[-1]]
    for step in range(1, sub_count):
        pairs = [(i, (i + step) % sub_count) for i in range(sub_count)]
        kept.append(lax.ppermute(parts[sub_count - 1 - step], "sub", pairs))

    def chip_sum(position):
        picked = [lax.dynamic_index_in_dim(p, position, 0, keepdims=False) for p in kept]
        return sum(p.astype(F32) for p in picked)

    base = driving[0].astype(F32) + chip_sum(lad)
    terms = [chip_sum(lax.rem(lad + step, lad_count)).astype(BF16) for step in range(1, lad_count)]
    returned = []
    for half in range(HALVES):
        blocks = [arrived[(k, half if k > 1 or not paired else 0)] for k in far_first]
        if returned:
            blocks, made = lax.optimization_barrier((blocks, made))
        made = apply_cycle(half, plan, operator, blocks, width)
        if not half:
            behind, terms = lax.optimization_barrier((made[2:], terms))
            made = [*made[:2], *behind]
        returned.append([exchange(block, k) for k, block in zip(far_first, made)])
    for step, term in enumerate(terms, 1):
        pairs = [(i, (i + step) % lad_count) for i in range(lad_count)]
        base = base + lax.ppermute(term, "lad", pairs).astype(F32)
    updated = None
    for half in range(HALVES):
        updated = finish(half, pick, base, part_column, hole_row, returned[half], updated)
    return updated[None]


def solution(mesh):
    placed = (
        P(("parts", "chan"), ("lad", "sub"), None),
        P(("parts", "chan"), ("lad", "sub"), None),
        P("chan", ("lad", "sub"), None),
        P("chan", None, ("lad", "sub")),
        P("chan", ("lad", "sub"), None, None),
        P("chan", ("lad", "sub"), None, None, None),
        P(("parts", "chan"), ("lad", "sub")),
        P("parts"),
    )
    return jax.shard_map(
        body,
        mesh=mesh,
        in_specs=placed,
        out_specs=P(("parts", "chan"), ("lad", "sub"), None),
        check_vma=False,
    )
```

```python
import functools

import jax
import jax.numpy as jnp
from jax import lax
from jax.experimental import pallas as pl
from jax.experimental.pallas import tpu as pltpu
from jax.sharding import PartitionSpec as P

VMEM_LIMIT = 36 * 1024 * 1024
F32 = jnp.float32
BF16 = jnp.bfloat16
CHEAP = pl.CostEstimate(flops=0, bytes_accessed=0, transcendentals=0)
DEAR = pl.CostEstimate(flops=3 * 10**10, bytes_accessed=10**6, transcendentals=0)


def params():
    return pltpu.CompilerParams(vmem_limit_bytes=VMEM_LIMIT)


def in_hbm(*arrays):
    return [pltpu.with_memory_space_constraint(a, pltpu.HBM) for a in arrays]


def whole(memory=pltpu.VMEM):
    return pl.BlockSpec(memory_space=memory)


def selection(match):
    return jnp.where(match, 1.0, 0.0).astype(BF16)


def block_offsets(paired, chan_count, send):
    chan = lax.axis_index("chan")
    return [(chan ^ k) * send for k in range(chan_count)] if paired else [0]


def slots_of(owners, send, names):
    lane = 128
    pieces = owners.shape[1] // lane
    before = selection(
        lax.broadcasted_iota(jnp.int32, (lane, 2 * lane), 0)
        < lax.broadcasted_iota(jnp.int32, (lane, 2 * lane), 1)
    )
    hot = [
        lax.broadcasted_iota(jnp.int32, (names, lane), 0) == owners[:, i * lane : (i + 1) * lane]
        for i in range(pieces)
    ]
    counts = jnp.dot(
        jnp.concatenate([selection(h) for h in hot], axis=0), before, preferred_element_type=F32
    )
    passed = jnp.zeros((names, lane), F32)
    slots = []
    for i in range(pieces):
        within = counts[i * names : (i + 1) * names]
        slots.append(jnp.sum(jnp.where(hot[i], within[:, :lane] + passed, 0.0), axis=0, keepdims=True))
        passed = passed + within[:, lane:]
    return owners * send + jnp.concatenate(slots, axis=1).astype(jnp.int32), passed


def pack_kernel(plan, given, route_in, amps_hbm, *refs):
    paired, chan_count, send, items = plan
    extra = 0 if given else 2
    outs, (route_ref, amps_ref, in_sems) = refs[: extra + len(items)], refs[extra + len(items) : extra + len(items) + 3]
    held, out_sems = refs[extra + len(items) + 3 : -1], refs[-1]
    amps_copy = pltpu.make_async_copy(amps_hbm, amps_ref, in_sems.at[1])
    if given:
        amps_copy.start()
        target = route_in[...]
    else:
        route_copy = pltpu.make_async_copy(route_in, route_ref, in_sems.at[0])
        route_copy.start()
        amps_copy.start()
        route_copy.wait()
        target, counts = slots_of(route_ref[...], send, outs[1].shape[0])
        outs[0][...] = target
        outs[1][...] = counts
    offsets = block_offsets(paired, chan_count, send)
    copies = []
    for i, (k, first, size) in enumerate(items):
        slot = lax.broadcasted_iota(jnp.int32, (size, target.shape[1]), 0)
        pick = selection(slot == target - (offsets[k] + first))
        if i == 0:
            amps_copy.wait()
        block_ref = held[i] if given else outs[extra + i]
        block_ref[...] = jnp.dot(pick, amps_ref[...], preferred_element_type=F32).astype(BF16)
        if given:
            copies.append(pltpu.make_async_copy(block_ref, outs[extra + i], out_sems.at[i]))
            copies[-1].start()
    for copy in copies:
        copy.wait()


def pack(plan, given, route_row, amps, name):
    rows, holes = amps.shape
    items = plan[3]
    extra = [] if given else [pltpu.VMEM((1, rows), jnp.int32), pltpu.VMEM((max(16, plan[1]), 128), F32)]
    place = pltpu.HBM if given else pltpu.VMEM
    return pl.pallas_call(
        functools.partial(pack_kernel, plan, given),
        out_shape=extra + [place((size, holes), BF16) for _, _, size in items],
        in_specs=[whole() if given else whole(pl.ANY), whole(pl.ANY)],
        out_specs=[whole()] * len(extra) + [whole(pl.ANY if given else pltpu.VMEM)] * len(items),
        scratch_shapes=[
            pltpu.VMEM((1, rows), jnp.int32),
            pltpu.VMEM((rows, holes), BF16),
            pltpu.SemaphoreType.DMA((2,)),
        ]
        + [pltpu.VMEM((size, holes), BF16) for _, _, size in items if given]
        + [pltpu.SemaphoreType.DMA((len(items),))],
        compiler_params=params(),
        cost_estimate=DEAR if given else CHEAP,
        name=name,
    )(*([route_row] if given else in_hbm(route_row)), *in_hbm(amps))


def unpack_kernel(off_ref, target_ref, out_ref):
    count = off_ref.shape[0]
    rows, capacity = out_ref.shape
    block_rows = capacity // count
    target = target_ref[...]
    slots = lax.broadcasted_iota(jnp.int32, (rows, block_rows), 1)
    for k in range(count):
        out_ref[:, pl.ds(k * block_rows, block_rows)] = selection(slots == target - off_ref[k])


def unpack_matrix(offsets, target_column, capacity):
    return pl.pallas_call(
        unpack_kernel,
        out_shape=jax.ShapeDtypeStruct((target_column.shape[0], capacity), BF16),
        in_specs=[whole(pltpu.SMEM), whole()],
        out_specs=whole(),
        compiler_params=params(),
        cost_estimate=CHEAP,
        name="unpack_matrix",
    )(offsets, target_column)


def prepare_kernel(sub_count, weight_hbm, amps_hbm, cycle_hbm, mixing_hbm, *refs):
    part_hbm, out_hbm = refs[:sub_count], refs[sub_count]
    weight_ref, amps_ref, cycle_ref, half_ref, mixing_ref, pair_ref, sems = refs[sub_count + 1 : sub_count + 8]
    part_ref, out_ref, out_sems = refs[sub_count + 8 :]
    rows, lad_count = amps_ref.shape[0], part_ref.shape[0] // sub_count
    chunks, chunk, capacity = cycle_ref.shape
    group = mixing_ref.shape[1]
    pairs, wide = pair_ref.shape[0], pair_ref.shape[1]
    sub = lax.axis_index("sub")
    moves, ladder = [(amps_hbm, amps_ref)], []
    for n in range(sub_count):
        share = lax.rem(sub + sub_count - 1 - n, sub_count)
        for i in range(lad_count):
            start = pl.multiple_of((i * sub_count + share) * rows, rows)
            moves.append((weight_hbm.at[pl.ds(start, rows), :], weight_ref.at[len(ladder)]))
            ladder.append((n, i))
    moves.append((mixing_hbm, mixing_ref))
    moves += [(cycle_hbm.at[pl.ds(i * chunk, chunk), :], cycle_ref.at[i]) for i in range(chunks)]
    copies = [pltpu.make_async_copy(source, held, sems.at[n]) for n, (source, held) in enumerate(moves)]
    for copy in copies:
        copy.start()
    pair_ref[...] = jnp.zeros(pair_ref.shape, BF16)
    copies[0].wait()
    out_copies = []
    for m, (n, i) in enumerate(ladder):
        copies[1 + m].wait()
        part_ref[m] = jnp.dot(weight_ref[m], amps_ref[...], preferred_element_type=F32).astype(BF16)
        out_copies.append(pltpu.make_async_copy(part_ref.at[m], part_hbm[n].at[i], out_sems.at[m]))
        out_copies[-1].start()
    copies[1 + len(ladder)].wait()
    for q in range(capacity // group):
        at = pl.ds(q * group % wide, group)
        pair_ref[q * group // wide, at, at] = mixing_ref[q]
    for i in range(chunks):
        copies[2 + len(ladder) + i].wait()
        for a in range(chunk // group):
            at = pl.ds(a * group, group)
            half_ref[pl.ds(i * chunk + a * group, group), :] = lax.dot_general(
                mixing_ref[i * chunk // group + a],
                cycle_ref[i, at, :],
                (((0,), (0,)), ((), ())),
                preferred_element_type=F32,
            ).astype(BF16)
    for j in range(pairs):
        at = pl.ds(j * wide, wide)
        out_ref[j] = jnp.dot(half_ref[:, at], pair_ref[j], preferred_element_type=F32).astype(BF16)
        out_copies.append(pltpu.make_async_copy(out_ref.at[j], out_hbm.at[:, at], out_sems.at[len(ladder) + j]))
        out_copies[-1].start()
    for copy in out_copies:
        copy.wait()


def prepare(weight, amps, cycle_weight, mixing, lad_count, sub_count):
    rows, holes = amps.shape
    capacity = cycle_weight.shape[0]
    groups, group = mixing.shape[0], mixing.shape[1]
    wide = group * (2 if groups % 2 == 0 else 1)
    chunks = groups // 3 if groups % 3 == 0 else 1
    outs = pl.pallas_call(
        functools.partial(prepare_kernel, sub_count),
        out_shape=[pltpu.HBM((lad_count, rows, holes), BF16)] * sub_count + [pltpu.HBM((capacity, capacity), BF16)],
        in_specs=[whole(pl.ANY)] * 4,
        out_specs=[whole(pl.ANY)] * (sub_count + 1),
        scratch_shapes=[
            pltpu.VMEM((lad_count * sub_count, rows, rows), BF16),
            pltpu.VMEM((rows, holes), BF16),
            pltpu.VMEM((chunks, capacity // chunks, capacity), BF16),
            pltpu.VMEM((capacity, capacity), BF16),
            pltpu.VMEM(mixing.shape, BF16),
            pltpu.VMEM((capacity // wide, wide, wide), BF16),
            pltpu.SemaphoreType.DMA((2 + lad_count * sub_count + chunks,)),
            pltpu.VMEM((lad_count * sub_count, rows, holes), BF16),
            pltpu.VMEM((capacity // wide, capacity, wide), BF16),
            pltpu.SemaphoreType.DMA((lad_count * sub_count + capacity // wide,)),
        ],
        compiler_params=params(),
        cost_estimate=DEAR,
        name="prepare",
    )(*in_hbm(weight, amps, cycle_weight, mixing))
    return outs[:sub_count], outs[sub_count]


def cycle_kernel(plan, operator_hbm, *refs):
    paired, chan_count, send, items = plan
    in_refs, out_refs, (block_ref, operator_ref, sems) = refs[: len(items)], refs[len(items) : -3], refs[-3:]
    offsets = block_offsets(paired, chan_count, send)
    align = 128 if paired else block_ref.shape[0]
    places, copies, held = [], [], 0
    for i, (k, first, size) in enumerate(items):
        places.append(pl.ds(pl.multiple_of(offsets[k] + first, align), size))
        mine = operator_ref.at[pl.ds(held, size), :]
        copies.append(pltpu.make_async_copy(operator_hbm.at[places[i], :], mine, sems.at[i]))
        copies[i].start()
        held += size
    for in_ref, at in zip(in_refs, places):
        block_ref[at, :] = in_ref[...]
    held = 0
    for i, out_ref in enumerate(out_refs):
        copies[i].wait()
        mine = operator_ref[pl.ds(held, out_ref.shape[0]), :]
        out_ref[...] = jnp.dot(mine, block_ref[...], preferred_element_type=F32).astype(BF16)
        held += out_ref.shape[0]


def apply_cycle(plan, operator, arrays):
    return pl.pallas_call(
        functools.partial(cycle_kernel, plan),
        out_shape=[jax.ShapeDtypeStruct(a.shape, BF16) for a in arrays],
        in_specs=[whole(pl.ANY)] + [whole()] * len(arrays),
        out_specs=[whole()] * len(arrays),
        scratch_shapes=[
            pltpu.VMEM((operator.shape[0], arrays[0].shape[1]), BF16),
            pltpu.VMEM(operator.shape, BF16),
            pltpu.SemaphoreType.DMA((len(arrays),)),
        ],
        compiler_params=params(),
        cost_estimate=DEAR,
        name="apply_cycle",
    )(*in_hbm(operator), *arrays)


def finish_kernel(plan, tiles, pick_ref, base_ref, part_ref, hole_ref, *refs):
    _, _, send, items = plan
    in_refs, (out_hbm, block_ref, out_ref, sems) = refs[: len(items)], refs[len(items) :]
    tile = out_ref.shape[0] // tiles
    for (k, first, size), in_ref in zip(items, in_refs):
        block_ref[pl.ds(k * send + first, size), :] = in_ref[...]
    copies = []
    for t in range(tiles):
        at = pl.ds(t * tile, tile)
        back = jnp.dot(pick_ref[at, :], block_ref[...], preferred_element_type=F32)
        total = base_ref[at, :] + back
        out_ref[at, :] = (total / (part_ref[at, :] + hole_ref[...])).astype(BF16)
        copies.append(pltpu.make_async_copy(out_ref.at[at, :], out_hbm.at[at, :], sems.at[t]))
        copies[-1].start()
    for copy in copies:
        copy.wait()


def finish(plan, pick, base, part_column, hole_row, arrays):
    rows, holes = base.shape
    tiles = 3
    operands = [pick, base, part_column, hole_row, *arrays]
    return pl.pallas_call(
        functools.partial(finish_kernel, plan, tiles),
        out_shape=jax.ShapeDtypeStruct((rows, holes), BF16),
        in_specs=[whole()] * len(operands),
        out_specs=whole(pl.ANY),
        scratch_shapes=[
            pltpu.VMEM((pick.shape[1], holes), BF16),
            pltpu.VMEM((rows, holes), BF16),
            pltpu.SemaphoreType.DMA((tiles,)),
        ],
        compiler_params=params(),
        cost_estimate=CHEAP,
        name="finish",
    )(*operands)


def body(amplitudes, driving, route, ladder_weight, ph_weight, recouple, gap_part, gap_hole):
    amps = amplitudes[0]
    rows, holes = amps.shape
    chan_count = lax.axis_size("chan")
    lad_count = lax.axis_size("lad")
    sub_count = lax.axis_size("sub")
    chan, lad, sub = lax.axis_index("chan"), lax.axis_index("lad"), lax.axis_index("sub")
    weight, mixing = ph_weight[0, 0], recouple[0, 0]
    capacity = weight.shape[0]
    send = capacity // chan_count
    sizes = (chan_count, lad_count, sub_count)
    paired = send % mixing.shape[1] == 0 and all(size & (size - 1) == 0 for size in sizes)
    if paired:
        offsets = jnp.stack([(chan ^ k) * send for k in range(chan_count)]).astype(jnp.int32)
        first = send - mixing.shape[1] if send > mixing.shape[1] else send
        early = [(k, 0, first) for k in reversed(range(1, chan_count))]
        late = [(k, first, send - first) for k in reversed(range(1, chan_count)) if send > first]
        own = [(0, 0, send)]
    else:
        offsets = jnp.zeros((1,), jnp.int32)
        early, late, own = [(0, 0, capacity)], [], []
    items = early + late + own
    plan = (paired, chan_count, send)

    def exchange(arrays):
        if not paired:
            split = arrays[0].reshape(chan_count, send, holes)
            split = lax.all_to_all(split, "chan", split_axis=0, concat_axis=0, tiled=True)
            return [split.reshape(capacity, holes)]
        return [
            lax.ppermute(a, "chan", [(i, i ^ k) for i in range(chan_count)]) for (k, _, _), a in zip(early, arrays)
        ]

    def highest(axis, bits, value):
        size = lax.axis_size(axis)
        for bit in bits:
            value = jnp.maximum(value, lax.ppermute(value, axis, [(i, i ^ bit) for i in range(size)]))
        return value

    def crowded(counts):
        over = (jnp.max(counts, axis=1)[:chan_count] > first).astype(jnp.int32)
        which = jnp.sum(over * (1 + jnp.arange(chan_count, dtype=jnp.int32)))
        return jnp.where(jnp.sum(over) > 1, chan_count + 1, which)

    def along(axis, arrays):
        size = lax.axis_size(axis)
        return [
            lax.ppermute(a, axis, [(i, (i + step) % size) for i in range(size)]) for step, a in enumerate(arrays, 1)
        ]

    def exchange_late(index, arrays, back):
        def case(pairs_of, *arrays):
            return [
                lax.ppermute(a, "chan", pairs_of(k)) if pairs_of else jnp.zeros_like(a)
                for (k, _, _), a in zip(late, arrays)
            ]

        def single(d, k):
            return [(d, d ^ k) if back else (d ^ k, d)]

        def several(k):
            return [(i, i ^ k) for i in range(chan_count)]

        if not late:
            return []
        kinds = [None] + [functools.partial(single, d) for d in range(chan_count)] + [several]
        return lax.switch(index, [functools.partial(case, kind) for kind in kinds], *arrays)

    route_row = route[0].reshape(1, rows)
    target, counts, *blocks = pack(plan + (early,), False, route_row, amps, "pack_first")
    arrived = exchange(blocks)
    amps, target, counts = lax.optimization_barrier((amps, target, counts))
    packed, index = [], None
    if late:
        counts = highest("chan", [1], counts[: -(-chan_count // 8) * 8])
        amps, target, counts = lax.optimization_barrier((amps, target, counts))
    if late or own:
        packed = pack(plan + (late + own,), True, target, amps, "pack_rest")
    if late:
        counts = highest("chan", [2**i for i in range(1, chan_count.bit_length() - 1)], counts)
        amps, packed, counts = lax.optimization_barrier((amps, packed, counts))
    pick = unpack_matrix(offsets, target.reshape(rows, 1), capacity)
    if late:
        counts = highest("lad", [2**i for i in range(lad_count.bit_length() - 1)], counts)
        amps, pick, counts = lax.optimization_barrier((amps, pick, counts))
    parts, operator = prepare(ladder_weight[0], amps, weight, mixing, lad_count, sub_count)
    if late:
        counts = highest("sub", [2**i for i in range(sub_count.bit_length() - 1)], counts)
        counts, operator, parts = lax.optimization_barrier((counts, operator, parts))
        index = crowded(counts)
    part_column, hole_row = gap_part[0].reshape(rows, 1), gap_hole.reshape(1, holes)
    extra, mine = packed[: len(late)], packed[len(late) :]
    extra, arrived = lax.optimization_barrier((extra, arrived))
    extra = exchange_late(index, extra, False)
    if late:
        extra, parts = lax.optimization_barrier((extra, parts))
    kept = [parts[-1], *along("sub", list(reversed(parts[:-1])))]

    def chip_sum(position):
        picked = [lax.dynamic_index_in_dim(p, position, 0, keepdims=False) for p in kept]
        return sum(p.astype(F32) for p in picked)

    base = driving[0].astype(F32) + chip_sum(lad)
    terms = [chip_sum(lax.rem(lad + step, lad_count)).astype(BF16) for step in range(1, lad_count)]
    for term in along("lad", terms):
        base = base + term.astype(F32)

    made = apply_cycle(plan + (items,), operator, [*arrived, *extra, *mine])
    made_early, made_late, made_own = made[: len(early)], made[len(early) : len(early + late)], made[len(early + late) :]
    returned = exchange(made_early)
    if late:
        made_late, base, returned[-1] = lax.optimization_barrier((made_late, base, returned[-1]))
    returned_late = exchange_late(index, made_late, True)
    updated = finish(plan + (items,), pick, base, part_column, hole_row, [*returned, *returned_late, *made_own])
    return updated[None]


def solution(mesh):
    placed = (
        P(("parts", "chan"), ("lad", "sub"), None),
        P(("parts", "chan"), ("lad", "sub"), None),
        P("chan", ("lad", "sub"), None),
        P("chan", None, ("lad", "sub")),
        P("chan", ("lad", "sub"), None, None),
        P("chan", ("lad", "sub"), None, None, None),
        P(("parts", "chan"), ("lad", "sub")),
        P("parts"),
    )
    return jax.shard_map(
        body,
        mesh=mesh,
        in_specs=placed,
        out_specs=P(("parts", "chan"), ("lad", "sub"), None),
        check_vma=False,
    )
```

```python
import functools

import jax
import jax.numpy as jnp
from jax import lax
from jax.experimental import pallas as pl
from jax.experimental.pallas import tpu as pltpu
from jax.sharding import PartitionSpec as P

VMEM_LIMIT = 28 * 1024 * 1024
F32 = jnp.float32
BF16 = jnp.bfloat16
CHEAP = pl.CostEstimate(flops=0, bytes_accessed=0, transcendentals=0)
DEAR = pl.CostEstimate(flops=3 * 10**10, bytes_accessed=10**6, transcendentals=0)


def params():
    return pltpu.CompilerParams(vmem_limit_bytes=VMEM_LIMIT)


def in_hbm(*arrays):
    return [pltpu.with_memory_space_constraint(a, pltpu.HBM) for a in arrays]


def whole(memory=pltpu.VMEM):
    return pl.BlockSpec(memory_space=memory)


def selection(match):
    return jnp.where(match, 1.0, 0.0).astype(BF16)


def block_offsets(paired, chan_count, block_rows):
    chan = lax.axis_index("chan")
    return [(chan ^ k) * block_rows for k in range(chan_count)] if paired else [0]


def slots_of(owners, send, names):
    lane = 128
    pieces = owners.shape[1] // lane
    before = selection(
        lax.broadcasted_iota(jnp.int32, (lane, 2 * lane), 0)
        < lax.broadcasted_iota(jnp.int32, (lane, 2 * lane), 1)
    )
    hot = [
        lax.broadcasted_iota(jnp.int32, (names, lane), 0) == owners[:, i * lane : (i + 1) * lane]
        for i in range(pieces)
    ]
    counts = jnp.dot(
        jnp.concatenate([selection(h) for h in hot], axis=0), before, preferred_element_type=F32
    )
    passed = jnp.zeros((names, lane), F32)
    slots = []
    for i in range(pieces):
        within = counts[i * names : (i + 1) * names]
        slots.append(jnp.sum(jnp.where(hot[i], within[:, :lane] + passed, 0.0), axis=0, keepdims=True))
        passed = passed + within[:, lane:]
    return owners * send + jnp.concatenate(slots, axis=1).astype(jnp.int32)


def pack_kernel(plan, given, route_in, amps_hbm, *refs):
    paired, chan_count, send, block_rows, items = plan
    outs, (route_ref, amps_ref, sems) = refs[:-3], refs[-3:]
    block_refs = outs if given else outs[1:]
    amps_copy = pltpu.make_async_copy(amps_hbm.at[:, pl.ds(0, amps_ref.shape[1])], amps_ref, sems.at[1])
    if given:
        amps_copy.start()
        target = route_in[...]
    else:
        route_copy = pltpu.make_async_copy(route_in, route_ref, sems.at[0])
        route_copy.start()
        amps_copy.start()
        route_copy.wait()
        target = slots_of(route_ref[...], send, max(16, chan_count))
        outs[0][...] = target
    offsets = block_offsets(paired, chan_count, block_rows)
    slot = lax.broadcasted_iota(jnp.int32, (block_rows, target.shape[1]), 0)
    for i, (k, first, width) in enumerate(items):
        pick = selection(slot == target - offsets[k])
        if i == 0:
            amps_copy.wait()
        block_refs[i][...] = jnp.dot(
            pick, amps_ref[:, pl.ds(first, width)], preferred_element_type=F32
        ).astype(BF16)


def pack(plan, given, route_row, amps, name):
    rows = amps.shape[0]
    block_rows, items = plan[3], plan[4]
    columns = max(first + width for _, first, width in items)
    extra = [] if given else [pltpu.VMEM((1, rows), jnp.int32)]
    return pl.pallas_call(
        functools.partial(pack_kernel, plan, given),
        out_shape=extra + [pltpu.VMEM((block_rows, width), BF16) for _, _, width in items],
        in_specs=[whole() if given else whole(pl.ANY), whole(pl.ANY)],
        out_specs=[whole()] * (len(extra) + len(items)),
        scratch_shapes=[
            pltpu.VMEM((1, rows), jnp.int32),
            pltpu.VMEM((rows, columns), BF16),
            pltpu.SemaphoreType.DMA((2,)),
        ],
        compiler_params=params(),
        name=name,
    )(*([route_row] if given else in_hbm(route_row)), *in_hbm(amps))


def unpack_kernel(off_ref, target_ref, out_ref):
    count = off_ref.shape[0]
    rows, capacity = out_ref.shape
    block_rows = capacity // count
    target = target_ref[...]
    slots = lax.broadcasted_iota(jnp.int32, (rows, block_rows), 1)
    for k in range(count):
        out_ref[:, pl.ds(k * block_rows, block_rows)] = selection(slots == target - off_ref[k])


def unpack_matrix(offsets, target_column, capacity):
    return pl.pallas_call(
        unpack_kernel,
        out_shape=jax.ShapeDtypeStruct((target_column.shape[0], capacity), BF16),
        in_specs=[whole(pltpu.SMEM), whole()],
        out_specs=whole(),
        compiler_params=params(),
        cost_estimate=CHEAP,
        name="unpack_matrix",
    )(offsets, target_column)


def prepare_kernel(sub_count, weight_hbm, amps_hbm, cycle_hbm, mixing_hbm, *refs):
    part_refs, out_ref = refs[:sub_count], refs[sub_count]
    weight_ref, amps_ref, cycle_ref, half_ref, mixing_ref, pair_ref, sems = refs[sub_count + 1 :]
    rows, lad_count = amps_ref.shape[0], part_refs[0].shape[0]
    chunks, chunk, capacity = cycle_ref.shape
    group = mixing_ref.shape[1]
    pairs, wide = pair_ref.shape[0], pair_ref.shape[1]
    sub = lax.axis_index("sub")
    moves, ladder = [(amps_hbm, amps_ref)], []
    for n in range(sub_count):
        share = lax.rem(sub + sub_count - 1 - n, sub_count)
        for i in range(lad_count):
            start = pl.multiple_of((i * sub_count + share) * rows, rows)
            moves.append((weight_hbm.at[pl.ds(start, rows), :], weight_ref.at[len(ladder)]))
            ladder.append((n, i))
    moves.append((mixing_hbm, mixing_ref))
    moves += [(cycle_hbm.at[pl.ds(i * chunk, chunk), :], cycle_ref.at[i]) for i in range(chunks)]
    copies = [pltpu.make_async_copy(source, held, sems.at[n]) for n, (source, held) in enumerate(moves)]
    for copy in copies:
        copy.start()
    pair_ref[...] = jnp.zeros(pair_ref.shape, BF16)
    copies[0].wait()
    for m, (n, i) in enumerate(ladder):
        copies[1 + m].wait()
        part_refs[n][i] = jnp.dot(weight_ref[m], amps_ref[...], preferred_element_type=F32).astype(BF16)
    copies[1 + len(ladder)].wait()
    for q in range(capacity // group):
        at = pl.ds(q * group % wide, group)
        pair_ref[q * group // wide, at, at] = mixing_ref[q]
    for i in range(chunks):
        copies[2 + len(ladder) + i].wait()
        for a in range(chunk // group):
            at = pl.ds(a * group, group)
            half_ref[pl.ds(i * chunk + a * group, group), :] = lax.dot_general(
                mixing_ref[i * chunk // group + a],
                cycle_ref[i, at, :],
                (((0,), (0,)), ((), ())),
                preferred_element_type=F32,
            ).astype(BF16)
    for j in range(pairs):
        at = pl.ds(j * wide, wide)
        out_ref[:, at] = jnp.dot(half_ref[:, at], pair_ref[j], preferred_element_type=F32).astype(BF16)


def prepare(weight, amps, cycle_weight, mixing, lad_count, sub_count):
    rows, holes = amps.shape
    capacity = cycle_weight.shape[0]
    groups, group = mixing.shape[0], mixing.shape[1]
    wide = group * (2 if groups % 2 == 0 else 1)
    chunks = groups // 3 if groups % 3 == 0 else 1
    outs = pl.pallas_call(
        functools.partial(prepare_kernel, sub_count),
        out_shape=[jax.ShapeDtypeStruct((lad_count, rows, holes), BF16)] * sub_count
        + [jax.ShapeDtypeStruct((capacity, capacity), BF16)],
        in_specs=[whole(pl.ANY)] * 4,
        out_specs=[whole()] * (sub_count + 1),
        scratch_shapes=[
            pltpu.VMEM((lad_count * sub_count, rows, rows), BF16),
            pltpu.VMEM((rows, holes), BF16),
            pltpu.VMEM((chunks, capacity // chunks, capacity), BF16),
            pltpu.VMEM((capacity, capacity), BF16),
            pltpu.VMEM(mixing.shape, BF16),
            pltpu.VMEM((capacity // wide, wide, wide), BF16),
            pltpu.SemaphoreType.DMA((2 + lad_count * sub_count + chunks,)),
        ],
        compiler_params=params(),
        cost_estimate=DEAR,
        name="prepare",
    )(*in_hbm(weight, amps, cycle_weight, mixing))
    return outs[:sub_count], outs[sub_count]


def cycle_kernel(start_column, plan, operator_ref, *refs):
    paired, chan_count, _, _ = plan
    count = len(refs) // 2
    in_refs, out_refs, block_ref = refs[:count], refs[count : 2 * count], refs[2 * count]
    block_rows, width = out_refs[0].shape
    offsets = block_offsets(paired, chan_count, block_rows)
    starts = [pl.multiple_of(offsets[count - 1 - i], block_rows) for i in range(count)]
    for in_ref, start in zip(in_refs, starts):
        part = in_ref[...] if in_ref.shape[1] == width else in_ref[:, pl.ds(start_column, width)]
        block_ref[pl.ds(start, block_rows), :] = part
    for out_ref, start in zip(out_refs, starts):
        out_ref[...] = jnp.dot(
            operator_ref[pl.ds(start, block_rows), :], block_ref[...], preferred_element_type=F32
        ).astype(BF16)


def apply_cycle(part, plan, operator, arrays):
    start_column, width = part
    block_rows = arrays[0].shape[0]
    return pl.pallas_call(
        functools.partial(cycle_kernel, start_column, plan),
        out_shape=[jax.ShapeDtypeStruct((block_rows, width), BF16)] * len(arrays),
        in_specs=[whole()] * (1 + len(arrays)),
        out_specs=[whole()] * len(arrays),
        scratch_shapes=[pltpu.VMEM((operator.shape[0], width), BF16)],
        compiler_params=params(),
        cost_estimate=DEAR,
        name="apply_cycle",
    )(operator, *arrays)


def finish_kernel(start_column, count, tiles, pick_ref, base_ref, part_ref, hole_ref, *refs):
    in_refs, (out_hbm, block_ref, out_ref, sems) = refs[:count], refs[-4:]
    block_rows, width = in_refs[0].shape
    tile = out_ref.shape[0] // tiles
    columns = pl.ds(start_column, width)
    for i, in_ref in enumerate(in_refs):
        block_ref[pl.ds((count - 1 - i) * block_rows, block_rows), :] = in_ref[...]
    copies = []
    for t in range(tiles):
        at = pl.ds(t * tile, tile)
        back = jnp.dot(pick_ref[at, :], block_ref[...], preferred_element_type=F32)
        total = base_ref[at, columns] + back
        out_ref[at, :] = (total / (part_ref[at, :] + hole_ref[:, columns])).astype(BF16)
        copies.append(pltpu.make_async_copy(out_ref.at[at, :], out_hbm.at[at, columns], sems.at[t]))
        copies[-1].start()
    for copy in copies:
        copy.wait()


def finish(part, pick, base, part_column, hole_row, arrays, earlier):
    rows, holes = base.shape
    tiles, (start_column, width) = 3, part
    operands = [pick, base, part_column, hole_row, *arrays]
    in_specs = [whole()] * len(operands)
    aliases = {}
    if earlier is not None:
        aliases = {len(operands): 0}
        operands.append(earlier)
        in_specs.append(whole(pl.ANY))
    return pl.pallas_call(
        functools.partial(finish_kernel, start_column, len(arrays), tiles),
        out_shape=jax.ShapeDtypeStruct((rows, holes), BF16),
        in_specs=in_specs,
        out_specs=whole(pl.ANY),
        scratch_shapes=[
            pltpu.VMEM((pick.shape[1], width), BF16),
            pltpu.VMEM((rows, width), BF16),
            pltpu.SemaphoreType.DMA((tiles,)),
        ],
        input_output_aliases=aliases,
        compiler_params=params(),
        cost_estimate=CHEAP,
        name="finish",
    )(*operands)


def body(amplitudes, driving, route, ladder_weight, ph_weight, recouple, gap_part, gap_hole):
    amps = amplitudes[0]
    rows, holes = amps.shape
    chan_count = lax.axis_size("chan")
    lad_count = lax.axis_size("lad")
    sub_count = lax.axis_size("sub")
    chan, lad, sub = lax.axis_index("chan"), lax.axis_index("lad"), lax.axis_index("sub")
    weight, mixing = ph_weight[0, 0], recouple[0, 0]
    capacity = weight.shape[0]
    send = capacity // chan_count
    paired = send % mixing.shape[1] == 0 and chan_count & (chan_count - 1) == 0
    if paired:
        block_rows = send
        block_index = jnp.stack([chan ^ k for k in range(chan_count)]).astype(jnp.int32)
    else:
        block_rows = capacity
        block_index = jnp.zeros((1,), jnp.int32)
    offsets = block_index * block_rows

    def exchange(block, k):
        if not paired:
            split = block.reshape(chan_count, send, -1)
            split = lax.all_to_all(split, "chan", split_axis=0, concat_axis=0, tiled=True)
            return split.reshape(capacity, -1)
        return lax.ppermute(block, "chan", [(i, i ^ k) for i in range(chan_count)]) if k else block

    far_first = list(reversed(range(block_index.shape[0])))
    count = len(far_first)
    wide = holes * 3 // 512 * 128
    columns = [(0, wide), (wide, holes - wide)] if paired else [(0, holes)]
    route_row = route[0].reshape(1, rows)
    plan = (paired, chan_count, send, block_rows)
    early = [(k, *columns[0]) for k in far_first if k or not paired]
    late = [(k, *part) for part in columns[1:] for k in far_first if k] + ([(0, 0, holes)] if paired else [])
    target, *blocks = pack(plan + (early,), False, route_row, amps, "pack_first")
    arrived = {(k, start): exchange(block, k) for (k, start, _), block in zip(early, blocks)}
    if paired:
        near = (1, 0)
        target, arrived[near] = lax.optimization_barrier((target, arrived[near]))
    blocks = []
    if late:
        blocks = pack(plan + (late,), True, target, amps, "pack_rest")
        for (k, start, _), block in zip(late, blocks):
            arrived[(k, start)] = exchange(block, k)
        amps, blocks = lax.optimization_barrier((amps, blocks))

    part_column, hole_row = gap_part[0].reshape(rows, 1), gap_hole.reshape(1, holes)
    pick = unpack_matrix(offsets, target.reshape(rows, 1), capacity)

    parts, operator = prepare(ladder_weight[0], amps, weight, mixing, lad_count, sub_count)
    kept = [parts[-1]]
    for step in range(1, sub_count):
        pairs = [(i, (i + step) % sub_count) for i in range(sub_count)]
        kept.append(lax.ppermute(parts[sub_count - 1 - step], "sub", pairs))

    def chip_sum(position):
        picked = [lax.dynamic_index_in_dim(p, position, 0, keepdims=False) for p in kept]
        return sum(p.astype(F32) for p in picked)

    base = driving[0].astype(F32) + chip_sum(lad)
    terms = [chip_sum(lax.rem(lad + step, lad_count)).astype(BF16) for step in range(1, lad_count)]
    returned = []
    for part in columns:
        blocks = [arrived[(k, part[0] if k or not paired else 0)] for k in far_first]
        if returned:
            blocks, made = lax.optimization_barrier((blocks, made))
        made = apply_cycle(part, plan, operator, blocks)
        if not returned:
            behind, terms = lax.optimization_barrier((made[2:], terms))
            made = [*made[:2], *behind]
        returned.append([exchange(block, k) for k, block in zip(far_first, made)])
    for step, term in enumerate(terms, 1):
        pairs = [(i, (i + step) % lad_count) for i in range(lad_count)]
        base = base + lax.ppermute(term, "lad", pairs).astype(F32)
    updated = None
    for part, arrays in zip(columns, returned):
        updated = finish(part, pick, base, part_column, hole_row, arrays, updated)
    return updated[None]


def solution(mesh):
    placed = (
        P(("parts", "chan"), ("lad", "sub"), None),
        P(("parts", "chan"), ("lad", "sub"), None),
        P("chan", ("lad", "sub"), None),
        P("chan", None, ("lad", "sub")),
        P("chan", ("lad", "sub"), None, None),
        P("chan", ("lad", "sub"), None, None, None),
        P(("parts", "chan"), ("lad", "sub")),
        P("parts"),
    )
    return jax.shard_map(
        body,
        mesh=mesh,
        in_specs=placed,
        out_specs=P(("parts", "chan"), ("lad", "sub"), None),
        check_vma=False,
    )
```

```python
import functools

import jax
import jax.numpy as jnp
from jax import lax
from jax.experimental import pallas as pl
from jax.experimental.pallas import tpu as pltpu
from jax.sharding import PartitionSpec as P

VMEM_LIMIT = 28 * 1024 * 1024
HALVES = 2
F32 = jnp.float32
BF16 = jnp.bfloat16
CHEAP = pl.CostEstimate(flops=0, bytes_accessed=0, transcendentals=0)
DEAR = pl.CostEstimate(flops=3 * 10**10, bytes_accessed=10**6, transcendentals=0)


def params():
    return pltpu.CompilerParams(vmem_limit_bytes=VMEM_LIMIT)


def in_hbm(*arrays):
    return [pltpu.with_memory_space_constraint(a, pltpu.HBM) for a in arrays]


def whole(memory=pltpu.VMEM):
    return pl.BlockSpec(memory_space=memory)


def selection(match):
    return jnp.where(match, 1.0, 0.0).astype(BF16)


def block_offsets(paired, chan_count, block_rows):
    chan = lax.axis_index("chan")
    return [(chan ^ k) * block_rows for k in range(chan_count)] if paired else [0]


def slots_of(owners, send, names):
    lane = 128
    pieces = owners.shape[1] // lane
    before = selection(
        lax.broadcasted_iota(jnp.int32, (lane, 2 * lane), 0)
        < lax.broadcasted_iota(jnp.int32, (lane, 2 * lane), 1)
    )
    hot = [
        lax.broadcasted_iota(jnp.int32, (names, lane), 0) == owners[:, i * lane : (i + 1) * lane]
        for i in range(pieces)
    ]
    counts = jnp.dot(
        jnp.concatenate([selection(h) for h in hot], axis=0), before, preferred_element_type=F32
    )
    passed = jnp.zeros((names, lane), F32)
    slots = []
    for i in range(pieces):
        within = counts[i * names : (i + 1) * names]
        slots.append(jnp.sum(jnp.where(hot[i], within[:, :lane] + passed, 0.0), axis=0, keepdims=True))
        passed = passed + within[:, lane:]
    return owners * send + jnp.concatenate(slots, axis=1).astype(jnp.int32)


def pack_kernel(plan, given, route_in, amps_hbm, *refs):
    paired, chan_count, send, block_rows, items = plan
    outs, (route_ref, amps_ref, sems) = refs[:-3], refs[-3:]
    block_refs = outs if given else outs[1:]
    amps_copy = pltpu.make_async_copy(amps_hbm.at[:, pl.ds(0, amps_ref.shape[1])], amps_ref, sems.at[1])
    if given:
        amps_copy.start()
        target = route_in[...]
    else:
        route_copy = pltpu.make_async_copy(route_in, route_ref, sems.at[0])
        route_copy.start()
        amps_copy.start()
        route_copy.wait()
        target = slots_of(route_ref[...], send, max(16, chan_count))
        outs[0][...] = target
    offsets = block_offsets(paired, chan_count, block_rows)
    slot = lax.broadcasted_iota(jnp.int32, (block_rows, target.shape[1]), 0)
    for i, (k, first, width) in enumerate(items):
        pick = selection(slot == target - offsets[k])
        if i == 0:
            amps_copy.wait()
        block_refs[i][...] = jnp.dot(
            pick, amps_ref[:, pl.ds(first, width)], preferred_element_type=F32
        ).astype(BF16)


def pack(plan, given, route_row, amps, name):
    rows = amps.shape[0]
    block_rows, items = plan[3], plan[4]
    columns = max(first + width for _, first, width in items)
    extra = [] if given else [pltpu.VMEM((1, rows), jnp.int32)]
    return pl.pallas_call(
        functools.partial(pack_kernel, plan, given),
        out_shape=extra + [pltpu.VMEM((block_rows, width), BF16) for _, _, width in items],
        in_specs=[whole() if given else whole(pl.ANY), whole(pl.ANY)],
        out_specs=[whole()] * (len(extra) + len(items)),
        scratch_shapes=[
            pltpu.VMEM((1, rows), jnp.int32),
            pltpu.VMEM((rows, columns), BF16),
            pltpu.SemaphoreType.DMA((2,)),
        ],
        compiler_params=params(),
        name=name,
    )(*([route_row] if given else in_hbm(route_row)), *in_hbm(amps))


def unpack_kernel(off_ref, target_ref, out_ref):
    count = off_ref.shape[0]
    rows, capacity = out_ref.shape
    block_rows = capacity // count
    target = target_ref[...]
    slots = lax.broadcasted_iota(jnp.int32, (rows, block_rows), 1)
    for k in range(count):
        out_ref[:, pl.ds(k * block_rows, block_rows)] = selection(slots == target - off_ref[k])


def unpack_matrix(offsets, target_column, capacity):
    return pl.pallas_call(
        unpack_kernel,
        out_shape=jax.ShapeDtypeStruct((target_column.shape[0], capacity), BF16),
        in_specs=[whole(pltpu.SMEM), whole()],
        out_specs=whole(),
        compiler_params=params(),
        cost_estimate=CHEAP,
        name="unpack_matrix",
    )(offsets, target_column)


def prepare_kernel(sub_count, weight_hbm, amps_hbm, cycle_hbm, mixing_hbm, *refs):
    part_refs, out_ref = refs[:sub_count], refs[sub_count]
    weight_ref, amps_ref, cycle_ref, half_ref, mixing_ref, pair_ref, sems = refs[sub_count + 1 :]
    rows, lad_count = amps_ref.shape[0], part_refs[0].shape[0]
    chunks, chunk, capacity = cycle_ref.shape
    group = mixing_ref.shape[1]
    pairs, wide = pair_ref.shape[0], pair_ref.shape[1]
    sub = lax.axis_index("sub")
    moves, ladder = [(amps_hbm, amps_ref)], []
    for n in range(sub_count):
        share = lax.rem(sub + sub_count - 1 - n, sub_count)
        for i in range(lad_count):
            start = pl.multiple_of((i * sub_count + share) * rows, rows)
            moves.append((weight_hbm.at[pl.ds(start, rows), :], weight_ref.at[len(ladder)]))
            ladder.append((n, i))
    moves.append((mixing_hbm, mixing_ref))
    moves += [(cycle_hbm.at[pl.ds(i * chunk, chunk), :], cycle_ref.at[i]) for i in range(chunks)]
    copies = [pltpu.make_async_copy(source, held, sems.at[n]) for n, (source, held) in enumerate(moves)]
    for copy in copies:
        copy.start()
    pair_ref[...] = jnp.zeros(pair_ref.shape, BF16)
    copies[0].wait()
    for m, (n, i) in enumerate(ladder):
        copies[1 + m].wait()
        part_refs[n][i] = jnp.dot(weight_ref[m], amps_ref[...], preferred_element_type=F32).astype(BF16)
    copies[1 + len(ladder)].wait()
    for q in range(capacity // group):
        at = pl.ds(q * group % wide, group)
        pair_ref[q * group // wide, at, at] = mixing_ref[q]
    for i in range(chunks):
        copies[2 + len(ladder) + i].wait()
        for a in range(chunk // group):
            at = pl.ds(a * group, group)
            half_ref[pl.ds(i * chunk + a * group, group), :] = lax.dot_general(
                mixing_ref[i * chunk // group + a],
                cycle_ref[i, at, :],
                (((0,), (0,)), ((), ())),
                preferred_element_type=F32,
            ).astype(BF16)
    for j in range(pairs):
        at = pl.ds(j * wide, wide)
        out_ref[:, at] = jnp.dot(half_ref[:, at], pair_ref[j], preferred_element_type=F32).astype(BF16)


def prepare(weight, amps, cycle_weight, mixing, lad_count, sub_count):
    rows, holes = amps.shape
    capacity = cycle_weight.shape[0]
    groups, group = mixing.shape[0], mixing.shape[1]
    wide = group * (2 if groups % 2 == 0 else 1)
    chunks = groups // 3 if groups % 3 == 0 else 1
    outs = pl.pallas_call(
        functools.partial(prepare_kernel, sub_count),
        out_shape=[jax.ShapeDtypeStruct((lad_count, rows, holes), BF16)] * sub_count
        + [jax.ShapeDtypeStruct((capacity, capacity), BF16)],
        in_specs=[whole(pl.ANY)] * 4,
        out_specs=[whole()] * (sub_count + 1),
        scratch_shapes=[
            pltpu.VMEM((lad_count * sub_count, rows, rows), BF16),
            pltpu.VMEM((rows, holes), BF16),
            pltpu.VMEM((chunks, capacity // chunks, capacity), BF16),
            pltpu.VMEM((capacity, capacity), BF16),
            pltpu.VMEM(mixing.shape, BF16),
            pltpu.VMEM((capacity // wide, wide, wide), BF16),
            pltpu.SemaphoreType.DMA((2 + lad_count * sub_count + chunks,)),
        ],
        compiler_params=params(),
        cost_estimate=DEAR,
        name="prepare",
    )(*in_hbm(weight, amps, cycle_weight, mixing))
    return outs[:sub_count], outs[sub_count]


def cycle_kernel(half, plan, operator_ref, *refs):
    paired, chan_count, _, _ = plan
    count = len(refs) // 2
    in_refs, out_refs, block_ref = refs[:count], refs[count : 2 * count], refs[2 * count]
    block_rows, width = out_refs[0].shape
    offsets = block_offsets(paired, chan_count, block_rows)
    starts = [pl.multiple_of(offsets[count - 1 - i], block_rows) for i in range(count)]
    for in_ref, start in zip(in_refs, starts):
        part = in_ref[...] if in_ref.shape[1] == width else in_ref[:, pl.ds(half * width, width)]
        block_ref[pl.ds(start, block_rows), :] = part
    for out_ref, start in zip(out_refs, starts):
        out_ref[...] = jnp.dot(
            operator_ref[pl.ds(start, block_rows), :], block_ref[...], preferred_element_type=F32
        ).astype(BF16)


def apply_cycle(half, plan, operator, arrays, width):
    block_rows = arrays[0].shape[0]
    return pl.pallas_call(
        functools.partial(cycle_kernel, half, plan),
        out_shape=[jax.ShapeDtypeStruct((block_rows, width), BF16)] * len(arrays),
        in_specs=[whole()] * (1 + len(arrays)),
        out_specs=[whole()] * len(arrays),
        scratch_shapes=[pltpu.VMEM((operator.shape[0], width), BF16)],
        compiler_params=params(),
        cost_estimate=DEAR,
        name="apply_cycle",
    )(operator, *arrays)


def finish_kernel(half, count, tiles, pick_ref, base_ref, part_ref, hole_ref, *refs):
    in_refs, (out_hbm, block_ref, out_ref, sems) = refs[:count], refs[-4:]
    block_rows, width = in_refs[0].shape
    tile = out_ref.shape[0] // tiles
    columns = pl.ds(half * width, width)
    for i, in_ref in enumerate(in_refs):
        block_ref[pl.ds((count - 1 - i) * block_rows, block_rows), :] = in_ref[...]
    copies = []
    for t in range(tiles):
        at = pl.ds(t * tile, tile)
        back = jnp.dot(pick_ref[at, :], block_ref[...], preferred_element_type=F32)
        total = base_ref[at, columns] + back
        out_ref[at, :] = (total / (part_ref[at, :] + hole_ref[:, columns])).astype(BF16)
        copies.append(pltpu.make_async_copy(out_ref.at[at, :], out_hbm.at[at, columns], sems.at[t]))
        copies[-1].start()
    for copy in copies:
        copy.wait()


def finish(half, pick, base, part_column, hole_row, arrays, earlier):
    rows, holes = base.shape
    tiles, width = 3, holes // HALVES
    operands = [pick, base, part_column, hole_row, *arrays]
    in_specs = [whole()] * len(operands)
    aliases = {}
    if earlier is not None:
        aliases = {len(operands): 0}
        operands.append(earlier)
        in_specs.append(whole(pl.ANY))
    return pl.pallas_call(
        functools.partial(finish_kernel, half, len(arrays), tiles),
        out_shape=jax.ShapeDtypeStruct((rows, holes), BF16),
        in_specs=in_specs,
        out_specs=whole(pl.ANY),
        scratch_shapes=[
            pltpu.VMEM((pick.shape[1], width), BF16),
            pltpu.VMEM((rows, width), BF16),
            pltpu.SemaphoreType.DMA((tiles,)),
        ],
        input_output_aliases=aliases,
        compiler_params=params(),
        cost_estimate=CHEAP,
        name="finish",
    )(*operands)


def body(amplitudes, driving, route, ladder_weight, ph_weight, recouple, gap_part, gap_hole):
    amps = amplitudes[0]
    rows, holes = amps.shape
    chan_count = lax.axis_size("chan")
    lad_count = lax.axis_size("lad")
    sub_count = lax.axis_size("sub")
    chan, lad, sub = lax.axis_index("chan"), lax.axis_index("lad"), lax.axis_index("sub")
    weight, mixing = ph_weight[0, 0], recouple[0, 0]
    capacity = weight.shape[0]
    send = capacity // chan_count
    paired = send % mixing.shape[1] == 0 and chan_count & (chan_count - 1) == 0
    if paired:
        block_rows = send
        block_index = jnp.stack([chan ^ k for k in range(chan_count)]).astype(jnp.int32)
    else:
        block_rows = capacity
        block_index = jnp.zeros((1,), jnp.int32)
    offsets = block_index * block_rows

    def exchange(block, k):
        if not paired:
            split = block.reshape(chan_count, send, -1)
            split = lax.all_to_all(split, "chan", split_axis=0, concat_axis=0, tiled=True)
            return split.reshape(capacity, -1)
        return lax.ppermute(block, "chan", [(i, i ^ k) for i in range(chan_count)]) if k else block

    far_first = list(reversed(range(block_index.shape[0])))
    count = len(far_first)
    width = holes // HALVES
    route_row = route[0].reshape(1, rows)
    plan = (paired, chan_count, send, block_rows)
    early = [(k, 0, width) for k in far_first if k or not paired]
    late = [(k, h * width, width) for h in range(1, HALVES) for k in far_first if k or not paired]
    late += [(0, 0, holes)] if paired else []
    target, *blocks = pack(plan + (early,), False, route_row, amps, "pack_first")
    arrived = {(k, 0): exchange(block, k) for (k, _, _), block in zip(early, blocks)}
    if paired:
        near = (1, 0)
        target, arrived[near] = lax.optimization_barrier((target, arrived[near]))
    blocks = pack(plan + (late,), True, target, amps, "pack_rest")
    for (k, first, _), block in zip(late, blocks):
        arrived[(k, first // width)] = exchange(block, k)

    part_column, hole_row = gap_part[0].reshape(rows, 1), gap_hole.reshape(1, holes)
    amps, blocks = lax.optimization_barrier((amps, blocks))

    parts, operator = prepare(ladder_weight[0], amps, weight, mixing, lad_count, sub_count)
    kept = [parts[-1]]
    for step in range(1, sub_count):
        pairs = [(i, (i + step) % sub_count) for i in range(sub_count)]
        kept.append(lax.ppermute(parts[sub_count - 1 - step], "sub", pairs))

    def chip_sum(position):
        picked = [lax.dynamic_index_in_dim(p, position, 0, keepdims=False) for p in kept]
        return sum(p.astype(F32) for p in picked)

    base = driving[0].astype(F32) + chip_sum(lad)
    terms = [chip_sum(lax.rem(lad + step, lad_count)).astype(BF16) for step in range(1, lad_count)]
    returned = []
    for half in range(HALVES):
        blocks = [arrived[(k, half if k or not paired else 0)] for k in far_first]
        if returned:
            blocks, made = lax.optimization_barrier((blocks, made))
        made = apply_cycle(half, plan, operator, blocks, width)
        if not half:
            behind, terms = lax.optimization_barrier((made[2:], terms))
            made = [*made[:2], *behind]
        returned.append([exchange(block, k) for k, block in zip(far_first, made)])
    for step, term in enumerate(terms, 1):
        pairs = [(i, (i + step) % lad_count) for i in range(lad_count)]
        base = base + lax.ppermute(term, "lad", pairs).astype(F32)
    target, made = lax.optimization_barrier((target, made))
    pick = unpack_matrix(offsets, target.reshape(rows, 1), capacity)
    updated = None
    for half in range(HALVES):
        updated = finish(half, pick, base, part_column, hole_row, returned[half], updated)
    return updated[None]


def solution(mesh):
    placed = (
        P(("parts", "chan"), ("lad", "sub"), None),
        P(("parts", "chan"), ("lad", "sub"), None),
        P("chan", ("lad", "sub"), None),
        P("chan", None, ("lad", "sub")),
        P("chan", ("lad", "sub"), None, None),
        P("chan", ("lad", "sub"), None, None, None),
        P(("parts", "chan"), ("lad", "sub")),
        P("parts"),
    )
    return jax.shard_map(
        body,
        mesh=mesh,
        in_specs=placed,
        out_specs=P(("parts", "chan"), ("lad", "sub"), None),
        check_vma=False,
    )
```

```python
import functools

import jax
import jax.numpy as jnp
from jax import lax
from jax.experimental import pallas as pl
from jax.experimental.pallas import tpu as pltpu
from jax.sharding import PartitionSpec as P

VMEM_LIMIT = 28 * 1024 * 1024
HALVES = 2
F32 = jnp.float32
BF16 = jnp.bfloat16
CHEAP = pl.CostEstimate(flops=0, bytes_accessed=0, transcendentals=0)
DEAR = pl.CostEstimate(flops=3 * 10**10, bytes_accessed=10**6, transcendentals=0)


def params():
    return pltpu.CompilerParams(vmem_limit_bytes=VMEM_LIMIT)


def in_hbm(*arrays):
    return [pltpu.with_memory_space_constraint(a, pltpu.HBM) for a in arrays]


def whole(memory=pltpu.VMEM):
    return pl.BlockSpec(memory_space=memory)


def selection(match):
    return jnp.where(match, 1.0, 0.0).astype(BF16)


def block_offsets(paired, chan_count, block_rows):
    chan = lax.axis_index("chan")
    return [(chan ^ k) * block_rows for k in range(chan_count)] if paired else [0]


def slots_of(owners, send, names):
    lane = 128
    pieces = owners.shape[1] // lane
    before = selection(
        lax.broadcasted_iota(jnp.int32, (lane, 2 * lane), 0)
        < lax.broadcasted_iota(jnp.int32, (lane, 2 * lane), 1)
    )
    hot = [
        lax.broadcasted_iota(jnp.int32, (names, lane), 0) == owners[:, i * lane : (i + 1) * lane]
        for i in range(pieces)
    ]
    counts = jnp.dot(
        jnp.concatenate([selection(h) for h in hot], axis=0), before, preferred_element_type=F32
    )
    passed = jnp.zeros((names, lane), F32)
    slots = []
    for i in range(pieces):
        within = counts[i * names : (i + 1) * names]
        slots.append(jnp.sum(jnp.where(hot[i], within[:, :lane] + passed, 0.0), axis=0, keepdims=True))
        passed = passed + within[:, lane:]
    return owners * send + jnp.concatenate(slots, axis=1).astype(jnp.int32)


def pack_kernel(plan, given, route_in, amps_hbm, *refs):
    paired, chan_count, send, block_rows, items = plan
    outs, (route_ref, amps_ref, sems) = refs[:-3], refs[-3:]
    block_refs = outs if given else outs[1:]
    amps_copy = pltpu.make_async_copy(amps_hbm.at[:, pl.ds(0, amps_ref.shape[1])], amps_ref, sems.at[1])
    if given:
        amps_copy.start()
        target = route_in[...]
    else:
        route_copy = pltpu.make_async_copy(route_in, route_ref, sems.at[0])
        route_copy.start()
        amps_copy.start()
        route_copy.wait()
        target = slots_of(route_ref[...], send, max(16, chan_count))
        outs[0][...] = target
    offsets = block_offsets(paired, chan_count, block_rows)
    slot = lax.broadcasted_iota(jnp.int32, (block_rows, target.shape[1]), 0)
    for i, (k, first, width) in enumerate(items):
        pick = selection(slot == target - offsets[k])
        if i == 0:
            amps_copy.wait()
        block_refs[i][...] = jnp.dot(
            pick, amps_ref[:, pl.ds(first, width)], preferred_element_type=F32
        ).astype(BF16)


def pack(plan, given, route_row, amps, name):
    rows = amps.shape[0]
    block_rows, items = plan[3], plan[4]
    columns = max(first + width for _, first, width in items)
    extra = [] if given else [pltpu.VMEM((1, rows), jnp.int32)]
    return pl.pallas_call(
        functools.partial(pack_kernel, plan, given),
        out_shape=extra + [pltpu.VMEM((block_rows, width), BF16) for _, _, width in items],
        in_specs=[whole() if given else whole(pl.ANY), whole(pl.ANY)],
        out_specs=[whole()] * (len(extra) + len(items)),
        scratch_shapes=[
            pltpu.VMEM((1, rows), jnp.int32),
            pltpu.VMEM((rows, columns), BF16),
            pltpu.SemaphoreType.DMA((2,)),
        ],
        compiler_params=params(),
        name=name,
    )(*([route_row] if given else in_hbm(route_row)), *in_hbm(amps))


def unpack_kernel(off_ref, target_ref, out_ref):
    count = off_ref.shape[0]
    rows, capacity = out_ref.shape
    block_rows = capacity // count
    target = target_ref[...]
    slots = lax.broadcasted_iota(jnp.int32, (rows, block_rows), 1)
    for k in range(count):
        out_ref[:, pl.ds(k * block_rows, block_rows)] = selection(slots == target - off_ref[k])


def unpack_matrix(offsets, target_column, capacity):
    return pl.pallas_call(
        unpack_kernel,
        out_shape=jax.ShapeDtypeStruct((target_column.shape[0], capacity), BF16),
        in_specs=[whole(pltpu.SMEM), whole()],
        out_specs=whole(),
        compiler_params=params(),
        cost_estimate=CHEAP,
        name="unpack_matrix",
    )(offsets, target_column)


def prepare_kernel(sub_count, weight_hbm, amps_hbm, cycle_hbm, mixing_hbm, *refs):
    part_refs, out_ref = refs[:sub_count], refs[sub_count]
    weight_ref, amps_ref, cycle_ref, half_ref, mixing_ref, pair_ref, sems = refs[sub_count + 1 :]
    rows, lad_count = amps_ref.shape[0], part_refs[0].shape[0]
    chunks, chunk, capacity = cycle_ref.shape
    group = mixing_ref.shape[1]
    pairs, wide = pair_ref.shape[0], pair_ref.shape[1]
    sub = lax.axis_index("sub")
    moves, ladder = [(amps_hbm, amps_ref)], []
    for n in range(sub_count):
        share = lax.rem(sub + sub_count - 1 - n, sub_count)
        for i in range(lad_count):
            start = pl.multiple_of((i * sub_count + share) * rows, rows)
            moves.append((weight_hbm.at[pl.ds(start, rows), :], weight_ref.at[len(ladder)]))
            ladder.append((n, i))
    moves.append((mixing_hbm, mixing_ref))
    moves += [(cycle_hbm.at[pl.ds(i * chunk, chunk), :], cycle_ref.at[i]) for i in range(chunks)]
    copies = [pltpu.make_async_copy(source, held, sems.at[n]) for n, (source, held) in enumerate(moves)]
    for copy in copies:
        copy.start()
    pair_ref[...] = jnp.zeros(pair_ref.shape, BF16)
    copies[0].wait()
    for m, (n, i) in enumerate(ladder):
        copies[1 + m].wait()
        part_refs[n][i] = jnp.dot(weight_ref[m], amps_ref[...], preferred_element_type=F32).astype(BF16)
    copies[1 + len(ladder)].wait()
    for q in range(capacity // group):
        at = pl.ds(q * group % wide, group)
        pair_ref[q * group // wide, at, at] = mixing_ref[q]
    for i in range(chunks):
        copies[2 + len(ladder) + i].wait()
        for a in range(chunk // group):
            at = pl.ds(a * group, group)
            half_ref[pl.ds(i * chunk + a * group, group), :] = lax.dot_general(
                mixing_ref[i * chunk // group + a],
                cycle_ref[i, at, :],
                (((0,), (0,)), ((), ())),
                preferred_element_type=F32,
            ).astype(BF16)
    for j in range(pairs):
        at = pl.ds(j * wide, wide)
        out_ref[:, at] = jnp.dot(half_ref[:, at], pair_ref[j], preferred_element_type=F32).astype(BF16)


def prepare(weight, amps, cycle_weight, mixing, lad_count, sub_count):
    rows, holes = amps.shape
    capacity = cycle_weight.shape[0]
    groups, group = mixing.shape[0], mixing.shape[1]
    wide = group * (2 if groups % 2 == 0 else 1)
    chunks = groups // 3 if groups % 3 == 0 else 1
    outs = pl.pallas_call(
        functools.partial(prepare_kernel, sub_count),
        out_shape=[jax.ShapeDtypeStruct((lad_count, rows, holes), BF16)] * sub_count
        + [jax.ShapeDtypeStruct((capacity, capacity), BF16)],
        in_specs=[whole(pl.ANY)] * 4,
        out_specs=[whole()] * (sub_count + 1),
        scratch_shapes=[
            pltpu.VMEM((lad_count * sub_count, rows, rows), BF16),
            pltpu.VMEM((rows, holes), BF16),
            pltpu.VMEM((chunks, capacity // chunks, capacity), BF16),
            pltpu.VMEM((capacity, capacity), BF16),
            pltpu.VMEM(mixing.shape, BF16),
            pltpu.VMEM((capacity // wide, wide, wide), BF16),
            pltpu.SemaphoreType.DMA((2 + lad_count * sub_count + chunks,)),
        ],
        compiler_params=params(),
        cost_estimate=DEAR,
        name="prepare",
    )(*in_hbm(weight, amps, cycle_weight, mixing))
    return outs[:sub_count], outs[sub_count]


def cycle_kernel(half, plan, operator_ref, *refs):
    paired, chan_count, _, _ = plan
    count = len(refs) // 2
    in_refs, out_refs, block_ref = refs[:count], refs[count : 2 * count], refs[2 * count]
    block_rows, width = out_refs[0].shape
    offsets = block_offsets(paired, chan_count, block_rows)
    starts = [pl.multiple_of(offsets[count - 1 - i], block_rows) for i in range(count)]
    for in_ref, start in zip(in_refs, starts):
        part = in_ref[...] if in_ref.shape[1] == width else in_ref[:, pl.ds(half * width, width)]
        block_ref[pl.ds(start, block_rows), :] = part
    for out_ref, start in zip(out_refs, starts):
        out_ref[...] = jnp.dot(
            operator_ref[pl.ds(start, block_rows), :], block_ref[...], preferred_element_type=F32
        ).astype(BF16)


def apply_cycle(half, plan, operator, arrays, width):
    block_rows = arrays[0].shape[0]
    return pl.pallas_call(
        functools.partial(cycle_kernel, half, plan),
        out_shape=[jax.ShapeDtypeStruct((block_rows, width), BF16)] * len(arrays),
        in_specs=[whole()] * (1 + len(arrays)),
        out_specs=[whole()] * len(arrays),
        scratch_shapes=[pltpu.VMEM((operator.shape[0], width), BF16)],
        compiler_params=params(),
        cost_estimate=DEAR,
        name="apply_cycle",
    )(operator, *arrays)


def finish_kernel(half, count, tiles, pick_ref, base_ref, part_ref, hole_ref, *refs):
    in_refs, (out_hbm, block_ref, out_ref, sems) = refs[:count], refs[-4:]
    block_rows, width = in_refs[0].shape
    tile = out_ref.shape[0] // tiles
    columns = pl.ds(half * width, width)
    for i, in_ref in enumerate(in_refs):
        block_ref[pl.ds((count - 1 - i) * block_rows, block_rows), :] = in_ref[...]
    copies = []
    for t in range(tiles):
        at = pl.ds(t * tile, tile)
        back = jnp.dot(pick_ref[at, :], block_ref[...], preferred_element_type=F32)
        total = base_ref[at, columns] + back
        out_ref[at, :] = (total / (part_ref[at, :] + hole_ref[:, columns])).astype(BF16)
        copies.append(pltpu.make_async_copy(out_ref.at[at, :], out_hbm.at[at, columns], sems.at[t]))
        copies[-1].start()
    for copy in copies:
        copy.wait()


def finish(half, pick, base, part_column, hole_row, arrays, earlier):
    rows, holes = base.shape
    tiles, width = 3, holes // HALVES
    operands = [pick, base, part_column, hole_row, *arrays]
    in_specs = [whole()] * len(operands)
    aliases = {}
    if earlier is not None:
        aliases = {len(operands): 0}
        operands.append(earlier)
        in_specs.append(whole(pl.ANY))
    return pl.pallas_call(
        functools.partial(finish_kernel, half, len(arrays), tiles),
        out_shape=jax.ShapeDtypeStruct((rows, holes), BF16),
        in_specs=in_specs,
        out_specs=whole(pl.ANY),
        scratch_shapes=[
            pltpu.VMEM((pick.shape[1], width), BF16),
            pltpu.VMEM((rows, width), BF16),
            pltpu.SemaphoreType.DMA((tiles,)),
        ],
        input_output_aliases=aliases,
        compiler_params=params(),
        cost_estimate=CHEAP,
        name="finish",
    )(*operands)


def body(amplitudes, driving, route, ladder_weight, ph_weight, recouple, gap_part, gap_hole):
    amps = amplitudes[0]
    rows, holes = amps.shape
    chan_count = lax.axis_size("chan")
    lad_count = lax.axis_size("lad")
    sub_count = lax.axis_size("sub")
    chan, lad, sub = lax.axis_index("chan"), lax.axis_index("lad"), lax.axis_index("sub")
    weight, mixing = ph_weight[0, 0], recouple[0, 0]
    capacity = weight.shape[0]
    send = capacity // chan_count
    paired = send % mixing.shape[1] == 0 and chan_count & (chan_count - 1) == 0
    if paired:
        block_rows = send
        block_index = jnp.stack([chan ^ k for k in range(chan_count)]).astype(jnp.int32)
    else:
        block_rows = capacity
        block_index = jnp.zeros((1,), jnp.int32)
    offsets = block_index * block_rows

    def exchange(block, k):
        if not paired:
            split = block.reshape(chan_count, send, -1)
            split = lax.all_to_all(split, "chan", split_axis=0, concat_axis=0, tiled=True)
            return split.reshape(capacity, -1)
        return lax.ppermute(block, "chan", [(i, i ^ k) for i in range(chan_count)]) if k else block

    far_first = list(reversed(range(block_index.shape[0])))
    count = len(far_first)
    width = holes // HALVES
    route_row = route[0].reshape(1, rows)
    plan = (paired, chan_count, send, block_rows)
    early = [(k, 0, width) for k in far_first if k or not paired]
    late = [(k, h * width, width) for h in range(1, HALVES) for k in far_first if k or not paired]
    late += [(0, 0, holes)] if paired else []
    target, *blocks = pack(plan + (early,), False, route_row, amps, "pack_first")
    arrived = {(k, 0): exchange(block, k) for (k, _, _), block in zip(early, blocks)}
    if paired:
        near = (1, 0)
        target, arrived[near] = lax.optimization_barrier((target, arrived[near]))
    blocks = pack(plan + (late,), True, target, amps, "pack_rest")
    for (k, first, _), block in zip(late, blocks):
        arrived[(k, first // width)] = exchange(block, k)

    part_column, hole_row = gap_part[0].reshape(rows, 1), gap_hole.reshape(1, holes)
    amps, blocks = lax.optimization_barrier((amps, blocks))
    pick = unpack_matrix(offsets, target.reshape(rows, 1), capacity)

    parts, operator = prepare(ladder_weight[0], amps, weight, mixing, lad_count, sub_count)
    kept = [parts[-1]]
    for step in range(1, sub_count):
        pairs = [(i, (i + step) % sub_count) for i in range(sub_count)]
        kept.append(lax.ppermute(parts[sub_count - 1 - step], "sub", pairs))

    def chip_sum(position):
        picked = [lax.dynamic_index_in_dim(p, position, 0, keepdims=False) for p in kept]
        return sum(p.astype(F32) for p in picked)

    base = driving[0].astype(F32) + chip_sum(lad)
    terms = [chip_sum(lax.rem(lad + step, lad_count)).astype(BF16) for step in range(1, lad_count)]
    returned, crossed = [], []
    for half in range(HALVES):
        blocks = [arrived[(k, half if k or not paired else 0)] for k in far_first]
        if returned:
            blocks, made = lax.optimization_barrier((blocks, made))
        made = apply_cycle(half, plan, operator, blocks, width)
        if not returned:
            behind, terms = lax.optimization_barrier((made[2:], terms))
            for step, term in enumerate(terms, 1):
                pairs = [(i, (i + step) % lad_count) for i in range(lad_count)]
                crossed.append(lax.ppermute(term, "lad", pairs))
        else:
            behind, crossed = lax.optimization_barrier((made[2:], crossed))
        made = [*made[:2], *behind]
        returned.append([exchange(block, k) for k, block in zip(far_first, made)])
    for term in crossed:
        base = base + term.astype(F32)
    updated = None
    for half in range(HALVES):
        updated = finish(half, pick, base, part_column, hole_row, returned[half], updated)
    return updated[None]


def solution(mesh):
    placed = (
        P(("parts", "chan"), ("lad", "sub"), None),
        P(("parts", "chan"), ("lad", "sub"), None),
        P("chan", ("lad", "sub"), None),
        P("chan", None, ("lad", "sub")),
        P("chan", ("lad", "sub"), None, None),
        P("chan", ("lad", "sub"), None, None, None),
        P(("parts", "chan"), ("lad", "sub")),
        P("parts"),
    )
    return jax.shard_map(
        body,
        mesh=mesh,
        in_specs=placed,
        out_specs=P(("parts", "chan"), ("lad", "sub"), None),
        check_vma=False,
    )
```

```python
import functools

import jax
import jax.numpy as jnp
from jax import lax
from jax.experimental import pallas as pl
from jax.experimental.pallas import tpu as pltpu
from jax.sharding import PartitionSpec as P

VMEM_LIMIT = 28 * 1024 * 1024
HALVES = 2
F32 = jnp.float32
BF16 = jnp.bfloat16
CHEAP = pl.CostEstimate(flops=0, bytes_accessed=0, transcendentals=0)
DEAR = pl.CostEstimate(flops=3 * 10**10, bytes_accessed=10**6, transcendentals=0)


def params():
    return pltpu.CompilerParams(vmem_limit_bytes=VMEM_LIMIT)


def in_hbm(*arrays):
    return [pltpu.with_memory_space_constraint(a, pltpu.HBM) for a in arrays]


def whole(memory=pltpu.VMEM):
    return pl.BlockSpec(memory_space=memory)


def selection(match):
    return jnp.where(match, 1.0, 0.0).astype(BF16)


def block_offsets(paired, chan_count, block_rows):
    chan = lax.axis_index("chan")
    return [(chan ^ k) * block_rows for k in range(chan_count)] if paired else [0]


def slots_of(owners, send, names):
    lane = 128
    pieces = owners.shape[1] // lane
    before = selection(
        lax.broadcasted_iota(jnp.int32, (lane, 2 * lane), 0)
        < lax.broadcasted_iota(jnp.int32, (lane, 2 * lane), 1)
    )
    hot = [
        lax.broadcasted_iota(jnp.int32, (names, lane), 0) == owners[:, i * lane : (i + 1) * lane]
        for i in range(pieces)
    ]
    counts = jnp.dot(
        jnp.concatenate([selection(h) for h in hot], axis=0), before, preferred_element_type=F32
    )
    passed = jnp.zeros((names, lane), F32)
    slots = []
    for i in range(pieces):
        within = counts[i * names : (i + 1) * names]
        slots.append(jnp.sum(jnp.where(hot[i], within[:, :lane] + passed, 0.0), axis=0, keepdims=True))
        passed = passed + within[:, lane:]
    return owners * send + jnp.concatenate(slots, axis=1).astype(jnp.int32)


def pack_kernel(plan, given, route_in, amps_hbm, *refs):
    paired, chan_count, send, block_rows, items = plan
    outs, (route_ref, amps_ref, sems) = refs[:-3], refs[-3:]
    block_refs = outs if given else outs[1:]
    amps_copy = pltpu.make_async_copy(amps_hbm.at[:, pl.ds(0, amps_ref.shape[1])], amps_ref, sems.at[1])
    if given:
        amps_copy.start()
        target = route_in[...]
    else:
        route_copy = pltpu.make_async_copy(route_in, route_ref, sems.at[0])
        route_copy.start()
        amps_copy.start()
        route_copy.wait()
        target = slots_of(route_ref[...], send, max(16, chan_count))
        outs[0][...] = target
    offsets = block_offsets(paired, chan_count, block_rows)
    slot = lax.broadcasted_iota(jnp.int32, (block_rows, target.shape[1]), 0)
    for i, (k, first, width) in enumerate(items):
        pick = selection(slot == target - offsets[k])
        if i == 0:
            amps_copy.wait()
        block_refs[i][...] = jnp.dot(
            pick, amps_ref[:, pl.ds(first, width)], preferred_element_type=F32
        ).astype(BF16)


def pack(plan, given, route_row, amps, name):
    rows = amps.shape[0]
    block_rows, items = plan[3], plan[4]
    columns = max(first + width for _, first, width in items)
    extra = [] if given else [pltpu.VMEM((1, rows), jnp.int32)]
    return pl.pallas_call(
        functools.partial(pack_kernel, plan, given),
        out_shape=extra + [pltpu.VMEM((block_rows, width), BF16) for _, _, width in items],
        in_specs=[whole() if given else whole(pl.ANY), whole(pl.ANY)],
        out_specs=[whole()] * (len(extra) + len(items)),
        scratch_shapes=[
            pltpu.VMEM((1, rows), jnp.int32),
            pltpu.VMEM((rows, columns), BF16),
            pltpu.SemaphoreType.DMA((2,)),
        ],
        compiler_params=params(),
        name=name,
    )(*([route_row] if given else in_hbm(route_row)), *in_hbm(amps))


def unpack_kernel(off_ref, target_ref, part_ref, hole_ref, out_ref, inverse_ref):
    count = off_ref.shape[0]
    rows, capacity = out_ref.shape
    block_rows = capacity // count
    target = target_ref[...]
    slots = lax.broadcasted_iota(jnp.int32, (rows, block_rows), 1)
    for k in range(count):
        out_ref[:, pl.ds(k * block_rows, block_rows)] = selection(slots == target - off_ref[k])
    inverse_ref[...] = 1.0 / (part_ref[...] + hole_ref[...])


def unpack_matrix(offsets, target_column, part_column, hole_row, capacity):
    rows, holes = part_column.shape[0], hole_row.shape[1]
    return pl.pallas_call(
        unpack_kernel,
        out_shape=[jax.ShapeDtypeStruct((rows, capacity), BF16), jax.ShapeDtypeStruct((rows, holes), F32)],
        in_specs=[whole(pltpu.SMEM), whole(), whole(), whole()],
        out_specs=[whole()] * 2,
        compiler_params=params(),
        cost_estimate=DEAR,
        name="unpack_matrix",
    )(offsets, target_column, part_column, hole_row)


def prepare_kernel(sub_count, weight_hbm, amps_hbm, cycle_hbm, mixing_hbm, *refs):
    part_refs, out_ref = refs[:sub_count], refs[sub_count]
    weight_ref, amps_ref, cycle_ref, half_ref, mixing_ref, pair_ref, sems = refs[sub_count + 1 :]
    rows, lad_count = amps_ref.shape[0], part_refs[0].shape[0]
    chunks, chunk, capacity = cycle_ref.shape
    group = mixing_ref.shape[1]
    pairs, wide = pair_ref.shape[0], pair_ref.shape[1]
    sub = lax.axis_index("sub")
    moves, ladder = [(amps_hbm, amps_ref)], []
    for n in range(sub_count):
        share = lax.rem(sub + sub_count - 1 - n, sub_count)
        for i in range(lad_count):
            start = pl.multiple_of((i * sub_count + share) * rows, rows)
            moves.append((weight_hbm.at[pl.ds(start, rows), :], weight_ref.at[len(ladder)]))
            ladder.append((n, i))
    moves.append((mixing_hbm, mixing_ref))
    moves += [(cycle_hbm.at[pl.ds(i * chunk, chunk), :], cycle_ref.at[i]) for i in range(chunks)]
    copies = [pltpu.make_async_copy(source, held, sems.at[n]) for n, (source, held) in enumerate(moves)]
    for copy in copies:
        copy.start()
    pair_ref[...] = jnp.zeros(pair_ref.shape, BF16)
    copies[0].wait()
    for m, (n, i) in enumerate(ladder):
        copies[1 + m].wait()
        part_refs[n][i] = jnp.dot(weight_ref[m], amps_ref[...], preferred_element_type=F32).astype(BF16)
    copies[1 + len(ladder)].wait()
    for q in range(capacity // group):
        at = pl.ds(q * group % wide, group)
        pair_ref[q * group // wide, at, at] = mixing_ref[q]
    for i in range(chunks):
        copies[2 + len(ladder) + i].wait()
        for a in range(chunk // group):
            at = pl.ds(a * group, group)
            half_ref[pl.ds(i * chunk + a * group, group), :] = lax.dot_general(
                mixing_ref[i * chunk // group + a],
                cycle_ref[i, at, :],
                (((0,), (0,)), ((), ())),
                preferred_element_type=F32,
            ).astype(BF16)
    for j in range(pairs):
        at = pl.ds(j * wide, wide)
        out_ref[:, at] = jnp.dot(half_ref[:, at], pair_ref[j], preferred_element_type=F32).astype(BF16)


def prepare(weight, amps, cycle_weight, mixing, lad_count, sub_count):
    rows, holes = amps.shape
    capacity = cycle_weight.shape[0]
    groups, group = mixing.shape[0], mixing.shape[1]
    wide = group * (2 if groups % 2 == 0 else 1)
    chunks = groups // 3 if groups % 3 == 0 else 1
    outs = pl.pallas_call(
        functools.partial(prepare_kernel, sub_count),
        out_shape=[jax.ShapeDtypeStruct((lad_count, rows, holes), BF16)] * sub_count
        + [jax.ShapeDtypeStruct((capacity, capacity), BF16)],
        in_specs=[whole(pl.ANY)] * 4,
        out_specs=[whole()] * (sub_count + 1),
        scratch_shapes=[
            pltpu.VMEM((lad_count * sub_count, rows, rows), BF16),
            pltpu.VMEM((rows, holes), BF16),
            pltpu.VMEM((chunks, capacity // chunks, capacity), BF16),
            pltpu.VMEM((capacity, capacity), BF16),
            pltpu.VMEM(mixing.shape, BF16),
            pltpu.VMEM((capacity // wide, wide, wide), BF16),
            pltpu.SemaphoreType.DMA((2 + lad_count * sub_count + chunks,)),
        ],
        compiler_params=params(),
        cost_estimate=DEAR,
        name="prepare",
    )(*in_hbm(weight, amps, cycle_weight, mixing))
    return outs[:sub_count], outs[sub_count]


def cycle_kernel(half, plan, operator_ref, *refs):
    paired, chan_count, _, _ = plan
    count = len(refs) // 2
    in_refs, out_refs, block_ref = refs[:count], refs[count : 2 * count], refs[2 * count]
    block_rows, width = out_refs[0].shape
    offsets = block_offsets(paired, chan_count, block_rows)
    starts = [pl.multiple_of(offsets[count - 1 - i], block_rows) for i in range(count)]
    for in_ref, start in zip(in_refs, starts):
        part = in_ref[...] if in_ref.shape[1] == width else in_ref[:, pl.ds(half * width, width)]
        block_ref[pl.ds(start, block_rows), :] = part
    for out_ref, start in zip(out_refs, starts):
        out_ref[...] = jnp.dot(
            operator_ref[pl.ds(start, block_rows), :], block_ref[...], preferred_element_type=F32
        ).astype(BF16)


def apply_cycle(half, plan, operator, arrays, width):
    block_rows = arrays[0].shape[0]
    return pl.pallas_call(
        functools.partial(cycle_kernel, half, plan),
        out_shape=[jax.ShapeDtypeStruct((block_rows, width), BF16)] * len(arrays),
        in_specs=[whole()] * (1 + len(arrays)),
        out_specs=[whole()] * len(arrays),
        scratch_shapes=[pltpu.VMEM((operator.shape[0], width), BF16)],
        compiler_params=params(),
        cost_estimate=DEAR,
        name="apply_cycle",
    )(operator, *arrays)


def gathered(blocks, block_ref):
    block_rows = blocks[0][1].shape[0]
    for n, (_, ref) in enumerate(blocks):
        block_ref[pl.ds(n * block_rows, block_rows), :] = ref[...]


def picked(blocks, pick_ref, rows_at):
    block_rows = blocks[0][1].shape[0]
    return jnp.concatenate([pick_ref[rows_at, pl.ds(k * block_rows, block_rows)] for k, _ in blocks], axis=1)


def partial_kernel(start_column, places, tiles, pick_ref, base_ref, *refs):
    blocks, (out_ref, block_ref) = list(zip(places, refs[:-2])), refs[-2:]
    tile, columns = out_ref.shape[0] // tiles, pl.ds(start_column, out_ref.shape[1])
    gathered(blocks, block_ref)
    for t in range(tiles):
        at = pl.ds(t * tile, tile)
        back = jnp.dot(picked(blocks, pick_ref, at), block_ref[...], preferred_element_type=F32)
        out_ref[at, :] = base_ref[at, columns] + back


def finish_kernel(start_column, places, tiles, pick_ref, base_ref, inverse_ref, *refs):
    blocks, (out_hbm, block_ref, out_ref, sems) = list(zip(places, refs)), refs[-4:]
    tile, width = out_ref.shape[0] // tiles, out_ref.shape[1]
    columns = pl.ds(start_column, width)
    base_columns = columns if base_ref.shape[1] > width else pl.ds(0, width)
    gathered(blocks, block_ref)
    copies = []
    for t in range(tiles):
        at = pl.ds(t * tile, tile)
        back = jnp.dot(picked(blocks, pick_ref, at), block_ref[...], preferred_element_type=F32)
        out_ref[at, :] = ((base_ref[at, base_columns] + back) * inverse_ref[at, columns]).astype(BF16)
        copies.append(pltpu.make_async_copy(out_ref.at[at, :], out_hbm.at[at, columns], sems.at[t]))
        copies[-1].start()
    for copy in copies:
        copy.wait()


def finish(half, pick, base, inverse, arrays, earlier):
    rows, holes = inverse.shape
    tiles, width = 3, holes // HALVES
    block_rows = arrays[0].shape[0]
    places = list(range(len(arrays)))
    if earlier is not None and len(arrays) > 1:
        last = min(2, len(arrays) - 1)
        places.remove(last)
        base = pl.pallas_call(
            functools.partial(partial_kernel, half * width, tuple(places), tiles),
            out_shape=jax.ShapeDtypeStruct((rows, width), F32),
            in_specs=[whole()] * (2 + len(places)),
            out_specs=whole(),
            scratch_shapes=[pltpu.VMEM((block_rows * len(places), width), BF16)],
            compiler_params=params(),
            cost_estimate=CHEAP,
            name="partial",
        )(pick, base, *[arrays[k] for k in places])
        places = [last]
    operands = [pick, base, inverse] + [arrays[k] for k in places]
    in_specs = [whole()] * len(operands)
    aliases = {}
    if earlier is not None:
        aliases = {len(operands): 0}
        operands.append(earlier)
        in_specs.append(whole(pl.ANY))
    return pl.pallas_call(
        functools.partial(finish_kernel, half * width, tuple(places), tiles),
        out_shape=jax.ShapeDtypeStruct((rows, holes), BF16),
        in_specs=in_specs,
        out_specs=whole(pl.ANY),
        scratch_shapes=[
            pltpu.VMEM((block_rows * len(places), width), BF16),
            pltpu.VMEM((rows, width), BF16),
            pltpu.SemaphoreType.DMA((tiles,)),
        ],
        input_output_aliases=aliases,
        compiler_params=params(),
        cost_estimate=CHEAP,
        name="finish",
    )(*operands)


def body(amplitudes, driving, route, ladder_weight, ph_weight, recouple, gap_part, gap_hole):
    amps = amplitudes[0]
    rows, holes = amps.shape
    chan_count = lax.axis_size("chan")
    lad_count = lax.axis_size("lad")
    sub_count = lax.axis_size("sub")
    chan, lad, sub = lax.axis_index("chan"), lax.axis_index("lad"), lax.axis_index("sub")
    weight, mixing = ph_weight[0, 0], recouple[0, 0]
    capacity = weight.shape[0]
    send = capacity // chan_count
    paired = send % mixing.shape[1] == 0 and chan_count & (chan_count - 1) == 0
    if paired:
        block_rows = send
        block_index = jnp.stack([chan ^ k for k in range(chan_count)]).astype(jnp.int32)
    else:
        block_rows = capacity
        block_index = jnp.zeros((1,), jnp.int32)
    offsets = block_index * block_rows

    def exchange(block, k):
        if not paired:
            split = block.reshape(chan_count, send, -1)
            split = lax.all_to_all(split, "chan", split_axis=0, concat_axis=0, tiled=True)
            return split.reshape(capacity, -1)
        return lax.ppermute(block, "chan", [(i, i ^ k) for i in range(chan_count)]) if k else block

    far_first = list(reversed(range(block_index.shape[0])))
    count = len(far_first)
    width = holes // HALVES
    route_row = route[0].reshape(1, rows)
    plan = (paired, chan_count, send, block_rows)
    early = [(k, 0, width) for k in far_first if k or not paired]
    late = [(k, h * width, width) for h in range(1, HALVES) for k in far_first if k or not paired]
    late += [(0, 0, holes)] if paired else []
    target, *blocks = pack(plan + (early,), False, route_row, amps, "pack_first")
    arrived = {(k, 0): exchange(block, k) for (k, _, _), block in zip(early, blocks)}
    if paired:
        near = (1, 0)
        target, arrived[near] = lax.optimization_barrier((target, arrived[near]))
    blocks = pack(plan + (late,), True, target, amps, "pack_rest")
    for (k, first, _), block in zip(late, blocks):
        arrived[(k, first // width)] = exchange(block, k)

    part_column, hole_row = gap_part[0].reshape(rows, 1), gap_hole.reshape(1, holes)
    amps, blocks = lax.optimization_barrier((amps, blocks))
    pick, inverse = unpack_matrix(offsets, target.reshape(rows, 1), part_column, hole_row, capacity)

    parts, operator = prepare(ladder_weight[0], amps, weight, mixing, lad_count, sub_count)
    kept = [parts[-1]]
    for step in range(1, sub_count):
        pairs = [(i, (i + step) % sub_count) for i in range(sub_count)]
        kept.append(lax.ppermute(parts[sub_count - 1 - step], "sub", pairs))

    def chip_sum(position):
        picked = [lax.dynamic_index_in_dim(p, position, 0, keepdims=False) for p in kept]
        return sum(p.astype(F32) for p in picked)

    base = driving[0].astype(F32) + chip_sum(lad)
    terms = [chip_sum(lax.rem(lad + step, lad_count)).astype(BF16) for step in range(1, lad_count)]
    returned, crossed = [], []
    for half in range(HALVES):
        blocks = [arrived[(k, half if k or not paired else 0)] for k in far_first]
        if returned:
            blocks, made = lax.optimization_barrier((blocks, made))
        made = apply_cycle(half, plan, operator, blocks, width)
        if not returned:
            behind, terms = lax.optimization_barrier((made[2:], terms))
            for step, term in enumerate(terms, 1):
                pairs = [(i, (i + step) % lad_count) for i in range(lad_count)]
                crossed.append(lax.ppermute(term, "lad", pairs))
        else:
            behind, crossed = lax.optimization_barrier((made[2:], crossed))
        made = [*made[:2], *behind]
        returned.append([exchange(block, k) for k, block in zip(far_first, made)])
    for term in crossed:
        base = base + term.astype(F32)
    updated = None
    for half in range(HALVES):
        updated = finish(half, pick, base, inverse, list(reversed(returned[half])), updated)
    return updated[None]


def solution(mesh):
    placed = (
        P(("parts", "chan"), ("lad", "sub"), None),
        P(("parts", "chan"), ("lad", "sub"), None),
        P("chan", ("lad", "sub"), None),
        P("chan", None, ("lad", "sub")),
        P("chan", ("lad", "sub"), None, None),
        P("chan", ("lad", "sub"), None, None, None),
        P(("parts", "chan"), ("lad", "sub")),
        P("parts"),
    )
    return jax.shard_map(
        body,
        mesh=mesh,
        in_specs=placed,
        out_specs=P(("parts", "chan"), ("lad", "sub"), None),
        check_vma=False,
    )
```

```python
import functools
import math

import jax
import jax.numpy as jnp
from jax import lax
from jax.experimental import pallas as pl
from jax.experimental.pallas import tpu as pltpu
from jax.sharding import PartitionSpec as P

VMEM_LIMIT = 28 * 1024 * 1024
HALVES = 2
F32 = jnp.float32
BF16 = jnp.bfloat16
CHEAP = pl.CostEstimate(flops=0, bytes_accessed=0, transcendentals=0)
DEAR = pl.CostEstimate(flops=3 * 10**10, bytes_accessed=10**6, transcendentals=0)


def params():
    return pltpu.CompilerParams(vmem_limit_bytes=VMEM_LIMIT)


def in_hbm(*arrays):
    return [pltpu.with_memory_space_constraint(a, pltpu.HBM) for a in arrays]


def whole(memory=pltpu.VMEM):
    return pl.BlockSpec(memory_space=memory)


def selection(match):
    return jnp.where(match, 1.0, 0.0).astype(BF16)


def block_offsets(paired, chan_count, block_rows):
    chan = lax.axis_index("chan")
    return [(chan ^ k) * block_rows for k in range(chan_count)] if paired else [0]


def slots_of(owners, send, names):
    lane = 128
    pieces = owners.shape[1] // lane
    before = selection(
        lax.broadcasted_iota(jnp.int32, (lane, 2 * lane), 0)
        < lax.broadcasted_iota(jnp.int32, (lane, 2 * lane), 1)
    )
    hot = [
        lax.broadcasted_iota(jnp.int32, (names, lane), 0) == owners[:, i * lane : (i + 1) * lane]
        for i in range(pieces)
    ]
    counts = jnp.dot(
        jnp.concatenate([selection(h) for h in hot], axis=0), before, preferred_element_type=F32
    )
    passed = jnp.zeros((names, lane), F32)
    slots = []
    for i in range(pieces):
        within = counts[i * names : (i + 1) * names]
        slots.append(jnp.sum(jnp.where(hot[i], within[:, :lane] + passed, 0.0), axis=0, keepdims=True))
        passed = passed + within[:, lane:]
    return owners * send + jnp.concatenate(slots, axis=1).astype(jnp.int32)


def pack_kernel(plan, given, route_in, amps_hbm, *refs):
    paired, chan_count, send, block_rows, items = plan
    outs, (route_ref, amps_ref, sems) = refs[:-3], refs[-3:]
    block_refs = outs if given else outs[1:]
    amps_copy = pltpu.make_async_copy(amps_hbm.at[:, pl.ds(0, amps_ref.shape[1])], amps_ref, sems.at[1])
    if given:
        amps_copy.start()
        target = route_in[...]
    else:
        route_copy = pltpu.make_async_copy(route_in, route_ref, sems.at[0])
        route_copy.start()
        amps_copy.start()
        route_copy.wait()
        target = slots_of(route_ref[...], send, max(16, chan_count))
        outs[0][...] = target
    offsets = block_offsets(paired, chan_count, block_rows)
    for i, (k, low, slots, first, width) in enumerate(items):
        slot = lax.broadcasted_iota(jnp.int32, (slots, target.shape[1]), 0)
        pick = selection(slot == target - (offsets[k] + low))
        if i == 0:
            amps_copy.wait()
        block_refs[i][...] = jnp.dot(
            pick, amps_ref[:, pl.ds(first, width)], preferred_element_type=F32
        ).astype(BF16)


def pack(plan, given, route_row, amps, name):
    rows = amps.shape[0]
    items = plan[4]
    columns = max(first + width for *_, first, width in items)
    extra = [] if given else [pltpu.VMEM((1, rows), jnp.int32)]
    return pl.pallas_call(
        functools.partial(pack_kernel, plan, given),
        out_shape=extra + [pltpu.VMEM((slots, width), BF16) for _, _, slots, _, width in items],
        in_specs=[whole() if given else whole(pl.ANY), whole(pl.ANY)],
        out_specs=[whole()] * (len(extra) + len(items)),
        scratch_shapes=[
            pltpu.VMEM((1, rows), jnp.int32),
            pltpu.VMEM((rows, columns), BF16),
            pltpu.SemaphoreType.DMA((2,)),
        ],
        compiler_params=params(),
        name=name,
    )(*([route_row] if given else in_hbm(route_row)), *in_hbm(amps))


def unpack_kernel(off_ref, target_ref, part_ref, hole_ref, out_ref, inverse_ref):
    count = off_ref.shape[0]
    rows, capacity = out_ref.shape
    block_rows = capacity // count
    target = target_ref[...]
    slots = lax.broadcasted_iota(jnp.int32, (rows, block_rows), 1)
    for k in range(count):
        out_ref[:, pl.ds(k * block_rows, block_rows)] = selection(slots == target - off_ref[k])
    inverse_ref[...] = 1.0 / (part_ref[...] + hole_ref[...])


def unpack_matrix(offsets, target_column, part_column, hole_row, capacity):
    rows, holes = part_column.shape[0], hole_row.shape[1]
    return pl.pallas_call(
        unpack_kernel,
        out_shape=[jax.ShapeDtypeStruct((rows, capacity), BF16), jax.ShapeDtypeStruct((rows, holes), F32)],
        in_specs=[whole(pltpu.SMEM), whole(), whole(), whole()],
        out_specs=[whole()] * 2,
        compiler_params=params(),
        cost_estimate=DEAR,
        name="unpack_matrix",
    )(offsets, target_column, part_column, hole_row)


def prepare_kernel(sub_count, weight_hbm, amps_hbm, cycle_hbm, mixing_hbm, *refs):
    part_refs, out_ref = refs[:sub_count], refs[sub_count]
    weight_ref, amps_ref, cycle_ref, half_ref, mixing_ref, pair_ref, sems = refs[sub_count + 1 :]
    rows, lad_count = amps_ref.shape[0], part_refs[0].shape[0]
    chunks, chunk, capacity = cycle_ref.shape
    group = mixing_ref.shape[1]
    pairs, wide = pair_ref.shape[0], pair_ref.shape[1]
    sub = lax.axis_index("sub")
    moves, ladder = [(amps_hbm, amps_ref)], []
    for n in range(sub_count):
        share = lax.rem(sub + sub_count - 1 - n, sub_count)
        for i in range(lad_count):
            start = pl.multiple_of((i * sub_count + share) * rows, rows)
            moves.append((weight_hbm.at[pl.ds(start, rows), :], weight_ref.at[len(ladder)]))
            ladder.append((n, i))
    moves.append((mixing_hbm, mixing_ref))
    moves += [(cycle_hbm.at[pl.ds(i * chunk, chunk), :], cycle_ref.at[i]) for i in range(chunks)]
    copies = [pltpu.make_async_copy(source, held, sems.at[n]) for n, (source, held) in enumerate(moves)]
    for copy in copies:
        copy.start()
    pair_ref[...] = jnp.zeros(pair_ref.shape, BF16)
    copies[0].wait()
    for m, (n, i) in enumerate(ladder):
        copies[1 + m].wait()
        part_refs[n][i] = jnp.dot(weight_ref[m], amps_ref[...], preferred_element_type=F32).astype(BF16)
    copies[1 + len(ladder)].wait()
    for q in range(capacity // group):
        at = pl.ds(q * group % wide, group)
        pair_ref[q * group // wide, at, at] = mixing_ref[q]
    for i in range(chunks):
        copies[2 + len(ladder) + i].wait()
        for a in range(chunk // group):
            at = pl.ds(a * group, group)
            half_ref[pl.ds(i * chunk + a * group, group), :] = lax.dot_general(
                mixing_ref[i * chunk // group + a],
                cycle_ref[i, at, :],
                (((0,), (0,)), ((), ())),
                preferred_element_type=F32,
            ).astype(BF16)
    for j in range(pairs):
        at = pl.ds(j * wide, wide)
        out_ref[:, at] = jnp.dot(half_ref[:, at], pair_ref[j], preferred_element_type=F32).astype(BF16)


def prepare(weight, amps, cycle_weight, mixing, lad_count, sub_count):
    rows, holes = amps.shape
    capacity = cycle_weight.shape[0]
    groups, group = mixing.shape[0], mixing.shape[1]
    wide = group * (2 if groups % 2 == 0 else 1)
    chunks = groups // 3 if groups % 3 == 0 else 1
    outs = pl.pallas_call(
        functools.partial(prepare_kernel, sub_count),
        out_shape=[jax.ShapeDtypeStruct((lad_count, rows, holes), BF16)] * sub_count
        + [jax.ShapeDtypeStruct((capacity, capacity), BF16)],
        in_specs=[whole(pl.ANY)] * 4,
        out_specs=[whole()] * (sub_count + 1),
        scratch_shapes=[
            pltpu.VMEM((lad_count * sub_count, rows, rows), BF16),
            pltpu.VMEM((rows, holes), BF16),
            pltpu.VMEM((chunks, capacity // chunks, capacity), BF16),
            pltpu.VMEM((capacity, capacity), BF16),
            pltpu.VMEM(mixing.shape, BF16),
            pltpu.VMEM((capacity // wide, wide, wide), BF16),
            pltpu.SemaphoreType.DMA((2 + lad_count * sub_count + chunks,)),
        ],
        compiler_params=params(),
        cost_estimate=DEAR,
        name="prepare",
    )(*in_hbm(weight, amps, cycle_weight, mixing))
    return outs[:sub_count], outs[sub_count]


def cycle_kernel(half, plan, places, operator_ref, *refs):
    paired, chan_count, _, block_rows = plan
    in_refs, out_refs, block_ref = refs[: len(places)], refs[len(places) : -1], refs[-1]
    width = out_refs[0].shape[1]
    offsets = block_offsets(paired, chan_count, block_rows)
    starts = [pl.multiple_of(offset, block_rows) for offset in reversed(offsets)]
    for in_ref, (k, low) in zip(in_refs, places):
        part = in_ref[...] if in_ref.shape[1] == width else in_ref[:, pl.ds(half * width, width)]
        start = pl.multiple_of(offsets[k] + low, math.gcd(low, block_rows))
        block_ref[pl.ds(start, in_ref.shape[0]), :] = part
    for out_ref, start in zip(out_refs, starts):
        out_ref[...] = jnp.dot(
            operator_ref[pl.ds(start, block_rows), :], block_ref[...], preferred_element_type=F32
        ).astype(BF16)


def apply_cycle(half, plan, operator, places, arrays, width):
    block_rows = plan[3]
    count = operator.shape[0] // block_rows
    return pl.pallas_call(
        functools.partial(cycle_kernel, half, plan, places),
        out_shape=[jax.ShapeDtypeStruct((block_rows, width), BF16)] * count,
        in_specs=[whole()] * (1 + len(arrays)),
        out_specs=[whole()] * count,
        scratch_shapes=[pltpu.VMEM((operator.shape[0], width), BF16)],
        compiler_params=params(),
        cost_estimate=DEAR,
        name="apply_cycle",
    )(operator, *arrays)


def gathered(blocks, block_ref):
    block_rows = blocks[0][1].shape[0]
    for n, (_, ref) in enumerate(blocks):
        block_ref[pl.ds(n * block_rows, block_rows), :] = ref[...]


def picked(blocks, pick_ref, rows_at):
    block_rows = blocks[0][1].shape[0]
    return jnp.concatenate([pick_ref[rows_at, pl.ds(k * block_rows, block_rows)] for k, _ in blocks], axis=1)


def partial_kernel(start_column, places, tiles, pick_ref, base_ref, *refs):
    blocks, (out_ref, block_ref) = list(zip(places, refs[:-2])), refs[-2:]
    tile, columns = out_ref.shape[0] // tiles, pl.ds(start_column, out_ref.shape[1])
    gathered(blocks, block_ref)
    for t in range(tiles):
        at = pl.ds(t * tile, tile)
        back = jnp.dot(picked(blocks, pick_ref, at), block_ref[...], preferred_element_type=F32)
        out_ref[at, :] = base_ref[at, columns] + back


def finish_kernel(start_column, places, tiles, pick_ref, base_ref, inverse_ref, *refs):
    blocks, (out_hbm, block_ref, out_ref, sems) = list(zip(places, refs)), refs[-4:]
    tile, width = out_ref.shape[0] // tiles, out_ref.shape[1]
    columns = pl.ds(start_column, width)
    base_columns = columns if base_ref.shape[1] > width else pl.ds(0, width)
    gathered(blocks, block_ref)
    copies = []
    for t in range(tiles):
        at = pl.ds(t * tile, tile)
        back = jnp.dot(picked(blocks, pick_ref, at), block_ref[...], preferred_element_type=F32)
        out_ref[at, :] = ((base_ref[at, base_columns] + back) * inverse_ref[at, columns]).astype(BF16)
        copies.append(pltpu.make_async_copy(out_ref.at[at, :], out_hbm.at[at, columns], sems.at[t]))
        copies[-1].start()
    for copy in copies:
        copy.wait()


def finish(half, pick, base, inverse, arrays, earlier):
    rows, holes = inverse.shape
    tiles, width = 3, holes // HALVES
    block_rows = arrays[0].shape[0]
    places = list(range(len(arrays)))
    if earlier is not None and len(arrays) > 1:
        last = min(2, len(arrays) - 1)
        places.remove(last)
        base = pl.pallas_call(
            functools.partial(partial_kernel, half * width, tuple(places), tiles),
            out_shape=jax.ShapeDtypeStruct((rows, width), F32),
            in_specs=[whole()] * (2 + len(places)),
            out_specs=whole(),
            scratch_shapes=[pltpu.VMEM((block_rows * len(places), width), BF16)],
            compiler_params=params(),
            cost_estimate=CHEAP,
            name="partial",
        )(pick, base, *[arrays[k] for k in places])
        places = [last]
    operands = [pick, base, inverse] + [arrays[k] for k in places]
    in_specs = [whole()] * len(operands)
    aliases = {}
    if earlier is not None:
        aliases = {len(operands): 0}
        operands.append(earlier)
        in_specs.append(whole(pl.ANY))
    return pl.pallas_call(
        functools.partial(finish_kernel, half * width, tuple(places), tiles),
        out_shape=jax.ShapeDtypeStruct((rows, holes), BF16),
        in_specs=in_specs,
        out_specs=whole(pl.ANY),
        scratch_shapes=[
            pltpu.VMEM((block_rows * len(places), width), BF16),
            pltpu.VMEM((rows, width), BF16),
            pltpu.SemaphoreType.DMA((tiles,)),
        ],
        input_output_aliases=aliases,
        compiler_params=params(),
        cost_estimate=CHEAP,
        name="finish",
    )(*operands)


def body(amplitudes, driving, route, ladder_weight, ph_weight, recouple, gap_part, gap_hole):
    amps = amplitudes[0]
    rows, holes = amps.shape
    chan_count = lax.axis_size("chan")
    lad_count = lax.axis_size("lad")
    sub_count = lax.axis_size("sub")
    chan, lad, sub = lax.axis_index("chan"), lax.axis_index("lad"), lax.axis_index("sub")
    weight, mixing = ph_weight[0, 0], recouple[0, 0]
    capacity = weight.shape[0]
    send = capacity // chan_count
    paired = send % mixing.shape[1] == 0 and chan_count & (chan_count - 1) == 0
    if paired:
        block_rows = send
        block_index = jnp.stack([chan ^ k for k in range(chan_count)]).astype(jnp.int32)
    else:
        block_rows = capacity
        block_index = jnp.zeros((1,), jnp.int32)
    offsets = block_index * block_rows

    def exchange(block, k):
        if not paired:
            split = block.reshape(chan_count, send, -1)
            split = lax.all_to_all(split, "chan", split_axis=0, concat_axis=0, tiled=True)
            return split.reshape(capacity, -1)
        return lax.ppermute(block, "chan", [(i, i ^ k) for i in range(chan_count)]) if k else block

    far_first = list(reversed(range(block_index.shape[0])))
    count = len(far_first)
    width = holes // HALVES
    route_row = route[0].reshape(1, rows)
    plan = (paired, chan_count, send, block_rows)
    leading = 128 if paired and count > 2 and block_rows > 128 else block_rows
    early = [(k, 0, block_rows, 0, width) for k in far_first if k or not paired]
    if leading < block_rows:
        early[:1] = [(early[0][0], 0, leading, 0, width), (early[0][0], leading, block_rows - leading, 0, width)]
    late = [(k, 0, block_rows, h * width, width) for h in range(1, HALVES) for k in far_first if k or not paired]
    late += [(0, 0, block_rows, 0, holes)] if paired else []
    target, *blocks = pack(plan + (early,), False, route_row, amps, "pack_first")
    arrived = {item: exchange(block, item[0]) for item, block in zip(early, blocks)}
    if paired:
        first = early[0]
        target, arrived[first] = lax.optimization_barrier((target, arrived[first]))
    blocks = pack(plan + (late,), True, target, amps, "pack_rest")
    arrived.update({item: exchange(block, item[0]) for item, block in zip(late, blocks)})

    part_column, hole_row = gap_part[0].reshape(rows, 1), gap_hole.reshape(1, holes)
    amps, blocks = lax.optimization_barrier((amps, blocks))
    pick, inverse = unpack_matrix(offsets, target.reshape(rows, 1), part_column, hole_row, capacity)

    parts, operator = prepare(ladder_weight[0], amps, weight, mixing, lad_count, sub_count)
    kept = [parts[-1]]
    for step in range(1, sub_count):
        pairs = [(i, (i + step) % sub_count) for i in range(sub_count)]
        kept.append(lax.ppermute(parts[sub_count - 1 - step], "sub", pairs))

    def chip_sum(position):
        picked = [lax.dynamic_index_in_dim(p, position, 0, keepdims=False) for p in kept]
        return sum(p.astype(F32) for p in picked)

    base = driving[0].astype(F32) + chip_sum(lad)
    terms = [chip_sum(lax.rem(lad + step, lad_count)).astype(BF16) for step in range(1, lad_count)]
    returned, crossed = [], []
    for half in range(HALVES):
        here = [item for item in early + late if item[3] == half * width or item[4] > width]
        blocks = [arrived[item] for item in here]
        if returned:
            blocks, made = lax.optimization_barrier((blocks, made))
        made = apply_cycle(half, plan, operator, [item[:2] for item in here], blocks, width)
        if not returned:
            behind, terms = lax.optimization_barrier((made[2:], terms))
            for step, term in enumerate(terms, 1):
                pairs = [(i, (i + step) % lad_count) for i in range(lad_count)]
                crossed.append(lax.ppermute(term, "lad", pairs))
        else:
            behind, crossed = lax.optimization_barrier((made[2:], crossed))
        made = [*made[:2], *behind]
        returned.append([exchange(block, k) for k, block in zip(far_first, made)])
    for term in crossed:
        base = base + term.astype(F32)
    updated = None
    for half in range(HALVES):
        updated = finish(half, pick, base, inverse, list(reversed(returned[half])), updated)
    return updated[None]


def solution(mesh):
    placed = (
        P(("parts", "chan"), ("lad", "sub"), None),
        P(("parts", "chan"), ("lad", "sub"), None),
        P("chan", ("lad", "sub"), None),
        P("chan", None, ("lad", "sub")),
        P("chan", ("lad", "sub"), None, None),
        P("chan", ("lad", "sub"), None, None, None),
        P(("parts", "chan"), ("lad", "sub")),
        P("parts"),
    )
    return jax.shard_map(
        body,
        mesh=mesh,
        in_specs=placed,
        out_specs=P(("parts", "chan"), ("lad", "sub"), None),
        check_vma=False,
    )
```

```python
import functools
import math

import jax
import jax.numpy as jnp
from jax import lax
from jax.experimental import pallas as pl
from jax.experimental.pallas import tpu as pltpu
from jax.sharding import PartitionSpec as P

VMEM_LIMIT = 28 * 1024 * 1024
HALVES = 2
F32 = jnp.float32
BF16 = jnp.bfloat16
CHEAP = pl.CostEstimate(flops=0, bytes_accessed=0, transcendentals=0)
DEAR = pl.CostEstimate(flops=3 * 10**10, bytes_accessed=10**6, transcendentals=0)


def params():
    return pltpu.CompilerParams(vmem_limit_bytes=VMEM_LIMIT)


def in_hbm(*arrays):
    return [pltpu.with_memory_space_constraint(a, pltpu.HBM) for a in arrays]


def whole(memory=pltpu.VMEM):
    return pl.BlockSpec(memory_space=memory)


def selection(match):
    return jnp.where(match, 1.0, 0.0).astype(BF16)


def block_offsets(paired, chan_count, block_rows):
    chan = lax.axis_index("chan")
    return [(chan ^ k) * block_rows for k in range(chan_count)] if paired else [0]


def slots_of(owners, send, names):
    lane = 128
    pieces = owners.shape[1] // lane
    before = selection(
        lax.broadcasted_iota(jnp.int32, (lane, 2 * lane), 0)
        < lax.broadcasted_iota(jnp.int32, (lane, 2 * lane), 1)
    )
    hot = [
        lax.broadcasted_iota(jnp.int32, (names, lane), 0) == owners[:, i * lane : (i + 1) * lane]
        for i in range(pieces)
    ]
    counts = jnp.dot(
        jnp.concatenate([selection(h) for h in hot], axis=0), before, preferred_element_type=F32
    )
    passed = jnp.zeros((names, lane), F32)
    slots = []
    for i in range(pieces):
        within = counts[i * names : (i + 1) * names]
        slots.append(jnp.sum(jnp.where(hot[i], within[:, :lane] + passed, 0.0), axis=0, keepdims=True))
        passed = passed + within[:, lane:]
    return owners * send + jnp.concatenate(slots, axis=1).astype(jnp.int32)


def pack_kernel(plan, given, route_in, amps_hbm, *refs):
    paired, chan_count, send, block_rows, items = plan
    outs, (route_ref, amps_ref, sems) = refs[:-3], refs[-3:]
    block_refs = outs if given else outs[1:]
    amps_copy = pltpu.make_async_copy(amps_hbm.at[:, pl.ds(0, amps_ref.shape[1])], amps_ref, sems.at[1])
    if given:
        amps_copy.start()
        target = route_in[...]
    else:
        route_copy = pltpu.make_async_copy(route_in, route_ref, sems.at[0])
        route_copy.start()
        amps_copy.start()
        route_copy.wait()
        target = slots_of(route_ref[...], send, max(16, chan_count))
        outs[0][...] = target
    offsets = block_offsets(paired, chan_count, block_rows)
    for i, (k, low, slots, first, width) in enumerate(items):
        slot = lax.broadcasted_iota(jnp.int32, (slots, target.shape[1]), 0)
        pick = selection(slot == target - (offsets[k] + low))
        if i == 0:
            amps_copy.wait()
        block_refs[i][...] = jnp.dot(
            pick, amps_ref[:, pl.ds(first, width)], preferred_element_type=F32
        ).astype(BF16)


def pack(plan, given, route_row, amps, name):
    rows = amps.shape[0]
    items = plan[4]
    columns = max(first + width for *_, first, width in items)
    extra = [] if given else [pltpu.VMEM((1, rows), jnp.int32)]
    return pl.pallas_call(
        functools.partial(pack_kernel, plan, given),
        out_shape=extra + [pltpu.VMEM((slots, width), BF16) for _, _, slots, _, width in items],
        in_specs=[whole() if given else whole(pl.ANY), whole(pl.ANY)],
        out_specs=[whole()] * (len(extra) + len(items)),
        scratch_shapes=[
            pltpu.VMEM((1, rows), jnp.int32),
            pltpu.VMEM((rows, columns), BF16),
            pltpu.SemaphoreType.DMA((2,)),
        ],
        compiler_params=params(),
        name=name,
    )(*([route_row] if given else in_hbm(route_row)), *in_hbm(amps))


def unpack_kernel(off_ref, target_ref, part_ref, hole_ref, out_ref, inverse_ref):
    count = off_ref.shape[0]
    rows, capacity = out_ref.shape
    block_rows = capacity // count
    target = target_ref[...]
    slots = lax.broadcasted_iota(jnp.int32, (rows, block_rows), 1)
    for k in range(count):
        out_ref[:, pl.ds(k * block_rows, block_rows)] = selection(slots == target - off_ref[k])
    inverse_ref[...] = 1.0 / (part_ref[...] + hole_ref[...])


def unpack_matrix(offsets, target_column, part_column, hole_row, capacity):
    rows, holes = part_column.shape[0], hole_row.shape[1]
    return pl.pallas_call(
        unpack_kernel,
        out_shape=[jax.ShapeDtypeStruct((rows, capacity), BF16), jax.ShapeDtypeStruct((rows, holes), F32)],
        in_specs=[whole(pltpu.SMEM), whole(), whole(), whole()],
        out_specs=[whole()] * 2,
        compiler_params=params(),
        cost_estimate=DEAR,
        name="unpack_matrix",
    )(offsets, target_column, part_column, hole_row)


def prepare_kernel(sub_count, weight_hbm, amps_hbm, cycle_hbm, mixing_hbm, *refs):
    part_refs, out_ref = refs[:sub_count], refs[sub_count]
    weight_ref, amps_ref, cycle_ref, half_ref, mixing_ref, pair_ref, sems = refs[sub_count + 1 :]
    rows, lad_count = amps_ref.shape[0], part_refs[0].shape[0]
    chunks, chunk, capacity = cycle_ref.shape
    group = mixing_ref.shape[1]
    pairs, wide = pair_ref.shape[0], pair_ref.shape[1]
    sub = lax.axis_index("sub")
    moves, ladder = [(amps_hbm, amps_ref)], []
    for n in range(sub_count):
        share = lax.rem(sub + sub_count - 1 - n, sub_count)
        for i in range(lad_count):
            start = pl.multiple_of((i * sub_count + share) * rows, rows)
            moves.append((weight_hbm.at[pl.ds(start, rows), :], weight_ref.at[len(ladder)]))
            ladder.append((n, i))
    moves.append((mixing_hbm, mixing_ref))
    moves += [(cycle_hbm.at[pl.ds(i * chunk, chunk), :], cycle_ref.at[i]) for i in range(chunks)]
    copies = [pltpu.make_async_copy(source, held, sems.at[n]) for n, (source, held) in enumerate(moves)]
    for copy in copies:
        copy.start()
    pair_ref[...] = jnp.zeros(pair_ref.shape, BF16)
    copies[0].wait()
    for m, (n, i) in enumerate(ladder):
        copies[1 + m].wait()
        part_refs[n][i] = jnp.dot(weight_ref[m], amps_ref[...], preferred_element_type=F32).astype(BF16)
    copies[1 + len(ladder)].wait()
    for q in range(capacity // group):
        at = pl.ds(q * group % wide, group)
        pair_ref[q * group // wide, at, at] = mixing_ref[q]
    for i in range(chunks):
        copies[2 + len(ladder) + i].wait()
        for a in range(chunk // group):
            at = pl.ds(a * group, group)
            half_ref[pl.ds(i * chunk + a * group, group), :] = lax.dot_general(
                mixing_ref[i * chunk // group + a],
                cycle_ref[i, at, :],
                (((0,), (0,)), ((), ())),
                preferred_element_type=F32,
            ).astype(BF16)
    for j in range(pairs):
        at = pl.ds(j * wide, wide)
        out_ref[:, at] = jnp.dot(half_ref[:, at], pair_ref[j], preferred_element_type=F32).astype(BF16)


def prepare(weight, amps, cycle_weight, mixing, lad_count, sub_count):
    rows, holes = amps.shape
    capacity = cycle_weight.shape[0]
    groups, group = mixing.shape[0], mixing.shape[1]
    wide = group * (2 if groups % 2 == 0 else 1)
    chunks = groups // 3 if groups % 3 == 0 else 1
    outs = pl.pallas_call(
        functools.partial(prepare_kernel, sub_count),
        out_shape=[jax.ShapeDtypeStruct((lad_count, rows, holes), BF16)] * sub_count
        + [jax.ShapeDtypeStruct((capacity, capacity), BF16)],
        in_specs=[whole(pl.ANY)] * 4,
        out_specs=[whole()] * (sub_count + 1),
        scratch_shapes=[
            pltpu.VMEM((lad_count * sub_count, rows, rows), BF16),
            pltpu.VMEM((rows, holes), BF16),
            pltpu.VMEM((chunks, capacity // chunks, capacity), BF16),
            pltpu.VMEM((capacity, capacity), BF16),
            pltpu.VMEM(mixing.shape, BF16),
            pltpu.VMEM((capacity // wide, wide, wide), BF16),
            pltpu.SemaphoreType.DMA((2 + lad_count * sub_count + chunks,)),
        ],
        compiler_params=params(),
        cost_estimate=DEAR,
        name="prepare",
    )(*in_hbm(weight, amps, cycle_weight, mixing))
    return outs[:sub_count], outs[sub_count]


def cycle_kernel(half, plan, places, operator_ref, *refs):
    paired, chan_count, _, block_rows = plan
    in_refs, out_refs, block_ref = refs[: len(places)], refs[len(places) : -1], refs[-1]
    width = out_refs[0].shape[1]
    offsets = block_offsets(paired, chan_count, block_rows)
    starts = [pl.multiple_of(offset, block_rows) for offset in reversed(offsets)]
    for in_ref, (k, low) in zip(in_refs, places):
        part = in_ref[...] if in_ref.shape[1] == width else in_ref[:, pl.ds(half * width, width)]
        start = pl.multiple_of(offsets[k] + low, math.gcd(low, block_rows))
        block_ref[pl.ds(start, in_ref.shape[0]), :] = part
    for out_ref, start in zip(out_refs, starts):
        out_ref[...] = jnp.dot(
            operator_ref[pl.ds(start, block_rows), :], block_ref[...], preferred_element_type=F32
        ).astype(BF16)


def apply_cycle(half, plan, operator, places, arrays, width):
    block_rows = plan[3]
    count = operator.shape[0] // block_rows
    return pl.pallas_call(
        functools.partial(cycle_kernel, half, plan, places),
        out_shape=[jax.ShapeDtypeStruct((block_rows, width), BF16)] * count,
        in_specs=[whole()] * (1 + len(arrays)),
        out_specs=[whole()] * count,
        scratch_shapes=[pltpu.VMEM((operator.shape[0], width), BF16)],
        compiler_params=params(),
        cost_estimate=DEAR,
        name="apply_cycle",
    )(operator, *arrays)


def gathered(blocks, block_ref):
    block_rows = blocks[0][1].shape[0]
    for n, (_, ref) in enumerate(blocks):
        block_ref[pl.ds(n * block_rows, block_rows), :] = ref[...]


def picked(blocks, pick_ref, rows_at):
    block_rows = blocks[0][1].shape[0]
    return jnp.concatenate([pick_ref[rows_at, pl.ds(k * block_rows, block_rows)] for k, _ in blocks], axis=1)


def partial_kernel(start_column, places, tiles, pick_ref, base_ref, *refs):
    blocks, (out_ref, block_ref) = list(zip(places, refs[:-2])), refs[-2:]
    tile, columns = out_ref.shape[0] // tiles, pl.ds(start_column, out_ref.shape[1])
    gathered(blocks, block_ref)
    for t in range(tiles):
        at = pl.ds(t * tile, tile)
        back = jnp.dot(picked(blocks, pick_ref, at), block_ref[...], preferred_element_type=F32)
        out_ref[at, :] = base_ref[at, columns] + back


def finish_kernel(start_column, places, tiles, pick_ref, base_ref, inverse_ref, *refs):
    blocks, (out_hbm, block_ref, out_ref, sems) = list(zip(places, refs)), refs[-4:]
    tile, width = out_ref.shape[0] // tiles, out_ref.shape[1]
    columns = pl.ds(start_column, width)
    base_columns = columns if base_ref.shape[1] > width else pl.ds(0, width)
    gathered(blocks, block_ref)
    copies = []
    for t in range(tiles):
        at = pl.ds(t * tile, tile)
        back = jnp.dot(picked(blocks, pick_ref, at), block_ref[...], preferred_element_type=F32)
        out_ref[at, :] = ((base_ref[at, base_columns] + back) * inverse_ref[at, columns]).astype(BF16)
        copies.append(pltpu.make_async_copy(out_ref.at[at, :], out_hbm.at[at, columns], sems.at[t]))
        copies[-1].start()
    for copy in copies:
        copy.wait()


def finish(half, pick, base, inverse, arrays, earlier):
    rows, holes = inverse.shape
    tiles, width = 3, holes // HALVES
    block_rows = arrays[0].shape[0]
    places = list(range(len(arrays)))
    if earlier is not None and len(arrays) > 1:
        last = min(2, len(arrays) - 1)
        places.remove(last)
        base = pl.pallas_call(
            functools.partial(partial_kernel, half * width, tuple(places), tiles),
            out_shape=jax.ShapeDtypeStruct((rows, width), F32),
            in_specs=[whole()] * (2 + len(places)),
            out_specs=whole(),
            scratch_shapes=[pltpu.VMEM((block_rows * len(places), width), BF16)],
            compiler_params=params(),
            cost_estimate=CHEAP,
            name="partial",
        )(pick, base, *[arrays[k] for k in places])
        places = [last]
    operands = [pick, base, inverse] + [arrays[k] for k in places]
    in_specs = [whole()] * len(operands)
    aliases = {}
    if earlier is not None:
        aliases = {len(operands): 0}
        operands.append(earlier)
        in_specs.append(whole(pl.ANY))
    return pl.pallas_call(
        functools.partial(finish_kernel, half * width, tuple(places), tiles),
        out_shape=jax.ShapeDtypeStruct((rows, holes), BF16),
        in_specs=in_specs,
        out_specs=whole(pl.ANY),
        scratch_shapes=[
            pltpu.VMEM((block_rows * len(places), width), BF16),
            pltpu.VMEM((rows, width), BF16),
            pltpu.SemaphoreType.DMA((tiles,)),
        ],
        input_output_aliases=aliases,
        compiler_params=params(),
        cost_estimate=CHEAP,
        name="finish",
    )(*operands)


def body(amplitudes, driving, route, ladder_weight, ph_weight, recouple, gap_part, gap_hole):
    amps = amplitudes[0]
    rows, holes = amps.shape
    chan_count = lax.axis_size("chan")
    lad_count = lax.axis_size("lad")
    sub_count = lax.axis_size("sub")
    chan, lad, sub = lax.axis_index("chan"), lax.axis_index("lad"), lax.axis_index("sub")
    weight, mixing = ph_weight[0, 0], recouple[0, 0]
    capacity = weight.shape[0]
    send = capacity // chan_count
    paired = send % mixing.shape[1] == 0 and chan_count & (chan_count - 1) == 0
    if paired:
        block_rows = send
        block_index = jnp.stack([chan ^ k for k in range(chan_count)]).astype(jnp.int32)
    else:
        block_rows = capacity
        block_index = jnp.zeros((1,), jnp.int32)
    offsets = block_index * block_rows

    def exchange(block, k):
        if not paired:
            split = block.reshape(chan_count, send, -1)
            split = lax.all_to_all(split, "chan", split_axis=0, concat_axis=0, tiled=True)
            return split.reshape(capacity, -1)
        return lax.ppermute(block, "chan", [(i, i ^ k) for i in range(chan_count)]) if k else block

    far_first = list(reversed(range(block_index.shape[0])))
    count = len(far_first)
    width = holes // HALVES
    route_row = route[0].reshape(1, rows)
    plan = (paired, chan_count, send, block_rows)
    leading = 128 if paired and count > 2 and block_rows > 128 else block_rows
    soon = count > 2 and paired
    early = [(k, 0, block_rows, 0, width) for k in far_first if k > soon or not paired]
    if leading < block_rows:
        early[:1] = [(early[0][0], 0, leading, 0, width), (early[0][0], leading, block_rows - leading, 0, width)]
    late = [(1, 0, block_rows, 0, width)] if soon else []
    late += [(k, 0, block_rows, h * width, width) for h in range(1, HALVES) for k in far_first if k or not paired]
    late += [(0, 0, block_rows, 0, holes)] if paired else []
    target, *blocks = pack(plan + (early,), False, route_row, amps, "pack_first")
    arrived = {item: exchange(block, item[0]) for item, block in zip(early, blocks)}
    if paired:
        first = early[0]
        target, arrived[first] = lax.optimization_barrier((target, arrived[first]))
    blocks = pack(plan + (late,), True, target, amps, "pack_rest")
    arrived.update({item: exchange(block, item[0]) for item, block in zip(late, blocks)})

    part_column, hole_row = gap_part[0].reshape(rows, 1), gap_hole.reshape(1, holes)
    amps, blocks = lax.optimization_barrier((amps, blocks))
    pick, inverse = unpack_matrix(offsets, target.reshape(rows, 1), part_column, hole_row, capacity)

    parts, operator = prepare(ladder_weight[0], amps, weight, mixing, lad_count, sub_count)
    kept = [parts[-1]]
    for step in range(1, sub_count):
        pairs = [(i, (i + step) % sub_count) for i in range(sub_count)]
        kept.append(lax.ppermute(parts[sub_count - 1 - step], "sub", pairs))

    def chip_sum(position):
        picked = [lax.dynamic_index_in_dim(p, position, 0, keepdims=False) for p in kept]
        return sum(p.astype(F32) for p in picked)

    base = driving[0].astype(F32) + chip_sum(lad)
    terms = [chip_sum(lax.rem(lad + step, lad_count)).astype(BF16) for step in range(1, lad_count)]
    returned, crossed = [], []
    for half in range(HALVES):
        here = [item for item in early + late if item[3] == half * width or item[4] > width]
        blocks = [arrived[item] for item in here]
        if returned:
            blocks, made = lax.optimization_barrier((blocks, made))
        made = apply_cycle(half, plan, operator, [item[:2] for item in here], blocks, width)
        if not returned:
            behind, terms = lax.optimization_barrier((made[2:], terms))
            for step, term in enumerate(terms, 1):
                pairs = [(i, (i + step) % lad_count) for i in range(lad_count)]
                crossed.append(lax.ppermute(term, "lad", pairs))
        else:
            behind, crossed = lax.optimization_barrier((made[2:], crossed))
        made = [*made[:2], *behind]
        returned.append([exchange(block, k) for k, block in zip(far_first, made)])
    for term in crossed:
        base = base + term.astype(F32)
    updated = None
    for half in range(HALVES):
        updated = finish(half, pick, base, inverse, list(reversed(returned[half])), updated)
    return updated[None]


def solution(mesh):
    placed = (
        P(("parts", "chan"), ("lad", "sub"), None),
        P(("parts", "chan"), ("lad", "sub"), None),
        P("chan", ("lad", "sub"), None),
        P("chan", None, ("lad", "sub")),
        P("chan", ("lad", "sub"), None, None),
        P("chan", ("lad", "sub"), None, None, None),
        P(("parts", "chan"), ("lad", "sub")),
        P("parts"),
    )
    return jax.shard_map(
        body,
        mesh=mesh,
        in_specs=placed,
        out_specs=P(("parts", "chan"), ("lad", "sub"), None),
        check_vma=False,
    )
```

```python
import functools
import math

import jax
import jax.numpy as jnp
from jax import lax
from jax.experimental import pallas as pl
from jax.experimental.pallas import tpu as pltpu
from jax.sharding import PartitionSpec as P

VMEM_LIMIT = 28 * 1024 * 1024
HALVES = 2
F32 = jnp.float32
BF16 = jnp.bfloat16
CHEAP = pl.CostEstimate(flops=0, bytes_accessed=0, transcendentals=0)
DEAR = pl.CostEstimate(flops=3 * 10**10, bytes_accessed=10**6, transcendentals=0)


def params():
    return pltpu.CompilerParams(vmem_limit_bytes=VMEM_LIMIT)


def in_hbm(*arrays):
    return [pltpu.with_memory_space_constraint(a, pltpu.HBM) for a in arrays]


def whole(memory=pltpu.VMEM):
    return pl.BlockSpec(memory_space=memory)


def selection(match):
    return jnp.where(match, 1.0, 0.0).astype(BF16)


def block_offsets(paired, chan_count, block_rows):
    chan = lax.axis_index("chan")
    return [(chan ^ k) * block_rows for k in range(chan_count)] if paired else [0]


def slots_of(owners, send, names):
    lane = 128
    pieces = owners.shape[1] // lane
    before = selection(
        lax.broadcasted_iota(jnp.int32, (lane, 2 * lane), 0)
        < lax.broadcasted_iota(jnp.int32, (lane, 2 * lane), 1)
    )
    hot = [
        lax.broadcasted_iota(jnp.int32, (names, lane), 0) == owners[:, i * lane : (i + 1) * lane]
        for i in range(pieces)
    ]
    counts = jnp.dot(
        jnp.concatenate([selection(h) for h in hot], axis=0), before, preferred_element_type=F32
    )
    passed = jnp.zeros((names, lane), F32)
    slots = []
    for i in range(pieces):
        within = counts[i * names : (i + 1) * names]
        slots.append(jnp.sum(jnp.where(hot[i], within[:, :lane] + passed, 0.0), axis=0, keepdims=True))
        passed = passed + within[:, lane:]
    return owners * send + jnp.concatenate(slots, axis=1).astype(jnp.int32)


def pack_kernel(plan, given, route_in, amps_hbm, *refs):
    paired, chan_count, send, block_rows, items = plan
    outs, (route_ref, amps_ref, sems) = refs[:-3], refs[-3:]
    block_refs = outs if given else outs[1:]
    amps_copy = pltpu.make_async_copy(amps_hbm.at[:, pl.ds(0, amps_ref.shape[1])], amps_ref, sems.at[1])
    if given:
        amps_copy.start()
        target = route_in[...]
    else:
        route_copy = pltpu.make_async_copy(route_in, route_ref, sems.at[0])
        route_copy.start()
        amps_copy.start()
        route_copy.wait()
        target = slots_of(route_ref[...], send, max(16, chan_count))
        outs[0][...] = target
    offsets = block_offsets(paired, chan_count, block_rows)
    for i, (k, low, slots, first, width) in enumerate(items):
        slot = lax.broadcasted_iota(jnp.int32, (slots, target.shape[1]), 0)
        pick = selection(slot == target - (offsets[k] + low))
        if i == 0:
            amps_copy.wait()
        block_refs[i][...] = jnp.dot(
            pick, amps_ref[:, pl.ds(first, width)], preferred_element_type=F32
        ).astype(BF16)


def pack(plan, given, route_row, amps, name):
    rows = amps.shape[0]
    items = plan[4]
    columns = max(first + width for *_, first, width in items)
    extra = [] if given else [pltpu.VMEM((1, rows), jnp.int32)]
    return pl.pallas_call(
        functools.partial(pack_kernel, plan, given),
        out_shape=extra + [pltpu.VMEM((slots, width), BF16) for _, _, slots, _, width in items],
        in_specs=[whole() if given else whole(pl.ANY), whole(pl.ANY)],
        out_specs=[whole()] * (len(extra) + len(items)),
        scratch_shapes=[
            pltpu.VMEM((1, rows), jnp.int32),
            pltpu.VMEM((rows, columns), BF16),
            pltpu.SemaphoreType.DMA((2,)),
        ],
        compiler_params=params(),
        name=name,
    )(*([route_row] if given else in_hbm(route_row)), *in_hbm(amps))


def unpack_kernel(off_ref, target_ref, part_ref, hole_ref, out_ref, inverse_ref):
    count = off_ref.shape[0]
    rows, capacity = out_ref.shape
    block_rows = capacity // count
    target = target_ref[...]
    slots = lax.broadcasted_iota(jnp.int32, (rows, block_rows), 1)
    for k in range(count):
        out_ref[:, pl.ds(k * block_rows, block_rows)] = selection(slots == target - off_ref[k])
    inverse_ref[...] = 1.0 / (part_ref[...] + hole_ref[...])


def unpack_matrix(offsets, target_column, part_column, hole_row, capacity):
    rows, holes = part_column.shape[0], hole_row.shape[1]
    return pl.pallas_call(
        unpack_kernel,
        out_shape=[jax.ShapeDtypeStruct((rows, capacity), BF16), jax.ShapeDtypeStruct((rows, holes), F32)],
        in_specs=[whole(pltpu.SMEM), whole(), whole(), whole()],
        out_specs=[whole()] * 2,
        compiler_params=params(),
        cost_estimate=DEAR,
        name="unpack_matrix",
    )(offsets, target_column, part_column, hole_row)


def prepare_kernel(sub_count, weight_hbm, amps_hbm, cycle_hbm, mixing_hbm, *refs):
    part_refs, out_ref = refs[:sub_count], refs[sub_count]
    weight_ref, amps_ref, cycle_ref, half_ref, mixing_ref, pair_ref, sems = refs[sub_count + 1 :]
    rows, lad_count = amps_ref.shape[0], part_refs[0].shape[0]
    chunks, chunk, capacity = cycle_ref.shape
    group = mixing_ref.shape[1]
    pairs, wide = pair_ref.shape[0], pair_ref.shape[1]
    sub = lax.axis_index("sub")
    moves, ladder = [(amps_hbm, amps_ref)], []
    for n in range(sub_count):
        share = lax.rem(sub + sub_count - 1 - n, sub_count)
        for i in range(lad_count):
            start = pl.multiple_of((i * sub_count + share) * rows, rows)
            moves.append((weight_hbm.at[pl.ds(start, rows), :], weight_ref.at[len(ladder)]))
            ladder.append((n, i))
    moves.append((mixing_hbm, mixing_ref))
    moves += [(cycle_hbm.at[pl.ds(i * chunk, chunk), :], cycle_ref.at[i]) for i in range(chunks)]
    copies = [pltpu.make_async_copy(source, held, sems.at[n]) for n, (source, held) in enumerate(moves)]
    for copy in copies:
        copy.start()
    pair_ref[...] = jnp.zeros(pair_ref.shape, BF16)
    copies[0].wait()
    for m, (n, i) in enumerate(ladder):
        copies[1 + m].wait()
        part_refs[n][i] = jnp.dot(weight_ref[m], amps_ref[...], preferred_element_type=F32).astype(BF16)
    copies[1 + len(ladder)].wait()
    for q in range(capacity // group):
        at = pl.ds(q * group % wide, group)
        pair_ref[q * group // wide, at, at] = mixing_ref[q]
    for i in range(chunks):
        copies[2 + len(ladder) + i].wait()
        for a in range(chunk // group):
            at = pl.ds(a * group, group)
            half_ref[pl.ds(i * chunk + a * group, group), :] = lax.dot_general(
                mixing_ref[i * chunk // group + a],
                cycle_ref[i, at, :],
                (((0,), (0,)), ((), ())),
                preferred_element_type=F32,
            ).astype(BF16)
    for j in range(pairs):
        at = pl.ds(j * wide, wide)
        out_ref[:, at] = jnp.dot(half_ref[:, at], pair_ref[j], preferred_element_type=F32).astype(BF16)


def prepare(weight, amps, cycle_weight, mixing, lad_count, sub_count):
    rows, holes = amps.shape
    capacity = cycle_weight.shape[0]
    groups, group = mixing.shape[0], mixing.shape[1]
    wide = group * (2 if groups % 2 == 0 else 1)
    chunks = groups // 3 if groups % 3 == 0 else 1
    outs = pl.pallas_call(
        functools.partial(prepare_kernel, sub_count),
        out_shape=[jax.ShapeDtypeStruct((lad_count, rows, holes), BF16)] * sub_count
        + [jax.ShapeDtypeStruct((capacity, capacity), BF16)],
        in_specs=[whole(pl.ANY)] * 4,
        out_specs=[whole()] * (sub_count + 1),
        scratch_shapes=[
            pltpu.VMEM((lad_count * sub_count, rows, rows), BF16),
            pltpu.VMEM((rows, holes), BF16),
            pltpu.VMEM((chunks, capacity // chunks, capacity), BF16),
            pltpu.VMEM((capacity, capacity), BF16),
            pltpu.VMEM(mixing.shape, BF16),
            pltpu.VMEM((capacity // wide, wide, wide), BF16),
            pltpu.SemaphoreType.DMA((2 + lad_count * sub_count + chunks,)),
        ],
        compiler_params=params(),
        cost_estimate=DEAR,
        name="prepare",
    )(*in_hbm(weight, amps, cycle_weight, mixing))
    return outs[:sub_count], outs[sub_count]


def cycle_kernel(half, plan, places, operator_ref, *refs):
    paired, chan_count, _, block_rows = plan
    in_refs, out_refs, block_ref = refs[: len(places)], refs[len(places) : -1], refs[-1]
    width = out_refs[0].shape[1]
    offsets = block_offsets(paired, chan_count, block_rows)
    starts = [pl.multiple_of(offset, block_rows) for offset in reversed(offsets)]
    for in_ref, (k, low) in zip(in_refs, places):
        part = in_ref[...] if in_ref.shape[1] == width else in_ref[:, pl.ds(half * width, width)]
        start = pl.multiple_of(offsets[k] + low, math.gcd(low, block_rows))
        block_ref[pl.ds(start, in_ref.shape[0]), :] = part
    for out_ref, start in zip(out_refs, starts):
        out_ref[...] = jnp.dot(
            operator_ref[pl.ds(start, block_rows), :], block_ref[...], preferred_element_type=F32
        ).astype(BF16)


def apply_cycle(half, plan, operator, places, arrays, width):
    block_rows = plan[3]
    count = operator.shape[0] // block_rows
    return pl.pallas_call(
        functools.partial(cycle_kernel, half, plan, places),
        out_shape=[jax.ShapeDtypeStruct((block_rows, width), BF16)] * count,
        in_specs=[whole()] * (1 + len(arrays)),
        out_specs=[whole()] * count,
        scratch_shapes=[pltpu.VMEM((operator.shape[0], width), BF16)],
        compiler_params=params(),
        cost_estimate=DEAR,
        name="apply_cycle",
    )(operator, *arrays)


def gathered(blocks, block_ref):
    block_rows = blocks[0][1].shape[0]
    for n, (_, ref) in enumerate(blocks):
        block_ref[pl.ds(n * block_rows, block_rows), :] = ref[...]


def picked(blocks, pick_ref, rows_at):
    block_rows = blocks[0][1].shape[0]
    return jnp.concatenate([pick_ref[rows_at, pl.ds(k * block_rows, block_rows)] for k, _ in blocks], axis=1)


def partial_kernel(start_column, places, tiles, pick_ref, base_ref, *refs):
    blocks, (out_ref, block_ref) = list(zip(places, refs[:-2])), refs[-2:]
    tile, columns = out_ref.shape[0] // tiles, pl.ds(start_column, out_ref.shape[1])
    gathered(blocks, block_ref)
    for t in range(tiles):
        at = pl.ds(t * tile, tile)
        back = jnp.dot(picked(blocks, pick_ref, at), block_ref[...], preferred_element_type=F32)
        out_ref[at, :] = base_ref[at, columns] + back


def finish_kernel(start_column, places, tiles, pick_ref, base_ref, inverse_ref, *refs):
    blocks, (out_hbm, block_ref, out_ref, sems) = list(zip(places, refs)), refs[-4:]
    tile, width = out_ref.shape[0] // tiles, out_ref.shape[1]
    columns = pl.ds(start_column, width)
    base_columns = columns if base_ref.shape[1] > width else pl.ds(0, width)
    gathered(blocks, block_ref)
    copies = []
    for t in range(tiles):
        at = pl.ds(t * tile, tile)
        back = jnp.dot(picked(blocks, pick_ref, at), block_ref[...], preferred_element_type=F32)
        out_ref[at, :] = ((base_ref[at, base_columns] + back) * inverse_ref[at, columns]).astype(BF16)
        copies.append(pltpu.make_async_copy(out_ref.at[at, :], out_hbm.at[at, columns], sems.at[t]))
        copies[-1].start()
    for copy in copies:
        copy.wait()


def finish(half, pick, base, inverse, arrays, earlier):
    rows, holes = inverse.shape
    tiles, width = 3, holes // HALVES
    block_rows = arrays[0].shape[0]
    places = list(range(len(arrays)))
    if earlier is not None and len(arrays) > 1:
        last = len(arrays) - 1
        places.remove(last)
        base = pl.pallas_call(
            functools.partial(partial_kernel, half * width, tuple(places), tiles),
            out_shape=jax.ShapeDtypeStruct((rows, width), F32),
            in_specs=[whole()] * (2 + len(places)),
            out_specs=whole(),
            scratch_shapes=[pltpu.VMEM((block_rows * len(places), width), BF16)],
            compiler_params=params(),
            cost_estimate=CHEAP,
            name="partial",
        )(pick, base, *[arrays[k] for k in places])
        places = [last]
    operands = [pick, base, inverse] + [arrays[k] for k in places]
    in_specs = [whole()] * len(operands)
    aliases = {}
    if earlier is not None:
        aliases = {len(operands): 0}
        operands.append(earlier)
        in_specs.append(whole(pl.ANY))
    return pl.pallas_call(
        functools.partial(finish_kernel, half * width, tuple(places), tiles),
        out_shape=jax.ShapeDtypeStruct((rows, holes), BF16),
        in_specs=in_specs,
        out_specs=whole(pl.ANY),
        scratch_shapes=[
            pltpu.VMEM((block_rows * len(places), width), BF16),
            pltpu.VMEM((rows, width), BF16),
            pltpu.SemaphoreType.DMA((tiles,)),
        ],
        input_output_aliases=aliases,
        compiler_params=params(),
        cost_estimate=CHEAP,
        name="finish",
    )(*operands)


def body(amplitudes, driving, route, ladder_weight, ph_weight, recouple, gap_part, gap_hole):
    amps = amplitudes[0]
    rows, holes = amps.shape
    chan_count = lax.axis_size("chan")
    lad_count = lax.axis_size("lad")
    sub_count = lax.axis_size("sub")
    chan, lad, sub = lax.axis_index("chan"), lax.axis_index("lad"), lax.axis_index("sub")
    weight, mixing = ph_weight[0, 0], recouple[0, 0]
    capacity = weight.shape[0]
    send = capacity // chan_count
    paired = send % mixing.shape[1] == 0 and chan_count & (chan_count - 1) == 0
    if paired:
        block_rows = send
        block_index = jnp.stack([chan ^ k for k in range(chan_count)]).astype(jnp.int32)
    else:
        block_rows = capacity
        block_index = jnp.zeros((1,), jnp.int32)
    offsets = block_index * block_rows

    def exchange(block, k):
        if not paired:
            split = block.reshape(chan_count, send, -1)
            split = lax.all_to_all(split, "chan", split_axis=0, concat_axis=0, tiled=True)
            return split.reshape(capacity, -1)
        return lax.ppermute(block, "chan", [(i, i ^ k) for i in range(chan_count)]) if k else block

    far_first = list(reversed(range(block_index.shape[0])))
    count = len(far_first)
    width = holes // HALVES
    route_row = route[0].reshape(1, rows)
    plan = (paired, chan_count, send, block_rows)
    leading = 128 if paired and count > 2 and block_rows > 128 else block_rows
    early = [(k, 0, block_rows, 0, width) for k in far_first if k or not paired]
    if leading < block_rows:
        early[:1] = [(early[0][0], 0, leading, 0, width), (early[0][0], leading, block_rows - leading, 0, width)]
    late = [(k, 0, block_rows, h * width, width) for h in range(1, HALVES) for k in far_first if k or not paired]
    late += [(0, 0, block_rows, 0, holes)] if paired else []
    target, *blocks = pack(plan + (early,), False, route_row, amps, "pack_first")
    arrived = {item: exchange(block, item[0]) for item, block in zip(early, blocks)}
    if paired:
        first = early[0]
        target, arrived[first] = lax.optimization_barrier((target, arrived[first]))
    blocks = pack(plan + (late,), True, target, amps, "pack_rest")
    arrived.update({item: exchange(block, item[0]) for item, block in zip(late, blocks)})

    part_column, hole_row = gap_part[0].reshape(rows, 1), gap_hole.reshape(1, holes)
    amps, blocks = lax.optimization_barrier((amps, blocks))
    pick, inverse = unpack_matrix(offsets, target.reshape(rows, 1), part_column, hole_row, capacity)

    parts, operator = prepare(ladder_weight[0], amps, weight, mixing, lad_count, sub_count)
    kept = [parts[-1]]
    for step in range(1, sub_count):
        pairs = [(i, (i + step) % sub_count) for i in range(sub_count)]
        kept.append(lax.ppermute(parts[sub_count - 1 - step], "sub", pairs))

    def chip_sum(position):
        picked = [lax.dynamic_index_in_dim(p, position, 0, keepdims=False) for p in kept]
        return sum(p.astype(F32) for p in picked)

    base = driving[0].astype(F32) + chip_sum(lad)
    terms = [chip_sum(lax.rem(lad + step, lad_count)).astype(BF16) for step in range(1, lad_count)]
    returned, crossed = [], []
    for half in range(HALVES):
        here = [item for item in early + late if item[3] == half * width or item[4] > width]
        blocks = [arrived[item] for item in here]
        if returned:
            blocks, made = lax.optimization_barrier((blocks, made))
        made = apply_cycle(half, plan, operator, [item[:2] for item in here], blocks, width)
        if not returned:
            behind, terms = lax.optimization_barrier((made[2:], terms))
            for step, term in enumerate(terms, 1):
                pairs = [(i, (i + step) % lad_count) for i in range(lad_count)]
                crossed.append(lax.ppermute(term, "lad", pairs))
        else:
            behind, crossed = lax.optimization_barrier((made[2:], crossed))
        made = [*made[:2], *behind]
        returned.append([exchange(block, k) for k, block in zip(far_first, made)])
    for term in crossed:
        base = base + term.astype(F32)
    updated = None
    for half in range(HALVES):
        updated = finish(half, pick, base, inverse, list(reversed(returned[half])), updated)
    return updated[None]


def solution(mesh):
    placed = (
        P(("parts", "chan"), ("lad", "sub"), None),
        P(("parts", "chan"), ("lad", "sub"), None),
        P("chan", ("lad", "sub"), None),
        P("chan", None, ("lad", "sub")),
        P("chan", ("lad", "sub"), None, None),
        P("chan", ("lad", "sub"), None, None, None),
        P(("parts", "chan"), ("lad", "sub")),
        P("parts"),
    )
    return jax.shard_map(
        body,
        mesh=mesh,
        in_specs=placed,
        out_specs=P(("parts", "chan"), ("lad", "sub"), None),
        check_vma=False,
    )
```

```python
import functools
import math

import jax
import jax.numpy as jnp
from jax import lax
from jax.experimental import pallas as pl
from jax.experimental.pallas import tpu as pltpu
from jax.sharding import PartitionSpec as P

VMEM_LIMIT = 28 * 1024 * 1024
HALVES = 2
F32 = jnp.float32
BF16 = jnp.bfloat16
CHEAP = pl.CostEstimate(flops=0, bytes_accessed=0, transcendentals=0)
DEAR = pl.CostEstimate(flops=3 * 10**10, bytes_accessed=10**6, transcendentals=0)


def params():
    return pltpu.CompilerParams(vmem_limit_bytes=VMEM_LIMIT)


def in_hbm(*arrays):
    return [pltpu.with_memory_space_constraint(a, pltpu.HBM) for a in arrays]


def whole(memory=pltpu.VMEM):
    return pl.BlockSpec(memory_space=memory)


def selection(match):
    return jnp.where(match, 1.0, 0.0).astype(BF16)


def block_offsets(paired, chan_count, block_rows):
    chan = lax.axis_index("chan")
    return [(chan ^ k) * block_rows for k in range(chan_count)] if paired else [0]


def slots_of(owners, send, names):
    lane = 128
    pieces = owners.shape[1] // lane
    before = selection(
        lax.broadcasted_iota(jnp.int32, (lane, 2 * lane), 0)
        < lax.broadcasted_iota(jnp.int32, (lane, 2 * lane), 1)
    )
    hot = [
        lax.broadcasted_iota(jnp.int32, (names, lane), 0) == owners[:, i * lane : (i + 1) * lane]
        for i in range(pieces)
    ]
    counts = jnp.dot(
        jnp.concatenate([selection(h) for h in hot], axis=0), before, preferred_element_type=F32
    )
    passed = jnp.zeros((names, lane), F32)
    slots = []
    for i in range(pieces):
        within = counts[i * names : (i + 1) * names]
        slots.append(jnp.sum(jnp.where(hot[i], within[:, :lane] + passed, 0.0), axis=0, keepdims=True))
        passed = passed + within[:, lane:]
    return owners * send + jnp.concatenate(slots, axis=1).astype(jnp.int32)


def pack_kernel(plan, given, route_in, amps_hbm, *refs):
    paired, chan_count, send, block_rows, items = plan
    outs, (route_ref, amps_ref, sems) = refs[:-3], refs[-3:]
    block_refs = outs if given else outs[1:]
    amps_copy = pltpu.make_async_copy(amps_hbm.at[:, pl.ds(0, amps_ref.shape[1])], amps_ref, sems.at[1])
    if given:
        amps_copy.start()
        target = route_in[...]
    else:
        route_copy = pltpu.make_async_copy(route_in, route_ref, sems.at[0])
        route_copy.start()
        amps_copy.start()
        route_copy.wait()
        target = slots_of(route_ref[...], send, max(16, chan_count))
        outs[0][...] = target
    offsets = block_offsets(paired, chan_count, block_rows)
    for i, (k, low, slots, first, width) in enumerate(items):
        slot = lax.broadcasted_iota(jnp.int32, (slots, target.shape[1]), 0)
        pick = selection(slot == target - (offsets[k] + low))
        if i == 0:
            amps_copy.wait()
        block_refs[i][...] = jnp.dot(
            pick, amps_ref[:, pl.ds(first, width)], preferred_element_type=F32
        ).astype(BF16)


def pack(plan, given, route_row, amps, name):
    rows = amps.shape[0]
    items = plan[4]
    columns = max(first + width for *_, first, width in items)
    extra = [] if given else [pltpu.VMEM((1, rows), jnp.int32)]
    return pl.pallas_call(
        functools.partial(pack_kernel, plan, given),
        out_shape=extra + [pltpu.VMEM((slots, width), BF16) for _, _, slots, _, width in items],
        in_specs=[whole() if given else whole(pl.ANY), whole(pl.ANY)],
        out_specs=[whole()] * (len(extra) + len(items)),
        scratch_shapes=[
            pltpu.VMEM((1, rows), jnp.int32),
            pltpu.VMEM((rows, columns), BF16),
            pltpu.SemaphoreType.DMA((2,)),
        ],
        compiler_params=params(),
        name=name,
    )(*([route_row] if given else in_hbm(route_row)), *in_hbm(amps))


def unpack_kernel(off_ref, target_ref, part_ref, hole_ref, out_ref, inverse_ref):
    count = off_ref.shape[0]
    rows, capacity = out_ref.shape
    block_rows = capacity // count
    target = target_ref[...]
    slots = lax.broadcasted_iota(jnp.int32, (rows, block_rows), 1)
    for k in range(count):
        out_ref[:, pl.ds(k * block_rows, block_rows)] = selection(slots == target - off_ref[k])
    inverse_ref[...] = 1.0 / (part_ref[...] + hole_ref[...])


def unpack_matrix(offsets, target_column, part_column, hole_row, capacity):
    rows, holes = part_column.shape[0], hole_row.shape[1]
    return pl.pallas_call(
        unpack_kernel,
        out_shape=[jax.ShapeDtypeStruct((rows, capacity), BF16), jax.ShapeDtypeStruct((rows, holes), F32)],
        in_specs=[whole(pltpu.SMEM), whole(), whole(), whole()],
        out_specs=[whole()] * 2,
        compiler_params=params(),
        cost_estimate=DEAR,
        name="unpack_matrix",
    )(offsets, target_column, part_column, hole_row)


def prepare_kernel(sub_count, weight_hbm, amps_hbm, cycle_hbm, mixing_hbm, *refs):
    part_refs, out_ref = refs[:sub_count], refs[sub_count]
    weight_ref, amps_ref, cycle_ref, half_ref, mixing_ref, pair_ref, sems = refs[sub_count + 1 :]
    rows, lad_count = amps_ref.shape[0], part_refs[0].shape[0]
    chunks, chunk, capacity = cycle_ref.shape
    group = mixing_ref.shape[1]
    pairs, wide = pair_ref.shape[0], pair_ref.shape[1]
    sub = lax.axis_index("sub")
    moves, ladder = [(amps_hbm, amps_ref)], []
    for n in range(sub_count):
        share = lax.rem(sub + sub_count - 1 - n, sub_count)
        for i in range(lad_count):
            start = pl.multiple_of((i * sub_count + share) * rows, rows)
            moves.append((weight_hbm.at[pl.ds(start, rows), :], weight_ref.at[len(ladder)]))
            ladder.append((n, i))
    moves.append((mixing_hbm, mixing_ref))
    moves += [(cycle_hbm.at[pl.ds(i * chunk, chunk), :], cycle_ref.at[i]) for i in range(chunks)]
    copies = [pltpu.make_async_copy(source, held, sems.at[n]) for n, (source, held) in enumerate(moves)]
    for copy in copies:
        copy.start()
    pair_ref[...] = jnp.zeros(pair_ref.shape, BF16)
    copies[0].wait()
    for m, (n, i) in enumerate(ladder):
        copies[1 + m].wait()
        part_refs[n][i] = jnp.dot(weight_ref[m], amps_ref[...], preferred_element_type=F32).astype(BF16)
    copies[1 + len(ladder)].wait()
    for q in range(capacity // group):
        at = pl.ds(q * group % wide, group)
        pair_ref[q * group // wide, at, at] = mixing_ref[q]
    for i in range(chunks):
        copies[2 + len(ladder) + i].wait()
        for a in range(chunk // group):
            at = pl.ds(a * group, group)
            half_ref[pl.ds(i * chunk + a * group, group), :] = lax.dot_general(
                mixing_ref[i * chunk // group + a],
                cycle_ref[i, at, :],
                (((0,), (0,)), ((), ())),
                preferred_element_type=F32,
            ).astype(BF16)
    for j in range(pairs):
        at = pl.ds(j * wide, wide)
        out_ref[:, at] = jnp.dot(half_ref[:, at], pair_ref[j], preferred_element_type=F32).astype(BF16)


def prepare(weight, amps, cycle_weight, mixing, lad_count, sub_count):
    rows, holes = amps.shape
    capacity = cycle_weight.shape[0]
    groups, group = mixing.shape[0], mixing.shape[1]
    wide = group * (2 if groups % 2 == 0 else 1)
    chunks = groups // 3 if groups % 3 == 0 else 1
    outs = pl.pallas_call(
        functools.partial(prepare_kernel, sub_count),
        out_shape=[jax.ShapeDtypeStruct((lad_count, rows, holes), BF16)] * sub_count
        + [jax.ShapeDtypeStruct((capacity, capacity), BF16)],
        in_specs=[whole(pl.ANY)] * 4,
        out_specs=[whole()] * (sub_count + 1),
        scratch_shapes=[
            pltpu.VMEM((lad_count * sub_count, rows, rows), BF16),
            pltpu.VMEM((rows, holes), BF16),
            pltpu.VMEM((chunks, capacity // chunks, capacity), BF16),
            pltpu.VMEM((capacity, capacity), BF16),
            pltpu.VMEM(mixing.shape, BF16),
            pltpu.VMEM((capacity // wide, wide, wide), BF16),
            pltpu.SemaphoreType.DMA((2 + lad_count * sub_count + chunks,)),
        ],
        compiler_params=params(),
        cost_estimate=DEAR,
        name="prepare",
    )(*in_hbm(weight, amps, cycle_weight, mixing))
    return outs[:sub_count], outs[sub_count]


def cycle_kernel(half, plan, places, operator_ref, *refs):
    paired, chan_count, _, block_rows = plan
    in_refs, out_refs, block_ref = refs[: len(places)], refs[len(places) : -1], refs[-1]
    width = out_refs[0].shape[1]
    offsets = block_offsets(paired, chan_count, block_rows)
    starts = [pl.multiple_of(offset, block_rows) for offset in reversed(offsets)]
    for in_ref, (k, low) in zip(in_refs, places):
        part = in_ref[...] if in_ref.shape[1] == width else in_ref[:, pl.ds(half * width, width)]
        start = pl.multiple_of(offsets[k] + low, math.gcd(low, block_rows))
        block_ref[pl.ds(start, in_ref.shape[0]), :] = part
    for out_ref, start in zip(out_refs, starts):
        out_ref[...] = jnp.dot(
            operator_ref[pl.ds(start, block_rows), :], block_ref[...], preferred_element_type=F32
        ).astype(BF16)


def apply_cycle(half, plan, operator, places, arrays, width):
    block_rows = plan[3]
    count = operator.shape[0] // block_rows
    return pl.pallas_call(
        functools.partial(cycle_kernel, half, plan, places),
        out_shape=[jax.ShapeDtypeStruct((block_rows, width), BF16)] * count,
        in_specs=[whole()] * (1 + len(arrays)),
        out_specs=[whole()] * count,
        scratch_shapes=[pltpu.VMEM((operator.shape[0], width), BF16)],
        compiler_params=params(),
        cost_estimate=DEAR,
        name="apply_cycle",
    )(operator, *arrays)


def gathered(blocks, block_ref):
    block_rows = blocks[0][1].shape[0]
    for n, (_, ref) in enumerate(blocks):
        block_ref[pl.ds(n * block_rows, block_rows), :] = ref[...]


def picked(blocks, pick_ref, rows_at):
    block_rows = blocks[0][1].shape[0]
    return jnp.concatenate([pick_ref[rows_at, pl.ds(k * block_rows, block_rows)] for k, _ in blocks], axis=1)


def partial_kernel(start_column, places, tiles, pick_ref, base_ref, *refs):
    blocks, (out_ref, block_ref) = list(zip(places, refs[:-2])), refs[-2:]
    tile, columns = out_ref.shape[0] // tiles, pl.ds(start_column, out_ref.shape[1])
    gathered(blocks, block_ref)
    for t in range(tiles):
        at = pl.ds(t * tile, tile)
        back = jnp.dot(picked(blocks, pick_ref, at), block_ref[...], preferred_element_type=F32)
        out_ref[at, :] = base_ref[at, columns] + back


def finish_kernel(start_column, places, tiles, pick_ref, base_ref, inverse_ref, *refs):
    blocks, (out_hbm, block_ref, out_ref, sems) = list(zip(places, refs)), refs[-4:]
    tile, width = out_ref.shape[0] // tiles, out_ref.shape[1]
    columns = pl.ds(start_column, width)
    base_columns = columns if base_ref.shape[1] > width else pl.ds(0, width)
    gathered(blocks, block_ref)
    copies = []
    for t in range(tiles):
        at = pl.ds(t * tile, tile)
        back = jnp.dot(picked(blocks, pick_ref, at), block_ref[...], preferred_element_type=F32)
        out_ref[at, :] = ((base_ref[at, base_columns] + back) * inverse_ref[at, columns]).astype(BF16)
        copies.append(pltpu.make_async_copy(out_ref.at[at, :], out_hbm.at[at, columns], sems.at[t]))
        copies[-1].start()
    for copy in copies:
        copy.wait()


def finish(half, pick, base, inverse, arrays, earlier):
    rows, holes = inverse.shape
    tiles, width = 3, holes // HALVES
    block_rows = arrays[0].shape[0]
    places = list(range(len(arrays)))
    if earlier is not None and len(arrays) > 1:
        last = 1
        places.remove(last)
        base = pl.pallas_call(
            functools.partial(partial_kernel, half * width, tuple(places), tiles),
            out_shape=jax.ShapeDtypeStruct((rows, width), F32),
            in_specs=[whole()] * (2 + len(places)),
            out_specs=whole(),
            scratch_shapes=[pltpu.VMEM((block_rows * len(places), width), BF16)],
            compiler_params=params(),
            cost_estimate=CHEAP,
            name="partial",
        )(pick, base, *[arrays[k] for k in places])
        places = [last]
    operands = [pick, base, inverse] + [arrays[k] for k in places]
    in_specs = [whole()] * len(operands)
    aliases = {}
    if earlier is not None:
        aliases = {len(operands): 0}
        operands.append(earlier)
        in_specs.append(whole(pl.ANY))
    return pl.pallas_call(
        functools.partial(finish_kernel, half * width, tuple(places), tiles),
        out_shape=jax.ShapeDtypeStruct((rows, holes), BF16),
        in_specs=in_specs,
        out_specs=whole(pl.ANY),
        scratch_shapes=[
            pltpu.VMEM((block_rows * len(places), width), BF16),
            pltpu.VMEM((rows, width), BF16),
            pltpu.SemaphoreType.DMA((tiles,)),
        ],
        input_output_aliases=aliases,
        compiler_params=params(),
        cost_estimate=CHEAP,
        name="finish",
    )(*operands)


def body(amplitudes, driving, route, ladder_weight, ph_weight, recouple, gap_part, gap_hole):
    amps = amplitudes[0]
    rows, holes = amps.shape
    chan_count = lax.axis_size("chan")
    lad_count = lax.axis_size("lad")
    sub_count = lax.axis_size("sub")
    chan, lad, sub = lax.axis_index("chan"), lax.axis_index("lad"), lax.axis_index("sub")
    weight, mixing = ph_weight[0, 0], recouple[0, 0]
    capacity = weight.shape[0]
    send = capacity // chan_count
    paired = send % mixing.shape[1] == 0 and chan_count & (chan_count - 1) == 0
    if paired:
        block_rows = send
        block_index = jnp.stack([chan ^ k for k in range(chan_count)]).astype(jnp.int32)
    else:
        block_rows = capacity
        block_index = jnp.zeros((1,), jnp.int32)
    offsets = block_index * block_rows

    def exchange(block, k):
        if not paired:
            split = block.reshape(chan_count, send, -1)
            split = lax.all_to_all(split, "chan", split_axis=0, concat_axis=0, tiled=True)
            return split.reshape(capacity, -1)
        return lax.ppermute(block, "chan", [(i, i ^ k) for i in range(chan_count)]) if k else block

    far_first = list(reversed(range(block_index.shape[0])))
    count = len(far_first)
    width = holes // HALVES
    route_row = route[0].reshape(1, rows)
    plan = (paired, chan_count, send, block_rows)
    leading = 128 if paired and count > 2 and block_rows > 128 else block_rows
    early = [(k, 0, block_rows, 0, width) for k in far_first if k or not paired]
    if leading < block_rows:
        early[:1] = [(early[0][0], 0, leading, 0, width), (early[0][0], leading, block_rows - leading, 0, width)]
    late = [(k, 0, block_rows, h * width, width) for h in range(1, HALVES) for k in far_first if k or not paired]
    late += [(0, 0, block_rows, 0, holes)] if paired else []
    target, *blocks = pack(plan + (early,), False, route_row, amps, "pack_first")
    arrived = {item: exchange(block, item[0]) for item, block in zip(early, blocks)}
    if paired:
        first = early[0]
        target, arrived[first] = lax.optimization_barrier((target, arrived[first]))
    blocks = pack(plan + (late,), True, target, amps, "pack_rest")
    arrived.update({item: exchange(block, item[0]) for item, block in zip(late, blocks)})

    part_column, hole_row = gap_part[0].reshape(rows, 1), gap_hole.reshape(1, holes)
    amps, blocks = lax.optimization_barrier((amps, blocks))
    pick, inverse = unpack_matrix(offsets, target.reshape(rows, 1), part_column, hole_row, capacity)

    parts, operator = prepare(ladder_weight[0], amps, weight, mixing, lad_count, sub_count)
    kept = [parts[-1]]
    for step in range(1, sub_count):
        pairs = [(i, (i + step) % sub_count) for i in range(sub_count)]
        kept.append(lax.ppermute(parts[sub_count - 1 - step], "sub", pairs))

    def chip_sum(position):
        picked = [lax.dynamic_index_in_dim(p, position, 0, keepdims=False) for p in kept]
        return sum(p.astype(F32) for p in picked)

    base = driving[0].astype(F32) + chip_sum(lad)
    terms = [chip_sum(lax.rem(lad + step, lad_count)).astype(BF16) for step in range(1, lad_count)]
    returned, crossed = [], []
    for half in range(HALVES):
        here = [item for item in early + late if item[3] == half * width or item[4] > width]
        blocks = [arrived[item] for item in here]
        if returned:
            blocks, made = lax.optimization_barrier((blocks, made))
        made = apply_cycle(half, plan, operator, [item[:2] for item in here], blocks, width)
        if not returned:
            behind, terms = lax.optimization_barrier((made[2:], terms))
            made = [*made[:2], *behind]
            for step, term in enumerate(terms, 1):
                pairs = [(i, (i + step) % lad_count) for i in range(lad_count)]
                crossed.append(lax.ppermute(term, "lad", pairs))
        else:
            behind, crossed = lax.optimization_barrier((made[0], crossed))
            made = [behind, *made[1:]]
        returned.append([exchange(block, k) for k, block in zip(far_first, made)])
    for term in crossed:
        base = base + term.astype(F32)
    updated = None
    for half in range(HALVES):
        updated = finish(half, pick, base, inverse, list(reversed(returned[half])), updated)
    return updated[None]


def solution(mesh):
    placed = (
        P(("parts", "chan"), ("lad", "sub"), None),
        P(("parts", "chan"), ("lad", "sub"), None),
        P("chan", ("lad", "sub"), None),
        P("chan", None, ("lad", "sub")),
        P("chan", ("lad", "sub"), None, None),
        P("chan", ("lad", "sub"), None, None, None),
        P(("parts", "chan"), ("lad", "sub")),
        P("parts"),
    )
    return jax.shard_map(
        body,
        mesh=mesh,
        in_specs=placed,
        out_specs=P(("parts", "chan"), ("lad", "sub"), None),
        check_vma=False,
    )
```

```python
import functools
import math

import jax
import jax.numpy as jnp
from jax import lax
from jax.experimental import pallas as pl
from jax.experimental.pallas import tpu as pltpu
from jax.sharding import PartitionSpec as P

VMEM_LIMIT = 28 * 1024 * 1024
HALVES = 2
F32 = jnp.float32
BF16 = jnp.bfloat16
CHEAP = pl.CostEstimate(flops=0, bytes_accessed=0, transcendentals=0)
DEAR = pl.CostEstimate(flops=3 * 10**10, bytes_accessed=10**6, transcendentals=0)


def params():
    return pltpu.CompilerParams(vmem_limit_bytes=VMEM_LIMIT)


def in_hbm(*arrays):
    return [pltpu.with_memory_space_constraint(a, pltpu.HBM) for a in arrays]


def whole(memory=pltpu.VMEM):
    return pl.BlockSpec(memory_space=memory)


def selection(match):
    return jnp.where(match, 1.0, 0.0).astype(BF16)


def block_offsets(paired, chan_count, block_rows):
    chan = lax.axis_index("chan")
    return [(chan ^ k) * block_rows for k in range(chan_count)] if paired else [0]


def slots_of(owners, send, names):
    lane = 128
    pieces = owners.shape[1] // lane
    before = selection(
        lax.broadcasted_iota(jnp.int32, (lane, 2 * lane), 0)
        < lax.broadcasted_iota(jnp.int32, (lane, 2 * lane), 1)
    )
    hot = [
        lax.broadcasted_iota(jnp.int32, (names, lane), 0) == owners[:, i * lane : (i + 1) * lane]
        for i in range(pieces)
    ]
    counts = jnp.dot(
        jnp.concatenate([selection(h) for h in hot], axis=0), before, preferred_element_type=F32
    )
    passed = jnp.zeros((names, lane), F32)
    slots = []
    for i in range(pieces):
        within = counts[i * names : (i + 1) * names]
        slots.append(jnp.sum(jnp.where(hot[i], within[:, :lane] + passed, 0.0), axis=0, keepdims=True))
        passed = passed + within[:, lane:]
    return owners * send + jnp.concatenate(slots, axis=1).astype(jnp.int32)


def pack_kernel(plan, given, route_in, amps_hbm, *refs):
    paired, chan_count, send, block_rows, items = plan
    outs, (route_ref, amps_ref, sems) = refs[:-3], refs[-3:]
    block_refs = outs if given else outs[1:]
    amps_copy = pltpu.make_async_copy(amps_hbm.at[:, pl.ds(0, amps_ref.shape[1])], amps_ref, sems.at[1])
    if given:
        amps_copy.start()
        target = route_in[...]
    else:
        route_copy = pltpu.make_async_copy(route_in, route_ref, sems.at[0])
        route_copy.start()
        amps_copy.start()
        route_copy.wait()
        target = slots_of(route_ref[...], send, max(16, chan_count))
        outs[0][...] = target
    offsets = block_offsets(paired, chan_count, block_rows)
    for i, (k, low, slots, first, width) in enumerate(items):
        slot = lax.broadcasted_iota(jnp.int32, (slots, target.shape[1]), 0)
        pick = selection(slot == target - (offsets[k] + low))
        if i == 0:
            amps_copy.wait()
        block_refs[i][...] = jnp.dot(
            pick, amps_ref[:, pl.ds(first, width)], preferred_element_type=F32
        ).astype(BF16)


def pack(plan, given, route_row, amps, name):
    rows = amps.shape[0]
    items = plan[4]
    columns = max(first + width for *_, first, width in items)
    extra = [] if given else [pltpu.VMEM((1, rows), jnp.int32)]
    return pl.pallas_call(
        functools.partial(pack_kernel, plan, given),
        out_shape=extra + [pltpu.VMEM((slots, width), BF16) for _, _, slots, _, width in items],
        in_specs=[whole() if given else whole(pl.ANY), whole(pl.ANY)],
        out_specs=[whole()] * (len(extra) + len(items)),
        scratch_shapes=[
            pltpu.VMEM((1, rows), jnp.int32),
            pltpu.VMEM((rows, columns), BF16),
            pltpu.SemaphoreType.DMA((2,)),
        ],
        compiler_params=params(),
        name=name,
    )(*([route_row] if given else in_hbm(route_row)), *in_hbm(amps))


def unpack_kernel(off_ref, target_ref, part_ref, hole_ref, out_ref, inverse_ref):
    count = off_ref.shape[0]
    rows, capacity = out_ref.shape
    block_rows = capacity // count
    target = target_ref[...]
    slots = lax.broadcasted_iota(jnp.int32, (rows, block_rows), 1)
    for k in range(count):
        out_ref[:, pl.ds(k * block_rows, block_rows)] = selection(slots == target - off_ref[k])
    inverse_ref[...] = 1.0 / (part_ref[...] + hole_ref[...])


def unpack_matrix(offsets, target_column, part_column, hole_row, capacity):
    rows, holes = part_column.shape[0], hole_row.shape[1]
    return pl.pallas_call(
        unpack_kernel,
        out_shape=[jax.ShapeDtypeStruct((rows, capacity), BF16), jax.ShapeDtypeStruct((rows, holes), F32)],
        in_specs=[whole(pltpu.SMEM), whole(), whole(), whole()],
        out_specs=[whole()] * 2,
        compiler_params=params(),
        cost_estimate=DEAR,
        name="unpack_matrix",
    )(offsets, target_column, part_column, hole_row)


def prepare_kernel(sub_count, weight_hbm, amps_hbm, cycle_hbm, mixing_hbm, *refs):
    part_refs, out_ref = refs[:sub_count], refs[sub_count]
    weight_ref, amps_ref, cycle_ref, half_ref, mixing_ref, pair_ref, sems = refs[sub_count + 1 :]
    rows, lad_count = amps_ref.shape[0], part_refs[0].shape[0]
    chunks, chunk, capacity = cycle_ref.shape
    group = mixing_ref.shape[1]
    pairs, wide = pair_ref.shape[0], pair_ref.shape[1]
    sub = lax.axis_index("sub")
    moves, ladder = [(amps_hbm, amps_ref)], []
    for n in range(sub_count):
        share = lax.rem(sub + sub_count - 1 - n, sub_count)
        for i in range(lad_count):
            start = pl.multiple_of((i * sub_count + share) * rows, rows)
            moves.append((weight_hbm.at[pl.ds(start, rows), :], weight_ref.at[len(ladder)]))
            ladder.append((n, i))
    moves.append((mixing_hbm, mixing_ref))
    moves += [(cycle_hbm.at[pl.ds(i * chunk, chunk), :], cycle_ref.at[i]) for i in range(chunks)]
    copies = [pltpu.make_async_copy(source, held, sems.at[n]) for n, (source, held) in enumerate(moves)]
    for copy in copies:
        copy.start()
    pair_ref[...] = jnp.zeros(pair_ref.shape, BF16)
    copies[0].wait()
    for m, (n, i) in enumerate(ladder):
        copies[1 + m].wait()
        part_refs[n][i] = jnp.dot(weight_ref[m], amps_ref[...], preferred_element_type=F32).astype(BF16)
    copies[1 + len(ladder)].wait()
    for q in range(capacity // group):
        at = pl.ds(q * group % wide, group)
        pair_ref[q * group // wide, at, at] = mixing_ref[q]
    for i in range(chunks):
        copies[2 + len(ladder) + i].wait()
        for a in range(chunk // group):
            at = pl.ds(a * group, group)
            half_ref[pl.ds(i * chunk + a * group, group), :] = lax.dot_general(
                mixing_ref[i * chunk // group + a],
                cycle_ref[i, at, :],
                (((0,), (0,)), ((), ())),
                preferred_element_type=F32,
            ).astype(BF16)
    for j in range(pairs):
        at = pl.ds(j * wide, wide)
        out_ref[:, at] = jnp.dot(half_ref[:, at], pair_ref[j], preferred_element_type=F32).astype(BF16)


def prepare(weight, amps, cycle_weight, mixing, lad_count, sub_count):
    rows, holes = amps.shape
    capacity = cycle_weight.shape[0]
    groups, group = mixing.shape[0], mixing.shape[1]
    wide = group * (2 if groups % 2 == 0 else 1)
    chunks = groups // 3 if groups % 3 == 0 else 1
    outs = pl.pallas_call(
        functools.partial(prepare_kernel, sub_count),
        out_shape=[jax.ShapeDtypeStruct((lad_count, rows, holes), BF16)] * sub_count
        + [jax.ShapeDtypeStruct((capacity, capacity), BF16)],
        in_specs=[whole(pl.ANY)] * 4,
        out_specs=[whole()] * (sub_count + 1),
        scratch_shapes=[
            pltpu.VMEM((lad_count * sub_count, rows, rows), BF16),
            pltpu.VMEM((rows, holes), BF16),
            pltpu.VMEM((chunks, capacity // chunks, capacity), BF16),
            pltpu.VMEM((capacity, capacity), BF16),
            pltpu.VMEM(mixing.shape, BF16),
            pltpu.VMEM((capacity // wide, wide, wide), BF16),
            pltpu.SemaphoreType.DMA((2 + lad_count * sub_count + chunks,)),
        ],
        compiler_params=params(),
        cost_estimate=DEAR,
        name="prepare",
    )(*in_hbm(weight, amps, cycle_weight, mixing))
    return outs[:sub_count], outs[sub_count]


def cycle_kernel(half, plan, places, operator_ref, *refs):
    paired, chan_count, _, block_rows = plan
    in_refs, out_refs, block_ref = refs[: len(places)], refs[len(places) : -1], refs[-1]
    width = out_refs[0].shape[1]
    offsets = block_offsets(paired, chan_count, block_rows)
    starts = [pl.multiple_of(offset, block_rows) for offset in reversed(offsets)]
    for in_ref, (k, low) in zip(in_refs, places):
        part = in_ref[...] if in_ref.shape[1] == width else in_ref[:, pl.ds(half * width, width)]
        start = pl.multiple_of(offsets[k] + low, math.gcd(low, block_rows))
        block_ref[pl.ds(start, in_ref.shape[0]), :] = part
    for out_ref, start in zip(out_refs, starts):
        out_ref[...] = jnp.dot(
            operator_ref[pl.ds(start, block_rows), :], block_ref[...], preferred_element_type=F32
        ).astype(BF16)


def apply_cycle(half, plan, operator, places, arrays, width):
    block_rows = plan[3]
    count = operator.shape[0] // block_rows
    return pl.pallas_call(
        functools.partial(cycle_kernel, half, plan, places),
        out_shape=[jax.ShapeDtypeStruct((block_rows, width), BF16)] * count,
        in_specs=[whole()] * (1 + len(arrays)),
        out_specs=[whole()] * count,
        scratch_shapes=[pltpu.VMEM((operator.shape[0], width), BF16)],
        compiler_params=params(),
        cost_estimate=DEAR,
        name="apply_cycle",
    )(operator, *arrays)


def gathered(blocks, block_ref):
    block_rows = blocks[0][1].shape[0]
    for n, (_, ref) in enumerate(blocks):
        block_ref[pl.ds(n * block_rows, block_rows), :] = ref[...]


def picked(blocks, pick_ref, rows_at):
    block_rows = blocks[0][1].shape[0]
    return jnp.concatenate([pick_ref[rows_at, pl.ds(k * block_rows, block_rows)] for k, _ in blocks], axis=1)


def partial_kernel(start_column, places, tiles, pick_ref, base_ref, *refs):
    blocks, (out_ref, block_ref) = list(zip(places, refs[:-2])), refs[-2:]
    tile, columns = out_ref.shape[0] // tiles, pl.ds(start_column, out_ref.shape[1])
    gathered(blocks, block_ref)
    for t in range(tiles):
        at = pl.ds(t * tile, tile)
        back = jnp.dot(picked(blocks, pick_ref, at), block_ref[...], preferred_element_type=F32)
        out_ref[at, :] = base_ref[at, columns] + back


def finish_kernel(start_column, places, tiles, pick_ref, base_ref, inverse_ref, *refs):
    blocks, (out_hbm, block_ref, out_ref, sems) = list(zip(places, refs)), refs[-4:]
    tile, width = out_ref.shape[0] // tiles, out_ref.shape[1]
    columns = pl.ds(start_column, width)
    base_columns = columns if base_ref.shape[1] > width else pl.ds(0, width)
    gathered(blocks, block_ref)
    copies = []
    for t in range(tiles):
        at = pl.ds(t * tile, tile)
        back = jnp.dot(picked(blocks, pick_ref, at), block_ref[...], preferred_element_type=F32)
        out_ref[at, :] = ((base_ref[at, base_columns] + back) * inverse_ref[at, columns]).astype(BF16)
        copies.append(pltpu.make_async_copy(out_ref.at[at, :], out_hbm.at[at, columns], sems.at[t]))
        copies[-1].start()
    for copy in copies:
        copy.wait()


def finish(half, pick, base, inverse, arrays, earlier):
    rows, holes = inverse.shape
    tiles, width = 3, holes // HALVES
    block_rows = arrays[0].shape[0]
    places = list(range(len(arrays)))
    if earlier is not None and len(arrays) > 1:
        last = 1
        places.remove(last)
        base = pl.pallas_call(
            functools.partial(partial_kernel, half * width, tuple(places), tiles),
            out_shape=jax.ShapeDtypeStruct((rows, width), F32),
            in_specs=[whole()] * (2 + len(places)),
            out_specs=whole(),
            scratch_shapes=[pltpu.VMEM((block_rows * len(places), width), BF16)],
            compiler_params=params(),
            cost_estimate=CHEAP,
            name="partial",
        )(pick, base, *[arrays[k] for k in places])
        places = [last]
    operands = [pick, base, inverse] + [arrays[k] for k in places]
    in_specs = [whole()] * len(operands)
    aliases = {}
    if earlier is not None:
        aliases = {len(operands): 0}
        operands.append(earlier)
        in_specs.append(whole(pl.ANY))
    return pl.pallas_call(
        functools.partial(finish_kernel, half * width, tuple(places), tiles),
        out_shape=jax.ShapeDtypeStruct((rows, holes), BF16),
        in_specs=in_specs,
        out_specs=whole(pl.ANY),
        scratch_shapes=[
            pltpu.VMEM((block_rows * len(places), width), BF16),
            pltpu.VMEM((rows, width), BF16),
            pltpu.SemaphoreType.DMA((tiles,)),
        ],
        input_output_aliases=aliases,
        compiler_params=params(),
        cost_estimate=CHEAP,
        name="finish",
    )(*operands)


def body(amplitudes, driving, route, ladder_weight, ph_weight, recouple, gap_part, gap_hole):
    amps = amplitudes[0]
    rows, holes = amps.shape
    chan_count = lax.axis_size("chan")
    lad_count = lax.axis_size("lad")
    sub_count = lax.axis_size("sub")
    chan, lad, sub = lax.axis_index("chan"), lax.axis_index("lad"), lax.axis_index("sub")
    weight, mixing = ph_weight[0, 0], recouple[0, 0]
    capacity = weight.shape[0]
    send = capacity // chan_count
    paired = send % mixing.shape[1] == 0 and chan_count & (chan_count - 1) == 0
    if paired:
        block_rows = send
        block_index = jnp.stack([chan ^ k for k in range(chan_count)]).astype(jnp.int32)
    else:
        block_rows = capacity
        block_index = jnp.zeros((1,), jnp.int32)
    offsets = block_index * block_rows

    def exchange(block, k):
        if not paired:
            split = block.reshape(chan_count, send, -1)
            split = lax.all_to_all(split, "chan", split_axis=0, concat_axis=0, tiled=True)
            return split.reshape(capacity, -1)
        return lax.ppermute(block, "chan", [(i, i ^ k) for i in range(chan_count)]) if k else block

    far_first = list(reversed(range(block_index.shape[0])))
    count = len(far_first)
    width = holes // HALVES
    route_row = route[0].reshape(1, rows)
    plan = (paired, chan_count, send, block_rows)
    leading = 256 if paired and count > 2 and block_rows > 256 else block_rows
    soon = count > 2 and paired
    early = [(k, 0, block_rows, 0, width) for k in far_first if k > soon or not paired]
    if leading < block_rows:
        early[:1] = [(early[0][0], 0, leading, 0, width), (early[0][0], leading, block_rows - leading, 0, width)]
    late = [(1, 0, block_rows, 0, width)] if soon else []
    late += [(k, 0, block_rows, h * width, width) for h in range(1, HALVES) for k in far_first if k or not paired]
    late += [(0, 0, block_rows, 0, holes)] if paired else []
    target, *blocks = pack(plan + (early,), False, route_row, amps, "pack_first")
    arrived = {item: exchange(block, item[0]) for item, block in zip(early, blocks)}
    if paired:
        first = early[0]
        target, arrived[first] = lax.optimization_barrier((target, arrived[first]))
    blocks = pack(plan + (late,), True, target, amps, "pack_rest")
    arrived.update({item: exchange(block, item[0]) for item, block in zip(late, blocks)})

    part_column, hole_row = gap_part[0].reshape(rows, 1), gap_hole.reshape(1, holes)
    amps, blocks = lax.optimization_barrier((amps, blocks))
    pick, inverse = unpack_matrix(offsets, target.reshape(rows, 1), part_column, hole_row, capacity)

    parts, operator = prepare(ladder_weight[0], amps, weight, mixing, lad_count, sub_count)
    kept = [parts[-1]]
    for step in range(1, sub_count):
        pairs = [(i, (i + step) % sub_count) for i in range(sub_count)]
        kept.append(lax.ppermute(parts[sub_count - 1 - step], "sub", pairs))

    def chip_sum(position):
        picked = [lax.dynamic_index_in_dim(p, position, 0, keepdims=False) for p in kept]
        return sum(p.astype(F32) for p in picked)

    base = driving[0].astype(F32) + chip_sum(lad)
    terms = [chip_sum(lax.rem(lad + step, lad_count)).astype(BF16) for step in range(1, lad_count)]
    returned, crossed = [], []
    for half in range(HALVES):
        here = [item for item in early + late if item[3] == half * width or item[4] > width]
        blocks = [arrived[item] for item in here]
        if returned:
            blocks, made = lax.optimization_barrier((blocks, made))
        made = apply_cycle(half, plan, operator, [item[:2] for item in here], blocks, width)
        if not returned:
            behind, terms = lax.optimization_barrier((made[2:], terms))
            made = [*made[:2], *behind]
            for step, term in enumerate(terms, 1):
                pairs = [(i, (i + step) % lad_count) for i in range(lad_count)]
                crossed.append(lax.ppermute(term, "lad", pairs))
        else:
            behind, crossed = lax.optimization_barrier((made[0], crossed))
            made = [behind, *made[1:]]
        returned.append([exchange(block, k) for k, block in zip(far_first, made)])
    for term in crossed:
        base = base + term.astype(F32)
    updated = None
    for half in range(HALVES):
        updated = finish(half, pick, base, inverse, list(reversed(returned[half])), updated)
    return updated[None]


def solution(mesh):
    placed = (
        P(("parts", "chan"), ("lad", "sub"), None),
        P(("parts", "chan"), ("lad", "sub"), None),
        P("chan", ("lad", "sub"), None),
        P("chan", None, ("lad", "sub")),
        P("chan", ("lad", "sub"), None, None),
        P("chan", ("lad", "sub"), None, None, None),
        P(("parts", "chan"), ("lad", "sub")),
        P("parts"),
    )
    return jax.shard_map(
        body,
        mesh=mesh,
        in_specs=placed,
        out_specs=P(("parts", "chan"), ("lad", "sub"), None),
        check_vma=False,
    )
```

```python
import functools
import math

import jax
import jax.numpy as jnp
from jax import lax
from jax.experimental import pallas as pl
from jax.experimental.pallas import tpu as pltpu
from jax.sharding import PartitionSpec as P

VMEM_LIMIT = 28 * 1024 * 1024
HALVES = 2
F32 = jnp.float32
BF16 = jnp.bfloat16
CHEAP = pl.CostEstimate(flops=0, bytes_accessed=0, transcendentals=0)
DEAR = pl.CostEstimate(flops=3 * 10**10, bytes_accessed=10**6, transcendentals=0)


def params():
    return pltpu.CompilerParams(vmem_limit_bytes=VMEM_LIMIT)


def in_hbm(*arrays):
    return [pltpu.with_memory_space_constraint(a, pltpu.HBM) for a in arrays]


def whole(memory=pltpu.VMEM):
    return pl.BlockSpec(memory_space=memory)


def selection(match):
    return jnp.where(match, 1.0, 0.0).astype(BF16)


def block_offsets(paired, chan_count, block_rows):
    chan = lax.axis_index("chan")
    return [(chan ^ k) * block_rows for k in range(chan_count)] if paired else [0]


def slots_of(owners, send, names):
    lane = 128
    pieces = owners.shape[1] // lane
    before = selection(
        lax.broadcasted_iota(jnp.int32, (lane, 2 * lane), 0)
        < lax.broadcasted_iota(jnp.int32, (lane, 2 * lane), 1)
    )
    hot = [
        lax.broadcasted_iota(jnp.int32, (names, lane), 0) == owners[:, i * lane : (i + 1) * lane]
        for i in range(pieces)
    ]
    counts = jnp.dot(
        jnp.concatenate([selection(h) for h in hot], axis=0), before, preferred_element_type=F32
    )
    passed = jnp.zeros((names, lane), F32)
    slots = []
    for i in range(pieces):
        within = counts[i * names : (i + 1) * names]
        slots.append(jnp.sum(jnp.where(hot[i], within[:, :lane] + passed, 0.0), axis=0, keepdims=True))
        passed = passed + within[:, lane:]
    return owners * send + jnp.concatenate(slots, axis=1).astype(jnp.int32)


def pack_kernel(plan, given, route_in, amps_hbm, *refs):
    paired, chan_count, send, block_rows, items = plan
    outs, (route_ref, amps_ref, sems) = refs[:-3], refs[-3:]
    block_refs = outs if given else outs[1:]
    amps_copy = pltpu.make_async_copy(amps_hbm.at[:, pl.ds(0, amps_ref.shape[1])], amps_ref, sems.at[1])
    if given:
        amps_copy.start()
        target = route_in[...]
    else:
        route_copy = pltpu.make_async_copy(route_in, route_ref, sems.at[0])
        route_copy.start()
        amps_copy.start()
        route_copy.wait()
        target = slots_of(route_ref[...], send, max(16, chan_count))
        outs[0][...] = target
    offsets = block_offsets(paired, chan_count, block_rows)
    for i, (k, low, slots, first, width) in enumerate(items):
        slot = lax.broadcasted_iota(jnp.int32, (slots, target.shape[1]), 0)
        pick = selection(slot == target - (offsets[k] + low))
        if i == 0:
            amps_copy.wait()
        block_refs[i][...] = jnp.dot(
            pick, amps_ref[:, pl.ds(first, width)], preferred_element_type=F32
        ).astype(BF16)


def pack(plan, given, route_row, amps, name):
    rows = amps.shape[0]
    items = plan[4]
    columns = max(first + width for *_, first, width in items)
    extra = [] if given else [pltpu.VMEM((1, rows), jnp.int32)]
    return pl.pallas_call(
        functools.partial(pack_kernel, plan, given),
        out_shape=extra + [pltpu.VMEM((slots, width), BF16) for _, _, slots, _, width in items],
        in_specs=[whole() if given else whole(pl.ANY), whole(pl.ANY)],
        out_specs=[whole()] * (len(extra) + len(items)),
        scratch_shapes=[
            pltpu.VMEM((1, rows), jnp.int32),
            pltpu.VMEM((rows, columns), BF16),
            pltpu.SemaphoreType.DMA((2,)),
        ],
        compiler_params=params(),
        name=name,
    )(*([route_row] if given else in_hbm(route_row)), *in_hbm(amps))


def unpack_kernel(off_ref, target_ref, part_ref, hole_ref, out_ref, inverse_ref):
    count = off_ref.shape[0]
    rows, capacity = out_ref.shape
    block_rows = capacity // count
    target = target_ref[...]
    slots = lax.broadcasted_iota(jnp.int32, (rows, block_rows), 1)
    for k in range(count):
        out_ref[:, pl.ds(k * block_rows, block_rows)] = selection(slots == target - off_ref[k])
    inverse_ref[...] = 1.0 / (part_ref[...] + hole_ref[...])


def unpack_matrix(offsets, target_column, part_column, hole_row, capacity):
    rows, holes = part_column.shape[0], hole_row.shape[1]
    return pl.pallas_call(
        unpack_kernel,
        out_shape=[jax.ShapeDtypeStruct((rows, capacity), BF16), jax.ShapeDtypeStruct((rows, holes), F32)],
        in_specs=[whole(pltpu.SMEM), whole(), whole(), whole()],
        out_specs=[whole()] * 2,
        compiler_params=params(),
        cost_estimate=DEAR,
        name="unpack_matrix",
    )(offsets, target_column, part_column, hole_row)


def prepare_kernel(sub_count, weight_hbm, amps_hbm, cycle_hbm, mixing_hbm, *refs):
    part_refs, out_ref = refs[:sub_count], refs[sub_count]
    weight_ref, amps_ref, cycle_ref, half_ref, mixing_ref, pair_ref, sems = refs[sub_count + 1 :]
    rows, lad_count = amps_ref.shape[0], part_refs[0].shape[0]
    chunks, chunk, capacity = cycle_ref.shape
    group = mixing_ref.shape[1]
    pairs, wide = pair_ref.shape[0], pair_ref.shape[1]
    sub = lax.axis_index("sub")
    moves, ladder = [(amps_hbm, amps_ref)], []
    for n in range(sub_count):
        share = lax.rem(sub + sub_count - 1 - n, sub_count)
        for i in range(lad_count):
            start = pl.multiple_of((i * sub_count + share) * rows, rows)
            moves.append((weight_hbm.at[pl.ds(start, rows), :], weight_ref.at[len(ladder)]))
            ladder.append((n, i))
    moves.append((mixing_hbm, mixing_ref))
    moves += [(cycle_hbm.at[pl.ds(i * chunk, chunk), :], cycle_ref.at[i]) for i in range(chunks)]
    copies = [pltpu.make_async_copy(source, held, sems.at[n]) for n, (source, held) in enumerate(moves)]
    for copy in copies:
        copy.start()
    pair_ref[...] = jnp.zeros(pair_ref.shape, BF16)
    copies[0].wait()
    for m, (n, i) in enumerate(ladder):
        copies[1 + m].wait()
        part_refs[n][i] = jnp.dot(weight_ref[m], amps_ref[...], preferred_element_type=F32).astype(BF16)
    copies[1 + len(ladder)].wait()
    for q in range(capacity // group):
        at = pl.ds(q * group % wide, group)
        pair_ref[q * group // wide, at, at] = mixing_ref[q]
    for i in range(chunks):
        copies[2 + len(ladder) + i].wait()
        for a in range(chunk // group):
            at = pl.ds(a * group, group)
            half_ref[pl.ds(i * chunk + a * group, group), :] = lax.dot_general(
                mixing_ref[i * chunk // group + a],
                cycle_ref[i, at, :],
                (((0,), (0,)), ((), ())),
                preferred_element_type=F32,
            ).astype(BF16)
    for j in range(pairs):
        at = pl.ds(j * wide, wide)
        out_ref[:, at] = jnp.dot(half_ref[:, at], pair_ref[j], preferred_element_type=F32).astype(BF16)


def prepare(weight, amps, cycle_weight, mixing, lad_count, sub_count):
    rows, holes = amps.shape
    capacity = cycle_weight.shape[0]
    groups, group = mixing.shape[0], mixing.shape[1]
    wide = group * (2 if groups % 2 == 0 else 1)
    chunks = groups // 3 if groups % 3 == 0 else 1
    outs = pl.pallas_call(
        functools.partial(prepare_kernel, sub_count),
        out_shape=[jax.ShapeDtypeStruct((lad_count, rows, holes), BF16)] * sub_count
        + [jax.ShapeDtypeStruct((capacity, capacity), BF16)],
        in_specs=[whole(pl.ANY)] * 4,
        out_specs=[whole()] * (sub_count + 1),
        scratch_shapes=[
            pltpu.VMEM((lad_count * sub_count, rows, rows), BF16),
            pltpu.VMEM((rows, holes), BF16),
            pltpu.VMEM((chunks, capacity // chunks, capacity), BF16),
            pltpu.VMEM((capacity, capacity), BF16),
            pltpu.VMEM(mixing.shape, BF16),
            pltpu.VMEM((capacity // wide, wide, wide), BF16),
            pltpu.SemaphoreType.DMA((2 + lad_count * sub_count + chunks,)),
        ],
        compiler_params=params(),
        cost_estimate=DEAR,
        name="prepare",
    )(*in_hbm(weight, amps, cycle_weight, mixing))
    return outs[:sub_count], outs[sub_count]


def cycle_kernel(half, plan, places, operator_ref, *refs):
    paired, chan_count, _, block_rows = plan
    in_refs, out_refs, block_ref = refs[: len(places)], refs[len(places) : -1], refs[-1]
    width = out_refs[0].shape[1]
    offsets = block_offsets(paired, chan_count, block_rows)
    starts = [pl.multiple_of(offset, block_rows) for offset in reversed(offsets)]
    for in_ref, (k, low) in zip(in_refs, places):
        part = in_ref[...] if in_ref.shape[1] == width else in_ref[:, pl.ds(half * width, width)]
        start = pl.multiple_of(offsets[k] + low, math.gcd(low, block_rows))
        block_ref[pl.ds(start, in_ref.shape[0]), :] = part
    for out_ref, start in zip(out_refs, starts):
        out_ref[...] = jnp.dot(
            operator_ref[pl.ds(start, block_rows), :], block_ref[...], preferred_element_type=F32
        ).astype(BF16)


def apply_cycle(half, plan, operator, places, arrays, width):
    block_rows = plan[3]
    count = operator.shape[0] // block_rows
    return pl.pallas_call(
        functools.partial(cycle_kernel, half, plan, places),
        out_shape=[jax.ShapeDtypeStruct((block_rows, width), BF16)] * count,
        in_specs=[whole()] * (1 + len(arrays)),
        out_specs=[whole()] * count,
        scratch_shapes=[pltpu.VMEM((operator.shape[0], width), BF16)],
        compiler_params=params(),
        cost_estimate=DEAR,
        name="apply_cycle",
    )(operator, *arrays)


def gathered(blocks, block_ref):
    block_rows = blocks[0][1].shape[0]
    for n, (_, ref) in enumerate(blocks):
        block_ref[pl.ds(n * block_rows, block_rows), :] = ref[...]


def picked(blocks, pick_ref, rows_at):
    block_rows = blocks[0][1].shape[0]
    return jnp.concatenate([pick_ref[rows_at, pl.ds(k * block_rows, block_rows)] for k, _ in blocks], axis=1)


def partial_kernel(start_column, places, tiles, pick_ref, base_ref, *refs):
    blocks, (out_ref, block_ref) = list(zip(places, refs[:-2])), refs[-2:]
    tile, columns = out_ref.shape[0] // tiles, pl.ds(start_column, out_ref.shape[1])
    gathered(blocks, block_ref)
    for t in range(tiles):
        at = pl.ds(t * tile, tile)
        back = jnp.dot(picked(blocks, pick_ref, at), block_ref[...], preferred_element_type=F32)
        out_ref[at, :] = base_ref[at, columns] + back


def finish_kernel(start_column, places, tiles, pick_ref, base_ref, inverse_ref, *refs):
    blocks, (out_hbm, block_ref, out_ref, sems) = list(zip(places, refs)), refs[-4:]
    tile, width = out_ref.shape[0] // tiles, out_ref.shape[1]
    columns = pl.ds(start_column, width)
    base_columns = columns if base_ref.shape[1] > width else pl.ds(0, width)
    gathered(blocks, block_ref)
    copies = []
    for t in range(tiles):
        at = pl.ds(t * tile, tile)
        back = jnp.dot(picked(blocks, pick_ref, at), block_ref[...], preferred_element_type=F32)
        out_ref[at, :] = ((base_ref[at, base_columns] + back) * inverse_ref[at, columns]).astype(BF16)
        copies.append(pltpu.make_async_copy(out_ref.at[at, :], out_hbm.at[at, columns], sems.at[t]))
        copies[-1].start()
    for copy in copies:
        copy.wait()


def finish(half, pick, base, inverse, arrays, earlier):
    rows, holes = inverse.shape
    tiles, width = 3, holes // HALVES
    block_rows = arrays[0].shape[0]
    places = list(range(len(arrays)))
    if earlier is not None and len(arrays) > 1:
        last = 1
        places.remove(last)
        base = pl.pallas_call(
            functools.partial(partial_kernel, half * width, tuple(places), tiles),
            out_shape=jax.ShapeDtypeStruct((rows, width), F32),
            in_specs=[whole()] * (2 + len(places)),
            out_specs=whole(),
            scratch_shapes=[pltpu.VMEM((block_rows * len(places), width), BF16)],
            compiler_params=params(),
            cost_estimate=CHEAP,
            name="partial",
        )(pick, base, *[arrays[k] for k in places])
        places = [last]
    operands = [pick, base, inverse] + [arrays[k] for k in places]
    in_specs = [whole()] * len(operands)
    aliases = {}
    if earlier is not None:
        aliases = {len(operands): 0}
        operands.append(earlier)
        in_specs.append(whole(pl.ANY))
    return pl.pallas_call(
        functools.partial(finish_kernel, half * width, tuple(places), tiles),
        out_shape=jax.ShapeDtypeStruct((rows, holes), BF16),
        in_specs=in_specs,
        out_specs=whole(pl.ANY),
        scratch_shapes=[
            pltpu.VMEM((block_rows * len(places), width), BF16),
            pltpu.VMEM((rows, width), BF16),
            pltpu.SemaphoreType.DMA((tiles,)),
        ],
        input_output_aliases=aliases,
        compiler_params=params(),
        cost_estimate=CHEAP,
        name="finish",
    )(*operands)


def body(amplitudes, driving, route, ladder_weight, ph_weight, recouple, gap_part, gap_hole):
    amps = amplitudes[0]
    rows, holes = amps.shape
    chan_count = lax.axis_size("chan")
    lad_count = lax.axis_size("lad")
    sub_count = lax.axis_size("sub")
    chan, lad, sub = lax.axis_index("chan"), lax.axis_index("lad"), lax.axis_index("sub")
    weight, mixing = ph_weight[0, 0], recouple[0, 0]
    capacity = weight.shape[0]
    send = capacity // chan_count
    paired = send % mixing.shape[1] == 0 and chan_count & (chan_count - 1) == 0
    if paired:
        block_rows = send
        block_index = jnp.stack([chan ^ k for k in range(chan_count)]).astype(jnp.int32)
    else:
        block_rows = capacity
        block_index = jnp.zeros((1,), jnp.int32)
    offsets = block_index * block_rows

    def exchange(block, k):
        if not paired:
            split = block.reshape(chan_count, send, -1)
            split = lax.all_to_all(split, "chan", split_axis=0, concat_axis=0, tiled=True)
            return split.reshape(capacity, -1)
        return lax.ppermute(block, "chan", [(i, i ^ k) for i in range(chan_count)]) if k else block

    far_first = list(reversed(range(block_index.shape[0])))
    count = len(far_first)
    width = holes // HALVES
    route_row = route[0].reshape(1, rows)
    plan = (paired, chan_count, send, block_rows)
    leading = 128 if paired and count > 2 and block_rows > 128 else block_rows
    soon = count > 2 and paired
    early = [(k, 0, block_rows, 0, width) for k in far_first if k > soon or not paired]
    if leading < block_rows:
        early[:1] = [(early[0][0], 0, leading, 0, width), (early[0][0], leading, block_rows - leading, 0, width)]
    late = [(1, 0, block_rows, 0, width)] if soon else []
    late += [(k, 0, block_rows, h * width, width) for h in range(1, HALVES) for k in far_first if k or not paired]
    late += [(0, 0, block_rows, 0, holes)] if paired else []
    target, *blocks = pack(plan + (early,), False, route_row, amps, "pack_first")
    arrived = {item: exchange(block, item[0]) for item, block in zip(early, blocks)}
    if paired:
        first = early[0]
        target, arrived[first] = lax.optimization_barrier((target, arrived[first]))
    blocks = pack(plan + (late,), True, target, amps, "pack_rest")
    arrived.update({item: exchange(block, item[0]) for item, block in zip(late, blocks)})

    part_column, hole_row = gap_part[0].reshape(rows, 1), gap_hole.reshape(1, holes)
    amps, blocks = lax.optimization_barrier((amps, blocks))
    pick, inverse = unpack_matrix(offsets, target.reshape(rows, 1), part_column, hole_row, capacity)

    parts, operator = prepare(ladder_weight[0], amps, weight, mixing, lad_count, sub_count)
    kept = [parts[-1]]
    for step in range(1, sub_count):
        pairs = [(i, (i + step) % sub_count) for i in range(sub_count)]
        kept.append(lax.ppermute(parts[sub_count - 1 - step], "sub", pairs))

    def chip_sum(position):
        picked = [lax.dynamic_index_in_dim(p, position, 0, keepdims=False) for p in kept]
        return sum(p.astype(F32) for p in picked)

    base = driving[0].astype(F32) + chip_sum(lad)
    terms = [chip_sum(lax.rem(lad + step, lad_count)).astype(BF16) for step in range(1, lad_count)]
    returned, crossed = [], []
    for half in range(HALVES):
        here = [item for item in early + late if item[3] == half * width or item[4] > width]
        blocks = [arrived[item] for item in here]
        if returned:
            blocks, made = lax.optimization_barrier((blocks, made))
        made = apply_cycle(half, plan, operator, [item[:2] for item in here], blocks, width)
        if not returned:
            behind, terms = lax.optimization_barrier((made[2:], terms))
            made = [*made[:2], *behind]
            for step, term in enumerate(terms, 1):
                pairs = [(i, (i + step) % lad_count) for i in range(lad_count)]
                crossed.append(lax.ppermute(term, "lad", pairs))
        else:
            behind, crossed = lax.optimization_barrier((made[0], crossed))
            made = [behind, *made[1:]]
        returned.append([exchange(block, k) for k, block in zip(far_first, made)])
    for term in crossed:
        base = base + term.astype(F32)
    updated = None
    for half in range(HALVES):
        updated = finish(half, pick, base, inverse, list(reversed(returned[half])), updated)
    return updated[None]


def solution(mesh):
    placed = (
        P(("parts", "chan"), ("lad", "sub"), None),
        P(("parts", "chan"), ("lad", "sub"), None),
        P("chan", ("lad", "sub"), None),
        P("chan", None, ("lad", "sub")),
        P("chan", ("lad", "sub"), None, None),
        P("chan", ("lad", "sub"), None, None, None),
        P(("parts", "chan"), ("lad", "sub")),
        P("parts"),
    )
    return jax.shard_map(
        body,
        mesh=mesh,
        in_specs=placed,
        out_specs=P(("parts", "chan"), ("lad", "sub"), None),
        check_vma=False,
    )
```

```python
import functools
import math

import jax
import jax.numpy as jnp
from jax import lax
from jax.experimental import pallas as pl
from jax.experimental.pallas import tpu as pltpu
from jax.sharding import PartitionSpec as P

VMEM_LIMIT = 28 * 1024 * 1024
HALVES = 2
F32 = jnp.float32
BF16 = jnp.bfloat16
CHEAP = pl.CostEstimate(flops=0, bytes_accessed=0, transcendentals=0)
DEAR = pl.CostEstimate(flops=3 * 10**10, bytes_accessed=10**6, transcendentals=0)


def params():
    return pltpu.CompilerParams(vmem_limit_bytes=VMEM_LIMIT)


def in_hbm(*arrays):
    return [pltpu.with_memory_space_constraint(a, pltpu.HBM) for a in arrays]


def whole(memory=pltpu.VMEM):
    return pl.BlockSpec(memory_space=memory)


def selection(match):
    return jnp.where(match, 1.0, 0.0).astype(BF16)


def block_offsets(paired, chan_count, block_rows):
    chan = lax.axis_index("chan")
    return [(chan ^ k) * block_rows for k in range(chan_count)] if paired else [0]


def slots_of(owners, send, names):
    lane = 128
    pieces = owners.shape[1] // lane
    before = selection(
        lax.broadcasted_iota(jnp.int32, (lane, 2 * lane), 0)
        < lax.broadcasted_iota(jnp.int32, (lane, 2 * lane), 1)
    )
    hot = [
        lax.broadcasted_iota(jnp.int32, (names, lane), 0) == owners[:, i * lane : (i + 1) * lane]
        for i in range(pieces)
    ]
    counts = jnp.dot(
        jnp.concatenate([selection(h) for h in hot], axis=0), before, preferred_element_type=F32
    )
    passed = jnp.zeros((names, lane), F32)
    slots = []
    for i in range(pieces):
        within = counts[i * names : (i + 1) * names]
        slots.append(jnp.sum(jnp.where(hot[i], within[:, :lane] + passed, 0.0), axis=0, keepdims=True))
        passed = passed + within[:, lane:]
    return owners * send + jnp.concatenate(slots, axis=1).astype(jnp.int32)


def pack_kernel(plan, given, route_in, amps_hbm, *refs):
    paired, chan_count, send, block_rows, items = plan
    outs, (route_ref, amps_ref, sems) = refs[:-3], refs[-3:]
    block_refs = outs if given else outs[1:]
    amps_copy = pltpu.make_async_copy(amps_hbm.at[:, pl.ds(0, amps_ref.shape[1])], amps_ref, sems.at[1])
    if given:
        amps_copy.start()
        target = route_in[...]
    else:
        route_copy = pltpu.make_async_copy(route_in, route_ref, sems.at[0])
        route_copy.start()
        amps_copy.start()
        route_copy.wait()
        target = slots_of(route_ref[...], send, max(16, chan_count))
        outs[0][...] = target
    offsets = block_offsets(paired, chan_count, block_rows)
    for i, (k, low, slots, first, width) in enumerate(items):
        slot = lax.broadcasted_iota(jnp.int32, (slots, target.shape[1]), 0)
        pick = selection(slot == target - (offsets[k] + low))
        if i == 0:
            amps_copy.wait()
        block_refs[i][...] = jnp.dot(
            pick, amps_ref[:, pl.ds(first, width)], preferred_element_type=F32
        ).astype(BF16)


def pack(plan, given, route_row, amps, name):
    rows = amps.shape[0]
    items = plan[4]
    columns = max(first + width for *_, first, width in items)
    extra = [] if given else [pltpu.VMEM((1, rows), jnp.int32)]
    return pl.pallas_call(
        functools.partial(pack_kernel, plan, given),
        out_shape=extra + [pltpu.VMEM((slots, width), BF16) for _, _, slots, _, width in items],
        in_specs=[whole() if given else whole(pl.ANY), whole(pl.ANY)],
        out_specs=[whole()] * (len(extra) + len(items)),
        scratch_shapes=[
            pltpu.VMEM((1, rows), jnp.int32),
            pltpu.VMEM((rows, columns), BF16),
            pltpu.SemaphoreType.DMA((2,)),
        ],
        compiler_params=params(),
        name=name,
    )(*([route_row] if given else in_hbm(route_row)), *in_hbm(amps))


def unpack_kernel(off_ref, target_ref, part_ref, hole_ref, out_ref, inverse_ref):
    count = off_ref.shape[0]
    rows, capacity = out_ref.shape
    block_rows = capacity // count
    target = target_ref[...]
    slots = lax.broadcasted_iota(jnp.int32, (rows, block_rows), 1)
    for k in range(count):
        out_ref[:, pl.ds(k * block_rows, block_rows)] = selection(slots == target - off_ref[k])
    inverse_ref[...] = 1.0 / (part_ref[...] + hole_ref[...])


def unpack_matrix(offsets, target_column, part_column, hole_row, capacity):
    rows, holes = part_column.shape[0], hole_row.shape[1]
    return pl.pallas_call(
        unpack_kernel,
        out_shape=[jax.ShapeDtypeStruct((rows, capacity), BF16), jax.ShapeDtypeStruct((rows, holes), F32)],
        in_specs=[whole(pltpu.SMEM), whole(), whole(), whole()],
        out_specs=[whole()] * 2,
        compiler_params=params(),
        cost_estimate=DEAR,
        name="unpack_matrix",
    )(offsets, target_column, part_column, hole_row)


def prepare_kernel(sub_count, weight_hbm, amps_hbm, cycle_hbm, mixing_hbm, *refs):
    part_refs, out_ref = refs[:sub_count], refs[sub_count]
    weight_ref, amps_ref, cycle_ref, half_ref, mixing_ref, pair_ref, sems = refs[sub_count + 1 :]
    rows, lad_count = amps_ref.shape[0], part_refs[0].shape[0]
    chunks, chunk, capacity = cycle_ref.shape
    group = mixing_ref.shape[1]
    pairs, wide = pair_ref.shape[0], pair_ref.shape[1]
    sub = lax.axis_index("sub")
    moves, ladder = [(amps_hbm, amps_ref)], []
    for n in range(sub_count):
        share = lax.rem(sub + sub_count - 1 - n, sub_count)
        for i in range(lad_count):
            start = pl.multiple_of((i * sub_count + share) * rows, rows)
            moves.append((weight_hbm.at[pl.ds(start, rows), :], weight_ref.at[len(ladder)]))
            ladder.append((n, i))
    moves.append((mixing_hbm, mixing_ref))
    moves += [(cycle_hbm.at[pl.ds(i * chunk, chunk), :], cycle_ref.at[i]) for i in range(chunks)]
    copies = [pltpu.make_async_copy(source, held, sems.at[n]) for n, (source, held) in enumerate(moves)]
    for copy in copies:
        copy.start()
    pair_ref[...] = jnp.zeros(pair_ref.shape, BF16)
    copies[0].wait()
    for m, (n, i) in enumerate(ladder):
        copies[1 + m].wait()
        part_refs[n][i] = jnp.dot(weight_ref[m], amps_ref[...], preferred_element_type=F32).astype(BF16)
    copies[1 + len(ladder)].wait()
    for q in range(capacity // group):
        at = pl.ds(q * group % wide, group)
        pair_ref[q * group // wide, at, at] = mixing_ref[q]
    for i in range(chunks):
        copies[2 + len(ladder) + i].wait()
        for a in range(chunk // group):
            at = pl.ds(a * group, group)
            half_ref[pl.ds(i * chunk + a * group, group), :] = lax.dot_general(
                mixing_ref[i * chunk // group + a],
                cycle_ref[i, at, :],
                (((0,), (0,)), ((), ())),
                preferred_element_type=F32,
            ).astype(BF16)
    for j in range(pairs):
        at = pl.ds(j * wide, wide)
        out_ref[:, at] = jnp.dot(half_ref[:, at], pair_ref[j], preferred_element_type=F32).astype(BF16)


def prepare(weight, amps, cycle_weight, mixing, lad_count, sub_count):
    rows, holes = amps.shape
    capacity = cycle_weight.shape[0]
    groups, group = mixing.shape[0], mixing.shape[1]
    wide = group * (2 if groups % 2 == 0 else 1)
    chunks = groups // 3 if groups % 3 == 0 else 1
    outs = pl.pallas_call(
        functools.partial(prepare_kernel, sub_count),
        out_shape=[jax.ShapeDtypeStruct((lad_count, rows, holes), BF16)] * sub_count
        + [jax.ShapeDtypeStruct((capacity, capacity), BF16)],
        in_specs=[whole(pl.ANY)] * 4,
        out_specs=[whole()] * (sub_count + 1),
        scratch_shapes=[
            pltpu.VMEM((lad_count * sub_count, rows, rows), BF16),
            pltpu.VMEM((rows, holes), BF16),
            pltpu.VMEM((chunks, capacity // chunks, capacity), BF16),
            pltpu.VMEM((capacity, capacity), BF16),
            pltpu.VMEM(mixing.shape, BF16),
            pltpu.VMEM((capacity // wide, wide, wide), BF16),
            pltpu.SemaphoreType.DMA((2 + lad_count * sub_count + chunks,)),
        ],
        compiler_params=params(),
        cost_estimate=DEAR,
        name="prepare",
    )(*in_hbm(weight, amps, cycle_weight, mixing))
    return outs[:sub_count], outs[sub_count]


def cycle_kernel(half, plan, places, operator_ref, *refs):
    paired, chan_count, _, block_rows = plan
    in_refs, out_refs, block_ref = refs[: len(places)], refs[len(places) : -1], refs[-1]
    width = out_refs[0].shape[1]
    offsets = block_offsets(paired, chan_count, block_rows)
    starts = [pl.multiple_of(offset, block_rows) for offset in reversed(offsets)]
    for in_ref, (k, low) in zip(in_refs, places):
        part = in_ref[...] if in_ref.shape[1] == width else in_ref[:, pl.ds(half * width, width)]
        start = pl.multiple_of(offsets[k] + low, math.gcd(low, block_rows))
        block_ref[pl.ds(start, in_ref.shape[0]), :] = part
    for out_ref, start in zip(out_refs, starts):
        out_ref[...] = jnp.dot(
            operator_ref[pl.ds(start, block_rows), :], block_ref[...], preferred_element_type=F32
        ).astype(BF16)


def apply_cycle(half, plan, operator, places, arrays, width):
    block_rows = plan[3]
    count = operator.shape[0] // block_rows
    return pl.pallas_call(
        functools.partial(cycle_kernel, half, plan, places),
        out_shape=[jax.ShapeDtypeStruct((block_rows, width), BF16)] * count,
        in_specs=[whole()] * (1 + len(arrays)),
        out_specs=[whole()] * count,
        scratch_shapes=[pltpu.VMEM((operator.shape[0], width), BF16)],
        compiler_params=params(),
        cost_estimate=DEAR,
        name="apply_cycle",
    )(operator, *arrays)


def gathered(blocks, block_ref):
    block_rows = blocks[0][1].shape[0]
    for n, (_, ref) in enumerate(blocks):
        block_ref[pl.ds(n * block_rows, block_rows), :] = ref[...]


def picked(blocks, pick_ref, rows_at):
    block_rows = blocks[0][1].shape[0]
    return jnp.concatenate([pick_ref[rows_at, pl.ds(k * block_rows, block_rows)] for k, _ in blocks], axis=1)


def partial_kernel(start_column, places, tiles, pick_ref, base_ref, *refs):
    blocks, (out_ref, block_ref) = list(zip(places, refs[:-2])), refs[-2:]
    tile, columns = out_ref.shape[0] // tiles, pl.ds(start_column, out_ref.shape[1])
    gathered(blocks, block_ref)
    for t in range(tiles):
        at = pl.ds(t * tile, tile)
        back = jnp.dot(picked(blocks, pick_ref, at), block_ref[...], preferred_element_type=F32)
        out_ref[at, :] = base_ref[at, columns] + back


def finish_kernel(start_column, places, tiles, pick_ref, base_ref, inverse_ref, *refs):
    blocks, (out_hbm, block_ref, out_ref, sems) = list(zip(places, refs)), refs[-4:]
    tile, width = out_ref.shape[0] // tiles, out_ref.shape[1]
    columns = pl.ds(start_column, width)
    base_columns = columns if base_ref.shape[1] > width else pl.ds(0, width)
    gathered(blocks, block_ref)
    copies = []
    for t in range(tiles):
        at = pl.ds(t * tile, tile)
        back = jnp.dot(picked(blocks, pick_ref, at), block_ref[...], preferred_element_type=F32)
        out_ref[at, :] = ((base_ref[at, base_columns] + back) * inverse_ref[at, columns]).astype(BF16)
        copies.append(pltpu.make_async_copy(out_ref.at[at, :], out_hbm.at[at, columns], sems.at[t]))
        copies[-1].start()
    for copy in copies:
        copy.wait()


def finish(half, pick, base, inverse, arrays, earlier):
    rows, holes = inverse.shape
    tiles, width = 2, holes // HALVES
    block_rows = arrays[0].shape[0]
    places = list(range(len(arrays)))
    if earlier is not None and len(arrays) > 1:
        last = 1
        places.remove(last)
        base = pl.pallas_call(
            functools.partial(partial_kernel, half * width, tuple(places), tiles),
            out_shape=jax.ShapeDtypeStruct((rows, width), F32),
            in_specs=[whole()] * (2 + len(places)),
            out_specs=whole(),
            scratch_shapes=[pltpu.VMEM((block_rows * len(places), width), BF16)],
            compiler_params=params(),
            cost_estimate=CHEAP,
            name="partial",
        )(pick, base, *[arrays[k] for k in places])
        places = [last]
    operands = [pick, base, inverse] + [arrays[k] for k in places]
    in_specs = [whole()] * len(operands)
    aliases = {}
    if earlier is not None:
        aliases = {len(operands): 0}
        operands.append(earlier)
        in_specs.append(whole(pl.ANY))
    return pl.pallas_call(
        functools.partial(finish_kernel, half * width, tuple(places), tiles),
        out_shape=jax.ShapeDtypeStruct((rows, holes), BF16),
        in_specs=in_specs,
        out_specs=whole(pl.ANY),
        scratch_shapes=[
            pltpu.VMEM((block_rows * len(places), width), BF16),
            pltpu.VMEM((rows, width), BF16),
            pltpu.SemaphoreType.DMA((tiles,)),
        ],
        input_output_aliases=aliases,
        compiler_params=params(),
        cost_estimate=CHEAP,
        name="finish",
    )(*operands)


def body(amplitudes, driving, route, ladder_weight, ph_weight, recouple, gap_part, gap_hole):
    amps = amplitudes[0]
    rows, holes = amps.shape
    chan_count = lax.axis_size("chan")
    lad_count = lax.axis_size("lad")
    sub_count = lax.axis_size("sub")
    chan, lad, sub = lax.axis_index("chan"), lax.axis_index("lad"), lax.axis_index("sub")
    weight, mixing = ph_weight[0, 0], recouple[0, 0]
    capacity = weight.shape[0]
    send = capacity // chan_count
    paired = send % mixing.shape[1] == 0 and chan_count & (chan_count - 1) == 0
    if paired:
        block_rows = send
        block_index = jnp.stack([chan ^ k for k in range(chan_count)]).astype(jnp.int32)
    else:
        block_rows = capacity
        block_index = jnp.zeros((1,), jnp.int32)
    offsets = block_index * block_rows

    def exchange(block, k):
        if not paired:
            split = block.reshape(chan_count, send, -1)
            split = lax.all_to_all(split, "chan", split_axis=0, concat_axis=0, tiled=True)
            return split.reshape(capacity, -1)
        return lax.ppermute(block, "chan", [(i, i ^ k) for i in range(chan_count)]) if k else block

    far_first = list(reversed(range(block_index.shape[0])))
    count = len(far_first)
    width = holes // HALVES
    route_row = route[0].reshape(1, rows)
    plan = (paired, chan_count, send, block_rows)
    leading = 128 if paired and count > 2 and block_rows > 128 else block_rows
    early = [(k, 0, block_rows, 0, width) for k in far_first if k or not paired]
    if leading < block_rows:
        early[:1] = [(early[0][0], 0, leading, 0, width), (early[0][0], leading, block_rows - leading, 0, width)]
    late = [(k, 0, block_rows, h * width, width) for h in range(1, HALVES) for k in far_first if k or not paired]
    late += [(0, 0, block_rows, 0, holes)] if paired else []
    target, *blocks = pack(plan + (early,), False, route_row, amps, "pack_first")
    arrived = {item: exchange(block, item[0]) for item, block in zip(early, blocks)}
    if paired:
        first = early[0]
        target, arrived[first] = lax.optimization_barrier((target, arrived[first]))
    blocks = pack(plan + (late,), True, target, amps, "pack_rest")
    arrived.update({item: exchange(block, item[0]) for item, block in zip(late, blocks)})

    part_column, hole_row = gap_part[0].reshape(rows, 1), gap_hole.reshape(1, holes)
    amps, blocks = lax.optimization_barrier((amps, blocks))
    pick, inverse = unpack_matrix(offsets, target.reshape(rows, 1), part_column, hole_row, capacity)

    parts, operator = prepare(ladder_weight[0], amps, weight, mixing, lad_count, sub_count)
    kept = [parts[-1]]
    for step in range(1, sub_count):
        pairs = [(i, (i + step) % sub_count) for i in range(sub_count)]
        kept.append(lax.ppermute(parts[sub_count - 1 - step], "sub", pairs))

    def chip_sum(position):
        picked = [lax.dynamic_index_in_dim(p, position, 0, keepdims=False) for p in kept]
        return sum(p.astype(F32) for p in picked)

    base = driving[0].astype(F32) + chip_sum(lad)
    terms = [chip_sum(lax.rem(lad + step, lad_count)).astype(BF16) for step in range(1, lad_count)]
    returned, crossed = [], []
    for half in range(HALVES):
        here = [item for item in early + late if item[3] == half * width or item[4] > width]
        blocks = [arrived[item] for item in here]
        if returned:
            blocks, made = lax.optimization_barrier((blocks, made))
        made = apply_cycle(half, plan, operator, [item[:2] for item in here], blocks, width)
        if not returned:
            behind, terms = lax.optimization_barrier((made[2:], terms))
            made = [*made[:2], *behind]
            for step, term in enumerate(terms, 1):
                pairs = [(i, (i + step) % lad_count) for i in range(lad_count)]
                crossed.append(lax.ppermute(term, "lad", pairs))
        else:
            behind, crossed = lax.optimization_barrier((made[0], crossed))
            made = [behind, *made[1:]]
        returned.append([exchange(block, k) for k, block in zip(far_first, made)])
    for term in crossed:
        base = base + term.astype(F32)
    updated = None
    for half in range(HALVES):
        updated = finish(half, pick, base, inverse, list(reversed(returned[half])), updated)
    return updated[None]


def solution(mesh):
    placed = (
        P(("parts", "chan"), ("lad", "sub"), None),
        P(("parts", "chan"), ("lad", "sub"), None),
        P("chan", ("lad", "sub"), None),
        P("chan", None, ("lad", "sub")),
        P("chan", ("lad", "sub"), None, None),
        P("chan", ("lad", "sub"), None, None, None),
        P(("parts", "chan"), ("lad", "sub")),
        P("parts"),
    )
    return jax.shard_map(
        body,
        mesh=mesh,
        in_specs=placed,
        out_specs=P(("parts", "chan"), ("lad", "sub"), None),
        check_vma=False,
    )
```
